32 devices in a mesh: seq: 8 (over z, y), frame: 4 (over x, core).
Axes of the slice: x: 2, y: 2, z: 4, core: 2. Of those that a mesh axis runs over, the one named last changes fastest.
Arguments:
- latents: float32 [24, 64, 1536], P('seq', 'frame'), may hold values from -6 to 6
- patch_feats: float32 [24, 2, 4, 256, 1536], P('seq', None, 'frame'), may hold values from -6 to 6
- image_counts: int32 [24], P('seq'), may hold values from 0 to 8, as said below
- time_index: int32 [24, 8], P('seq'), may hold values from 0 to 7
- query_proj: float32 [1536, 1536], P(('seq', 'frame')), may hold values from -0.15625 to 0.15625
- key_proj: float32 [1536, 1536], P(('seq', 'frame')), may hold values from -0.15625 to 0.15625
- value_proj: float32 [1536, 1536], P(('seq', 'frame')), may hold values from -0.15625 to 0.15625
- out_proj: float32 [1536, 1536], P(('seq', 'frame')), may hold values from -0.625 to 0.625
- up_proj: float32 [1536, 6144], P(('seq', 'frame')), may hold values from -0.15625 to 0.15625
- down_proj: float32 [6144, 1536], P(('seq', 'frame')), may hold values from -0.078125 to 0.078125
- media_gain: float32 [1536], P(('seq', 'frame')), may hold values from 0.1 to 1.9
- media_bias: float32 [1536], P(('seq', 'frame')), may hold values from -4 to 4
- latent_gain: float32 [1536], P(('seq', 'frame')), may hold values from 0.1 to 1.9
- latent_bias: float32 [1536], P(('seq', 'frame')), may hold values from -4 to 4
- feed_gain: float32 [1536], P(('seq', 'frame')), may hold values from 0.1 to 1.9
- feed_bias: float32 [1536], P(('seq', 'frame')), may hold values from -4 to 4
- time_table: float32 [8, 1536], P(None, ('seq', 'frame')), may hold values from -6 to 6
- out_cotangent: float32 [24, 64, 1536], P('seq', 'frame'), may hold values from -6 to 6
Outputs:
- new_latents: float32 [24, 64, 1536], P('seq', 'frame')
- latent_grads: float32 [24, 64, 1536], P('seq', 'frame')
- patch_grads: float32 [24, 2, 4, 256, 1536], P('seq', None, 'frame')
- grad_query: float32 [1536, 1536], P(('seq', 'frame'))
- grad_key: float32 [1536, 1536], P(('seq', 'frame'))
- grad_value: float32 [1536, 1536], P(('seq', 'frame'))
- grad_out: float32 [1536, 1536], P(('seq', 'frame'))
- grad_up: float32 [1536, 6144], P(('seq', 'frame'))
- grad_down: float32 [6144, 1536], P(('seq', 'frame'))
- grad_media_gain: float32 [1536], P(('seq', 'frame'))
- grad_media_bias: float32 [1536], P(('seq', 'frame'))
- grad_latent_gain: float32 [1536], P(('seq', 'frame'))
- grad_latent_bias: float32 [1536], P(('seq', 'frame'))
- grad_feed_gain: float32 [1536], P(('seq', 'frame'))
- grad_feed_bias: float32 [1536], P(('seq', 'frame'))
- grad_time_table: float32 [8, 1536], P(None, ('seq', 'frame'))
The draws below stay inside these ranges and needn't reach their ends.
Inputs may be any that keep to these rules, and one draw needn't show every extreme that they name: `image_counts`: each aligned block of 3 sequences holds one with 4 images or more, and some sequence has 8.
All inputs are finite; a program needn't handle non-finite values.
Results may differ from the reference program's by a relative error of at most 0.0003.
Values sent between devices are 32-bit elements; how exact they have to be, the bound alone decides.
A program may use at most 512 MiB of HBM per device.

```python
import math
import jax
import jax.numpy as jnp
from jax import lax

D = 1536
HEADS = 16
HEAD = 96
FF = 6144
LAT = 64
T_EMB = 8
SLOTS = 8
PATCHES = 256
SEQ_DEV = 3
SEQS = 24
ROUNDS = 2
N_FRAME = 4


def draw_image_counts(key, part):
    key = jax.random.fold_in(key, 11)
    base_key, pick_key, full_key, top_key = jax.random.split(key, 4)
    baseline = jax.random.randint(base_key, (SEQS,), 0, SLOTS + 1)
    groups = SEQS // SEQ_DEV
    picked = jax.random.randint(pick_key, (groups,), 0, SEQ_DEV)
    filled = jax.random.randint(full_key, (groups,), SLOTS // ROUNDS, SLOTS + 1)
    position = jnp.arange(SEQS)
    chosen = position % SEQ_DEV == picked[position // SEQ_DEV]
    counted = jnp.where(chosen, filled[position // SEQ_DEV], baseline)
    topmost = jax.random.randint(top_key, (), 0, SEQS)
    return jnp.where(position == topmost, SLOTS, counted).astype(jnp.int32)


def plant(values, stream_key, low, high):
    index_at = [jax.random.randint(jax.random.fold_in(stream_key, axis), (), 0, length) for axis, length in enumerate(values.shape)]
    widest = values.shape.index(max(values.shape))
    neighbour = index_at[:widest] + [(index_at[widest] + 1) % values.shape[widest]] + index_at[widest + 1:]
    return values.at[tuple(index_at)].set(low).at[tuple(neighbour)].set(high)


def shard_levels(key, extent, cuts, smallest, top_value):
    level, own = 1.0, jax.random.fold_in(key, 6)
    for axis_at, blocks in cuts:
        draws = jnp.exp(jax.random.uniform(jax.random.fold_in(own, axis_at), (blocks,), jnp.float32, smallest / len(cuts), top_value / len(cuts)))
        level = level * jnp.repeat(draws, extent[axis_at] // blocks).reshape([-1 if axis == axis_at else 1 for axis in range(len(extent))])
    return level


def normal_values(stream_key, shape, scale, bound, shards=(), kind=jnp.bfloat16):
    entries = jax.random.normal(stream_key, shape, jnp.float32) * scale
    if len(shards) > 0:
        entries = shard_levels(stream_key, shape, shards, -0.22, 0.18) * entries
    return jnp.clip(entries, min=-bound, max=bound).astype(kind)


def setup_inputs(seed: int = 0) -> dict:
    arg_keys = jax.random.split(jax.random.key(seed), 19)
    return {
        "latents": normal_values(arg_keys[0], (SEQS, LAT, D), 1.0, 6.0, ((0, 8), (1, 4)), jnp.float32),
        "patch_feats": normal_values(arg_keys[1], (SEQS, ROUNDS, N_FRAME, PATCHES, D), 1.0, 6.0, ((0, 8), (2, 4)), jnp.float32),
        "image_counts": draw_image_counts(jax.random.fold_in(arg_keys[18], 71), 0),
        "time_index": plant(jax.random.randint(arg_keys[3], (SEQS, SLOTS), 0, T_EMB), jax.random.fold_in(arg_keys[3], 1), 0, T_EMB - 1).astype(jnp.int32),
        "query_proj": normal_values(arg_keys[4], (D, D), D ** -0.5, 0.15625, ((0, 32),), jnp.float32),
        "key_proj": normal_values(arg_keys[5], (D, D), D ** -0.5, 0.15625, ((0, 32),), jnp.float32),
        "value_proj": normal_values(arg_keys[6], (D, D), D ** -0.5, 0.15625, ((0, 32),), jnp.float32),
        "out_proj": normal_values(arg_keys[7], (D, D), (D // 16) ** -0.5, 0.625, ((0, 32),), jnp.float32),
        "up_proj": normal_values(arg_keys[8], (D, FF), D ** -0.5, 0.15625, ((0, 32),), jnp.float32),
        "down_proj": normal_values(arg_keys[9], (FF, D), FF ** -0.5, 0.078125, ((0, 32),), jnp.float32),
        "media_gain": jnp.clip(1.0 + 0.18 * jax.random.normal(arg_keys[10], (D,), jnp.float32), 0.1, 1.9),
        "media_bias": normal_values(arg_keys[11], (D,), 0.3, 4.0, ((0, 32),), jnp.float32),
        "latent_gain": jnp.clip(1.0 + 0.18 * jax.random.normal(arg_keys[12], (D,), jnp.float32), 0.1, 1.9),
        "latent_bias": normal_values(arg_keys[13], (D,), 0.3, 4.0, ((0, 32),), jnp.float32),
        "feed_gain": jnp.clip(1.0 + 0.18 * jax.random.normal(arg_keys[14], (D,), jnp.float32), 0.1, 1.9),
        "feed_bias": normal_values(arg_keys[15], (D,), 0.3, 4.0, ((0, 32),), jnp.float32),
        "time_table": normal_values(arg_keys[16], (T_EMB, D), 0.5, 6.0, ((1, 32),), jnp.float32),
        "out_cotangent": normal_values(arg_keys[17], (SEQS, LAT, D), 1.0, 6.0, ((0, 8), (1, 4)), jnp.float32),
    }


@jax.custom_vjp
def low(v):
    return lax.optimization_barrier(v.astype(jnp.bfloat16)).astype(jnp.float32)

@jax.custom_vjp
def low_back(v):
    return v

def low_keep(v):
    return (low(v), None)

def low_pass(kept, grad):
    return (grad,)

def back_keep(v):
    return (v, None)

def back_low(kept, grad):
    return (low(grad),)
low.defvjp(low_keep, low_pass)
low_back.defvjp(back_keep, back_low)
HIGHEST = lax.Precision.HIGHEST
EPSILON = 1e-05
MASKED = -1e+30

def product(left, right):
    return jnp.dot(left, right, precision=HIGHEST, preferred_element_type=jnp.float32)

def layer_norm(values, gain_vec, bias_vec):
    centred = values - lax.optimization_barrier(jnp.mean(values, axis=-1, keepdims=True))
    inv_std = lax.rsqrt(lax.optimization_barrier(jnp.mean(centred * centred, axis=-1, keepdims=True)) + EPSILON)
    return centred * inv_std * gain_vec + bias_vec

def one_sequence(weights, latent_in, media_in, count, times):
    query_proj, key_proj, value_proj, out_proj, up_proj, down_proj, media_gain, media_bias, latent_gain, latent_bias, feed_gain, feed_bias, time_table = weights
    slot_numbers = jnp.arange(SLOTS, dtype=jnp.int32)
    present = slot_numbers < count
    one_hot = (times[:, None] == jnp.arange(T_EMB, dtype=jnp.int32)[None, :]).astype(jnp.float32)
    slot_embed = product(one_hot, time_table)
    embedded = media_in + slot_embed[:, None, :]
    media_normed = layer_norm(embedded, media_gain, media_bias).reshape(SLOTS * PATCHES, D)
    latent_normed = layer_norm(latent_in, latent_gain, latent_bias)
    queries = product(latent_normed, query_proj)
    inputs = jnp.concatenate([latent_normed, media_normed], axis=0)
    keys = product(inputs, key_proj)
    values = product(inputs, value_proj)
    keep = jnp.concatenate([jnp.ones((LAT,), dtype=bool), jnp.repeat(present, PATCHES)])
    query_heads = queries.reshape(LAT, HEADS, HEAD)
    key_heads = keys.reshape(-1, HEADS, HEAD)
    value_heads = values.reshape(-1, HEADS, HEAD)
    scores = jnp.einsum('qhe,khe->hqk', query_heads, key_heads, precision=HIGHEST) * (1.0 / math.sqrt(HEAD))
    scores = jnp.where(keep[None, None, :], scores, MASKED)
    row_top = lax.optimization_barrier(jnp.max(scores, axis=-1, keepdims=True))
    expo = jnp.exp(scores - row_top)
    prob = expo / lax.optimization_barrier(jnp.sum(expo, axis=-1, keepdims=True))
    attended = jnp.einsum('hqk,khe->qhe', prob, value_heads, precision=HIGHEST).reshape(LAT, D)
    middle = latent_in + product(attended, out_proj)
    hidden = product(layer_norm(middle, feed_gain, feed_bias), up_proj)
    return middle + product(jax.nn.gelu(hidden), down_proj)

def reference(latents, patch_feats, image_counts, time_index, query_proj, key_proj, value_proj, out_proj, up_proj, down_proj, media_gain, media_bias, latent_gain, latent_bias, feed_gain, feed_bias, time_table, out_cotangent):
    params = (query_proj, key_proj, value_proj, out_proj, up_proj, down_proj, media_gain, media_bias, latent_gain, latent_bias, feed_gain, feed_bias, time_table)
    slots_all = patch_feats.reshape(SEQS, SLOTS, PATCHES, D)

    def forward(weights, latent_all, media_all):
        stepper = jax.checkpoint(one_sequence)

        def per_sequence(element):
            return stepper(weights, element[0], element[1], element[2], element[3])
        return lax.map(per_sequence, (latent_all, media_all, image_counts, time_index))
    new_latents, puller = jax.vjp(forward, params, latents, slots_all)
    param_grads, latent_grads, media_grads = puller(out_cotangent)
    return (new_latents, latent_grads, media_grads.reshape(patch_feats.shape), param_grads[0], param_grads[1], param_grads[2], param_grads[3], param_grads[4], param_grads[5], param_grads[6], param_grads[7], param_grads[8], param_grads[9], param_grads[10], param_grads[11], param_grads[12])
```

```python
import functools
import math

import jax
import jax.numpy as jnp
from jax import lax
from jax.experimental import pallas as pl
from jax.experimental.pallas import tpu as pltpu
from jax.sharding import PartitionSpec as P

HEADS = 16


HIGHEST = lax.Precision.HIGHEST
EPSILON = 1e-05
MASKED = -1e30


def product(left, right):
    return jnp.dot(left, right, precision=HIGHEST, preferred_element_type=jnp.float32)


def product_tn(left, right):
    return lax.dot_general(
        left, right, (((0,), (0,)), ((), ())), precision=HIGHEST, preferred_element_type=jnp.float32
    )


def product_nt(left, right):
    return lax.dot_general(
        left, right, (((1,), (1,)), ((), ())), precision=HIGHEST, preferred_element_type=jnp.float32
    )


def flatten(values):
    return values.reshape(-1, values.shape[-1])


def norm_forward(values, gain_vec, bias_vec):
    centred = values - jnp.mean(values, axis=-1, keepdims=True)
    inv_std = lax.rsqrt(jnp.mean(centred * centred, axis=-1, keepdims=True) + EPSILON)
    unit_vals = centred * inv_std
    return (unit_vals * gain_vec + bias_vec, unit_vals, inv_std)


def norm_backward(incoming, unit_vals, inv_std, gain_vec):
    scaled = incoming * gain_vec
    result = inv_std * (
        scaled
        - jnp.mean(scaled, axis=-1, keepdims=True)
        - unit_vals * jnp.mean(scaled * unit_vals, axis=-1, keepdims=True)
    )
    flat_in = flatten(incoming)
    return (result, jnp.sum(flat_in * flatten(unit_vals), axis=0), jnp.sum(flat_in, axis=0))


def heads_last(stats):
    return jnp.transpose(stats, (0, 2, 1))[..., None]


def per_slot(action, operands):
    return lax.map(action, operands)


def body_general(
    latents,
    patch_feats,
    image_counts,
    time_index,
    query_proj,
    key_proj,
    value_proj,
    out_proj,
    up_proj,
    down_proj,
    media_gain,
    media_bias,
    latent_gain,
    latent_bias,
    feed_gain,
    feed_bias,
    time_table,
    out_cotangent,
):
    gathered = (
        lax.all_gather(query_proj, ("seq", "frame"), axis=0, tiled=True),
        lax.all_gather(key_proj, ("seq", "frame"), axis=0, tiled=True),
        lax.all_gather(value_proj, ("seq", "frame"), axis=0, tiled=True),
        lax.all_gather(out_proj, ("seq", "frame"), axis=0, tiled=True),
        lax.all_gather(up_proj, ("seq", "frame"), axis=0, tiled=True),
        lax.all_gather(down_proj, ("seq", "frame"), axis=0, tiled=True),
        lax.all_gather(media_gain, ("seq", "frame"), axis=0, tiled=True),
        lax.all_gather(media_bias, ("seq", "frame"), axis=0, tiled=True),
        lax.all_gather(latent_gain, ("seq", "frame"), axis=0, tiled=True),
        lax.all_gather(latent_bias, ("seq", "frame"), axis=0, tiled=True),
        lax.all_gather(feed_gain, ("seq", "frame"), axis=0, tiled=True),
        lax.all_gather(feed_bias, ("seq", "frame"), axis=0, tiled=True),
        lax.all_gather(time_table, ("seq", "frame"), axis=1, tiled=True),
    )
    gathered = lax.optimization_barrier(gathered)
    (
        query_full,
        key_full,
        value_full,
        out_full,
        up_full,
        down_full,
        mgain_full,
        mbias_full,
        lgain_full,
        lbias_full,
        fgain_full,
        fbias_full,
        table_full,
    ) = gathered
    frame_index = lax.axis_index("frame")
    frame_count = lax.axis_size("frame")
    seq_local, lat_rows, model_width = latents.shape
    round_count = patch_feats.shape[1]
    patch_count = patch_feats.shape[3]
    slot_total = time_index.shape[1]
    table_rows = time_table.shape[0]
    latent_total = lat_rows * frame_count
    head_size = model_width // HEADS
    inv_root = 1.0 / math.sqrt(head_size)
    latent_all = lax.all_gather(latents, "frame", axis=1, tiled=True)
    latent_norm, latent_unit, latent_std = norm_forward(latent_all, lgain_full, lbias_full)
    row_start = frame_index * lat_rows
    own_norm = lax.dynamic_slice_in_dim(latent_norm, row_start, lat_rows, 1)
    own_unit = lax.dynamic_slice_in_dim(latent_unit, row_start, lat_rows, 1)
    own_std = lax.dynamic_slice_in_dim(latent_std, row_start, lat_rows, 1)
    queries = product(flatten(latent_norm), query_full).reshape(
        seq_local, latent_total, model_width
    )
    own_keys = product(flatten(own_norm), key_full).reshape(seq_local, lat_rows, model_width)
    own_values = product(flatten(own_norm), value_full).reshape(seq_local, lat_rows, model_width)
    slot_ids = jnp.arange(round_count, dtype=jnp.int32) * frame_count + frame_index
    present = slot_ids[None, :] < image_counts[:, None]
    picks = jnp.arange(slot_total, dtype=jnp.int32)[None, :] == slot_ids[:, None]
    slot_times = jnp.sum(jnp.where(picks[None, :, :], time_index[:, None, :], 0), axis=-1)
    one_hot = (
        slot_times.reshape(-1)[:, None] == jnp.arange(table_rows, dtype=jnp.int32)[None, :]
    ).astype(jnp.float32)
    slot_embed = product(one_hot, table_full)
    slot_feats = patch_feats.reshape(seq_local * round_count, patch_count, model_width)

    def media_forward(element):
        normed, unit_part, std_part = norm_forward(
            element[0] + element[1][None, :], mgain_full, mbias_full
        )
        return (normed, unit_part, std_part, product(normed, key_full), product(normed, value_full))

    media_norm, media_unit, media_std, media_keys, media_values = per_slot(
        media_forward, (slot_feats, slot_embed)
    )
    key_total = lat_rows + round_count * patch_count
    all_keys = jnp.concatenate(
        [own_keys, media_keys.reshape(seq_local, round_count * patch_count, model_width)], axis=1
    )
    all_values = jnp.concatenate(
        [own_values, media_values.reshape(seq_local, round_count * patch_count, model_width)],
        axis=1,
    )
    keep = jnp.concatenate(
        [jnp.ones((seq_local, lat_rows), dtype=bool), jnp.repeat(present, patch_count, axis=1)],
        axis=1,
    )
    query_four = queries.reshape(seq_local, latent_total, HEADS, head_size)
    key_four = all_keys.reshape(seq_local, key_total, HEADS, head_size)
    value_four = all_values.reshape(seq_local, key_total, HEADS, head_size)

    def masked_scores():
        raw_scores = (
            jnp.einsum(
                "bqhe,bkhe->bhqk",
                query_four,
                key_four,
                precision=HIGHEST,
                preferred_element_type=jnp.float32,
            )
            * inv_root
        )
        return jnp.where(keep[:, None, None, :], raw_scores, MASKED)

    scores = masked_scores()
    row_top = jnp.max(scores, axis=-1)
    expo = jnp.exp(scores - row_top[..., None])
    row_total = jnp.sum(expo, axis=-1)
    partial_out = jnp.einsum(
        "bhqk,bkhe->bqhe", expo, value_four, precision=HIGHEST, preferred_element_type=jnp.float32
    )
    glob_top = lax.pmax(row_top, "frame")
    ratio = jnp.exp(row_top - glob_top)
    glob_total, glob_out = lax.psum((row_total * ratio, partial_out * heads_last(ratio)), "frame")
    attended = glob_out / heads_last(glob_total)
    log_total = glob_top + jnp.log(glob_total)
    attended_flat = attended.reshape(seq_local, latent_total, model_width)
    own_attended = lax.dynamic_slice_in_dim(attended_flat, row_start, lat_rows, 1)
    middle = latents + product(flatten(own_attended), out_full).reshape(
        seq_local, lat_rows, model_width
    )
    feed_norm, feed_unit, feed_std = norm_forward(middle, fgain_full, fbias_full)
    hidden_pre = product(flatten(feed_norm), up_full)
    activated, gelu_pull = jax.vjp(jax.nn.gelu, hidden_pre)
    new_latents = middle + product(activated, down_full).reshape(seq_local, lat_rows, model_width)
    regathered = (
        lax.all_gather(query_proj, ("seq", "frame"), axis=0, tiled=True),
        lax.all_gather(key_proj, ("seq", "frame"), axis=0, tiled=True),
        lax.all_gather(value_proj, ("seq", "frame"), axis=0, tiled=True),
        lax.all_gather(out_proj, ("seq", "frame"), axis=0, tiled=True),
        lax.all_gather(up_proj, ("seq", "frame"), axis=0, tiled=True),
        lax.all_gather(down_proj, ("seq", "frame"), axis=0, tiled=True),
        lax.all_gather(media_gain, ("seq", "frame"), axis=0, tiled=True),
        lax.all_gather(media_bias, ("seq", "frame"), axis=0, tiled=True),
        lax.all_gather(latent_gain, ("seq", "frame"), axis=0, tiled=True),
        lax.all_gather(latent_bias, ("seq", "frame"), axis=0, tiled=True),
        lax.all_gather(feed_gain, ("seq", "frame"), axis=0, tiled=True),
        lax.all_gather(feed_bias, ("seq", "frame"), axis=0, tiled=True),
        lax.all_gather(time_table, ("seq", "frame"), axis=1, tiled=True),
    )
    regathered = lax.optimization_barrier(regathered)
    query_back = regathered[0]
    key_back = regathered[1]
    value_back = regathered[2]
    out_back = regathered[3]
    up_back = regathered[4]
    down_back = regathered[5]
    mgain_back = regathered[6]
    lgain_back = regathered[8]
    fgain_back = regathered[10]
    cotangent = flatten(out_cotangent)
    grad_down = product_tn(activated, cotangent)
    grad_hidden = gelu_pull(product_nt(cotangent, down_back))[0]
    grad_up = product_tn(flatten(feed_norm), grad_hidden)
    grad_feed_norm = product_nt(grad_hidden, up_back).reshape(seq_local, lat_rows, model_width)
    grad_mid_norm, grad_fgain, grad_fbias = norm_backward(
        grad_feed_norm, feed_unit, feed_std, fgain_back
    )
    grad_middle = out_cotangent + grad_mid_norm
    grad_out_w = product_tn(flatten(own_attended), flatten(grad_middle))
    grad_own_att = product_nt(flatten(grad_middle), out_back).reshape(
        seq_local, lat_rows, model_width
    )
    grad_attended = lax.all_gather(grad_own_att, "frame", axis=1, tiled=True)
    grad_four = grad_attended.reshape(seq_local, latent_total, HEADS, head_size)
    delta_rows = jnp.einsum(
        "bqhe,bqhe->bhq", grad_four, attended, precision=HIGHEST, preferred_element_type=jnp.float32
    )
    probs = jnp.exp(masked_scores() - log_total[..., None])
    grad_probs = jnp.einsum(
        "bqhe,bkhe->bhqk",
        grad_four,
        value_four,
        precision=HIGHEST,
        preferred_element_type=jnp.float32,
    )
    grad_scores = probs * (grad_probs - delta_rows[..., None]) * inv_root
    grad_query_part = jnp.einsum(
        "bhqk,bkhe->bqhe",
        grad_scores,
        key_four,
        precision=HIGHEST,
        preferred_element_type=jnp.float32,
    ).reshape(seq_local, latent_total, model_width)
    grad_keys = jnp.einsum(
        "bhqk,bqhe->bkhe",
        grad_scores,
        query_four,
        precision=HIGHEST,
        preferred_element_type=jnp.float32,
    ).reshape(seq_local, key_total, model_width)
    grad_values = jnp.einsum(
        "bhqk,bqhe->bkhe", probs, grad_four, precision=HIGHEST, preferred_element_type=jnp.float32
    ).reshape(seq_local, key_total, model_width)
    grad_query_own = lax.psum_scatter(grad_query_part, "frame", scatter_dimension=1, tiled=True)
    grad_key_lat = flatten(grad_keys[:, :lat_rows])
    grad_value_lat = flatten(grad_values[:, :lat_rows])
    grad_key_media = grad_keys[:, lat_rows:].reshape(
        seq_local * round_count, patch_count, model_width
    )
    grad_value_media = grad_values[:, lat_rows:].reshape(
        seq_local * round_count, patch_count, model_width
    )
    grad_query_w = product_tn(flatten(own_norm), flatten(grad_query_own))
    grad_key_w = product_tn(flatten(own_norm), grad_key_lat) + product_tn(
        flatten(media_norm), flatten(grad_key_media)
    )
    grad_value_w = product_tn(flatten(own_norm), grad_value_lat) + product_tn(
        flatten(media_norm), flatten(grad_value_media)
    )
    grad_own_norm = (
        product_nt(flatten(grad_query_own), query_back)
        + product_nt(grad_key_lat, key_back)
        + product_nt(grad_value_lat, value_back)
    ).reshape(seq_local, lat_rows, model_width)
    grad_lat_in, grad_lgain, grad_lbias = norm_backward(
        grad_own_norm, own_unit, own_std, lgain_back
    )
    latent_grads = grad_middle + grad_lat_in

    def media_backward(element):
        normed_grad = product_nt(element[0], key_back) + product_nt(element[1], value_back)
        feats_grad, gain_part, bias_part = norm_backward(
            normed_grad, element[2], element[3], mgain_back
        )
        return (feats_grad, gain_part, bias_part, jnp.sum(feats_grad, axis=0))

    feats_grads, gain_parts, bias_parts, slot_sums = per_slot(
        media_backward, (grad_key_media, grad_value_media, media_unit, media_std)
    )
    grad_mgain = jnp.sum(gain_parts, axis=0)
    grad_mbias = jnp.sum(bias_parts, axis=0)
    grad_table = product_tn(one_hot, slot_sums)
    patch_grads = feats_grads.reshape(patch_feats.shape)
    (
        grad_query_w,
        grad_key_w,
        grad_value_w,
        grad_out_w,
        grad_up,
        grad_down,
    ) = lax.optimization_barrier(
        (grad_query_w, grad_key_w, grad_value_w, grad_out_w, grad_up, grad_down)
    )
    summed = (
        lax.psum_scatter(grad_query_w, ("seq", "frame"), scatter_dimension=0, tiled=True),
        lax.psum_scatter(grad_key_w, ("seq", "frame"), scatter_dimension=0, tiled=True),
        lax.psum_scatter(grad_value_w, ("seq", "frame"), scatter_dimension=0, tiled=True),
        lax.psum_scatter(grad_out_w, ("seq", "frame"), scatter_dimension=0, tiled=True),
        lax.psum_scatter(grad_up, ("seq", "frame"), scatter_dimension=0, tiled=True),
        lax.psum_scatter(grad_down, ("seq", "frame"), scatter_dimension=0, tiled=True),
        lax.psum_scatter(grad_mgain, ("seq", "frame"), scatter_dimension=0, tiled=True),
        lax.psum_scatter(grad_mbias, ("seq", "frame"), scatter_dimension=0, tiled=True),
        lax.psum_scatter(grad_lgain, ("seq", "frame"), scatter_dimension=0, tiled=True),
        lax.psum_scatter(grad_lbias, ("seq", "frame"), scatter_dimension=0, tiled=True),
        lax.psum_scatter(grad_fgain, ("seq", "frame"), scatter_dimension=0, tiled=True),
        lax.psum_scatter(grad_fbias, ("seq", "frame"), scatter_dimension=0, tiled=True),
        lax.psum_scatter(grad_table, ("seq", "frame"), scatter_dimension=1, tiled=True),
    )
    return (
        new_latents,
        latent_grads,
        patch_grads,
        summed[0],
        summed[1],
        summed[2],
        summed[3],
        summed[4],
        summed[5],
        summed[6],
        summed[7],
        summed[8],
        summed[9],
        summed[10],
        summed[11],
        summed[12],
    )


MESH = pl.DeviceIdType.MESH
F32 = jnp.float32
ANY = pl.BlockSpec(memory_space=pl.ANY)
GRID = (4, 2, 2, 2)


def place(z, y, x, c):
    return (z * 2 + y, x * 2 + c)


class Here:
    def __init__(self):
        seq, frame = lax.axis_index("seq"), lax.axis_index("frame")
        self.z, self.y, self.x, self.c = z, y, x, c = seq // 2, seq % 2, frame // 2, frame % 2
        self.ox, self.oy, self.oc = ox, oy, oc = 1 - x, 1 - y, 1 - c
        self.at_x, self.at_y, self.at_c = place(z, y, ox, c), place(z, oy, x, c), place(z, y, x, oc)
        self.ahead = [lax.rem(z + k, 4) for k in range(4)]
        self.behind = [lax.rem(z + 4 - k, 4) for k in range(4)]
        self.at_z = [place(o, y, x, c) for o in self.ahead]

    def greet(self):
        barrier = pltpu.get_barrier_semaphore()
        for peer in self.at_z[1:] + [self.at_x, self.at_y, self.at_c]:
            pl.semaphore_signal(barrier, inc=1, device_id=peer, device_id_type=MESH)
        pl.semaphore_wait(barrier, 6)


def remote(src, dst, send_sem, recv_sem, peer):
    return pltpu.make_async_remote_copy(
        src_ref=src, dst_ref=dst, send_sem=send_sem, recv_sem=recv_sem, device_id=peer, device_id_type=MESH
    )


class Gather:
    def __init__(self, here, shards, fulls, cuts, sems):
        self.here, self.count = here, len(cuts)
        self.loc, self.zs, self.zr, self.xs, self.xr, self.ys, self.yr, self.ds, self.dr, self.cs, self.cr = sems
        self.shard = [shards[a].at[:, lo:hi] for a, lo, hi in cuts]
        self.full = [(lambda *at, a=a, lo=lo, hi=hi: fulls[a].at[at + (slice(lo, hi),)]) for a, lo, hi in cuts]
        self.half = [shards[a].shape[0] // 2 for a, lo, hi in cuts]

    @staticmethod
    def semaphores(count):
        dma = pltpu.SemaphoreType.DMA
        shapes = [(), (3,), (3,), (4,), (4,), (4,), (4,), (2, 4), (2, 4), (4,), (4,)]
        return [dma((count,) + s) for s in shapes]

    def local(self, p):
        h = self.here
        return pltpu.make_async_copy(self.shard[p], self.full[p](h.z, h.y, h.x, h.c, slice(None)), self.loc.at[p])

    def over_z(self, p, k):
        h = self.here
        dst = self.full[p](h.z, h.y, h.x, h.c, slice(None))
        return remote(self.shard[p], dst, self.zs.at[p, k - 1], self.zr.at[p, k - 1], h.at_z[k])

    def over_x(self, p, k):
        h = self.here
        block = self.full[p](h.behind[k], h.y, h.x, h.c, slice(None))
        return remote(self.shard[p] if k == 0 else block, block, self.xs.at[p, k], self.xr.at[p, k], h.at_x)

    def over_y(self, p, k):
        h = self.here
        block = self.full[p](h.behind[k], h.y, h.x, h.c, slice(None))
        return remote(self.shard[p] if k == 0 else block, block, self.ys.at[p, k], self.yr.at[p, k], h.at_y)

    def on_y(self, p, k):
        h = self.here
        part = self.full[p](h.behind[k], h.y, h.ox, h.c, slice(self.half[p], 2 * self.half[p]))
        return remote(part, part, self.ds.at[p, 0, k], self.dr.at[p, 0, k], h.at_y)

    def on_x(self, p, k):
        h = self.here
        part = self.full[p](h.behind[k], h.oy, h.x, h.c, slice(0, self.half[p]))
        return remote(part, part, self.ds.at[p, 1, k], self.dr.at[p, 1, k], h.at_x)

    def to_core(self, p, i):
        h = self.here
        yy, xx = ((h.y, h.x), (h.y, h.ox), (h.oy, h.x), (h.oy, h.ox))[i]
        blocks = self.full[p](slice(None), yy, xx, h.c, slice(None))
        return remote(blocks, blocks, self.cs.at[p, i], self.cr.at[p, i], h.at_c)

    def own(self, p):
        self.local(p).start()
        for k in (1, 2, 3):
            self.over_z(p, k).start()
        self.over_x(p, 0).start()
        self.over_y(p, 0).start()

    def along_z(self, p):
        for k in (1, 2, 3):
            self.over_z(p, k).wait_recv()
            self.over_x(p, k).start()
            self.over_y(p, k).start()

    def across(self, p):
        for k in range(4):
            self.over_x(p, k).wait_recv()
            self.on_y(p, k).start()
            self.over_y(p, k).wait_recv()
            self.on_x(p, k).start()
        self.local(p).wait()
        for i in range(3):
            self.to_core(p, i).start()

    def corner(self, p):
        for k in range(4):
            self.on_y(p, k).wait_recv()
            self.on_x(p, k).wait_recv()
        self.to_core(p, 3).start()

    def done(self, p):
        for i in range(4):
            self.to_core(p, i).wait()
        for k in (1, 2, 3):
            self.over_z(p, k).wait_send()
        for k in range(4):
            for copy in (self.over_x, self.over_y, self.on_x, self.on_y):
                copy(p, k).wait_send()

    def stages(self):
        return (self.own, self.along_z, self.across, self.corner)


LAG = 2


def waves_of(plan):
    stages = plan.stages()
    order = [0] + list(range(len(stages) - 1, 0, -1))
    return [
        [functools.partial(stages[s], t - s * LAG) for s in order if 0 <= t - s * LAG < plan.count]
        for t in range(plan.count + (len(stages) - 1) * LAG)
    ]


def finish_all(plan):
    for p in range(plan.count):
        plan.done(p)


class Scatter:
    def __init__(self, here, count, mine, theirs, load, out, scratch):
        self.here, self.count, self.mine, self.theirs, self.load, self.out = here, count, mine, theirs, load, out
        self.got, self.gx, self.gy, self.hx, self.hy, self.gz = scratch[:6]
        self.cs, self.cr, self.fs, self.fr, self.ss, self.sr, self.zs, self.zr = scratch[6:]
        self.half = self.got.shape[-2] // 2

    @staticmethod
    def scratch(count, r, w):
        dma = pltpu.SemaphoreType.DMA
        leads = [(4, 2, 2, r), (4, 2, r // 2), (4, 2, r // 2), (4, r // 2), (4, r // 2), (3, r)]
        return [pltpu.VMEM((count,) + s + (w,), F32) for s in leads] + [
            dma((count,) + s) for s in ((), (), (2,), (2,), (2,), (2,), (3,), (3,))
        ]

    def to_core(self, p):
        return remote(self.theirs(p), self.got.at[p], self.cs.at[p], self.cr.at[p], self.here.at_c)

    def first(self, p, way):
        h, half, tot = self.here, self.half, self.mine(p)
        if way == 0:
            return remote(tot.at[:, :, h.ox, :half], self.gx.at[p], self.fs.at[p, 0], self.fr.at[p, 0], h.at_x)
        return remote(tot.at[:, h.oy, :, half:], self.gy.at[p], self.fs.at[p, 1], self.fr.at[p, 1], h.at_y)

    def second(self, p, way):
        h, half, tot = self.here, self.half, self.mine(p)
        if way == 0:
            return remote(tot.at[:, h.oy, h.x, :half], self.hy.at[p], self.ss.at[p, 0], self.sr.at[p, 0], h.at_y)
        return remote(tot.at[:, h.y, h.ox, half:], self.hx.at[p], self.ss.at[p, 1], self.sr.at[p, 1], h.at_x)

    def over_z(self, p, k):
        h = self.here
        src = self.mine(p).at[h.ahead[k], h.y, h.x]
        return remote(src, self.gz.at[p, k - 1], self.zs.at[p, k - 1], self.zr.at[p, k - 1], h.at_z[k])

    def start(self, p):
        if self.load is not None:
            self.load(p).start()
        self.to_core(p).start()

    def cores(self, p):
        tot, got = self.mine(p), self.got.at[p]
        if self.load is not None:
            self.load(p).wait()
        self.to_core(p).wait_recv()

        @pl.loop(0, 16)
        def _(i):
            at = (i // 4, (i // 2) % 2, i % 2)
            tot[at] = tot[at] + got[at]

        self.first(p, 0).start()
        self.first(p, 1).start()

    def sides(self, p):
        h, half, tot = self.here, self.half, self.mine(p)
        gx, gy = self.gx.at[p], self.gy.at[p]
        self.first(p, 0).wait_recv()

        @pl.loop(0, 8)
        def _(i):
            zi, yi = i // 2, i % 2
            tot[zi, yi, h.x, :half] = tot[zi, yi, h.x, :half] + gx[zi, yi]

        self.second(p, 0).start()
        self.first(p, 1).wait_recv()

        @pl.loop(0, 8)
        def _(i):
            zi, xi = i // 2, i % 2
            tot[zi, h.y, xi, half:] = tot[zi, h.y, xi, half:] + gy[zi, xi]

        self.second(p, 1).start()

    def column(self, p):
        h, half, tot = self.here, self.half, self.mine(p)
        hx, hy = self.hx.at[p], self.hy.at[p]
        self.second(p, 0).wait_recv()
        self.second(p, 1).wait_recv()

        @pl.loop(0, 4)
        def _(zi):
            tot[zi, h.y, h.x, :half] = tot[zi, h.y, h.x, :half] + hy[zi]
            tot[zi, h.y, h.x, half:] = tot[zi, h.y, h.x, half:] + hx[zi]

        for k in (1, 2, 3):
            self.over_z(p, k).start()

    def finish(self, p):
        h, gz = self.here, self.gz.at[p]
        for k in (1, 2, 3):
            self.over_z(p, k).wait_recv()
        self.out(p)[...] = (self.mine(p)[h.z, h.y, h.x] + gz[0]) + (gz[1] + gz[2])

    def done(self, p):
        self.to_core(p).wait_send()
        for way in (0, 1):
            self.first(p, way).wait_send()
            self.second(p, way).wait_send()
        for k in (1, 2, 3):
            self.over_z(p, k).wait_send()

    def stages(self):
        return (self.start, self.cores, self.sides, self.column, self.finish)


def run(wave):
    for action in wave:
        action()


def run_tick(step, steps, part, parts, waves):
    ticks, total, before, starts = steps * parts, sum(len(w) for w in waves), 0, []
    for wave in waves:
        starts.append(ticks * before // total)
        before += len(wave)
    for tick in range(part, ticks, parts):
        now = [wave for wave, start in zip(waves, starts) if start == tick]
        if now:

            @pl.when(step == tick // parts)
            def _():
                for wave in now:
                    run(wave)


def run_last(step, steps, plan):
    @pl.when(step == steps - 1)
    def _():
        finish_all(plan)


def column_cuts(widths, pieces):
    return [(a, w * i // n, w * (i + 1) // n) for a, (w, n) in enumerate(zip(widths, pieces)) for i in range(n)]


class GroupGather:
    def __init__(self, here, shards, fulls, sems):
        self.here, self.shards, self.fulls, self.count = here, shards, fulls, len(shards)
        self.loc, self.ss, self.rs = sems

    @staticmethod
    def semaphores(count):
        dma = pltpu.SemaphoreType.DMA
        return [dma((count,)), dma((count, 3)), dma((count, 3))]

    def local(self, a):
        h = self.here
        return pltpu.make_async_copy(self.shards[a], self.fulls[a].at[:, h.x * 2 + h.c], self.loc.at[a])

    def copy(self, a, i):
        h = self.here
        mine = self.fulls[a].at[:, h.x * 2 + h.c]
        if i < 2:
            return remote(self.shards[a], mine, self.ss.at[a, i], self.rs.at[a, i], (h.at_x, h.at_c)[i])
        block = self.fulls[a].at[:, h.ox * 2 + h.c]
        return remote(block, block, self.ss.at[a, 2], self.rs.at[a, 2], h.at_c)

    def start(self):
        for a in range(self.count):
            self.local(a).start()
            self.copy(a, 0).start()
            self.copy(a, 1).start()

    def forward(self):
        for a in range(self.count):
            self.copy(a, 0).wait_recv()
            self.copy(a, 2).start()

    def done(self):
        for a in range(self.count):
            self.local(a).wait()
            self.copy(a, 0).wait_send()
            self.copy(a, 1).wait()
            self.copy(a, 2).wait()


def first_kernel(count, cuts, *refs):
    here = Here()
    group = GroupGather(here, refs[count : count + 1], refs[2 * count + 1 : 2 * count + 2], refs[-3:])
    plan = Gather(here, refs[:count], refs[count + 1 : 2 * count + 1], cuts, refs[2 * count + 2 : -3])
    waves = waves_of(plan)
    waves[0] = [here.greet, group.start] + waves[0]
    waves[3].append(group.forward)
    for wave in waves:
        run(wave)
    group.done()
    finish_all(plan)


def gather_first(shards, pieces, rows, collective_id):
    count = len(shards)
    cuts = column_cuts([s.shape[1] for s in shards], pieces)
    s, r, w = rows.shape
    *outs, group = pl.pallas_call(
        functools.partial(first_kernel, count, cuts),
        out_shape=full_shapes(shards) + [jax.ShapeDtypeStruct((s, 4, r, w), F32)],
        in_specs=[ANY] * (count + 1),
        out_specs=[ANY] * (count + 1),
        scratch_shapes=Gather.semaphores(len(cuts)) + GroupGather.semaphores(1),
        compiler_params=pltpu.CompilerParams(collective_id=collective_id, has_side_effects=True),
        name="gather_first",
    )(*shards, rows)
    return [flat_full(o) for o in outs], group


def flat_full(full):
    return full.reshape((-1, full.shape[-1]))


def full_shapes(shards):
    return [jax.ShapeDtypeStruct(GRID + s.shape, s.dtype) for s in shards]


def gather_kernel(count, cuts, *refs):
    here = Here()
    here.greet()
    plan = Gather(here, refs[:count], refs[count : 2 * count], cuts, refs[2 * count :])
    for wave in waves_of(plan):
        run(wave)
    finish_all(plan)


def gather_all(shards, pieces, collective_id):
    count = len(shards)
    cuts = column_cuts([s.shape[1] for s in shards], pieces)
    outs = pl.pallas_call(
        functools.partial(gather_kernel, count, cuts),
        out_shape=full_shapes(shards),
        in_specs=[ANY] * count,
        out_specs=[ANY] * count,
        scratch_shapes=Gather.semaphores(len(cuts)),
        compiler_params=pltpu.CompilerParams(collective_id=collective_id, has_side_effects=True),
        name="gather_all",
    )(*shards)
    return [flat_full(o) for o in outs]


class Summed:
    def __init__(self, parts, pieces):
        self.arrays, self.pieces = len(parts), pieces
        self.rows, self.width = parts[0].shape[0] // 32, parts[0].shape[1]
        self.cut = self.width // pieces
        self.operands = [p.reshape(GRID + (self.rows, self.width)) for p in parts]
        self.in_specs = [ANY] * len(parts)
        self.out_shape = [jax.ShapeDtypeStruct((self.rows, self.width), F32)] * len(parts)
        self.out_specs = [whole((self.rows, self.width))] * len(parts)
        n = self.count = len(parts) * pieces
        self.scratch = [pltpu.VMEM((n, 4, 2, 2, self.rows, self.cut), F32), pltpu.SemaphoreType.DMA((n,))]
        self.scratch += Scatter.scratch(n, self.rows, self.cut)

    def bind(self, here, ins, outs, scratch):
        tots, loc = scratch[:2]

        def cut(p):
            return p // self.pieces, pl.ds(p % self.pieces * self.cut, self.cut)

        def part(p, core):
            a, cols = cut(p)
            return ins[a].at[:, :, :, core, :, cols]

        def out(p):
            a, cols = cut(p)
            return outs[a].at[:, cols]

        return Scatter(
            here,
            self.count,
            lambda p: tots.at[p],
            lambda p: part(p, here.oc),
            lambda p: pltpu.make_async_copy(part(p, here.c), tots.at[p], loc.at[p]),
            out,
            scratch[2:],
        )


def scatter_kernel(plan, *refs):
    n = plan.arrays
    here = Here()
    here.greet()
    sums = plan.bind(here, refs[:n], refs[n : 2 * n], refs[2 * n :])
    for wave in waves_of(sums):
        run(wave)
    finish_all(sums)


def scatter_all(parts, pieces, collective_id):
    plan = Summed(parts, pieces)
    return pl.pallas_call(
        functools.partial(scatter_kernel, plan),
        out_shape=plan.out_shape,
        in_specs=plan.in_specs,
        out_specs=[pl.BlockSpec(memory_space=pltpu.VMEM)] * len(parts),
        scratch_shapes=plan.scratch,
        compiler_params=pltpu.CompilerParams(
            collective_id=collective_id, has_side_effects=True, vmem_limit_bytes=60 * 2**20
        ),
        name="scatter_all",
    )(*plan.operands)


def greet(peers):
    barrier = pltpu.get_barrier_semaphore()
    for peer in peers:
        pl.semaphore_signal(barrier, inc=1, device_id=peer, device_id_type=MESH)
    pl.semaphore_wait(barrier, len(peers))


def group_gather_kernel(count, *refs):
    shards, fulls = refs[:count], refs[count : 2 * count]
    loc, ss, rs = refs[2 * count :]
    here = Here()
    x, c, ox, at_x, at_c = here.x, here.c, here.ox, here.at_x, here.at_c
    greet([at_x, at_c])
    waits = []
    for a in range(count):
        mine = fulls[a].at[:, x * 2 + c]
        copy = pltpu.make_async_copy(shards[a], mine, loc.at[a])
        copy.start()
        over = remote(shards[a], mine, ss.at[a, 0], rs.at[a, 0], at_x)
        over.start()
        side = remote(shards[a], mine, ss.at[a, 1], rs.at[a, 1], at_c)
        side.start()
        waits.append((copy, over, side))
    last = []
    for a in range(count):
        waits[a][1].wait_recv()
        block = fulls[a].at[:, ox * 2 + c]
        on = remote(block, block, ss.at[a, 2], rs.at[a, 2], at_c)
        on.start()
        last.append(on)
    for a in range(count):
        copy, over, side = waits[a]
        copy.wait()
        over.wait_send()
        side.wait()
        last[a].wait()


def group_gather(shards, collective_id):
    count = len(shards)
    dma = pltpu.SemaphoreType.DMA
    return pl.pallas_call(
        functools.partial(group_gather_kernel, count),
        out_shape=[jax.ShapeDtypeStruct((s.shape[0], 4) + s.shape[1:], F32) for s in shards],
        in_specs=[ANY] * count,
        out_specs=[ANY] * count,
        scratch_shapes=[dma((count,)), dma((count, 3)), dma((count, 3))],
        compiler_params=pltpu.CompilerParams(collective_id=collective_id, has_side_effects=True),
        name="group_gather",
    )(*shards)


def group_swap_kernel(count, *refs):
    shards, fulls = refs[:count], refs[count : 2 * count]
    loc, ss, rs = refs[2 * count :]
    here = Here()
    z, y, x, c = here.z, here.y, here.x, here.c
    me = x * 2 + c
    peers = [(x, 1 - c), (1 - x, c), (1 - x, 1 - c)]
    greet([place(z, y, *p) for p in peers])
    waits = []
    for a in range(count):
        copy = pltpu.make_async_copy(shards[a].at[:, me], fulls[a].at[:, me], loc.at[a])
        copy.start()
        waits.append(copy)
        for k in (1, 2, 0):
            px, pc = peers[k]
            on = remote(
                shards[a].at[:, px * 2 + pc], fulls[a].at[:, me], ss.at[a, k], rs.at[a, k], place(z, y, px, pc)
            )
            on.start()
            waits.append(on)
    for copy in waits:
        copy.wait()


def group_swap(shards, collective_id):
    count = len(shards)
    dma = pltpu.SemaphoreType.DMA
    return pl.pallas_call(
        functools.partial(group_swap_kernel, count),
        out_shape=[jax.ShapeDtypeStruct(s.shape, F32) for s in shards],
        in_specs=[ANY] * count,
        out_specs=[ANY] * count,
        scratch_shapes=[dma((count,)), dma((count, 3)), dma((count, 3))],
        compiler_params=pltpu.CompilerParams(collective_id=collective_id, has_side_effects=True),
        name="group_swap",
    )(*shards)


BF16 = jnp.bfloat16
HIGH = lax.Precision.HIGH
BLOCK = 256


def dot(left, right, dims=(1, 0)):
    return lax.dot_general(
        left, right, (((dims[0],), (dims[1],)), ((), ())), precision=HIGH, preferred_element_type=F32
    )


def dot3(left, right, dims=(1, 0)):
    numbers = (((dims[0],), (dims[1],)), ((), ()))
    one = functools.partial(lax.dot_general, dimension_numbers=numbers, preferred_element_type=F32)
    return one(left[0], right[0]) + (one(left[0], right[1]) + one(left[1], right[0]))


def halves(values):
    top = values.astype(BF16)
    return top, (values - top.astype(F32)).astype(BF16)


def split_weights(sources, pairs, stage, sems):
    step = stage.shape[1]
    chunks = [(i, r) for i, s in enumerate(sources) for r in range(0, s.shape[0], step)]

    def copy(n):
        i, r = chunks[n]
        return pltpu.make_async_copy(sources[i].at[r : r + step], stage.at[n % 2], sems.at[n % 2])

    copy(0).start()
    for n, (i, r) in enumerate(chunks):
        if n + 1 < len(chunks):
            copy(n + 1).start()
        copy(n).wait()
        pairs[i][0][r : r + step], pairs[i][1][r : r + step] = halves(stage[n % 2])


def unit_of(values):
    centred = values - jnp.mean(values, axis=-1, keepdims=True)
    inv_std = lax.rsqrt(jnp.mean(centred * centred, axis=-1, keepdims=True) + EPSILON)
    return centred * inv_std, inv_std


def staging(width):
    return [pltpu.VMEM((width, width), BF16)] * 4 + [pltpu.VMEM((2, 128, width), F32), pltpu.SemaphoreType.DMA((2,))]


def media_kernel(cuts, steps, *refs):
    feats, embed, gain, bias, own, key_w, value_w = refs[:7]
    n = max(a for a, _, _ in cuts) + 1
    shards, outs = refs[7 : 7 + n], refs[7 + n :]
    keys, values, own_keys, own_values, xt_top, xt_low = outs[:6]
    fulls, (kt, kl, vt, vl, stage, sems), rest = outs[6 : 6 + n], outs[6 + n : 12 + n], outs[12 + n :]
    step = pl.program_id(0)
    here = Here()
    moved = Gather(here, shards, fulls, cuts, rest)
    waves = waves_of(moved)
    waves[0].insert(0, here.greet)

    @pl.when(step == 0)
    def _():
        split_weights((key_w, value_w), ((kt, kl), (vt, vl)), stage, sems)
        mine = halves(own[...])
        own_keys[...] = dot3(mine, (kt[...], kl[...]))
        own_values[...] = dot3(mine, (vt[...], vl[...]))

    unit, _ = unit_of(feats[...] + embed[...])
    normed = unit * gain[...] + bias[...]
    flipped = halves(jnp.swapaxes(normed, 0, 1))
    xt_top[...], xt_low[...] = flipped
    pair = halves(normed)
    for i in range(6):
        run_tick(step, steps, i, 6, waves)
        cols = slice(i % 3 * 512, i % 3 * 512 + 512)
        if i < 3:
            keys[:, cols] = dot3(pair, (kt[:, cols], kl[:, cols]))
        else:
            values[:, cols] = dot3(pair, (vt[:, cols], vl[:, cols]))
    run_last(step, steps, moved)


def whole(shape, buffers=1):
    return pl.BlockSpec(shape, lambda *i: (0,) * len(shape), pipeline_mode=pl.Buffered(buffers))


def media_forward(feats, embed, gain, bias, own, key_w, value_w, shards, pieces, collective_id):
    rows, width = feats.shape
    own_rows = own.shape[0]
    cuts = column_cuts([s.shape[1] for s in shards], pieces)
    row_block = pl.BlockSpec((BLOCK, width), lambda i: (i, 0))
    full = jax.ShapeDtypeStruct((rows, width), F32)
    small = jax.ShapeDtypeStruct((own_rows, width), F32)
    turned = jax.ShapeDtypeStruct((width, rows), BF16)
    turned_block = pl.BlockSpec((width, BLOCK), lambda i: (0, i))
    outs = pl.pallas_call(
        functools.partial(media_kernel, cuts, rows // BLOCK),
        grid=(rows // BLOCK,),
        in_specs=[
            row_block,
            pl.BlockSpec((None, 1, width), lambda i: (i, 0, 0)),
            whole((1, width)),
            whole((1, width)),
            whole((own_rows, width)),
            ANY,
            ANY,
        ]
        + [ANY] * len(shards),
        out_specs=[row_block, row_block, whole((own_rows, width)), whole((own_rows, width)), turned_block, turned_block]
        + [ANY] * len(shards),
        out_shape=[full, full, small, small, turned, turned] + full_shapes(shards),
        scratch_shapes=staging(width) + Gather.semaphores(len(cuts)),
        compiler_params=pltpu.CompilerParams(
            collective_id=collective_id, has_side_effects=True, vmem_limit_bytes=60 * 2**20
        ),
        name="media_forward",
    )(feats, embed, gain, bias, own, key_w, value_w, *shards)
    return outs[:6], [flat_full(o) for o in outs[6:]]


def pair_rows(values, first, head):
    lane = lax.broadcasted_iota(jnp.int32, values.shape, 1)
    return jnp.concatenate(
        [
            jnp.where((lane >= first) & (lane < first + head), values, 0.0),
            jnp.where((lane >= first + head) & (lane < first + 2 * head), values, 0.0),
        ],
        axis=0,
    )


def pair_merge(stacked, first, head):
    half = stacked.shape[0] // 2
    lane = lax.broadcasted_iota(jnp.int32, (half, stacked.shape[1]), 1)
    one = jnp.where((lane >= first) & (lane < first + head), stacked[:half], 0.0)
    return one + jnp.where((lane >= first + head) & (lane < first + 2 * head), stacked[half:], 0.0)


def join(left, right):
    return jnp.concatenate([left[:, :128], left[:, 128:] + right[:, :128], right[:, 128:]], axis=1)


def windows(head):
    return ((slice(0, 256), 0), (slice(128, 384), 2 * head - 128))


def score_block(present, seq, keys, own_keys, q_pair, window, inv_root):
    at = keys.shape[0]
    scores = jnp.concatenate([dot(keys[:, window], q_pair, (1, 1)), dot(own_keys[:, window], q_pair, (1, 1))], axis=0)
    row = lax.broadcasted_iota(jnp.int32, scores.shape, 0)
    keep = (row >= at) | ((row < at // 2) & (present[seq, 0] > 0)) | ((row >= at // 2) & (present[seq, 1] > 0))
    return jnp.where(keep, scores * inv_root, MASKED)


def attend_kernel(inv_root, head, cuts, steps, *refs):
    present, queries, keys, values, own_keys, own_values, shard, out, tops, sums, full = refs[:11]
    seq, group = pl.program_id(0), pl.program_id(1)
    step = seq * pl.num_programs(1) + group
    here = Here()
    moved = Gather(here, [shard], [full], cuts, refs[11:])
    waves = waves_of(moved)
    waves[0].insert(0, here.greet)
    merged = []
    for p, (window, first) in enumerate(windows(head)):
        run_tick(step, steps, p, 2, waves)
        q_pair = pair_rows(queries[:, window], first, head)
        scores = score_block(present, seq, keys, own_keys, q_pair, window, inv_root)
        top = jnp.max(scores, axis=0, keepdims=True)
        expo = jnp.exp(scores - top)
        tops[pl.ds(group * 2 + p, 1)] = top
        sums[pl.ds(group * 2 + p, 1)] = jnp.sum(expo, axis=0, keepdims=True)
        at = keys.shape[0]
        stacked = dot(expo[:at], values[:, window], (0, 0)) + dot(expo[at:], own_values[:, window], (0, 0))
        merged.append(pair_merge(stacked, first, head))
    out[...] = join(*merged)
    run_last(step, steps, moved)


def attend_specs(lat, media, rows):
    group = 384
    query = pl.BlockSpec((None, lat, group), lambda b, g: (b, 0, g))
    key = pl.BlockSpec((media, group), lambda b, g: (b, g))
    own = pl.BlockSpec((rows, group), lambda b, g: (b, g))
    stat = pl.BlockSpec((None, 8, 128), lambda b, g: (b, 0, 0))
    return query, key, own, stat


SMEM = pl.BlockSpec(memory_space=pltpu.SMEM)


def attend(present, queries, keys, values, own_keys, own_values, shard, pieces, collective_id):
    seqs, lat, width = queries.shape
    head = width // HEADS
    query, key, own, stat = attend_specs(lat, keys.shape[0] // seqs, own_keys.shape[0] // seqs)
    stat_shape = jax.ShapeDtypeStruct((seqs, 8, 128), F32)
    cuts = column_cuts([shard.shape[1]], [pieces])
    grid = (seqs, width // 384)
    *outs, full = pl.pallas_call(
        functools.partial(attend_kernel, 1.0 / math.sqrt(head), head, cuts, grid[0] * grid[1]),
        grid=grid,
        in_specs=[SMEM, query, key, key, own, own, ANY],
        out_specs=[query, stat, stat, ANY],
        out_shape=[jax.ShapeDtypeStruct(queries.shape, F32), stat_shape, stat_shape] + full_shapes([shard]),
        scratch_shapes=Gather.semaphores(len(cuts)),
        compiler_params=pltpu.CompilerParams(
            collective_id=collective_id, has_side_effects=True, vmem_limit_bytes=60 * 2**20
        ),
        name="attend",
    )(present, queries, keys, values, own_keys, own_values, shard)
    return outs, flat_full(full)


def attend_back_kernel(inv_root, head, plan, steps, *refs):
    present, queries, grads, logs, deltas, keys, values, own_keys, own_values = refs[:9]
    n = plan.arrays
    query_out, key_out, value_out, own_key_out, own_value_out = refs[9 + n : 14 + n]
    seq, group = pl.program_id(0), pl.program_id(1)
    step = seq * pl.num_programs(1) + group
    here = Here()
    moved = plan.bind(here, refs[9 : 9 + n], refs[14 + n : 14 + 2 * n], refs[14 + 2 * n :])
    waves = waves_of(moved)
    waves[0].insert(0, here.greet)
    merged, key_grads, value_grads = [], [], []
    at = keys.shape[0]
    for p, (window, first) in enumerate(windows(head)):
        run_tick(step, steps, p, 2, waves)
        q_pair = pair_rows(queries[:, window], first, head)
        g_pair = pair_rows(grads[:, window], first, head)
        scores = score_block(present, seq, keys, own_keys, q_pair, window, inv_root)
        probs = jnp.exp(scores - logs[pl.ds(group * 2 + p, 1)])
        grad_probs = jnp.concatenate(
            [dot(values[:, window], g_pair, (1, 1)), dot(own_values[:, window], g_pair, (1, 1))], axis=0
        )
        grad_scores = probs * (grad_probs - deltas[pl.ds(group * 2 + p, 1)]) * inv_root
        stacked = dot(grad_scores[:at], keys[:, window], (0, 0)) + dot(grad_scores[at:], own_keys[:, window], (0, 0))
        merged.append(pair_merge(stacked, first, head))
        key_grads.append(dot(grad_scores, q_pair))
        value_grads.append(dot(probs, g_pair))
    query_out[...] = join(*merged)
    key_grad, value_grad = join(*key_grads), join(*value_grads)
    key_out[...], own_key_out[...] = key_grad[:at], key_grad[at:]
    value_out[...], own_value_out[...] = value_grad[:at], value_grad[at:]
    run_last(step, steps, moved)


def attend_back(present, queries, grads, logs, deltas, keys, values, own_keys, own_values, plan, collective_id):
    seqs, lat, width = queries.shape
    head = width // HEADS
    query, key, own, stat = attend_specs(lat, keys.shape[0] // seqs, own_keys.shape[0] // seqs)
    shape = lambda v: jax.ShapeDtypeStruct(v.shape, F32)
    grid = (seqs, width // 384)
    outs = pl.pallas_call(
        functools.partial(attend_back_kernel, 1.0 / math.sqrt(head), head, plan, grid[0] * grid[1]),
        grid=grid,
        in_specs=[SMEM, query, query, stat, stat, key, key, own, own] + plan.in_specs,
        out_specs=[query, key, key, own, own] + plan.out_specs,
        out_shape=[shape(queries), shape(keys), shape(values), shape(own_keys), shape(own_values)] + plan.out_shape,
        scratch_shapes=plan.scratch,
        compiler_params=pltpu.CompilerParams(
            collective_id=collective_id, has_side_effects=True, vmem_limit_bytes=60 * 2**20
        ),
        name="attend_back",
    )(present, queries, grads, logs, deltas, keys, values, own_keys, own_values, *plan.operands)
    return outs[:5], outs[5:]


def weight_kernel(steps, xt_top, xt_low, own, grad_keys, grad_values, own_gk, own_gv, vec, outs, vec_out, mats, *rest):
    n = pl.program_id(0)
    here = Here()
    cut = grad_keys.shape[1]
    sums = Scatter(
        here,
        2 * steps,
        lambda p: mats.at[p, :, :, :, here.c],
        lambda p: mats.at[p, :, :, :, here.oc],
        None,
        lambda p: outs.at[p % 2, :, pl.ds(pl.multiple_of(p // 2 * cut, cut), cut)],
        rest[:14],
    )
    tot, loc = rest[14:16]
    small = Scatter(
        here,
        1,
        lambda p: tot,
        lambda p: vec.at[:, :, :, here.oc],
        lambda p: pltpu.make_async_copy(vec.at[:, :, :, here.c], tot, loc.at[p]),
        lambda p: vec_out,
        rest[16:],
    )
    stages = sums.stages()

    @pl.when(n == 0)
    def _():
        here.greet()

    own_flat = own[...]
    for w, (grad, own_grad) in enumerate(((grad_keys, own_gk), (grad_values, own_gv))):
        pair = halves(grad[...])

        @pl.loop(0, 4)
        def _(zi):
            rows = pl.ds(pl.multiple_of(zi * 384, 384), 384)
            made = dot3((xt_top[rows], xt_low[rows]), pair) + dot(own[:, rows], own_grad[...], (0, 0))
            mats[2 * n + w, zi] = made.reshape((2, 2, 2, 48, cut))

        sums.start(2 * n + w)
        for s in (4, 3, 2, 1):
            p = 2 * n + w - LAG * s

            @pl.when(p >= 0)
            def _():
                stages[s](p)

        if w == 1:
            for s in range(5):

                @pl.when(n == s)
                def _():
                    small.stages()[s](0)

    @pl.when(n == steps - 1)
    def _():
        for t in range(2 * steps, 2 * steps + 4 * LAG):
            for s in (4, 3, 2, 1):
                if 0 <= t - LAG * s < 2 * steps:
                    stages[s](t - LAG * s)

        @pl.loop(0, 2 * steps)
        def _(p):
            sums.done(p)

        small.done(0)


def weight_grads(xt_top, xt_low, own, grad_keys, grad_values, own_gk, own_gv, vec, collective_id):
    width, rows = xt_top.shape
    own_rows = own.shape[0]
    steps = width // BLOCK
    cols = lambda n: pl.BlockSpec((n, BLOCK), lambda i: (0, i))
    r = width // 32
    vr, vw = vec.shape[0] // 32, vec.shape[1]
    outs, vec_sum = pl.pallas_call(
        functools.partial(weight_kernel, steps),
        grid=(steps,),
        in_specs=[
            whole((width, rows)),
            whole((width, rows)),
            whole((own_rows, width)),
            cols(rows),
            cols(rows),
            cols(own_rows),
            cols(own_rows),
            ANY,
        ],
        out_specs=[whole((2, r, width)), whole((vr, vw))],
        out_shape=[jax.ShapeDtypeStruct((2, r, width), F32), jax.ShapeDtypeStruct((vr, vw), F32)],
        scratch_shapes=[pltpu.VMEM((2 * steps,) + GRID + (r, BLOCK), F32)]
        + Scatter.scratch(2 * steps, r, BLOCK)
        + [pltpu.VMEM((4, 2, 2, vr, vw), F32), pltpu.SemaphoreType.DMA((1,))]
        + Scatter.scratch(1, vr, vw),
        compiler_params=pltpu.CompilerParams(
            collective_id=collective_id, has_side_effects=True, vmem_limit_bytes=62 * 2**20
        ),
        name="weight_grads",
    )(xt_top, xt_low, own, grad_keys, grad_values, own_gk, own_gv, vec.reshape(GRID + (vr, vw)))
    return outs[0], outs[1], vec_sum


def media_back_kernel(plan, steps, *refs):
    feats, embed, gain, grad_keys, grad_values, own_gk, own_gv, key_w, value_w = refs[:9]
    n = plan.arrays
    out, own_out, sums = refs[9 + n : 12 + n]
    kt, kl, vt, vl, stage, sems = refs[12 + 2 * n : 18 + 2 * n]
    step = pl.program_id(0)
    here = Here()
    moved = plan.bind(here, refs[9 : 9 + n], refs[12 + n : 12 + 2 * n], refs[18 + 2 * n :])
    waves = waves_of(moved)
    waves[0].insert(0, here.greet)

    @pl.when(step == 0)
    def _():
        split_weights((key_w, value_w), ((kt, kl), (vt, vl)), stage, sems)
        own_out[...] = dot3(halves(own_gk[...]), (kt[...], kl[...]), (1, 1)) + dot3(
            halves(own_gv[...]), (vt[...], vl[...]), (1, 1)
        )
        sums[...] = jnp.zeros_like(sums)

    key_pair, value_pair = halves(grad_keys[...]), halves(grad_values[...])
    for i in range(3):
        run_tick(step, steps, i, 3, waves)
        rows = slice(i * 512, i * 512 + 512)
        out[:, rows] = dot3(key_pair, (kt[rows], kl[rows]), (1, 1)) + dot3(value_pair, (vt[rows], vl[rows]), (1, 1))
    strip = 64

    @pl.loop(0, out.shape[0] // strip)
    def _(i):
        rows = pl.ds(pl.multiple_of(i * strip, strip), strip)
        incoming = out[rows]
        unit, inv_std = unit_of(feats[rows] + embed[...])
        sums[pl.ds(0, 1)] += jnp.sum(incoming * unit, axis=0, keepdims=True)
        sums[pl.ds(1, 1)] += jnp.sum(incoming, axis=0, keepdims=True)
        scaled = incoming * gain[...]
        result = inv_std * (
            scaled
            - jnp.mean(scaled, axis=-1, keepdims=True)
            - unit * jnp.mean(scaled * unit, axis=-1, keepdims=True)
        )
        out[rows] = result
        sums[pl.ds(2 + step, 1)] += jnp.sum(result, axis=0, keepdims=True)

    run_last(step, steps, moved)


def media_backward(feats, embed, gain, grad_keys, grad_values, own_gk, own_gv, key_w, value_w, plan, collective_id):
    rows, width = feats.shape
    own_rows = own_gk.shape[0]
    row_block = pl.BlockSpec((BLOCK, width), lambda i: (i, 0))
    one_block = pl.BlockSpec((BLOCK, width), lambda i: (i, 0), pipeline_mode=pl.Buffered(1))
    steps = rows // BLOCK
    outs = pl.pallas_call(
        functools.partial(media_back_kernel, plan, steps),
        grid=(steps,),
        in_specs=[
            one_block,
            pl.BlockSpec((None, 1, width), lambda i: (i, 0, 0)),
            whole((1, width)),
            row_block,
            row_block,
            whole((own_rows, width)),
            whole((own_rows, width)),
            ANY,
            ANY,
        ]
        + plan.in_specs,
        out_specs=[one_block, whole((own_rows, width)), whole((8, width))] + plan.out_specs,
        out_shape=[
            jax.ShapeDtypeStruct((rows, width), F32),
            jax.ShapeDtypeStruct((own_rows, width), F32),
            jax.ShapeDtypeStruct((8, width), F32),
        ]
        + plan.out_shape,
        scratch_shapes=staging(width) + plan.scratch,
        compiler_params=pltpu.CompilerParams(
            collective_id=collective_id, has_side_effects=True, vmem_limit_bytes=64 * 2**20 - 2**16
        ),
        name="media_backward",
    )(feats, embed, gain, grad_keys, grad_values, own_gk, own_gv, key_w, value_w, *plan.operands)
    return outs[:3], outs[3:]


GELU_A = math.sqrt(2.0 / math.pi)
GELU_B = 0.044715


def feed_kernel(feed, cot, up, down, feed_part, new_part, grad_up_t, grad_down):
    @pl.when(pl.program_id(0) == 0)
    def _():
        grad_up_t[...] = jnp.zeros_like(grad_up_t)
        grad_down[...] = jnp.zeros_like(grad_down)

    hidden = dot(feed[...], up[...])
    grad_act = dot(cot[...], down[...], (1, 1))
    square = hidden * hidden
    bent = jnp.tanh(GELU_A * (hidden + GELU_B * hidden * square))
    activated = 0.5 * hidden * (1.0 + bent)
    slope = 0.5 * (1.0 + bent) + 0.5 * hidden * (1.0 - bent * bent) * (GELU_A * (1.0 + 3.0 * GELU_B * square))
    grad_hidden = grad_act * slope
    feed_part[...] = dot(grad_hidden, up[...], (1, 1))
    new_part[...] = dot(activated, down[...])
    grad_up_t[...] += dot(grad_hidden, feed[...], (0, 0))
    grad_down[...] += dot(activated, cot[...], (0, 0))


def feed_forward(feed, cot, up, down):
    rows, width = feed.shape
    units = up.shape[1]
    row_block = pl.BlockSpec((BLOCK, width), lambda i: (i, 0))
    one_block = pl.BlockSpec((BLOCK, width), lambda i: (i, 0), pipeline_mode=pl.Buffered(1))
    big = jax.ShapeDtypeStruct((rows, width), F32)
    slim = jax.ShapeDtypeStruct((units, width), F32)
    return pl.pallas_call(
        feed_kernel,
        grid=(rows // BLOCK,),
        in_specs=[row_block, row_block, whole((width, units)), whole((units, width))],
        out_specs=[row_block, row_block, whole((units, width)), whole((units, width))],
        out_shape=[big, big, slim, slim],
        compiler_params=pltpu.CompilerParams(vmem_limit_bytes=60 * 2**20),
        name="feed_forward",
    )(feed, cot, up, down)


def mm(left, right):
    return jnp.dot(left, right, precision=HIGH, preferred_element_type=F32)


def mm_tn(left, right):
    return lax.dot_general(left, right, (((0,), (0,)), ((), ())), precision=HIGH, preferred_element_type=F32)


def mm_nt(left, right):
    return lax.dot_general(left, right, (((1,), (1,)), ((), ())), precision=HIGH, preferred_element_type=F32)


def body_fast(
    latents,
    patch_feats,
    image_counts,
    time_index,
    query_proj,
    key_proj,
    value_proj,
    out_proj,
    up_proj,
    down_proj,
    media_gain,
    media_bias,
    latent_gain,
    latent_bias,
    feed_gain,
    feed_bias,
    time_table,
    out_cotangent,
):
    frame = lax.axis_index("frame")
    frames = lax.axis_size("frame")
    seqs, rows, width = latents.shape
    rounds, patches = patch_feats.shape[1], patch_feats.shape[3]
    lat = rows * frames
    head = width // HEADS
    strip = media_gain.shape[0]

    vectors = jnp.concatenate(
        [jnp.stack([media_gain, media_bias, latent_gain, latent_bias, feed_gain, feed_bias]), time_table], axis=0
    )
    packed = jnp.pad(vectors, ((0, 2), (0, 128 - strip)))
    (packed_all, key_w, value_w), lat_blocks = gather_first([packed, key_proj, value_proj], [1, 6, 6], latents, 0)
    vec_all = packed_all.reshape(-1, 16, 128)[:, :14, :strip].transpose(1, 0, 2).reshape(14, width)
    mgain, mbias, lgain, lbias, fgain, fbias = (vec_all[i] for i in range(6))
    table = vec_all[6:]
    up_cols = lax.all_to_all(
        up_proj.reshape(strip, 32, -1), ("seq", "frame"), split_axis=1, concat_axis=0, tiled=True
    ).reshape(width, -1)

    latent_all = lat_blocks.reshape(seqs, lat, width)
    latent_norm, latent_unit, latent_std = norm_forward(latent_all, lgain, lbias)
    own_rows = lambda v: lax.dynamic_slice_in_dim(v, frame * rows, rows, 1)
    own_norm, own_unit, own_std = own_rows(latent_norm), own_rows(latent_unit), own_rows(latent_std)
    slot_ids = jnp.arange(rounds, dtype=jnp.int32) * frames + frame
    present = slot_ids[None, :] < image_counts[:, None]
    picks = jnp.arange(time_index.shape[1], dtype=jnp.int32)[None, :] == slot_ids[:, None]
    slot_times = jnp.sum(jnp.where(picks[None, :, :], time_index[:, None, :], 0), axis=-1)
    one_hot = slot_times[:, :, None] == jnp.arange(time_table.shape[0], dtype=jnp.int32)
    slot_embed = jnp.sum(jnp.where(one_hot[..., None], table, 0.0), axis=2)
    feats = patch_feats.reshape(-1, width)
    embed = slot_embed.reshape(-1, 1, width)
    own_flat = flatten(own_norm)
    (keys, values, own_keys, own_values, xt_top, xt_low), (query_w, cot_all) = media_forward(
        feats, embed, mgain[None], mbias[None], own_flat, key_w, value_w, [query_proj, flatten(out_cotangent)], [6, 6], 1
    )
    queries = mm(flatten(latent_norm), query_w).reshape(seqs, lat, width)
    present = present.astype(jnp.int32)

    (partial, row_top, row_sum), out_w = attend(
        present, queries, keys, values, own_keys, own_values, out_proj, 6, 9
    )
    stats = jnp.concatenate([row_top.reshape(seqs, HEADS, lat), row_sum.reshape(seqs, HEADS, lat)], axis=1)
    stats = jnp.pad(stats.transpose(0, 2, 1), ((0, 0), (0, 0), (0, 128 - 2 * HEADS)))
    part_all, stat_all = group_swap(
        [partial.reshape(seqs, frames, rows, width), stats.reshape(seqs, frames, rows, 128)], 2
    )
    tops, sums = stat_all[..., :HEADS], stat_all[..., HEADS : 2 * HEADS]
    top = jnp.max(tops, axis=1)
    ratio = jnp.exp(tops - top[:, None])
    row_total = jnp.sum(sums * ratio, axis=1)
    weight = ratio / row_total[:, None]
    attended = jnp.sum(part_all.reshape(seqs, frames, rows, HEADS, head) * weight[..., None], axis=1)
    log_total = top + jnp.log(row_total)
    attended_flat = attended.reshape(seqs, rows, width)
    middle = latents + mm(flatten(attended_flat), out_w).reshape(seqs, rows, width)

    feed_norm, feed_unit, feed_std = norm_forward(middle, fgain, fbias)
    (feed_all,) = gather_all([flatten(feed_norm)], [6], 3)
    feed_part, new_part, grad_up_t, grad_down = feed_forward(feed_all, cot_all, up_cols, down_proj)
    (grad_feed_norm,) = scatter_all([feed_part], 6, 4)
    grad_up = lax.all_to_all(
        grad_up_t.reshape(-1, 32, strip).transpose(1, 2, 0), ("seq", "frame"), split_axis=0, concat_axis=2, tiled=True
    ).reshape(strip, -1)
    grad_mid_norm, grad_fgain, grad_fbias = norm_backward(
        grad_feed_norm.reshape(seqs, rows, width), feed_unit, feed_std, fgain
    )
    grad_middle = out_cotangent + grad_mid_norm
    grad_out_w = mm_tn(flatten(attended_flat), flatten(grad_middle))
    grad_own = mm_nt(flatten(grad_middle), out_w).reshape(seqs, rows, HEADS, head)
    delta = jnp.sum(grad_own * attended, axis=-1)
    back_stats = jnp.pad(jnp.concatenate([log_total, delta], axis=-1), ((0, 0), (0, 0), (0, 128 - 2 * HEADS)))
    grad_blocks, back_blocks = group_gather([grad_own.reshape(seqs, rows, width), back_stats], 5)
    back_all = back_blocks.reshape(seqs, lat, 128).transpose(0, 2, 1)
    logs_all, delta_all = (back_all[:, i * HEADS : (i + 1) * HEADS].reshape(seqs, 8, 128) for i in range(2))

    (query_part, grad_keys, grad_values, own_gk, own_gv), (new_rows,) = attend_back(
        present,
        queries,
        grad_blocks.reshape(seqs, lat, width),
        logs_all,
        delta_all,
        keys,
        values,
        own_keys,
        own_values,
        Summed([new_part], 6),
        10,
    )
    new_latents = middle + new_rows.reshape(seqs, rows, width)
    (query_blocks,) = group_swap([query_part.reshape(seqs, frames, rows, width)], 6)
    grad_queries = flatten(jnp.sum(query_blocks, axis=1))

    grad_query_w = mm_tn(own_flat, grad_queries)
    (patch_grads, own_back, media_sums), (sum_query, sum_out) = media_backward(
        feats,
        embed,
        mgain[None],
        grad_keys,
        grad_values,
        own_gk,
        own_gv,
        key_w,
        value_w,
        Summed([grad_query_w, grad_out_w], 6),
        7,
    )
    grad_own_norm = (mm_nt(grad_queries, query_w) + own_back).reshape(seqs, rows, width)
    grad_lat_in, grad_lgain, grad_lbias = norm_backward(grad_own_norm, own_unit, own_std, lgain)
    latent_grads = grad_middle + grad_lat_in
    grad_mgain, grad_mbias = media_sums[0], media_sums[1]
    slot_sums = media_sums[2:].reshape(seqs, rounds, width)
    grad_table = jnp.sum(jnp.where(one_hot[..., None], slot_sums[:, :, None, :], 0.0), axis=(0, 1))
    vec_grads = jnp.concatenate(
        [jnp.stack([grad_mgain, grad_mbias, grad_lgain, grad_lbias, grad_fgain, grad_fbias]), grad_table], axis=0
    )
    vec_blocks = jnp.pad(vec_grads.reshape(14, 32, strip).transpose(1, 0, 2), ((0, 0), (0, 2), (0, 128 - strip)))
    sum_key, sum_value, sum_vec = weight_grads(
        xt_top, xt_low, own_flat, grad_keys, grad_values, own_gk, own_gv, vec_blocks.reshape(-1, 128), 8
    )
    vec = sum_vec[:14, :strip]
    return (
        new_latents,
        latent_grads,
        patch_grads.reshape(patch_feats.shape),
        sum_query,
        sum_key,
        sum_value,
        sum_out,
        grad_up,
        grad_down,
        vec[0],
        vec[1],
        vec[2],
        vec[3],
        vec[4],
        vec[5],
        vec[6:],
    )


def solution(mesh):
    fast = dict(mesh.shape) == {"seq": 8, "frame": 4}
    return jax.shard_map(
        body_fast if fast else body_general,
        mesh=mesh,
        in_specs=(
            P("seq", "frame", None),
            P("seq", None, "frame", None, None),
            P("seq"),
            P("seq", None),
            P(("seq", "frame"), None),
            P(("seq", "frame"), None),
            P(("seq", "frame"), None),
            P(("seq", "frame"), None),
            P(("seq", "frame"), None),
            P(("seq", "frame"), None),
            P(("seq", "frame")),
            P(("seq", "frame")),
            P(("seq", "frame")),
            P(("seq", "frame")),
            P(("seq", "frame")),
            P(("seq", "frame")),
            P(None, ("seq", "frame")),
            P("seq", "frame", None),
        ),
        out_specs=(
            P("seq", "frame", None),
            P("seq", "frame", None),
            P("seq", None, "frame", None, None),
            P(("seq", "frame"), None),
            P(("seq", "frame"), None),
            P(("seq", "frame"), None),
            P(("seq", "frame"), None),
            P(("seq", "frame"), None),
            P(("seq", "frame"), None),
            P(("seq", "frame")),
            P(("seq", "frame")),
            P(("seq", "frame")),
            P(("seq", "frame")),
            P(("seq", "frame")),
            P(("seq", "frame")),
            P(None, ("seq", "frame")),
        ),
        check_vma=False,
    )
```

```python
import functools
import math

import jax
import jax.numpy as jnp
from jax import lax
from jax.experimental import pallas as pl
from jax.experimental.pallas import tpu as pltpu
from jax.sharding import PartitionSpec as P

HEADS = 16


HIGHEST = lax.Precision.HIGHEST
EPSILON = 1e-05
MASKED = -1e30


def product(left, right):
    return jnp.dot(left, right, precision=HIGHEST, preferred_element_type=jnp.float32)


def product_tn(left, right):
    return lax.dot_general(
        left, right, (((0,), (0,)), ((), ())), precision=HIGHEST, preferred_element_type=jnp.float32
    )


def product_nt(left, right):
    return lax.dot_general(
        left, right, (((1,), (1,)), ((), ())), precision=HIGHEST, preferred_element_type=jnp.float32
    )


def flatten(values):
    return values.reshape(-1, values.shape[-1])


def norm_forward(values, gain_vec, bias_vec):
    centred = values - jnp.mean(values, axis=-1, keepdims=True)
    inv_std = lax.rsqrt(jnp.mean(centred * centred, axis=-1, keepdims=True) + EPSILON)
    unit_vals = centred * inv_std
    return (unit_vals * gain_vec + bias_vec, unit_vals, inv_std)


def norm_backward(incoming, unit_vals, inv_std, gain_vec):
    scaled = incoming * gain_vec
    result = inv_std * (
        scaled
        - jnp.mean(scaled, axis=-1, keepdims=True)
        - unit_vals * jnp.mean(scaled * unit_vals, axis=-1, keepdims=True)
    )
    flat_in = flatten(incoming)
    return (result, jnp.sum(flat_in * flatten(unit_vals), axis=0), jnp.sum(flat_in, axis=0))


def heads_last(stats):
    return jnp.transpose(stats, (0, 2, 1))[..., None]


def per_slot(action, operands):
    return lax.map(action, operands)


def body_general(
    latents,
    patch_feats,
    image_counts,
    time_index,
    query_proj,
    key_proj,
    value_proj,
    out_proj,
    up_proj,
    down_proj,
    media_gain,
    media_bias,
    latent_gain,
    latent_bias,
    feed_gain,
    feed_bias,
    time_table,
    out_cotangent,
):
    gathered = (
        lax.all_gather(query_proj, ("seq", "frame"), axis=0, tiled=True),
        lax.all_gather(key_proj, ("seq", "frame"), axis=0, tiled=True),
        lax.all_gather(value_proj, ("seq", "frame"), axis=0, tiled=True),
        lax.all_gather(out_proj, ("seq", "frame"), axis=0, tiled=True),
        lax.all_gather(up_proj, ("seq", "frame"), axis=0, tiled=True),
        lax.all_gather(down_proj, ("seq", "frame"), axis=0, tiled=True),
        lax.all_gather(media_gain, ("seq", "frame"), axis=0, tiled=True),
        lax.all_gather(media_bias, ("seq", "frame"), axis=0, tiled=True),
        lax.all_gather(latent_gain, ("seq", "frame"), axis=0, tiled=True),
        lax.all_gather(latent_bias, ("seq", "frame"), axis=0, tiled=True),
        lax.all_gather(feed_gain, ("seq", "frame"), axis=0, tiled=True),
        lax.all_gather(feed_bias, ("seq", "frame"), axis=0, tiled=True),
        lax.all_gather(time_table, ("seq", "frame"), axis=1, tiled=True),
    )
    gathered = lax.optimization_barrier(gathered)
    (
        query_full,
        key_full,
        value_full,
        out_full,
        up_full,
        down_full,
        mgain_full,
        mbias_full,
        lgain_full,
        lbias_full,
        fgain_full,
        fbias_full,
        table_full,
    ) = gathered
    frame_index = lax.axis_index("frame")
    frame_count = lax.axis_size("frame")
    seq_local, lat_rows, model_width = latents.shape
    round_count = patch_feats.shape[1]
    patch_count = patch_feats.shape[3]
    slot_total = time_index.shape[1]
    table_rows = time_table.shape[0]
    latent_total = lat_rows * frame_count
    head_size = model_width // HEADS
    inv_root = 1.0 / math.sqrt(head_size)
    latent_all = lax.all_gather(latents, "frame", axis=1, tiled=True)
    latent_norm, latent_unit, latent_std = norm_forward(latent_all, lgain_full, lbias_full)
    row_start = frame_index * lat_rows
    own_norm = lax.dynamic_slice_in_dim(latent_norm, row_start, lat_rows, 1)
    own_unit = lax.dynamic_slice_in_dim(latent_unit, row_start, lat_rows, 1)
    own_std = lax.dynamic_slice_in_dim(latent_std, row_start, lat_rows, 1)
    queries = product(flatten(latent_norm), query_full).reshape(
        seq_local, latent_total, model_width
    )
    own_keys = product(flatten(own_norm), key_full).reshape(seq_local, lat_rows, model_width)
    own_values = product(flatten(own_norm), value_full).reshape(seq_local, lat_rows, model_width)
    slot_ids = jnp.arange(round_count, dtype=jnp.int32) * frame_count + frame_index
    present = slot_ids[None, :] < image_counts[:, None]
    picks = jnp.arange(slot_total, dtype=jnp.int32)[None, :] == slot_ids[:, None]
    slot_times = jnp.sum(jnp.where(picks[None, :, :], time_index[:, None, :], 0), axis=-1)
    one_hot = (
        slot_times.reshape(-1)[:, None] == jnp.arange(table_rows, dtype=jnp.int32)[None, :]
    ).astype(jnp.float32)
    slot_embed = product(one_hot, table_full)
    slot_feats = patch_feats.reshape(seq_local * round_count, patch_count, model_width)

    def media_forward(element):
        normed, unit_part, std_part = norm_forward(
            element[0] + element[1][None, :], mgain_full, mbias_full
        )
        return (normed, unit_part, std_part, product(normed, key_full), product(normed, value_full))

    media_norm, media_unit, media_std, media_keys, media_values = per_slot(
        media_forward, (slot_feats, slot_embed)
    )
    key_total = lat_rows + round_count * patch_count
    all_keys = jnp.concatenate(
        [own_keys, media_keys.reshape(seq_local, round_count * patch_count, model_width)], axis=1
    )
    all_values = jnp.concatenate(
        [own_values, media_values.reshape(seq_local, round_count * patch_count, model_width)],
        axis=1,
    )
    keep = jnp.concatenate(
        [jnp.ones((seq_local, lat_rows), dtype=bool), jnp.repeat(present, patch_count, axis=1)],
        axis=1,
    )
    query_four = queries.reshape(seq_local, latent_total, HEADS, head_size)
    key_four = all_keys.reshape(seq_local, key_total, HEADS, head_size)
    value_four = all_values.reshape(seq_local, key_total, HEADS, head_size)

    def masked_scores():
        raw_scores = (
            jnp.einsum(
                "bqhe,bkhe->bhqk",
                query_four,
                key_four,
                precision=HIGHEST,
                preferred_element_type=jnp.float32,
            )
            * inv_root
        )
        return jnp.where(keep[:, None, None, :], raw_scores, MASKED)

    scores = masked_scores()
    row_top = jnp.max(scores, axis=-1)
    expo = jnp.exp(scores - row_top[..., None])
    row_total = jnp.sum(expo, axis=-1)
    partial_out = jnp.einsum(
        "bhqk,bkhe->bqhe", expo, value_four, precision=HIGHEST, preferred_element_type=jnp.float32
    )
    glob_top = lax.pmax(row_top, "frame")
    ratio = jnp.exp(row_top - glob_top)
    glob_total, glob_out = lax.psum((row_total * ratio, partial_out * heads_last(ratio)), "frame")
    attended = glob_out / heads_last(glob_total)
    log_total = glob_top + jnp.log(glob_total)
    attended_flat = attended.reshape(seq_local, latent_total, model_width)
    own_attended = lax.dynamic_slice_in_dim(attended_flat, row_start, lat_rows, 1)
    middle = latents + product(flatten(own_attended), out_full).reshape(
        seq_local, lat_rows, model_width
    )
    feed_norm, feed_unit, feed_std = norm_forward(middle, fgain_full, fbias_full)
    hidden_pre = product(flatten(feed_norm), up_full)
    activated, gelu_pull = jax.vjp(jax.nn.gelu, hidden_pre)
    new_latents = middle + product(activated, down_full).reshape(seq_local, lat_rows, model_width)
    regathered = (
        lax.all_gather(query_proj, ("seq", "frame"), axis=0, tiled=True),
        lax.all_gather(key_proj, ("seq", "frame"), axis=0, tiled=True),
        lax.all_gather(value_proj, ("seq", "frame"), axis=0, tiled=True),
        lax.all_gather(out_proj, ("seq", "frame"), axis=0, tiled=True),
        lax.all_gather(up_proj, ("seq", "frame"), axis=0, tiled=True),
        lax.all_gather(down_proj, ("seq", "frame"), axis=0, tiled=True),
        lax.all_gather(media_gain, ("seq", "frame"), axis=0, tiled=True),
        lax.all_gather(media_bias, ("seq", "frame"), axis=0, tiled=True),
        lax.all_gather(latent_gain, ("seq", "frame"), axis=0, tiled=True),
        lax.all_gather(latent_bias, ("seq", "frame"), axis=0, tiled=True),
        lax.all_gather(feed_gain, ("seq", "frame"), axis=0, tiled=True),
        lax.all_gather(feed_bias, ("seq", "frame"), axis=0, tiled=True),
        lax.all_gather(time_table, ("seq", "frame"), axis=1, tiled=True),
    )
    regathered = lax.optimization_barrier(regathered)
    query_back = regathered[0]
    key_back = regathered[1]
    value_back = regathered[2]
    out_back = regathered[3]
    up_back = regathered[4]
    down_back = regathered[5]
    mgain_back = regathered[6]
    lgain_back = regathered[8]
    fgain_back = regathered[10]
    cotangent = flatten(out_cotangent)
    grad_down = product_tn(activated, cotangent)
    grad_hidden = gelu_pull(product_nt(cotangent, down_back))[0]
    grad_up = product_tn(flatten(feed_norm), grad_hidden)
    grad_feed_norm = product_nt(grad_hidden, up_back).reshape(seq_local, lat_rows, model_width)
    grad_mid_norm, grad_fgain, grad_fbias = norm_backward(
        grad_feed_norm, feed_unit, feed_std, fgain_back
    )
    grad_middle = out_cotangent + grad_mid_norm
    grad_out_w = product_tn(flatten(own_attended), flatten(grad_middle))
    grad_own_att = product_nt(flatten(grad_middle), out_back).reshape(
        seq_local, lat_rows, model_width
    )
    grad_attended = lax.all_gather(grad_own_att, "frame", axis=1, tiled=True)
    grad_four = grad_attended.reshape(seq_local, latent_total, HEADS, head_size)
    delta_rows = jnp.einsum(
        "bqhe,bqhe->bhq", grad_four, attended, precision=HIGHEST, preferred_element_type=jnp.float32
    )
    probs = jnp.exp(masked_scores() - log_total[..., None])
    grad_probs = jnp.einsum(
        "bqhe,bkhe->bhqk",
        grad_four,
        value_four,
        precision=HIGHEST,
        preferred_element_type=jnp.float32,
    )
    grad_scores = probs * (grad_probs - delta_rows[..., None]) * inv_root
    grad_query_part = jnp.einsum(
        "bhqk,bkhe->bqhe",
        grad_scores,
        key_four,
        precision=HIGHEST,
        preferred_element_type=jnp.float32,
    ).reshape(seq_local, latent_total, model_width)
    grad_keys = jnp.einsum(
        "bhqk,bqhe->bkhe",
        grad_scores,
        query_four,
        precision=HIGHEST,
        preferred_element_type=jnp.float32,
    ).reshape(seq_local, key_total, model_width)
    grad_values = jnp.einsum(
        "bhqk,bqhe->bkhe", probs, grad_four, precision=HIGHEST, preferred_element_type=jnp.float32
    ).reshape(seq_local, key_total, model_width)
    grad_query_own = lax.psum_scatter(grad_query_part, "frame", scatter_dimension=1, tiled=True)
    grad_key_lat = flatten(grad_keys[:, :lat_rows])
    grad_value_lat = flatten(grad_values[:, :lat_rows])
    grad_key_media = grad_keys[:, lat_rows:].reshape(
        seq_local * round_count, patch_count, model_width
    )
    grad_value_media = grad_values[:, lat_rows:].reshape(
        seq_local * round_count, patch_count, model_width
    )
    grad_query_w = product_tn(flatten(own_norm), flatten(grad_query_own))
    grad_key_w = product_tn(flatten(own_norm), grad_key_lat) + product_tn(
        flatten(media_norm), flatten(grad_key_media)
    )
    grad_value_w = product_tn(flatten(own_norm), grad_value_lat) + product_tn(
        flatten(media_norm), flatten(grad_value_media)
    )
    grad_own_norm = (
        product_nt(flatten(grad_query_own), query_back)
        + product_nt(grad_key_lat, key_back)
        + product_nt(grad_value_lat, value_back)
    ).reshape(seq_local, lat_rows, model_width)
    grad_lat_in, grad_lgain, grad_lbias = norm_backward(
        grad_own_norm, own_unit, own_std, lgain_back
    )
    latent_grads = grad_middle + grad_lat_in

    def media_backward(element):
        normed_grad = product_nt(element[0], key_back) + product_nt(element[1], value_back)
        feats_grad, gain_part, bias_part = norm_backward(
            normed_grad, element[2], element[3], mgain_back
        )
        return (feats_grad, gain_part, bias_part, jnp.sum(feats_grad, axis=0))

    feats_grads, gain_parts, bias_parts, slot_sums = per_slot(
        media_backward, (grad_key_media, grad_value_media, media_unit, media_std)
    )
    grad_mgain = jnp.sum(gain_parts, axis=0)
    grad_mbias = jnp.sum(bias_parts, axis=0)
    grad_table = product_tn(one_hot, slot_sums)
    patch_grads = feats_grads.reshape(patch_feats.shape)
    (
        grad_query_w,
        grad_key_w,
        grad_value_w,
        grad_out_w,
        grad_up,
        grad_down,
    ) = lax.optimization_barrier(
        (grad_query_w, grad_key_w, grad_value_w, grad_out_w, grad_up, grad_down)
    )
    summed = (
        lax.psum_scatter(grad_query_w, ("seq", "frame"), scatter_dimension=0, tiled=True),
        lax.psum_scatter(grad_key_w, ("seq", "frame"), scatter_dimension=0, tiled=True),
        lax.psum_scatter(grad_value_w, ("seq", "frame"), scatter_dimension=0, tiled=True),
        lax.psum_scatter(grad_out_w, ("seq", "frame"), scatter_dimension=0, tiled=True),
        lax.psum_scatter(grad_up, ("seq", "frame"), scatter_dimension=0, tiled=True),
        lax.psum_scatter(grad_down, ("seq", "frame"), scatter_dimension=0, tiled=True),
        lax.psum_scatter(grad_mgain, ("seq", "frame"), scatter_dimension=0, tiled=True),
        lax.psum_scatter(grad_mbias, ("seq", "frame"), scatter_dimension=0, tiled=True),
        lax.psum_scatter(grad_lgain, ("seq", "frame"), scatter_dimension=0, tiled=True),
        lax.psum_scatter(grad_lbias, ("seq", "frame"), scatter_dimension=0, tiled=True),
        lax.psum_scatter(grad_fgain, ("seq", "frame"), scatter_dimension=0, tiled=True),
        lax.psum_scatter(grad_fbias, ("seq", "frame"), scatter_dimension=0, tiled=True),
        lax.psum_scatter(grad_table, ("seq", "frame"), scatter_dimension=1, tiled=True),
    )
    return (
        new_latents,
        latent_grads,
        patch_grads,
        summed[0],
        summed[1],
        summed[2],
        summed[3],
        summed[4],
        summed[5],
        summed[6],
        summed[7],
        summed[8],
        summed[9],
        summed[10],
        summed[11],
        summed[12],
    )


MESH = pl.DeviceIdType.MESH
F32 = jnp.float32
ANY = pl.BlockSpec(memory_space=pl.ANY)
GRID = (4, 2, 2, 2)


def place(z, y, x, c):
    return (z * 2 + y, x * 2 + c)


class Here:
    def __init__(self):
        seq, frame = lax.axis_index("seq"), lax.axis_index("frame")
        self.z, self.y, self.x, self.c = z, y, x, c = seq // 2, seq % 2, frame // 2, frame % 2
        self.ox, self.oy, self.oc = ox, oy, oc = 1 - x, 1 - y, 1 - c
        self.at_x, self.at_y, self.at_c = place(z, y, ox, c), place(z, oy, x, c), place(z, y, x, oc)
        self.ahead = [lax.rem(z + k, 4) for k in range(4)]
        self.behind = [lax.rem(z + 4 - k, 4) for k in range(4)]
        self.at_z = [place(o, y, x, c) for o in self.ahead]

    def greet(self):
        barrier = pltpu.get_barrier_semaphore()
        for peer in self.at_z[1:] + [self.at_x, self.at_y, self.at_c]:
            pl.semaphore_signal(barrier, inc=1, device_id=peer, device_id_type=MESH)
        pl.semaphore_wait(barrier, 6)


def remote(src, dst, send_sem, recv_sem, peer):
    return pltpu.make_async_remote_copy(
        src_ref=src, dst_ref=dst, send_sem=send_sem, recv_sem=recv_sem, device_id=peer, device_id_type=MESH
    )


class Gather:
    eager = True

    def __init__(self, here, shards, fulls, cuts, sems):
        self.here, self.count = here, len(cuts)
        self.loc, self.zs, self.zr, self.xs, self.xr, self.ys, self.yr, self.ds, self.dr, self.cs, self.cr = sems
        self.shard = [shards[a].at[:, lo:hi] for a, lo, hi in cuts]
        self.full = [(lambda *at, a=a, lo=lo, hi=hi: fulls[a].at[at + (slice(lo, hi),)]) for a, lo, hi in cuts]
        halves_at = [(shards[a].shape[0] // 2, shards[a].shape[0]) for a, lo, hi in cuts]
        self.rows = [(slice(0, r), slice(0, h), slice(h, r)) for h, r in halves_at]

    @staticmethod
    def semaphores(count):
        dma = pltpu.SemaphoreType.DMA
        shapes = [(), (3,), (3,), (4,), (4,), (4,), (4,), (2,), (2,), (4,), (4,)]
        return [dma((count,) + s) for s in shapes]

    def local(self, p):
        h = self.here
        return pltpu.make_async_copy(self.shard[p], self.full[p](h.z, h.y, h.x, h.c, self.rows[p][0]), self.loc.at[p])

    def over_z(self, p, k):
        h = self.here
        dst = self.full[p](h.z, h.y, h.x, h.c, self.rows[p][0])
        return remote(self.shard[p], dst, self.zs.at[p, k - 1], self.zr.at[p, k - 1], h.at_z[k])

    def counts(self, p):
        return range(4 if p == 0 else 1)

    def side(self, p, k, way):
        h = self.here
        block = self.full[p](h.behind[k] if p == 0 else slice(None), h.y, h.x, h.c, self.rows[p][0])
        src = self.shard[p] if p == 0 and k == 0 else block
        if way == 0:
            return remote(src, block, self.xs.at[p, k], self.xr.at[p, k], h.at_x)
        return remote(src, block, self.ys.at[p, k], self.yr.at[p, k], h.at_y)

    def on_y(self, p):
        h = self.here
        part = self.full[p](slice(None), h.y, h.ox, h.c, self.rows[p][2])
        return remote(part, part, self.ds.at[p, 0], self.dr.at[p, 0], h.at_y)

    def on_x(self, p):
        h = self.here
        part = self.full[p](slice(None), h.oy, h.x, h.c, self.rows[p][1])
        return remote(part, part, self.ds.at[p, 1], self.dr.at[p, 1], h.at_x)

    def to_core(self, p, i):
        h = self.here
        yy, xx = ((h.y, h.x), (h.y, h.ox), (h.oy, h.x), (h.oy, h.ox))[i]
        blocks = self.full[p](slice(None), yy, xx, h.c, self.rows[p][0])
        return remote(blocks, blocks, self.cs.at[p, i], self.cr.at[p, i], h.at_c)

    def own(self, p):
        self.local(p).start()
        for k in (1, 2, 3):
            self.over_z(p, k).start()
        if p == 0:
            self.side(p, 0, 0).start()
            self.side(p, 0, 1).start()

    def along_z(self, p):
        for k in (1, 2, 3):
            self.over_z(p, k).wait_recv()
            if p == 0:
                self.side(p, k, 0).start()
                self.side(p, k, 1).start()
        self.local(p).wait()
        if p > 0:
            self.side(p, 0, 0).start()
            self.side(p, 0, 1).start()
        self.to_core(p, 0).start()

    def across(self, p):
        for k in self.counts(p):
            self.side(p, k, 0).wait_recv()
        self.on_y(p).start()
        for k in self.counts(p):
            self.side(p, k, 1).wait_recv()
        self.on_x(p).start()
        self.to_core(p, 1).start()
        self.to_core(p, 2).start()

    def corner(self, p):
        self.on_y(p).wait_recv()
        self.on_x(p).wait_recv()
        self.to_core(p, 3).start()

    def arrived(self, p):
        for i in range(4):
            self.to_core(p, i).wait_recv()

    def done(self, p, here=False):
        if not here:
            self.arrived(p)
        for i in range(4):
            self.to_core(p, i).wait_send()
        for k in (1, 2, 3):
            self.over_z(p, k).wait_send()
        for k in self.counts(p):
            self.side(p, k, 0).wait_send()
            self.side(p, k, 1).wait_send()
        self.on_y(p).wait_send()
        self.on_x(p).wait_send()

    def stages(self):
        return (self.own, self.along_z, self.across, self.corner)


LAG = 2


def waves_of(plan, ahead=None):
    first, *stages = plan.stages()
    count, last = plan.count, len(stages) - 1
    ahead = count if ahead is None else min(ahead, count)
    waves = [[functools.partial(first, p) for p in range(ahead)]]
    for t in range(count + last * LAG):
        wave = [functools.partial(first, t + ahead)] if t + ahead < count else []
        order = range(last + 1) if plan.eager else range(last, -1, -1)
        waves.append(wave + [functools.partial(stages[s], t - s * LAG) for s in order if 0 <= t - s * LAG < count])
    return waves


def finish_all(plan):
    for p in range(plan.count):
        plan.done(p)


class Scatter:
    eager = False

    def __init__(self, here, count, mine, theirs, load, out, scratch):
        self.here, self.count, self.mine, self.theirs, self.load, self.out = here, count, mine, theirs, load, out
        self.got, self.gx, self.gy, self.hx, self.hy, self.gz = scratch[:6]
        self.cs, self.cr, self.fs, self.fr, self.ss, self.sr, self.zs, self.zr = scratch[6:]
        self.half = self.got.shape[-2] // 2

    @staticmethod
    def scratch(count, r, w):
        dma = pltpu.SemaphoreType.DMA
        leads = [(4, 2, 2, r), (4, 2, r // 2), (4, 2, r // 2), (4, r // 2), (4, r // 2), (3, r)]
        return [pltpu.VMEM((count,) + s + (w,), F32) for s in leads] + [
            dma((count,) + s) for s in ((), (), (2,), (2,), (2,), (2,), (3,), (3,))
        ]

    def to_core(self, p):
        return remote(self.theirs(p), self.got.at[p], self.cs.at[p], self.cr.at[p], self.here.at_c)

    def first(self, p, way):
        h, half, tot = self.here, self.half, self.mine(p)
        if way == 0:
            return remote(tot.at[:, :, h.ox, :half], self.gx.at[p], self.fs.at[p, 0], self.fr.at[p, 0], h.at_x)
        return remote(tot.at[:, h.oy, :, half:], self.gy.at[p], self.fs.at[p, 1], self.fr.at[p, 1], h.at_y)

    def second(self, p, way):
        h, half, tot = self.here, self.half, self.mine(p)
        if way == 0:
            return remote(tot.at[:, h.oy, h.x, :half], self.hy.at[p], self.ss.at[p, 0], self.sr.at[p, 0], h.at_y)
        return remote(tot.at[:, h.y, h.ox, half:], self.hx.at[p], self.ss.at[p, 1], self.sr.at[p, 1], h.at_x)

    def over_z(self, p, k):
        h = self.here
        src = self.mine(p).at[h.ahead[k], h.y, h.x]
        return remote(src, self.gz.at[p, k - 1], self.zs.at[p, k - 1], self.zr.at[p, k - 1], h.at_z[k])

    def start(self, p):
        if self.load is not None:
            self.load(p).start()
        self.to_core(p).start()

    def cores(self, p):
        tot, got = self.mine(p), self.got.at[p]
        if self.load is not None:
            self.load(p).wait()
        self.to_core(p).wait_recv()

        @pl.loop(0, 16)
        def _(i):
            at = (i // 4, (i // 2) % 2, i % 2)
            tot[at] = tot[at] + got[at]

        self.first(p, 0).start()
        self.first(p, 1).start()

    def sides(self, p):
        h, half, tot = self.here, self.half, self.mine(p)
        gx, gy = self.gx.at[p], self.gy.at[p]
        self.first(p, 0).wait_recv()

        @pl.loop(0, 8)
        def _(i):
            zi, yi = i // 2, i % 2
            tot[zi, yi, h.x, :half] = tot[zi, yi, h.x, :half] + gx[zi, yi]

        self.second(p, 0).start()
        self.first(p, 1).wait_recv()

        @pl.loop(0, 8)
        def _(i):
            zi, xi = i // 2, i % 2
            tot[zi, h.y, xi, half:] = tot[zi, h.y, xi, half:] + gy[zi, xi]

        self.second(p, 1).start()

    def column(self, p):
        h, half, tot = self.here, self.half, self.mine(p)
        hx, hy = self.hx.at[p], self.hy.at[p]
        self.second(p, 0).wait_recv()
        self.second(p, 1).wait_recv()

        @pl.loop(0, 4)
        def _(zi):
            tot[zi, h.y, h.x, :half] = tot[zi, h.y, h.x, :half] + hy[zi]
            tot[zi, h.y, h.x, half:] = tot[zi, h.y, h.x, half:] + hx[zi]

        for k in (1, 2, 3):
            self.over_z(p, k).start()

    def finish(self, p):
        h, gz = self.here, self.gz.at[p]
        for k in (1, 2, 3):
            self.over_z(p, k).wait_recv()
        self.out(p)[...] = (self.mine(p)[h.z, h.y, h.x] + gz[0]) + (gz[1] + gz[2])

    def done(self, p):
        self.to_core(p).wait_send()
        for way in (0, 1):
            self.first(p, way).wait_send()
            self.second(p, way).wait_send()
        for k in (1, 2, 3):
            self.over_z(p, k).wait_send()

    def stages(self):
        return (self.start, self.cores, self.sides, self.column, self.finish)


def run(wave):
    for action in wave:
        action()


class Pace:
    def __init__(self, step, steps, lead, parts, waves):
        self.step, self.steps, self.lead, self.parts = step, steps, lead, parts
        ticks, total, before = lead + steps * parts, 1 + sum(len(w) for w in waves[1:]), 0
        self.waves = [[] for _ in range(ticks)]
        for wave in waves:
            self.waves[ticks * before // total] += wave
            before += len(wave) if before else 1

    def at_lead(self, i):
        run(self.waves[i])

    def at(self, part):
        for s in range(self.steps):
            now = self.waves[self.lead + s * self.parts + part]
            if now:
                pl.when(self.step == s)(functools.partial(run, now))


def run_last(step, steps, plan):
    @pl.when(step == steps - 1)
    def _():
        finish_all(plan)


def column_cuts(shards):
    return [(a, lo, min(lo + 256, s.shape[1])) for a, s in enumerate(shards) for lo in range(0, s.shape[1], 256)]


class GroupGather:
    def __init__(self, here, shards, fulls, sems):
        self.here, self.shards, self.fulls, self.count = here, shards, fulls, len(shards)
        self.loc, self.ss, self.rs = sems

    @staticmethod
    def semaphores(count):
        dma = pltpu.SemaphoreType.DMA
        return [dma((count,)), dma((count, 3)), dma((count, 3))]

    def local(self, a):
        h = self.here
        return pltpu.make_async_copy(self.shards[a], self.fulls[a].at[:, h.x * 2 + h.c], self.loc.at[a])

    def copy(self, a, i):
        h = self.here
        mine = self.fulls[a].at[:, h.x * 2 + h.c]
        if i < 2:
            return remote(self.shards[a], mine, self.ss.at[a, i], self.rs.at[a, i], (h.at_x, h.at_c)[i])
        block = self.fulls[a].at[:, h.ox * 2 + h.c]
        return remote(block, block, self.ss.at[a, 2], self.rs.at[a, 2], h.at_c)

    def start(self):
        for a in range(self.count):
            self.local(a).start()
            self.copy(a, 0).start()
            self.copy(a, 1).start()

    def forward(self):
        for a in range(self.count):
            self.copy(a, 0).wait_recv()
            self.copy(a, 2).start()

    def done(self):
        for a in range(self.count):
            self.local(a).wait()
            self.copy(a, 0).wait_send()
            self.copy(a, 1).wait()
            self.copy(a, 2).wait()


def flat_full(full):
    return full.reshape((-1, full.shape[-1]))


def full_shapes(shards):
    return [jax.ShapeDtypeStruct(GRID + s.shape, s.dtype) for s in shards]


def gather_kernel(count, cuts, *refs):
    here = Here()
    here.greet()
    plan = Gather(here, refs[:count], refs[count : 2 * count], cuts, refs[2 * count :])
    for wave in waves_of(plan):
        run(wave)
    finish_all(plan)


def gather_all(shards, collective_id):
    count = len(shards)
    cuts = column_cuts(shards)
    outs = pl.pallas_call(
        functools.partial(gather_kernel, count, cuts),
        out_shape=full_shapes(shards),
        in_specs=[ANY] * count,
        out_specs=[ANY] * count,
        scratch_shapes=Gather.semaphores(len(cuts)),
        compiler_params=pltpu.CompilerParams(collective_id=collective_id, has_side_effects=True),
        name="gather_all",
    )(*shards)
    return [flat_full(o) for o in outs]


class Summed:
    def __init__(self, parts):
        self.arrays = len(parts)
        self.rows, self.width = parts[0].shape[0] // 32, parts[0].shape[1]
        self.cut = min(256, self.width)
        self.pieces = self.width // self.cut
        self.operands = [p.reshape(GRID + (self.rows, self.width)) for p in parts]
        self.in_specs = [ANY] * len(parts)
        self.out_shape = [jax.ShapeDtypeStruct((self.rows, self.width), F32)] * len(parts)
        self.out_specs = [whole((self.rows, self.width))] * len(parts)
        n = self.count = len(parts) * self.pieces
        self.scratch = [pltpu.VMEM((n, 4, 2, 2, self.rows, self.cut), F32), pltpu.SemaphoreType.DMA((n,))]
        self.scratch += Scatter.scratch(n, self.rows, self.cut)

    def bind(self, here, ins, outs, scratch):
        tots, loc = scratch[:2]

        def cut(p):
            lo = p % self.pieces * self.cut
            return p // self.pieces, slice(lo, lo + self.cut)

        def part(p, core):
            a, cols = cut(p)
            return ins[a].at[:, :, :, core, :, cols]

        def out(p):
            a, cols = cut(p)
            return outs[a].at[:, cols]

        return Scatter(
            here,
            self.count,
            lambda p: tots.at[p],
            lambda p: part(p, here.oc),
            lambda p: pltpu.make_async_copy(part(p, here.c), tots.at[p], loc.at[p]),
            out,
            scratch[2:],
        )


def scatter_kernel(plan, *refs):
    n = plan.arrays
    here = Here()
    here.greet()
    sums = plan.bind(here, refs[:n], refs[n : 2 * n], refs[2 * n :])
    for wave in waves_of(sums):
        run(wave)
    finish_all(sums)


def scatter_all(parts, collective_id):
    plan = Summed(parts)
    return pl.pallas_call(
        functools.partial(scatter_kernel, plan),
        out_shape=plan.out_shape,
        in_specs=plan.in_specs,
        out_specs=[pl.BlockSpec(memory_space=pltpu.VMEM)] * len(parts),
        scratch_shapes=plan.scratch,
        compiler_params=pltpu.CompilerParams(
            collective_id=collective_id, has_side_effects=True, vmem_limit_bytes=60 * 2**20
        ),
        name="scatter_all",
    )(*plan.operands)


def greet(peers):
    barrier = pltpu.get_barrier_semaphore()
    for peer in peers:
        pl.semaphore_signal(barrier, inc=1, device_id=peer, device_id_type=MESH)
    pl.semaphore_wait(barrier, len(peers))


def group_gather_kernel(count, *refs):
    shards, fulls = refs[:count], refs[count : 2 * count]
    loc, ss, rs = refs[2 * count :]
    here = Here()
    x, c, ox, at_x, at_c = here.x, here.c, here.ox, here.at_x, here.at_c
    greet([at_x, at_c])
    waits = []
    for a in range(count):
        mine = fulls[a].at[:, x * 2 + c]
        copy = pltpu.make_async_copy(shards[a], mine, loc.at[a])
        copy.start()
        over = remote(shards[a], mine, ss.at[a, 0], rs.at[a, 0], at_x)
        over.start()
        side = remote(shards[a], mine, ss.at[a, 1], rs.at[a, 1], at_c)
        side.start()
        waits.append((copy, over, side))
    last = []
    for a in range(count):
        waits[a][1].wait_recv()
        block = fulls[a].at[:, ox * 2 + c]
        on = remote(block, block, ss.at[a, 2], rs.at[a, 2], at_c)
        on.start()
        last.append(on)
    for a in range(count):
        copy, over, side = waits[a]
        copy.wait()
        over.wait_send()
        side.wait()
        last[a].wait()


def group_gather(shards, collective_id):
    count = len(shards)
    dma = pltpu.SemaphoreType.DMA
    return pl.pallas_call(
        functools.partial(group_gather_kernel, count),
        out_shape=[jax.ShapeDtypeStruct((s.shape[0], 4) + s.shape[1:], F32) for s in shards],
        in_specs=[ANY] * count,
        out_specs=[ANY] * count,
        scratch_shapes=[dma((count,)), dma((count, 3)), dma((count, 3))],
        compiler_params=pltpu.CompilerParams(collective_id=collective_id, has_side_effects=True),
        name="group_gather",
    )(*shards)


def group_swap_kernel(count, *refs):
    shards, fulls = refs[:count], refs[count : 2 * count]
    loc, ss, rs = refs[2 * count :]
    here = Here()
    z, y, x, c = here.z, here.y, here.x, here.c
    me = x * 2 + c
    peers = [(x, 1 - c), (1 - x, c), (1 - x, 1 - c)]
    greet([place(z, y, *p) for p in peers])
    waits = []
    for a in range(count):
        copy = pltpu.make_async_copy(shards[a].at[:, me], fulls[a].at[:, me], loc.at[a])
        copy.start()
        waits.append(copy)
        for k in (1, 2, 0):
            px, pc = peers[k]
            on = remote(
                shards[a].at[:, px * 2 + pc], fulls[a].at[:, me], ss.at[a, k], rs.at[a, k], place(z, y, px, pc)
            )
            on.start()
            waits.append(on)
    for copy in waits:
        copy.wait()


def group_swap(shards, collective_id):
    count = len(shards)
    dma = pltpu.SemaphoreType.DMA
    return pl.pallas_call(
        functools.partial(group_swap_kernel, count),
        out_shape=[jax.ShapeDtypeStruct(s.shape, F32) for s in shards],
        in_specs=[ANY] * count,
        out_specs=[ANY] * count,
        scratch_shapes=[dma((count,)), dma((count, 3)), dma((count, 3))],
        compiler_params=pltpu.CompilerParams(collective_id=collective_id, has_side_effects=True),
        name="group_swap",
    )(*shards)


BF16 = jnp.bfloat16
HIGH = lax.Precision.HIGH
BLOCK = 256


def dot(left, right, dims=(1, 0)):
    return lax.dot_general(
        left, right, (((dims[0],), (dims[1],)), ((), ())), precision=HIGH, preferred_element_type=F32
    )


def dot3(left, right, dims=(1, 0)):
    numbers = (((dims[0],), (dims[1],)), ((), ()))
    one = functools.partial(lax.dot_general, dimension_numbers=numbers, preferred_element_type=F32)
    return one(left[0], right[0]) + (one(left[0], right[1]) + one(left[1], right[0]))


def halves(values):
    top = values.astype(BF16)
    return top, (values - top.astype(F32)).astype(BF16)


def split_weights(sources, pairs, stage, sems, pace):
    step = stage.shape[1]
    chunks = [(i, r) for i, s in enumerate(sources) for r in range(0, s.shape[0], step)]

    def copy(n):
        i, r = chunks[n]
        return pltpu.make_async_copy(sources[i].at[r : r + step], stage.at[n % 2], sems.at[n % 2])

    copy(0).start()
    for n, (i, r) in enumerate(chunks):
        if n * pace.lead % len(chunks) == 0:
            pace.at_lead(n * pace.lead // len(chunks))
        if n + 1 < len(chunks):
            copy(n + 1).start()
        copy(n).wait()
        pairs[i][0][r : r + step], pairs[i][1][r : r + step] = halves(stage[n % 2])


def unit_of(values):
    centred = values - jnp.mean(values, axis=-1, keepdims=True)
    inv_std = lax.rsqrt(jnp.mean(centred * centred, axis=-1, keepdims=True) + EPSILON)
    return centred * inv_std, inv_std


def staging(width):
    return [pltpu.VMEM((width, width), BF16)] * 4 + [pltpu.VMEM((2, 128, width), F32), pltpu.SemaphoreType.DMA((2,))]


def whole(shape, buffers=1):
    return pl.BlockSpec(shape, lambda *i: (0,) * len(shape), pipeline_mode=pl.Buffered(buffers))


def opening_kernel(cuts, *refs):
    times, feats, latents = refs[:3]
    shards, group_shard = refs[3:9], refs[9:10]
    vec, keys, values, own_keys, own_values, queries, xt_top, xt_low = refs[10:18]
    fulls, group_full = refs[18:24], refs[24:25]
    pk, top, low, own_top, own_low, lat, lat_top, lat_low, stage, load = refs[25:35]
    sems, group_sems = refs[35:46], refs[46:]
    step = pl.program_id(0)
    here = Here()
    moved = Gather(here, shards, fulls, cuts, sems)
    group = GroupGather(here, group_shard, group_full, group_sems)
    waves = waves_of(moved, 6)
    waves[0] = [here.greet, group.start] + waves[0]
    waves[2].append(group.forward)
    cut = keys.shape[1]
    slots, chunks = top.shape[0] // BLOCK, shards[1].shape[1] // cut
    head = 6

    def run_waves(lo, hi):
        for wave in waves[lo:hi]:
            run(wave)

    def at(s, action):
        pl.when(step == s)(action)

    def start():
        run_waves(0, head)
        moved.arrived(0)
        copy = pltpu.make_async_copy(fulls[0], pk, load.at[0])
        copy.start()
        copy.wait()
        strip = shards[1].shape[0]
        vec[...] = jnp.concatenate([pk[i // 8, i // 4 % 2, i // 2 % 2, i % 2][:, :strip] for i in range(32)], axis=1)
        own_top[...], own_low[...] = halves(unit_of(latents[...])[0] * vec[2:3] + vec[3:4])

    at(0, start)
    for s in range(1, 4):
        at(s, functools.partial(run_waves, head + s - 1, head + s))

    @pl.when(step < slots)
    def _():
        embed = vec[pl.ds(6 + times[step], 1)]
        normed = unit_of(feats[...] + embed)[0] * vec[0:1] + vec[1:2]
        rows = pl.ds(pl.multiple_of(step * BLOCK, BLOCK), BLOCK)
        top[rows], low[rows] = halves(normed)
        xt_top[...], xt_low[...] = halves(jnp.swapaxes(normed, 0, 1))

    def chunk(array, n, piece, left, right, out, own_out):
        moved.arrived(piece)
        copy = pltpu.make_async_copy(fulls[array].at[:, :, :, :, :, n * cut : (n + 1) * cut], stage.at[array % 2], load.at[0])
        copy.start()
        copy.wait()
        pair = halves(stage[array % 2].reshape((-1, cut)))
        step_rows = min(512, left.shape[0])

        @pl.loop(0, left.shape[0] // step_rows)
        def _(m):
            rows = pl.ds(pl.multiple_of(m * step_rows, step_rows), step_rows)
            out[rows] = dot3((left[rows], right[rows]), pair)

        if own_out is not None:
            own_out[...] = dot3((own_top[...], own_low[...]), pair)

    lead = head + 3
    for n in range(chunks):

        def both(n=n):
            run_waves(lead + 2 * n, lead + 2 * n + 1)
            chunk(1, n, 1 + 2 * n, top, low, keys, own_keys)
            run_waves(lead + 2 * n + 1, lead + 2 * n + 2)
            chunk(2, n, 2 + 2 * n, top, low, values, own_values)

        at(slots + n, both)

    rest = len(waves) - lead - 2 * chunks
    for n in range(chunks):

        def query(n=n):
            if n == 0:
                group.done()
                copy = pltpu.make_async_copy(group_full[0], lat, load.at[0])
                copy.start()
                copy.wait()
                flat = lat[...].reshape(lat_top.shape)
                lat_top[...], lat_low[...] = halves(unit_of(flat)[0] * vec[2:3] + vec[3:4])
            chunk(3, n, 1 + 2 * chunks + n, lat_top, lat_low, queries, None)
            first = lead + 2 * chunks
            run_waves(first + rest * n // chunks, first + rest * (n + 1) // chunks)
            if n == chunks - 1:
                for p in range(moved.count):
                    moved.done(p, p <= 3 * chunks)

        at(slots + chunks + n, query)


def opening(times, feats, latents, packed, key_w, value_w, query_w, cot, out_w, collective_id):
    rows, width = feats.shape
    seqs, own_each, _ = latents.shape
    own_rows, lat_rows = seqs * own_each, seqs * own_each * 4
    slots, cut = rows // BLOCK, 256
    chunks = width // cut
    shards = [packed, key_w, value_w, query_w, cot, out_w]
    cuts = [(0, 0, 128)] + [(a, lo, lo + cut) for lo in range(0, width, cut) for a in (1, 2)]
    cuts += [(a, lo, lo + cut) for a in (3, 4, 5) for lo in range(0, width, cut)]
    clip = lambda i, lo: jnp.clip(i - lo, 0, chunks - 1)
    chunk_of = lambda n, lo: pl.BlockSpec((n, cut), lambda i: (0, clip(i, lo)))
    turned = pl.BlockSpec((width, BLOCK), lambda i: (0, jnp.minimum(i, slots - 1)))
    full = lambda n, kind=F32: jax.ShapeDtypeStruct((n, width), kind)
    outs = pl.pallas_call(
        functools.partial(opening_kernel, cuts),
        grid=(slots + 2 * chunks,),
        in_specs=[
            SMEM,
            pl.BlockSpec((BLOCK, width), lambda i: (jnp.minimum(i, slots - 1), 0)),
            whole((own_rows, width)),
        ]
        + [ANY] * 7,
        out_specs=[
            whole((16, width)),
            chunk_of(rows, slots),
            chunk_of(rows, slots),
            chunk_of(own_rows, slots),
            chunk_of(own_rows, slots),
            chunk_of(lat_rows, slots + chunks),
            turned,
            turned,
        ]
        + [ANY] * 7,
        out_shape=[full(16), full(rows), full(rows), full(own_rows), full(own_rows), full(lat_rows)]
        + [jax.ShapeDtypeStruct((width, rows), BF16)] * 2
        + full_shapes(shards)
        + [jax.ShapeDtypeStruct((seqs, 4, own_each, width), F32)],
        scratch_shapes=[
            pltpu.VMEM(GRID + packed.shape, F32),
            pltpu.VMEM((rows, width), BF16),
            pltpu.VMEM((rows, width), BF16),
            pltpu.VMEM((own_rows, width), BF16),
            pltpu.VMEM((own_rows, width), BF16),
            pltpu.VMEM((seqs, 4, own_each, width), F32),
            pltpu.VMEM((lat_rows, width), BF16),
            pltpu.VMEM((lat_rows, width), BF16),
            pltpu.VMEM((2,) + GRID + (width // 32, cut), F32),
            pltpu.SemaphoreType.DMA((1,)),
        ]
        + Gather.semaphores(len(cuts))
        + GroupGather.semaphores(1),
        compiler_params=pltpu.CompilerParams(
            collective_id=collective_id, has_side_effects=True, vmem_limit_bytes=60 * 2**20
        ),
        name="opening",
    )(times, feats, latents.reshape(own_rows, width), *shards, latents)
    return outs[:8], [flat_full(o) for o in outs[9:14]], outs[14]


def pair_rows(values, first, head):
    lane = lax.broadcasted_iota(jnp.int32, values.shape, 1)
    return jnp.concatenate(
        [
            jnp.where((lane >= first) & (lane < first + head), values, 0.0),
            jnp.where((lane >= first + head) & (lane < first + 2 * head), values, 0.0),
        ],
        axis=0,
    )


def pair_merge(stacked, first, head):
    half = stacked.shape[0] // 2
    lane = lax.broadcasted_iota(jnp.int32, (half, stacked.shape[1]), 1)
    one = jnp.where((lane >= first) & (lane < first + head), stacked[:half], 0.0)
    return one + jnp.where((lane >= first + head) & (lane < first + 2 * head), stacked[half:], 0.0)


def join(left, right):
    return jnp.concatenate([left[:, :128], left[:, 128:] + right[:, :128], right[:, 128:]], axis=1)


def windows(head):
    return ((slice(0, 256), 0), (slice(128, 384), 2 * head - 128))


def score_block(present, seq, keys, own_keys, q_pair, window, inv_root):
    at = keys.shape[0]
    scores = jnp.concatenate([dot(keys[:, window], q_pair, (1, 1)), dot(own_keys[:, window], q_pair, (1, 1))], axis=0)
    row = lax.broadcasted_iota(jnp.int32, scores.shape, 0)
    keep = (row >= at) | ((row < at // 2) & (present[seq, 0] > 0)) | ((row >= at // 2) & (present[seq, 1] > 0))
    return jnp.where(keep, scores * inv_root, MASKED)


def attend_kernel(inv_root, head, present, queries, keys, values, own_keys, own_values, out, tops, sums):
    seq, group = pl.program_id(0), pl.program_id(1)
    merged = []
    for p, (window, first) in enumerate(windows(head)):
        q_pair = pair_rows(queries[:, window], first, head)
        scores = score_block(present, seq, keys, own_keys, q_pair, window, inv_root)
        top = jnp.max(scores, axis=0, keepdims=True)
        expo = jnp.exp(scores - top)
        tops[pl.ds(group * 2 + p, 1)] = top
        sums[pl.ds(group * 2 + p, 1)] = jnp.sum(expo, axis=0, keepdims=True)
        at = keys.shape[0]
        stacked = dot(expo[:at], values[:, window], (0, 0)) + dot(expo[at:], own_values[:, window], (0, 0))
        merged.append(pair_merge(stacked, first, head))
    out[...] = join(*merged)


def attend_specs(lat, media, rows):
    group = 384
    query = pl.BlockSpec((None, lat, group), lambda b, g: (b, 0, g))
    key = pl.BlockSpec((media, group), lambda b, g: (b, g))
    own = pl.BlockSpec((rows, group), lambda b, g: (b, g))
    stat = pl.BlockSpec((None, 8, 128), lambda b, g: (b, 0, 0))
    return query, key, own, stat


SMEM = pl.BlockSpec(memory_space=pltpu.SMEM)


def attend(present, queries, keys, values, own_keys, own_values):
    seqs, lat, width = queries.shape
    head = width // HEADS
    query, key, own, stat = attend_specs(lat, keys.shape[0] // seqs, own_keys.shape[0] // seqs)
    stat_shape = jax.ShapeDtypeStruct((seqs, 8, 128), F32)
    return pl.pallas_call(
        functools.partial(attend_kernel, 1.0 / math.sqrt(head), head),
        grid=(seqs, width // 384),
        in_specs=[SMEM, query, key, key, own, own],
        out_specs=[query, stat, stat],
        out_shape=[jax.ShapeDtypeStruct(queries.shape, F32), stat_shape, stat_shape],
        compiler_params=pltpu.CompilerParams(vmem_limit_bytes=60 * 2**20),
        name="attend",
    )(present, queries, keys, values, own_keys, own_values)


def attend_back_kernel(inv_root, head, plan, steps, *refs):
    present, queries, grads, logs, deltas, keys, values, own_keys, own_values = refs[:9]
    n = plan.arrays
    query_out, key_out, value_out, own_key_out, own_value_out = refs[9 + n : 14 + n]
    seq, group = pl.program_id(0), pl.program_id(1)
    step = seq * pl.num_programs(1) + group
    here = Here()
    moved = plan.bind(here, refs[9 : 9 + n], refs[14 + n : 14 + 2 * n], refs[14 + 2 * n :])
    waves = waves_of(moved)
    waves[0].insert(0, here.greet)
    pace = Pace(step, steps, 0, 2, waves)
    merged, key_grads, value_grads = [], [], []
    at = keys.shape[0]
    for p, (window, first) in enumerate(windows(head)):
        pace.at(p)
        q_pair = pair_rows(queries[:, window], first, head)
        g_pair = pair_rows(grads[:, window], first, head)
        scores = score_block(present, seq, keys, own_keys, q_pair, window, inv_root)
        probs = jnp.exp(scores - logs[pl.ds(group * 2 + p, 1)])
        grad_probs = jnp.concatenate(
            [dot(values[:, window], g_pair, (1, 1)), dot(own_values[:, window], g_pair, (1, 1))], axis=0
        )
        grad_scores = probs * (grad_probs - deltas[pl.ds(group * 2 + p, 1)]) * inv_root
        stacked = dot(grad_scores[:at], keys[:, window], (0, 0)) + dot(grad_scores[at:], own_keys[:, window], (0, 0))
        merged.append(pair_merge(stacked, first, head))
        key_grads.append(dot(grad_scores, q_pair))
        value_grads.append(dot(probs, g_pair))
    query_out[...] = join(*merged)
    key_grad, value_grad = join(*key_grads), join(*value_grads)
    key_out[...], own_key_out[...] = key_grad[:at], key_grad[at:]
    value_out[...], own_value_out[...] = value_grad[:at], value_grad[at:]
    run_last(step, steps, moved)


def attend_back(present, queries, grads, logs, deltas, keys, values, own_keys, own_values, plan, collective_id):
    seqs, lat, width = queries.shape
    head = width // HEADS
    query, key, own, stat = attend_specs(lat, keys.shape[0] // seqs, own_keys.shape[0] // seqs)
    shape = lambda v: jax.ShapeDtypeStruct(v.shape, F32)
    grid = (seqs, width // 384)
    outs = pl.pallas_call(
        functools.partial(attend_back_kernel, 1.0 / math.sqrt(head), head, plan, grid[0] * grid[1]),
        grid=grid,
        in_specs=[SMEM, query, query, stat, stat, key, key, own, own] + plan.in_specs,
        out_specs=[query, key, key, own, own] + plan.out_specs,
        out_shape=[shape(queries), shape(keys), shape(values), shape(own_keys), shape(own_values)] + plan.out_shape,
        scratch_shapes=plan.scratch,
        compiler_params=pltpu.CompilerParams(
            collective_id=collective_id, has_side_effects=True, vmem_limit_bytes=60 * 2**20
        ),
        name="attend_back",
    )(present, queries, grads, logs, deltas, keys, values, own_keys, own_values, *plan.operands)
    return outs[:5], outs[5:]


def weight_kernel(steps, xt_top, xt_low, own_t, grad_keys, grad_values, own_gk, own_gv, vec, outs, vec_out, mats, *rest):
    n = pl.program_id(0)
    here = Here()
    cut = grad_keys.shape[1]
    sums = Scatter(
        here,
        2 * steps,
        lambda p: mats.at[p, :, :, :, here.c],
        lambda p: mats.at[p, :, :, :, here.oc],
        None,
        lambda p: outs.at[p % 2, :, pl.ds(pl.multiple_of(p // 2 * cut, cut), cut)],
        rest[:14],
    )
    tot, loc = rest[14:16]
    small = Scatter(
        here,
        1,
        lambda p: tot,
        lambda p: vec.at[:, :, :, here.oc],
        lambda p: pltpu.make_async_copy(vec.at[:, :, :, here.c], tot, loc.at[p]),
        lambda p: vec_out,
        rest[16:],
    )
    stages = sums.stages()

    @pl.when(n == 0)
    def _():
        here.greet()

    for w, (grad, own_grad) in enumerate(((grad_keys, own_gk), (grad_values, own_gv))):
        pair = halves(grad[...])
        top, low = halves(own_grad[...])
        stacked = jnp.concatenate([top, low, top], axis=0)

        @pl.loop(0, 2)
        def _(i):
            rows = pl.ds(pl.multiple_of(i * 768, 768), 768)
            made = dot3((xt_top[rows], xt_low[rows]), pair)
            made += jnp.dot(own_t[rows], stacked, preferred_element_type=F32)
            mats[2 * n + w, pl.ds(i * 2, 2)] = made.reshape((2, 2, 2, 2, 48, cut))

        sums.start(2 * n + w)
        for s in (4, 3, 2, 1):
            p = 2 * n + w - LAG * s

            @pl.when(p >= 0)
            def _():
                stages[s](p)

        if w == 1:
            for s in range(5):

                @pl.when(n == s)
                def _():
                    small.stages()[s](0)

    @pl.when(n == steps - 1)
    def _():
        for t in range(2 * steps, 2 * steps + 4 * LAG):
            for s in (4, 3, 2, 1):
                if 0 <= t - LAG * s < 2 * steps:
                    stages[s](t - LAG * s)

        @pl.loop(0, 2 * steps)
        def _(p):
            sums.done(p)

        small.done(0)


def weight_grads(xt_top, xt_low, own_t, grad_keys, grad_values, own_gk, own_gv, vec, collective_id):
    width, rows = xt_top.shape
    own_rows = own_gk.shape[0]
    steps = width // BLOCK
    cols = lambda n: pl.BlockSpec((n, BLOCK), lambda i: (0, i))
    r = width // 32
    vr, vw = vec.shape[0] // 32, vec.shape[1]
    outs, vec_sum = pl.pallas_call(
        functools.partial(weight_kernel, steps),
        grid=(steps,),
        in_specs=[
            whole((width, rows)),
            whole((width, rows)),
            whole(own_t.shape),
            cols(rows),
            cols(rows),
            cols(own_rows),
            cols(own_rows),
            ANY,
        ],
        out_specs=[whole((2, r, width)), whole((vr, vw))],
        out_shape=[jax.ShapeDtypeStruct((2, r, width), F32), jax.ShapeDtypeStruct((vr, vw), F32)],
        scratch_shapes=[pltpu.VMEM((2 * steps,) + GRID + (r, BLOCK), F32)]
        + Scatter.scratch(2 * steps, r, BLOCK)
        + [pltpu.VMEM((4, 2, 2, vr, vw), F32), pltpu.SemaphoreType.DMA((1,))]
        + Scatter.scratch(1, vr, vw),
        compiler_params=pltpu.CompilerParams(
            collective_id=collective_id, has_side_effects=True, vmem_limit_bytes=62 * 2**20
        ),
        name="weight_grads",
    )(xt_top, xt_low, own_t, grad_keys, grad_values, own_gk, own_gv, vec.reshape(GRID + (vr, vw)))
    return outs[0], outs[1], vec_sum


def media_back_kernel(plan, steps, *refs):
    feats, embed, gain, grad_keys, grad_values, own_gk, own_gv, key_w, value_w = refs[:9]
    n = plan.arrays
    out, own_out, sums = refs[9 + n : 12 + n]
    kt, kl, vt, vl, stage, sems = refs[12 + 2 * n : 18 + 2 * n]
    step = pl.program_id(0)
    here = Here()
    moved = plan.bind(here, refs[9 : 9 + n], refs[12 + n : 12 + 2 * n], refs[18 + 2 * n :])
    waves = waves_of(moved)
    waves[0].insert(0, here.greet)
    pace = Pace(step, steps, 4, 3, waves)

    @pl.when(step == 0)
    def _():
        split_weights((key_w, value_w), ((kt, kl), (vt, vl)), stage, sems, pace)
        own_out[...] = dot3(halves(own_gk[...]), (kt[...], kl[...]), (1, 1)) + dot3(
            halves(own_gv[...]), (vt[...], vl[...]), (1, 1)
        )
        sums[...] = jnp.zeros_like(sums)

    key_pair, value_pair = halves(grad_keys[...]), halves(grad_values[...])
    for i in range(3):
        pace.at(i)
        rows = slice(i * 512, i * 512 + 512)
        out[:, rows] = dot3(key_pair, (kt[rows], kl[rows]), (1, 1)) + dot3(value_pair, (vt[rows], vl[rows]), (1, 1))
    strip = 64

    @pl.loop(0, out.shape[0] // strip)
    def _(i):
        rows = pl.ds(pl.multiple_of(i * strip, strip), strip)
        incoming = out[rows]
        unit, inv_std = unit_of(feats[rows] + embed[...])
        sums[pl.ds(0, 1)] += jnp.sum(incoming * unit, axis=0, keepdims=True)
        sums[pl.ds(1, 1)] += jnp.sum(incoming, axis=0, keepdims=True)
        scaled = incoming * gain[...]
        result = inv_std * (
            scaled
            - jnp.mean(scaled, axis=-1, keepdims=True)
            - unit * jnp.mean(scaled * unit, axis=-1, keepdims=True)
        )
        out[rows] = result
        sums[pl.ds(2 + step, 1)] += jnp.sum(result, axis=0, keepdims=True)

    run_last(step, steps, moved)


def media_backward(feats, embed, gain, grad_keys, grad_values, own_gk, own_gv, key_w, value_w, plan, collective_id):
    rows, width = feats.shape
    own_rows = own_gk.shape[0]
    row_block = pl.BlockSpec((BLOCK, width), lambda i: (i, 0))
    one_block = pl.BlockSpec((BLOCK, width), lambda i: (i, 0), pipeline_mode=pl.Buffered(1))
    steps = rows // BLOCK
    outs = pl.pallas_call(
        functools.partial(media_back_kernel, plan, steps),
        grid=(steps,),
        in_specs=[
            one_block,
            pl.BlockSpec((None, 1, width), lambda i: (i, 0, 0)),
            whole((1, width)),
            row_block,
            row_block,
            whole((own_rows, width)),
            whole((own_rows, width)),
            ANY,
            ANY,
        ]
        + plan.in_specs,
        out_specs=[one_block, whole((own_rows, width)), whole((8, width))] + plan.out_specs,
        out_shape=[
            jax.ShapeDtypeStruct((rows, width), F32),
            jax.ShapeDtypeStruct((own_rows, width), F32),
            jax.ShapeDtypeStruct((8, width), F32),
        ]
        + plan.out_shape,
        scratch_shapes=staging(width) + plan.scratch,
        compiler_params=pltpu.CompilerParams(
            collective_id=collective_id, has_side_effects=True, vmem_limit_bytes=64 * 2**20 - 2**16
        ),
        name="media_backward",
    )(feats, embed, gain, grad_keys, grad_values, own_gk, own_gv, key_w, value_w, *plan.operands)
    return outs[:3], outs[3:]


GELU_A = math.sqrt(2.0 / math.pi)
GELU_B = 0.044715


def feed_kernel(feed, cot, up, down, feed_part, new_part, grad_up_t, grad_down):
    @pl.when(pl.program_id(0) == 0)
    def _():
        grad_up_t[...] = jnp.zeros_like(grad_up_t)
        grad_down[...] = jnp.zeros_like(grad_down)

    hidden = dot(feed[...], up[...])
    grad_act = dot(cot[...], down[...], (1, 1))
    square = hidden * hidden
    bent = jnp.tanh(GELU_A * (hidden + GELU_B * hidden * square))
    activated = 0.5 * hidden * (1.0 + bent)
    slope = 0.5 * (1.0 + bent) + 0.5 * hidden * (1.0 - bent * bent) * (GELU_A * (1.0 + 3.0 * GELU_B * square))
    grad_hidden = grad_act * slope
    feed_part[...] = dot(grad_hidden, up[...], (1, 1))
    new_part[...] = dot(activated, down[...])
    grad_up_t[...] += dot(grad_hidden, feed[...], (0, 0))
    grad_down[...] += dot(activated, cot[...], (0, 0))


def feed_forward(feed, cot, up, down):
    rows, width = feed.shape
    units = up.shape[1]
    row_block = pl.BlockSpec((BLOCK, width), lambda i: (i, 0))
    one_block = pl.BlockSpec((BLOCK, width), lambda i: (i, 0), pipeline_mode=pl.Buffered(1))
    big = jax.ShapeDtypeStruct((rows, width), F32)
    slim = jax.ShapeDtypeStruct((units, width), F32)
    return pl.pallas_call(
        feed_kernel,
        grid=(rows // BLOCK,),
        in_specs=[row_block, row_block, whole((width, units)), whole((units, width))],
        out_specs=[row_block, row_block, whole((units, width)), whole((units, width))],
        out_shape=[big, big, slim, slim],
        compiler_params=pltpu.CompilerParams(vmem_limit_bytes=60 * 2**20),
        name="feed_forward",
    )(feed, cot, up, down)


def mm(left, right):
    return jnp.dot(left, right, precision=HIGH, preferred_element_type=F32)


def mm_tn(left, right):
    return lax.dot_general(left, right, (((0,), (0,)), ((), ())), precision=HIGH, preferred_element_type=F32)


def mm_nt(left, right):
    return lax.dot_general(left, right, (((1,), (1,)), ((), ())), precision=HIGH, preferred_element_type=F32)


def body_fast(
    latents,
    patch_feats,
    image_counts,
    time_index,
    query_proj,
    key_proj,
    value_proj,
    out_proj,
    up_proj,
    down_proj,
    media_gain,
    media_bias,
    latent_gain,
    latent_bias,
    feed_gain,
    feed_bias,
    time_table,
    out_cotangent,
):
    frame = lax.axis_index("frame")
    frames = lax.axis_size("frame")
    seqs, rows, width = latents.shape
    rounds, patches = patch_feats.shape[1], patch_feats.shape[3]
    lat = rows * frames
    head = width // HEADS
    strip = media_gain.shape[0]

    vectors = jnp.concatenate(
        [jnp.stack([media_gain, media_bias, latent_gain, latent_bias, feed_gain, feed_bias]), time_table], axis=0
    )
    packed = jnp.pad(vectors, ((0, 2), (0, 128 - strip)))
    up_cols = lax.all_to_all(
        up_proj.reshape(strip, 32, -1), ("seq", "frame"), split_axis=1, concat_axis=0, tiled=True
    ).reshape(width, -1)

    slot_ids = jnp.arange(rounds, dtype=jnp.int32) * frames + frame
    present = slot_ids[None, :] < image_counts[:, None]
    picks = jnp.arange(time_index.shape[1], dtype=jnp.int32)[None, :] == slot_ids[:, None]
    slot_times = jnp.sum(jnp.where(picks[None, :, :], time_index[:, None, :], 0), axis=-1)
    feats = patch_feats.reshape(-1, width)

    (vec_all, keys, values, own_keys, own_values, queries, xt_top, xt_low), gathered, lat_blocks = opening(
        slot_times.reshape(-1), feats, latents, packed, key_proj, value_proj, query_proj, flatten(out_cotangent), out_proj, 0
    )
    key_w, value_w, query_w, cot_all, out_w = gathered
    mgain, mbias, lgain, lbias, fgain, fbias = (vec_all[i] for i in range(6))
    table = vec_all[6:14]
    queries = queries.reshape(seqs, lat, width)
    latent_norm, latent_unit, latent_std = norm_forward(lat_blocks.reshape(seqs, lat, width), lgain, lbias)
    own_rows = lambda v: lax.dynamic_slice_in_dim(v, frame * rows, rows, 1)
    own_norm, own_unit, own_std = own_rows(latent_norm), own_rows(latent_unit), own_rows(latent_std)
    one_hot = slot_times[:, :, None] == jnp.arange(time_table.shape[0], dtype=jnp.int32)
    slot_embed = jnp.sum(jnp.where(one_hot[..., None], table, 0.0), axis=2)
    embed = slot_embed.reshape(-1, 1, width)
    own_flat = flatten(own_norm)
    present = present.astype(jnp.int32)

    partial, row_top, row_sum = attend(present, queries, keys, values, own_keys, own_values)
    stats = jnp.concatenate([row_top.reshape(seqs, HEADS, lat), row_sum.reshape(seqs, HEADS, lat)], axis=1)
    stats = jnp.pad(stats.transpose(0, 2, 1), ((0, 0), (0, 0), (0, 128 - 2 * HEADS)))
    part_all, stat_all = group_swap(
        [partial.reshape(seqs, frames, rows, width), stats.reshape(seqs, frames, rows, 128)], 2
    )
    tops, sums = stat_all[..., :HEADS], stat_all[..., HEADS : 2 * HEADS]
    top = jnp.max(tops, axis=1)
    ratio = jnp.exp(tops - top[:, None])
    row_total = jnp.sum(sums * ratio, axis=1)
    weight = ratio / row_total[:, None]
    attended = jnp.sum(part_all.reshape(seqs, frames, rows, HEADS, head) * weight[..., None], axis=1)
    log_total = top + jnp.log(row_total)
    attended_flat = attended.reshape(seqs, rows, width)
    middle = latents + mm(flatten(attended_flat), out_w).reshape(seqs, rows, width)

    feed_norm, feed_unit, feed_std = norm_forward(middle, fgain, fbias)
    (feed_all,) = gather_all([flatten(feed_norm)], 3)
    feed_part, new_part, grad_up_t, grad_down = feed_forward(feed_all, cot_all, up_cols, down_proj)
    (grad_feed_norm,) = scatter_all([feed_part], 4)
    grad_up = lax.all_to_all(
        grad_up_t.reshape(-1, 32, strip).transpose(1, 2, 0), ("seq", "frame"), split_axis=0, concat_axis=2, tiled=True
    ).reshape(strip, -1)
    grad_mid_norm, grad_fgain, grad_fbias = norm_backward(
        grad_feed_norm.reshape(seqs, rows, width), feed_unit, feed_std, fgain
    )
    grad_middle = out_cotangent + grad_mid_norm
    grad_out_w = mm_tn(flatten(attended_flat), flatten(grad_middle))
    grad_own = mm_nt(flatten(grad_middle), out_w).reshape(seqs, rows, HEADS, head)
    delta = jnp.sum(grad_own * attended, axis=-1)
    back_stats = jnp.pad(jnp.concatenate([log_total, delta], axis=-1), ((0, 0), (0, 0), (0, 128 - 2 * HEADS)))
    grad_blocks, back_blocks = group_gather([grad_own.reshape(seqs, rows, width), back_stats], 5)
    back_all = back_blocks.reshape(seqs, lat, 128).transpose(0, 2, 1)
    logs_all, delta_all = (back_all[:, i * HEADS : (i + 1) * HEADS].reshape(seqs, 8, 128) for i in range(2))

    (query_part, grad_keys, grad_values, own_gk, own_gv), (new_rows,) = attend_back(
        present,
        queries,
        grad_blocks.reshape(seqs, lat, width),
        logs_all,
        delta_all,
        keys,
        values,
        own_keys,
        own_values,
        Summed([new_part]),
        10,
    )
    new_latents = middle + new_rows.reshape(seqs, rows, width)
    (query_blocks,) = group_swap([query_part.reshape(seqs, frames, rows, width)], 6)
    grad_queries = flatten(jnp.sum(query_blocks, axis=1))

    grad_query_w = mm_tn(own_flat, grad_queries)
    (patch_grads, own_back, media_sums), (sum_query, sum_out) = media_backward(
        feats,
        embed,
        mgain[None],
        grad_keys,
        grad_values,
        own_gk,
        own_gv,
        key_w,
        value_w,
        Summed([grad_query_w, grad_out_w]),
        7,
    )
    grad_own_norm = (mm_nt(grad_queries, query_w) + own_back).reshape(seqs, rows, width)
    grad_lat_in, grad_lgain, grad_lbias = norm_backward(grad_own_norm, own_unit, own_std, lgain)
    latent_grads = grad_middle + grad_lat_in
    grad_mgain, grad_mbias = media_sums[0], media_sums[1]
    slot_sums = media_sums[2:].reshape(seqs, rounds, width)
    grad_table = jnp.sum(jnp.where(one_hot[..., None], slot_sums[:, :, None, :], 0.0), axis=(0, 1))
    vec_grads = jnp.concatenate(
        [jnp.stack([grad_mgain, grad_mbias, grad_lgain, grad_lbias, grad_fgain, grad_fbias]), grad_table], axis=0
    )
    vec_blocks = jnp.pad(vec_grads.reshape(14, 32, strip).transpose(1, 0, 2), ((0, 0), (0, 2), (0, 128 - strip)))
    top, low = halves(own_flat)
    own_t = jnp.concatenate([top, top, low], axis=0).T
    sum_key, sum_value, sum_vec = weight_grads(
        xt_top, xt_low, own_t, grad_keys, grad_values, own_gk, own_gv, vec_blocks.reshape(-1, 128), 8
    )
    vec = sum_vec[:14, :strip]
    return (
        new_latents,
        latent_grads,
        patch_grads.reshape(patch_feats.shape),
        sum_query,
        sum_key,
        sum_value,
        sum_out,
        grad_up,
        grad_down,
        vec[0],
        vec[1],
        vec[2],
        vec[3],
        vec[4],
        vec[5],
        vec[6:],
    )


def solution(mesh):
    fast = dict(mesh.shape) == {"seq": 8, "frame": 4}
    return jax.shard_map(
        body_fast if fast else body_general,
        mesh=mesh,
        in_specs=(
            P("seq", "frame", None),
            P("seq", None, "frame", None, None),
            P("seq"),
            P("seq", None),
            P(("seq", "frame"), None),
            P(("seq", "frame"), None),
            P(("seq", "frame"), None),
            P(("seq", "frame"), None),
            P(("seq", "frame"), None),
            P(("seq", "frame"), None),
            P(("seq", "frame")),
            P(("seq", "frame")),
            P(("seq", "frame")),
            P(("seq", "frame")),
            P(("seq", "frame")),
            P(("seq", "frame")),
            P(None, ("seq", "frame")),
            P("seq", "frame", None),
        ),
        out_specs=(
            P("seq", "frame", None),
            P("seq", "frame", None),
            P("seq", None, "frame", None, None),
            P(("seq", "frame"), None),
            P(("seq", "frame"), None),
            P(("seq", "frame"), None),
            P(("seq", "frame"), None),
            P(("seq", "frame"), None),
            P(("seq", "frame"), None),
            P(("seq", "frame")),
            P(("seq", "frame")),
            P(("seq", "frame")),
            P(("seq", "frame")),
            P(("seq", "frame")),
            P(("seq", "frame")),
            P(None, ("seq", "frame")),
        ),
        check_vma=False,
    )
```

```python
import functools
import math

import jax
import jax.numpy as jnp
from jax import lax
from jax.experimental import pallas as pl
from jax.experimental.pallas import tpu as pltpu
from jax.sharding import PartitionSpec as P

HEADS = 16


HIGHEST = lax.Precision.HIGHEST
EPSILON = 1e-05
MASKED = -1e30


def product(left, right):
    return jnp.dot(left, right, precision=HIGHEST, preferred_element_type=jnp.float32)


def product_tn(left, right):
    return lax.dot_general(
        left, right, (((0,), (0,)), ((), ())), precision=HIGHEST, preferred_element_type=jnp.float32
    )


def product_nt(left, right):
    return lax.dot_general(
        left, right, (((1,), (1,)), ((), ())), precision=HIGHEST, preferred_element_type=jnp.float32
    )


def flatten(values):
    return values.reshape(-1, values.shape[-1])


def norm_forward(values, gain_vec, bias_vec):
    centred = values - jnp.mean(values, axis=-1, keepdims=True)
    inv_std = lax.rsqrt(jnp.mean(centred * centred, axis=-1, keepdims=True) + EPSILON)
    unit_vals = centred * inv_std
    return (unit_vals * gain_vec + bias_vec, unit_vals, inv_std)


def norm_backward(incoming, unit_vals, inv_std, gain_vec):
    scaled = incoming * gain_vec
    result = inv_std * (
        scaled
        - jnp.mean(scaled, axis=-1, keepdims=True)
        - unit_vals * jnp.mean(scaled * unit_vals, axis=-1, keepdims=True)
    )
    flat_in = flatten(incoming)
    return (result, jnp.sum(flat_in * flatten(unit_vals), axis=0), jnp.sum(flat_in, axis=0))


def heads_last(stats):
    return jnp.transpose(stats, (0, 2, 1))[..., None]


def per_slot(action, operands):
    return lax.map(action, operands)


def body_general(
    latents,
    patch_feats,
    image_counts,
    time_index,
    query_proj,
    key_proj,
    value_proj,
    out_proj,
    up_proj,
    down_proj,
    media_gain,
    media_bias,
    latent_gain,
    latent_bias,
    feed_gain,
    feed_bias,
    time_table,
    out_cotangent,
):
    gathered = (
        lax.all_gather(query_proj, ("seq", "frame"), axis=0, tiled=True),
        lax.all_gather(key_proj, ("seq", "frame"), axis=0, tiled=True),
        lax.all_gather(value_proj, ("seq", "frame"), axis=0, tiled=True),
        lax.all_gather(out_proj, ("seq", "frame"), axis=0, tiled=True),
        lax.all_gather(up_proj, ("seq", "frame"), axis=0, tiled=True),
        lax.all_gather(down_proj, ("seq", "frame"), axis=0, tiled=True),
        lax.all_gather(media_gain, ("seq", "frame"), axis=0, tiled=True),
        lax.all_gather(media_bias, ("seq", "frame"), axis=0, tiled=True),
        lax.all_gather(latent_gain, ("seq", "frame"), axis=0, tiled=True),
        lax.all_gather(latent_bias, ("seq", "frame"), axis=0, tiled=True),
        lax.all_gather(feed_gain, ("seq", "frame"), axis=0, tiled=True),
        lax.all_gather(feed_bias, ("seq", "frame"), axis=0, tiled=True),
        lax.all_gather(time_table, ("seq", "frame"), axis=1, tiled=True),
    )
    gathered = lax.optimization_barrier(gathered)
    (
        query_full,
        key_full,
        value_full,
        out_full,
        up_full,
        down_full,
        mgain_full,
        mbias_full,
        lgain_full,
        lbias_full,
        fgain_full,
        fbias_full,
        table_full,
    ) = gathered
    frame_index = lax.axis_index("frame")
    frame_count = lax.axis_size("frame")
    seq_local, lat_rows, model_width = latents.shape
    round_count = patch_feats.shape[1]
    patch_count = patch_feats.shape[3]
    slot_total = time_index.shape[1]
    table_rows = time_table.shape[0]
    latent_total = lat_rows * frame_count
    head_size = model_width // HEADS
    inv_root = 1.0 / math.sqrt(head_size)
    latent_all = lax.all_gather(latents, "frame", axis=1, tiled=True)
    latent_norm, latent_unit, latent_std = norm_forward(latent_all, lgain_full, lbias_full)
    row_start = frame_index * lat_rows
    own_norm = lax.dynamic_slice_in_dim(latent_norm, row_start, lat_rows, 1)
    own_unit = lax.dynamic_slice_in_dim(latent_unit, row_start, lat_rows, 1)
    own_std = lax.dynamic_slice_in_dim(latent_std, row_start, lat_rows, 1)
    queries = product(flatten(latent_norm), query_full).reshape(
        seq_local, latent_total, model_width
    )
    own_keys = product(flatten(own_norm), key_full).reshape(seq_local, lat_rows, model_width)
    own_values = product(flatten(own_norm), value_full).reshape(seq_local, lat_rows, model_width)
    slot_ids = jnp.arange(round_count, dtype=jnp.int32) * frame_count + frame_index
    present = slot_ids[None, :] < image_counts[:, None]
    picks = jnp.arange(slot_total, dtype=jnp.int32)[None, :] == slot_ids[:, None]
    slot_times = jnp.sum(jnp.where(picks[None, :, :], time_index[:, None, :], 0), axis=-1)
    one_hot = (
        slot_times.reshape(-1)[:, None] == jnp.arange(table_rows, dtype=jnp.int32)[None, :]
    ).astype(jnp.float32)
    slot_embed = product(one_hot, table_full)
    slot_feats = patch_feats.reshape(seq_local * round_count, patch_count, model_width)

    def media_forward(element):
        normed, unit_part, std_part = norm_forward(
            element[0] + element[1][None, :], mgain_full, mbias_full
        )
        return (normed, unit_part, std_part, product(normed, key_full), product(normed, value_full))

    media_norm, media_unit, media_std, media_keys, media_values = per_slot(
        media_forward, (slot_feats, slot_embed)
    )
    key_total = lat_rows + round_count * patch_count
    all_keys = jnp.concatenate(
        [own_keys, media_keys.reshape(seq_local, round_count * patch_count, model_width)], axis=1
    )
    all_values = jnp.concatenate(
        [own_values, media_values.reshape(seq_local, round_count * patch_count, model_width)],
        axis=1,
    )
    keep = jnp.concatenate(
        [jnp.ones((seq_local, lat_rows), dtype=bool), jnp.repeat(present, patch_count, axis=1)],
        axis=1,
    )
    query_four = queries.reshape(seq_local, latent_total, HEADS, head_size)
    key_four = all_keys.reshape(seq_local, key_total, HEADS, head_size)
    value_four = all_values.reshape(seq_local, key_total, HEADS, head_size)

    def masked_scores():
        raw_scores = (
            jnp.einsum(
                "bqhe,bkhe->bhqk",
                query_four,
                key_four,
                precision=HIGHEST,
                preferred_element_type=jnp.float32,
            )
            * inv_root
        )
        return jnp.where(keep[:, None, None, :], raw_scores, MASKED)

    scores = masked_scores()
    row_top = jnp.max(scores, axis=-1)
    expo = jnp.exp(scores - row_top[..., None])
    row_total = jnp.sum(expo, axis=-1)
    partial_out = jnp.einsum(
        "bhqk,bkhe->bqhe", expo, value_four, precision=HIGHEST, preferred_element_type=jnp.float32
    )
    glob_top = lax.pmax(row_top, "frame")
    ratio = jnp.exp(row_top - glob_top)
    glob_total, glob_out = lax.psum((row_total * ratio, partial_out * heads_last(ratio)), "frame")
    attended = glob_out / heads_last(glob_total)
    log_total = glob_top + jnp.log(glob_total)
    attended_flat = attended.reshape(seq_local, latent_total, model_width)
    own_attended = lax.dynamic_slice_in_dim(attended_flat, row_start, lat_rows, 1)
    middle = latents + product(flatten(own_attended), out_full).reshape(
        seq_local, lat_rows, model_width
    )
    feed_norm, feed_unit, feed_std = norm_forward(middle, fgain_full, fbias_full)
    hidden_pre = product(flatten(feed_norm), up_full)
    activated, gelu_pull = jax.vjp(jax.nn.gelu, hidden_pre)
    new_latents = middle + product(activated, down_full).reshape(seq_local, lat_rows, model_width)
    regathered = (
        lax.all_gather(query_proj, ("seq", "frame"), axis=0, tiled=True),
        lax.all_gather(key_proj, ("seq", "frame"), axis=0, tiled=True),
        lax.all_gather(value_proj, ("seq", "frame"), axis=0, tiled=True),
        lax.all_gather(out_proj, ("seq", "frame"), axis=0, tiled=True),
        lax.all_gather(up_proj, ("seq", "frame"), axis=0, tiled=True),
        lax.all_gather(down_proj, ("seq", "frame"), axis=0, tiled=True),
        lax.all_gather(media_gain, ("seq", "frame"), axis=0, tiled=True),
        lax.all_gather(media_bias, ("seq", "frame"), axis=0, tiled=True),
        lax.all_gather(latent_gain, ("seq", "frame"), axis=0, tiled=True),
        lax.all_gather(latent_bias, ("seq", "frame"), axis=0, tiled=True),
        lax.all_gather(feed_gain, ("seq", "frame"), axis=0, tiled=True),
        lax.all_gather(feed_bias, ("seq", "frame"), axis=0, tiled=True),
        lax.all_gather(time_table, ("seq", "frame"), axis=1, tiled=True),
    )
    regathered = lax.optimization_barrier(regathered)
    query_back = regathered[0]
    key_back = regathered[1]
    value_back = regathered[2]
    out_back = regathered[3]
    up_back = regathered[4]
    down_back = regathered[5]
    mgain_back = regathered[6]
    lgain_back = regathered[8]
    fgain_back = regathered[10]
    cotangent = flatten(out_cotangent)
    grad_down = product_tn(activated, cotangent)
    grad_hidden = gelu_pull(product_nt(cotangent, down_back))[0]
    grad_up = product_tn(flatten(feed_norm), grad_hidden)
    grad_feed_norm = product_nt(grad_hidden, up_back).reshape(seq_local, lat_rows, model_width)
    grad_mid_norm, grad_fgain, grad_fbias = norm_backward(
        grad_feed_norm, feed_unit, feed_std, fgain_back
    )
    grad_middle = out_cotangent + grad_mid_norm
    grad_out_w = product_tn(flatten(own_attended), flatten(grad_middle))
    grad_own_att = product_nt(flatten(grad_middle), out_back).reshape(
        seq_local, lat_rows, model_width
    )
    grad_attended = lax.all_gather(grad_own_att, "frame", axis=1, tiled=True)
    grad_four = grad_attended.reshape(seq_local, latent_total, HEADS, head_size)
    delta_rows = jnp.einsum(
        "bqhe,bqhe->bhq", grad_four, attended, precision=HIGHEST, preferred_element_type=jnp.float32
    )
    probs = jnp.exp(masked_scores() - log_total[..., None])
    grad_probs = jnp.einsum(
        "bqhe,bkhe->bhqk",
        grad_four,
        value_four,
        precision=HIGHEST,
        preferred_element_type=jnp.float32,
    )
    grad_scores = probs * (grad_probs - delta_rows[..., None]) * inv_root
    grad_query_part = jnp.einsum(
        "bhqk,bkhe->bqhe",
        grad_scores,
        key_four,
        precision=HIGHEST,
        preferred_element_type=jnp.float32,
    ).reshape(seq_local, latent_total, model_width)
    grad_keys = jnp.einsum(
        "bhqk,bqhe->bkhe",
        grad_scores,
        query_four,
        precision=HIGHEST,
        preferred_element_type=jnp.float32,
    ).reshape(seq_local, key_total, model_width)
    grad_values = jnp.einsum(
        "bhqk,bqhe->bkhe", probs, grad_four, precision=HIGHEST, preferred_element_type=jnp.float32
    ).reshape(seq_local, key_total, model_width)
    grad_query_own = lax.psum_scatter(grad_query_part, "frame", scatter_dimension=1, tiled=True)
    grad_key_lat = flatten(grad_keys[:, :lat_rows])
    grad_value_lat = flatten(grad_values[:, :lat_rows])
    grad_key_media = grad_keys[:, lat_rows:].reshape(
        seq_local * round_count, patch_count, model_width
    )
    grad_value_media = grad_values[:, lat_rows:].reshape(
        seq_local * round_count, patch_count, model_width
    )
    grad_query_w = product_tn(flatten(own_norm), flatten(grad_query_own))
    grad_key_w = product_tn(flatten(own_norm), grad_key_lat) + product_tn(
        flatten(media_norm), flatten(grad_key_media)
    )
    grad_value_w = product_tn(flatten(own_norm), grad_value_lat) + product_tn(
        flatten(media_norm), flatten(grad_value_media)
    )
    grad_own_norm = (
        product_nt(flatten(grad_query_own), query_back)
        + product_nt(grad_key_lat, key_back)
        + product_nt(grad_value_lat, value_back)
    ).reshape(seq_local, lat_rows, model_width)
    grad_lat_in, grad_lgain, grad_lbias = norm_backward(
        grad_own_norm, own_unit, own_std, lgain_back
    )
    latent_grads = grad_middle + grad_lat_in

    def media_backward(element):
        normed_grad = product_nt(element[0], key_back) + product_nt(element[1], value_back)
        feats_grad, gain_part, bias_part = norm_backward(
            normed_grad, element[2], element[3], mgain_back
        )
        return (feats_grad, gain_part, bias_part, jnp.sum(feats_grad, axis=0))

    feats_grads, gain_parts, bias_parts, slot_sums = per_slot(
        media_backward, (grad_key_media, grad_value_media, media_unit, media_std)
    )
    grad_mgain = jnp.sum(gain_parts, axis=0)
    grad_mbias = jnp.sum(bias_parts, axis=0)
    grad_table = product_tn(one_hot, slot_sums)
    patch_grads = feats_grads.reshape(patch_feats.shape)
    (
        grad_query_w,
        grad_key_w,
        grad_value_w,
        grad_out_w,
        grad_up,
        grad_down,
    ) = lax.optimization_barrier(
        (grad_query_w, grad_key_w, grad_value_w, grad_out_w, grad_up, grad_down)
    )
    summed = (
        lax.psum_scatter(grad_query_w, ("seq", "frame"), scatter_dimension=0, tiled=True),
        lax.psum_scatter(grad_key_w, ("seq", "frame"), scatter_dimension=0, tiled=True),
        lax.psum_scatter(grad_value_w, ("seq", "frame"), scatter_dimension=0, tiled=True),
        lax.psum_scatter(grad_out_w, ("seq", "frame"), scatter_dimension=0, tiled=True),
        lax.psum_scatter(grad_up, ("seq", "frame"), scatter_dimension=0, tiled=True),
        lax.psum_scatter(grad_down, ("seq", "frame"), scatter_dimension=0, tiled=True),
        lax.psum_scatter(grad_mgain, ("seq", "frame"), scatter_dimension=0, tiled=True),
        lax.psum_scatter(grad_mbias, ("seq", "frame"), scatter_dimension=0, tiled=True),
        lax.psum_scatter(grad_lgain, ("seq", "frame"), scatter_dimension=0, tiled=True),
        lax.psum_scatter(grad_lbias, ("seq", "frame"), scatter_dimension=0, tiled=True),
        lax.psum_scatter(grad_fgain, ("seq", "frame"), scatter_dimension=0, tiled=True),
        lax.psum_scatter(grad_fbias, ("seq", "frame"), scatter_dimension=0, tiled=True),
        lax.psum_scatter(grad_table, ("seq", "frame"), scatter_dimension=1, tiled=True),
    )
    return (
        new_latents,
        latent_grads,
        patch_grads,
        summed[0],
        summed[1],
        summed[2],
        summed[3],
        summed[4],
        summed[5],
        summed[6],
        summed[7],
        summed[8],
        summed[9],
        summed[10],
        summed[11],
        summed[12],
    )


MESH = pl.DeviceIdType.MESH
F32 = jnp.float32
ANY = pl.BlockSpec(memory_space=pl.ANY)
GRID = (4, 2, 2, 2)


def place(z, y, x, c):
    return (z * 2 + y, x * 2 + c)


class Here:
    def __init__(self):
        seq, frame = lax.axis_index("seq"), lax.axis_index("frame")
        self.z, self.y, self.x, self.c = z, y, x, c = seq // 2, seq % 2, frame // 2, frame % 2
        self.ox, self.oy, self.oc = ox, oy, oc = 1 - x, 1 - y, 1 - c
        self.at_x, self.at_y, self.at_c = place(z, y, ox, c), place(z, oy, x, c), place(z, y, x, oc)
        self.ahead = [lax.rem(z + k, 4) for k in range(4)]
        self.behind = [lax.rem(z + 4 - k, 4) for k in range(4)]
        self.at_z = [place(o, y, x, c) for o in self.ahead]

    def greet(self):
        barrier = pltpu.get_barrier_semaphore()
        for peer in self.at_z[1:] + [self.at_x, self.at_y, self.at_c]:
            pl.semaphore_signal(barrier, inc=1, device_id=peer, device_id_type=MESH)
        pl.semaphore_wait(barrier, 6)


def remote(src, dst, send_sem, recv_sem, peer):
    return pltpu.make_async_remote_copy(
        src_ref=src, dst_ref=dst, send_sem=send_sem, recv_sem=recv_sem, device_id=peer, device_id_type=MESH
    )


class Gather:
    lag = 1

    def __init__(self, here, shards, fulls, cuts, sems):
        self.here, self.count = here, len(cuts)
        self.loc, self.zs, self.zr, self.xs, self.xr, self.ys, self.yr, self.ds, self.dr, self.cs, self.cr = sems
        self.shard = [shards[a].at[:, lo:hi] for a, lo, hi in cuts]
        self.full = [(lambda *at, a=a, lo=lo, hi=hi: fulls[a].at[at + (slice(lo, hi),)]) for a, lo, hi in cuts]
        self.half = [shards[a].shape[0] // 2 for a, lo, hi in cuts]

    @staticmethod
    def semaphores(count):
        dma = pltpu.SemaphoreType.DMA
        shapes = [(), (3,), (3,), (4,), (4,), (4,), (4,), (2, 4), (2, 4), (4,), (4,)]
        return [dma((count,) + s) for s in shapes]

    def local(self, p):
        h = self.here
        return pltpu.make_async_copy(self.shard[p], self.full[p](h.z, h.y, h.x, h.c, slice(None)), self.loc.at[p])

    def over_z(self, p, k):
        h = self.here
        dst = self.full[p](h.z, h.y, h.x, h.c, slice(None))
        return remote(self.shard[p], dst, self.zs.at[p, k - 1], self.zr.at[p, k - 1], h.at_z[k])

    def over_x(self, p, k):
        h = self.here
        block = self.full[p](h.behind[k], h.y, h.x, h.c, slice(None))
        return remote(self.shard[p] if k == 0 else block, block, self.xs.at[p, k], self.xr.at[p, k], h.at_x)

    def over_y(self, p, k):
        h = self.here
        block = self.full[p](h.behind[k], h.y, h.x, h.c, slice(None))
        return remote(self.shard[p] if k == 0 else block, block, self.ys.at[p, k], self.yr.at[p, k], h.at_y)

    def on_y(self, p, k):
        h = self.here
        part = self.full[p](h.behind[k], h.y, h.ox, h.c, slice(self.half[p], 2 * self.half[p]))
        return remote(part, part, self.ds.at[p, 0, k], self.dr.at[p, 0, k], h.at_y)

    def on_x(self, p, k):
        h = self.here
        part = self.full[p](h.behind[k], h.oy, h.x, h.c, slice(0, self.half[p]))
        return remote(part, part, self.ds.at[p, 1, k], self.dr.at[p, 1, k], h.at_x)

    def to_core(self, p, i):
        h = self.here
        yy, xx = ((h.y, h.x), (h.y, h.ox), (h.oy, h.x), (h.oy, h.ox))[i]
        blocks = self.full[p](slice(None), yy, xx, h.c, slice(None))
        return remote(blocks, blocks, self.cs.at[p, i], self.cr.at[p, i], h.at_c)

    def own(self, p):
        self.local(p).start()
        for k in (1, 2, 3):
            self.over_z(p, k).start()
        self.over_x(p, 0).start()
        self.over_y(p, 0).start()

    def along_z(self, p):
        for k in (1, 2, 3):
            self.over_z(p, k).wait_recv()
            self.over_x(p, k).start()
            self.over_y(p, k).start()

    def across(self, p):
        for k in range(4):
            self.over_x(p, k).wait_recv()
            self.on_y(p, k).start()
            self.over_y(p, k).wait_recv()
            self.on_x(p, k).start()
        self.local(p).wait()
        for i in range(3):
            self.to_core(p, i).start()

    def corner(self, p):
        for k in range(4):
            self.on_y(p, k).wait_recv()
            self.on_x(p, k).wait_recv()
        self.to_core(p, 3).start()

    def arrived(self, p):
        for i in range(4):
            self.to_core(p, i).wait_recv()

    def done(self, p, here=False):
        if not here:
            self.arrived(p)
        for i in range(4):
            self.to_core(p, i).wait_send()
        for k in (1, 2, 3):
            self.over_z(p, k).wait_send()
        for k in range(4):
            for copy in (self.over_x, self.over_y, self.on_x, self.on_y):
                copy(p, k).wait_send()

    def stages(self):
        return (self.own, self.along_z, self.across, self.corner)


LAG = 2


def waves_of(plan, ahead):
    first, *stages = plan.stages()
    count, last, lag = plan.count, len(stages) - 1, plan.lag
    ahead = min(ahead, count)
    waves = [[functools.partial(first, p) for p in range(ahead)]]
    for t in range(count + last * lag):
        wave = [functools.partial(first, t + ahead)] if t + ahead < count else []
        order = range(last, -1, -1)
        waves.append(wave + [functools.partial(stages[s], t - s * lag) for s in order if 0 <= t - s * lag < count])
    return waves


def finish_all(plan):
    for p in range(plan.count):
        plan.done(p)


class Scatter:
    lag = LAG

    def __init__(self, here, count, mine, theirs, load, out, scratch):
        self.here, self.count, self.mine, self.theirs, self.load, self.out = here, count, mine, theirs, load, out
        self.got, self.gx, self.gy, self.hx, self.hy, self.gz = scratch[:6]
        self.cs, self.cr, self.fs, self.fr, self.ss, self.sr, self.zs, self.zr = scratch[6:]
        self.half = self.got.shape[-2] // 2

    @staticmethod
    def scratch(count, r, w):
        dma = pltpu.SemaphoreType.DMA
        leads = [(4, 2, 2, r), (4, 2, r // 2), (4, 2, r // 2), (4, r // 2), (4, r // 2), (3, r)]
        return [pltpu.VMEM((count,) + s + (w,), F32) for s in leads] + [
            dma((count,) + s) for s in ((), (), (2,), (2,), (2,), (2,), (3,), (3,))
        ]

    def to_core(self, p):
        return remote(self.theirs(p), self.got.at[p], self.cs.at[p], self.cr.at[p], self.here.at_c)

    def first(self, p, way):
        h, half, tot = self.here, self.half, self.mine(p)
        if way == 0:
            return remote(tot.at[:, :, h.ox, :half], self.gx.at[p], self.fs.at[p, 0], self.fr.at[p, 0], h.at_x)
        return remote(tot.at[:, h.oy, :, half:], self.gy.at[p], self.fs.at[p, 1], self.fr.at[p, 1], h.at_y)

    def second(self, p, way):
        h, half, tot = self.here, self.half, self.mine(p)
        if way == 0:
            return remote(tot.at[:, h.oy, h.x, :half], self.hy.at[p], self.ss.at[p, 0], self.sr.at[p, 0], h.at_y)
        return remote(tot.at[:, h.y, h.ox, half:], self.hx.at[p], self.ss.at[p, 1], self.sr.at[p, 1], h.at_x)

    def over_z(self, p, k):
        h = self.here
        src = self.mine(p).at[h.ahead[k], h.y, h.x]
        return remote(src, self.gz.at[p, k - 1], self.zs.at[p, k - 1], self.zr.at[p, k - 1], h.at_z[k])

    def start(self, p):
        if self.load is not None:
            self.load(p).start()
        self.to_core(p).start()

    def cores(self, p):
        tot, got = self.mine(p), self.got.at[p]
        if self.load is not None:
            self.load(p).wait()
        self.to_core(p).wait_recv()

        @pl.loop(0, 16)
        def _(i):
            at = (i // 4, (i // 2) % 2, i % 2)
            tot[at] = tot[at] + got[at]

        self.first(p, 0).start()
        self.first(p, 1).start()

    def sides(self, p):
        h, half, tot = self.here, self.half, self.mine(p)
        gx, gy = self.gx.at[p], self.gy.at[p]
        self.first(p, 0).wait_recv()

        @pl.loop(0, 8)
        def _(i):
            zi, yi = i // 2, i % 2
            tot[zi, yi, h.x, :half] = tot[zi, yi, h.x, :half] + gx[zi, yi]

        self.second(p, 0).start()
        self.first(p, 1).wait_recv()

        @pl.loop(0, 8)
        def _(i):
            zi, xi = i // 2, i % 2
            tot[zi, h.y, xi, half:] = tot[zi, h.y, xi, half:] + gy[zi, xi]

        self.second(p, 1).start()

    def column(self, p):
        h, half, tot = self.here, self.half, self.mine(p)
        hx, hy = self.hx.at[p], self.hy.at[p]
        self.second(p, 0).wait_recv()
        self.second(p, 1).wait_recv()

        @pl.loop(0, 4)
        def _(zi):
            tot[zi, h.y, h.x, :half] = tot[zi, h.y, h.x, :half] + hy[zi]
            tot[zi, h.y, h.x, half:] = tot[zi, h.y, h.x, half:] + hx[zi]

        for k in (1, 2, 3):
            self.over_z(p, k).start()

    def finish(self, p):
        h, gz = self.here, self.gz.at[p]
        for k in (1, 2, 3):
            self.over_z(p, k).wait_recv()
        self.out(p)[...] = (self.mine(p)[h.z, h.y, h.x] + gz[0]) + (gz[1] + gz[2])

    def done(self, p):
        self.to_core(p).wait_send()
        for way in (0, 1):
            self.first(p, way).wait_send()
            self.second(p, way).wait_send()
        for k in (1, 2, 3):
            self.over_z(p, k).wait_send()

    def stages(self):
        return (self.start, self.cores, self.sides, self.column, self.finish)


def run(wave):
    for action in wave:
        action()


class Pace:
    def __init__(self, step, steps, lead, parts, waves):
        self.step, self.steps, self.lead, self.parts = step, steps, lead, parts
        ticks, total, before = lead + steps * parts, 1 + sum(len(w) for w in waves[1:]), 0
        self.waves = [[] for _ in range(ticks)]
        for wave in waves:
            self.waves[ticks * before // total] += wave
            before += len(wave) if before else 1

    def at_lead(self, i):
        run(self.waves[i])

    def at(self, part):
        for s in range(self.steps):
            now = self.waves[self.lead + s * self.parts + part]
            if now:
                pl.when(self.step == s)(functools.partial(run, now))


def run_last(step, steps, plan):
    @pl.when(step == steps - 1)
    def _():
        finish_all(plan)


WIDE = 768


def column_cuts(shards):
    return [(a, lo, min(lo + WIDE, s.shape[1])) for a, s in enumerate(shards) for lo in range(0, s.shape[1], WIDE)]


class GroupGather:
    def __init__(self, here, shards, fulls, sems):
        self.here, self.shards, self.fulls, self.count = here, shards, fulls, len(shards)
        self.loc, self.ss, self.rs = sems

    @staticmethod
    def semaphores(count):
        dma = pltpu.SemaphoreType.DMA
        return [dma((count,)), dma((count, 3)), dma((count, 3))]

    def local(self, a):
        h = self.here
        return pltpu.make_async_copy(self.shards[a], self.fulls[a].at[:, h.x * 2 + h.c], self.loc.at[a])

    def copy(self, a, i):
        h = self.here
        mine = self.fulls[a].at[:, h.x * 2 + h.c]
        if i < 2:
            return remote(self.shards[a], mine, self.ss.at[a, i], self.rs.at[a, i], (h.at_x, h.at_c)[i])
        block = self.fulls[a].at[:, h.ox * 2 + h.c]
        return remote(block, block, self.ss.at[a, 2], self.rs.at[a, 2], h.at_c)

    def start(self):
        for a in range(self.count):
            self.local(a).start()
            self.copy(a, 0).start()
            self.copy(a, 1).start()

    def forward(self):
        for a in range(self.count):
            self.copy(a, 0).wait_recv()
            self.copy(a, 2).start()

    def done(self):
        for a in range(self.count):
            self.local(a).wait()
            self.copy(a, 0).wait_send()
            self.copy(a, 1).wait()
            self.copy(a, 2).wait()


def flat_full(full):
    return full.reshape((-1, full.shape[-1]))


def full_shapes(shards):
    return [jax.ShapeDtypeStruct(GRID + s.shape, s.dtype) for s in shards]


def gather_kernel(count, cuts, *refs):
    here = Here()
    here.greet()
    plan = Gather(here, refs[:count], refs[count : 2 * count], cuts, refs[2 * count :])
    for wave in waves_of(plan, 2):
        run(wave)
    finish_all(plan)


def gather_all(shards, collective_id):
    count = len(shards)
    cuts = column_cuts(shards)
    outs = pl.pallas_call(
        functools.partial(gather_kernel, count, cuts),
        out_shape=full_shapes(shards),
        in_specs=[ANY] * count,
        out_specs=[ANY] * count,
        scratch_shapes=Gather.semaphores(len(cuts)),
        compiler_params=pltpu.CompilerParams(collective_id=collective_id, has_side_effects=True),
        name="gather_all",
    )(*shards)
    return [flat_full(o) for o in outs]


class Summed:
    def __init__(self, parts):
        self.arrays = len(parts)
        self.rows, self.width = parts[0].shape[0] // 32, parts[0].shape[1]
        self.cut = min(256, self.width)
        self.pieces = self.width // self.cut
        self.operands = [p.reshape(GRID + (self.rows, self.width)) for p in parts]
        self.in_specs = [ANY] * len(parts)
        self.out_shape = [jax.ShapeDtypeStruct((self.rows, self.width), F32)] * len(parts)
        self.out_specs = [whole((self.rows, self.width))] * len(parts)
        n = self.count = len(parts) * self.pieces
        self.scratch = [pltpu.VMEM((n, 4, 2, 2, self.rows, self.cut), F32), pltpu.SemaphoreType.DMA((n,))]
        self.scratch += Scatter.scratch(n, self.rows, self.cut)

    def bind(self, here, ins, outs, scratch):
        tots, loc = scratch[:2]

        def cut(p):
            lo = p % self.pieces * self.cut
            return p // self.pieces, slice(lo, lo + self.cut)

        def part(p, core):
            a, cols = cut(p)
            return ins[a].at[:, :, :, core, :, cols]

        def out(p):
            a, cols = cut(p)
            return outs[a].at[:, cols]

        return Scatter(
            here,
            self.count,
            lambda p: tots.at[p],
            lambda p: part(p, here.oc),
            lambda p: pltpu.make_async_copy(part(p, here.c), tots.at[p], loc.at[p]),
            out,
            scratch[2:],
        )


def scatter_kernel(plan, *refs):
    n = plan.arrays
    here = Here()
    here.greet()
    sums = plan.bind(here, refs[:n], refs[n : 2 * n], refs[2 * n :])
    for wave in waves_of(sums, sums.count):
        run(wave)
    finish_all(sums)


def scatter_all(parts, collective_id):
    plan = Summed(parts)
    return pl.pallas_call(
        functools.partial(scatter_kernel, plan),
        out_shape=plan.out_shape,
        in_specs=plan.in_specs,
        out_specs=[pl.BlockSpec(memory_space=pltpu.VMEM)] * len(parts),
        scratch_shapes=plan.scratch,
        compiler_params=pltpu.CompilerParams(
            collective_id=collective_id, has_side_effects=True, vmem_limit_bytes=60 * 2**20
        ),
        name="scatter_all",
    )(*plan.operands)


def greet(peers):
    barrier = pltpu.get_barrier_semaphore()
    for peer in peers:
        pl.semaphore_signal(barrier, inc=1, device_id=peer, device_id_type=MESH)
    pl.semaphore_wait(barrier, len(peers))


def group_gather_kernel(count, *refs):
    shards, fulls = refs[:count], refs[count : 2 * count]
    loc, ss, rs = refs[2 * count :]
    here = Here()
    x, c, ox, at_x, at_c = here.x, here.c, here.ox, here.at_x, here.at_c
    greet([at_x, at_c])
    waits = []
    for a in range(count):
        mine = fulls[a].at[:, x * 2 + c]
        copy = pltpu.make_async_copy(shards[a], mine, loc.at[a])
        copy.start()
        over = remote(shards[a], mine, ss.at[a, 0], rs.at[a, 0], at_x)
        over.start()
        side = remote(shards[a], mine, ss.at[a, 1], rs.at[a, 1], at_c)
        side.start()
        waits.append((copy, over, side))
    last = []
    for a in range(count):
        waits[a][1].wait_recv()
        block = fulls[a].at[:, ox * 2 + c]
        on = remote(block, block, ss.at[a, 2], rs.at[a, 2], at_c)
        on.start()
        last.append(on)
    for a in range(count):
        copy, over, side = waits[a]
        copy.wait()
        over.wait_send()
        side.wait()
        last[a].wait()


def group_gather(shards, collective_id):
    count = len(shards)
    dma = pltpu.SemaphoreType.DMA
    return pl.pallas_call(
        functools.partial(group_gather_kernel, count),
        out_shape=[jax.ShapeDtypeStruct((s.shape[0], 4) + s.shape[1:], F32) for s in shards],
        in_specs=[ANY] * count,
        out_specs=[ANY] * count,
        scratch_shapes=[dma((count,)), dma((count, 3)), dma((count, 3))],
        compiler_params=pltpu.CompilerParams(collective_id=collective_id, has_side_effects=True),
        name="group_gather",
    )(*shards)


def group_swap_kernel(count, *refs):
    shards, fulls = refs[:count], refs[count : 2 * count]
    loc, ss, rs = refs[2 * count :]
    here = Here()
    z, y, x, c = here.z, here.y, here.x, here.c
    me = x * 2 + c
    peers = [(x, 1 - c), (1 - x, c), (1 - x, 1 - c)]
    greet([place(z, y, *p) for p in peers])
    waits = []
    for a in range(count):
        copy = pltpu.make_async_copy(shards[a].at[:, me], fulls[a].at[:, me], loc.at[a])
        copy.start()
        waits.append(copy)
        for k in (1, 2, 0):
            px, pc = peers[k]
            on = remote(
                shards[a].at[:, px * 2 + pc], fulls[a].at[:, me], ss.at[a, k], rs.at[a, k], place(z, y, px, pc)
            )
            on.start()
            waits.append(on)
    for copy in waits:
        copy.wait()


def group_swap(shards, collective_id):
    count = len(shards)
    dma = pltpu.SemaphoreType.DMA
    return pl.pallas_call(
        functools.partial(group_swap_kernel, count),
        out_shape=[jax.ShapeDtypeStruct(s.shape, F32) for s in shards],
        in_specs=[ANY] * count,
        out_specs=[ANY] * count,
        scratch_shapes=[dma((count,)), dma((count, 3)), dma((count, 3))],
        compiler_params=pltpu.CompilerParams(collective_id=collective_id, has_side_effects=True),
        name="group_swap",
    )(*shards)


BF16 = jnp.bfloat16
HIGH = lax.Precision.HIGH
BLOCK = 256


def dot(left, right, dims=(1, 0)):
    return lax.dot_general(
        left, right, (((dims[0],), (dims[1],)), ((), ())), precision=HIGH, preferred_element_type=F32
    )


def dot3(left, right, dims=(1, 0)):
    numbers = (((dims[0],), (dims[1],)), ((), ()))
    one = functools.partial(lax.dot_general, dimension_numbers=numbers, preferred_element_type=F32)
    return one(left[0], right[0]) + (one(left[0], right[1]) + one(left[1], right[0]))


def halves(values):
    top = values.astype(BF16)
    return top, (values - top.astype(F32)).astype(BF16)


def split_weights(sources, pairs, stage, sems, pace):
    step = stage.shape[1]
    chunks = [(i, r) for i, s in enumerate(sources) for r in range(0, s.shape[0], step)]

    def copy(n):
        i, r = chunks[n]
        return pltpu.make_async_copy(sources[i].at[r : r + step], stage.at[n % 2], sems.at[n % 2])

    copy(0).start()
    for n, (i, r) in enumerate(chunks):
        if n * pace.lead % len(chunks) == 0:
            pace.at_lead(n * pace.lead // len(chunks))
        if n + 1 < len(chunks):
            copy(n + 1).start()
        copy(n).wait()
        pairs[i][0][r : r + step], pairs[i][1][r : r + step] = halves(stage[n % 2])


def unit_of(values):
    centred = values - jnp.mean(values, axis=-1, keepdims=True)
    inv_std = lax.rsqrt(jnp.mean(centred * centred, axis=-1, keepdims=True) + EPSILON)
    return centred * inv_std, inv_std


def staging(width):
    return [pltpu.VMEM((width, width), BF16)] * 4 + [pltpu.VMEM((2, 128, width), F32), pltpu.SemaphoreType.DMA((2,))]


def whole(shape, buffers=1):
    return pl.BlockSpec(shape, lambda *i: (0,) * len(shape), pipeline_mode=pl.Buffered(buffers))


def opening_kernel(cuts, *refs):
    times, feats, latents = refs[:3]
    shards, group_shard = refs[3:9], refs[9:10]
    vec, keys, values, own_keys, own_values, queries, xt_top, xt_low = refs[10:18]
    fulls, group_full = refs[18:24], refs[24:25]
    pk, top, low, own_top, own_low, lat, lat_top, lat_low, stage, load = refs[25:35]
    step = pl.program_id(0)
    here = Here()
    vectors = Gather(here, shards[:1], fulls[:1], [(0, 0, 128)], refs[35:46])
    moved = Gather(here, shards[1:], fulls[1:], cuts, refs[46:57])
    group = GroupGather(here, group_shard, group_full, refs[57:])
    waves = waves_of(moved, 2)
    cut = keys.shape[1]
    slots, chunks = top.shape[0] // BLOCK, shards[1].shape[1] // cut

    def start():
        here.greet()
        vectors.own(0)
        run(waves[0])
        group.start()
        vectors.along_z(0)
        vectors.across(0)
        vectors.corner(0)
        vectors.arrived(0)
        copy = pltpu.make_async_copy(fulls[0], pk, load.at[0])
        copy.start()
        copy.wait()
        strip = shards[1].shape[0]
        vec[...] = jnp.concatenate([pk[i // 8, i // 4 % 2, i // 2 % 2, i % 2][:, :strip] for i in range(32)], axis=1)
        own_top[...], own_low[...] = halves(unit_of(latents[...])[0] * vec[2:3] + vec[3:4])
        run(waves[1])
        group.forward()

    pl.when(step == 0)(start)
    at_step = {2: 2, 4: 3, 5: 4, slots + 1: 5, slots + 2: 6, slots + 4: 7, slots + 5: 8}
    at_step.update({slots + chunks + i: 8 + i for i in range(1, 5)})
    for s, w in at_step.items():
        pl.when(step == s)(functools.partial(run, waves[w]))

    @pl.when(step < slots)
    def _():
        embed = vec[pl.ds(6 + times[step], 1)]
        normed = unit_of(feats[...] + embed)[0] * vec[0:1] + vec[1:2]
        rows = pl.ds(pl.multiple_of(step * BLOCK, BLOCK), BLOCK)
        top[rows], low[rows] = halves(normed)
        xt_top[...], xt_low[...] = halves(jnp.swapaxes(normed, 0, 1))

    def chunk(array, n, left, right, out, own_out):
        cols = pl.ds(pl.multiple_of(n * cut, cut), cut)
        copy = pltpu.make_async_copy(fulls[array].at[:, :, :, :, :, cols], stage.at[array % 2], load.at[0])
        copy.start()
        copy.wait()
        pair = halves(stage[array % 2].reshape((-1, cut)))
        step_rows = min(512, left.shape[0])

        @pl.loop(0, left.shape[0] // step_rows)
        def _(m):
            rows = pl.ds(pl.multiple_of(m * step_rows, step_rows), step_rows)
            out[rows] = dot3((left[rows], right[rows]), pair)

        if own_out is not None:
            own_out[...] = dot3((own_top[...], own_low[...]), pair)

    half = chunks // 2
    for first in (0, 1):

        @pl.when(step == slots + first * half)
        def _():
            moved.arrived(2 * first)
            moved.arrived(2 * first + 1)

    @pl.when((step >= slots) & (step < slots + chunks))
    def _():
        chunk(1, step - slots, top, low, keys, own_keys)
        chunk(2, step - slots, top, low, values, own_values)

    @pl.when(step == slots + chunks)
    def _():
        moved.arrived(4)
        moved.arrived(5)
        group.done()
        copy = pltpu.make_async_copy(group_full[0], lat, load.at[0])
        copy.start()
        copy.wait()
        lat_top[...], lat_low[...] = halves(unit_of(lat[...].reshape(lat_top.shape))[0] * vec[2:3] + vec[3:4])

    @pl.when(step >= slots + chunks)
    def _():
        chunk(3, step - slots - chunks, lat_top, lat_low, queries, None)

    @pl.when(step == slots + 2 * chunks - 1)
    def _():
        vectors.done(0, True)
        for p in range(moved.count):
            moved.done(p, p < 6)


def opening(times, feats, latents, packed, key_w, value_w, query_w, cot, out_w, collective_id):
    rows, width = feats.shape
    seqs, own_each, _ = latents.shape
    own_rows, lat_rows = seqs * own_each, seqs * own_each * 4
    slots, cut = rows // BLOCK, 256
    chunks = width // cut
    shards = [packed, key_w, value_w, query_w, cot, out_w]
    cuts = [(a, lo, lo + WIDE) for lo in range(0, width, WIDE) for a in (0, 1)]
    cuts += [(a, lo, lo + WIDE) for a in (2, 3, 4) for lo in range(0, width, WIDE)]
    clip = lambda i, lo: jnp.clip(i - lo, 0, chunks - 1)
    chunk_of = lambda n, lo: pl.BlockSpec((n, cut), lambda i: (0, clip(i, lo)))
    turned = pl.BlockSpec((width, BLOCK), lambda i: (0, jnp.minimum(i, slots - 1)))
    full = lambda n, kind=F32: jax.ShapeDtypeStruct((n, width), kind)
    outs = pl.pallas_call(
        functools.partial(opening_kernel, cuts),
        grid=(slots + 2 * chunks,),
        in_specs=[
            SMEM,
            pl.BlockSpec((BLOCK, width), lambda i: (jnp.minimum(i, slots - 1), 0)),
            whole((own_rows, width)),
        ]
        + [ANY] * 7,
        out_specs=[
            whole((16, width)),
            chunk_of(rows, slots),
            chunk_of(rows, slots),
            chunk_of(own_rows, slots),
            chunk_of(own_rows, slots),
            chunk_of(lat_rows, slots + chunks),
            turned,
            turned,
        ]
        + [ANY] * 7,
        out_shape=[full(16), full(rows), full(rows), full(own_rows), full(own_rows), full(lat_rows)]
        + [jax.ShapeDtypeStruct((width, rows), BF16)] * 2
        + full_shapes(shards)
        + [jax.ShapeDtypeStruct((seqs, 4, own_each, width), F32)],
        scratch_shapes=[
            pltpu.VMEM(GRID + packed.shape, F32),
            pltpu.VMEM((rows, width), BF16),
            pltpu.VMEM((rows, width), BF16),
            pltpu.VMEM((own_rows, width), BF16),
            pltpu.VMEM((own_rows, width), BF16),
            pltpu.VMEM((seqs, 4, own_each, width), F32),
            pltpu.VMEM((lat_rows, width), BF16),
            pltpu.VMEM((lat_rows, width), BF16),
            pltpu.VMEM((2,) + GRID + (width // 32, cut), F32),
            pltpu.SemaphoreType.DMA((1,)),
        ]
        + Gather.semaphores(1)
        + Gather.semaphores(len(cuts))
        + GroupGather.semaphores(1),
        compiler_params=pltpu.CompilerParams(
            collective_id=collective_id, has_side_effects=True, vmem_limit_bytes=60 * 2**20
        ),
        name="opening",
    )(times, feats, latents.reshape(own_rows, width), *shards, latents)
    return outs[:8], [flat_full(o) for o in outs[9:14]], outs[14]


def pair_rows(values, first, head):
    lane = lax.broadcasted_iota(jnp.int32, values.shape, 1)
    return jnp.concatenate(
        [
            jnp.where((lane >= first) & (lane < first + head), values, 0.0),
            jnp.where((lane >= first + head) & (lane < first + 2 * head), values, 0.0),
        ],
        axis=0,
    )


def pair_merge(stacked, first, head):
    half = stacked.shape[0] // 2
    lane = lax.broadcasted_iota(jnp.int32, (half, stacked.shape[1]), 1)
    one = jnp.where((lane >= first) & (lane < first + head), stacked[:half], 0.0)
    return one + jnp.where((lane >= first + head) & (lane < first + 2 * head), stacked[half:], 0.0)


def join(left, right):
    return jnp.concatenate([left[:, :128], left[:, 128:] + right[:, :128], right[:, 128:]], axis=1)


def windows(head):
    return ((slice(0, 256), 0), (slice(128, 384), 2 * head - 128))


def score_block(present, seq, keys, own_keys, q_pair, window, inv_root):
    at = keys.shape[0]
    scores = jnp.concatenate([dot(keys[:, window], q_pair, (1, 1)), dot(own_keys[:, window], q_pair, (1, 1))], axis=0)
    row = lax.broadcasted_iota(jnp.int32, scores.shape, 0)
    keep = (row >= at) | ((row < at // 2) & (present[seq, 0] > 0)) | ((row >= at // 2) & (present[seq, 1] > 0))
    return jnp.where(keep, scores * inv_root, MASKED)


def attend_kernel(inv_root, head, present, queries, keys, values, own_keys, own_values, out, tops, sums):
    seq, group = pl.program_id(0), pl.program_id(1)
    merged = []
    for p, (window, first) in enumerate(windows(head)):
        q_pair = pair_rows(queries[:, window], first, head)
        scores = score_block(present, seq, keys, own_keys, q_pair, window, inv_root)
        top = jnp.max(scores, axis=0, keepdims=True)
        expo = jnp.exp(scores - top)
        tops[pl.ds(group * 2 + p, 1)] = top
        sums[pl.ds(group * 2 + p, 1)] = jnp.sum(expo, axis=0, keepdims=True)
        at = keys.shape[0]
        stacked = dot(expo[:at], values[:, window], (0, 0)) + dot(expo[at:], own_values[:, window], (0, 0))
        merged.append(pair_merge(stacked, first, head))
    out[...] = join(*merged)


def attend_specs(lat, media, rows):
    group = 384
    query = pl.BlockSpec((None, lat, group), lambda b, g: (b, 0, g))
    key = pl.BlockSpec((media, group), lambda b, g: (b, g))
    own = pl.BlockSpec((rows, group), lambda b, g: (b, g))
    stat = pl.BlockSpec((None, 8, 128), lambda b, g: (b, 0, 0))
    return query, key, own, stat


SMEM = pl.BlockSpec(memory_space=pltpu.SMEM)


def attend(present, queries, keys, values, own_keys, own_values):
    seqs, lat, width = queries.shape
    head = width // HEADS
    query, key, own, stat = attend_specs(lat, keys.shape[0] // seqs, own_keys.shape[0] // seqs)
    stat_shape = jax.ShapeDtypeStruct((seqs, 8, 128), F32)
    return pl.pallas_call(
        functools.partial(attend_kernel, 1.0 / math.sqrt(head), head),
        grid=(seqs, width // 384),
        in_specs=[SMEM, query, key, key, own, own],
        out_specs=[query, stat, stat],
        out_shape=[jax.ShapeDtypeStruct(queries.shape, F32), stat_shape, stat_shape],
        compiler_params=pltpu.CompilerParams(vmem_limit_bytes=60 * 2**20),
        name="attend",
    )(present, queries, keys, values, own_keys, own_values)


def attend_back_kernel(inv_root, head, plan, steps, *refs):
    present, queries, grads, logs, deltas, keys, values, own_keys, own_values = refs[:9]
    n = plan.arrays
    query_out, key_out, value_out, own_key_out, own_value_out = refs[9 + n : 14 + n]
    seq, group = pl.program_id(0), pl.program_id(1)
    step = seq * pl.num_programs(1) + group
    here = Here()
    moved = plan.bind(here, refs[9 : 9 + n], refs[14 + n : 14 + 2 * n], refs[14 + 2 * n :])
    waves = waves_of(moved, moved.count)
    waves[0].insert(0, here.greet)
    pace = Pace(step, steps, 0, 2, waves)
    merged, key_grads, value_grads = [], [], []
    at = keys.shape[0]
    for p, (window, first) in enumerate(windows(head)):
        pace.at(p)
        q_pair = pair_rows(queries[:, window], first, head)
        g_pair = pair_rows(grads[:, window], first, head)
        scores = score_block(present, seq, keys, own_keys, q_pair, window, inv_root)
        probs = jnp.exp(scores - logs[pl.ds(group * 2 + p, 1)])
        grad_probs = jnp.concatenate(
            [dot(values[:, window], g_pair, (1, 1)), dot(own_values[:, window], g_pair, (1, 1))], axis=0
        )
        grad_scores = probs * (grad_probs - deltas[pl.ds(group * 2 + p, 1)]) * inv_root
        stacked = dot(grad_scores[:at], keys[:, window], (0, 0)) + dot(grad_scores[at:], own_keys[:, window], (0, 0))
        merged.append(pair_merge(stacked, first, head))
        key_grads.append(dot(grad_scores, q_pair))
        value_grads.append(dot(probs, g_pair))
    query_out[...] = join(*merged)
    key_grad, value_grad = join(*key_grads), join(*value_grads)
    key_out[...], own_key_out[...] = key_grad[:at], key_grad[at:]
    value_out[...], own_value_out[...] = value_grad[:at], value_grad[at:]
    run_last(step, steps, moved)


def attend_back(present, queries, grads, logs, deltas, keys, values, own_keys, own_values, plan, collective_id):
    seqs, lat, width = queries.shape
    head = width // HEADS
    query, key, own, stat = attend_specs(lat, keys.shape[0] // seqs, own_keys.shape[0] // seqs)
    shape = lambda v: jax.ShapeDtypeStruct(v.shape, F32)
    grid = (seqs, width // 384)
    outs = pl.pallas_call(
        functools.partial(attend_back_kernel, 1.0 / math.sqrt(head), head, plan, grid[0] * grid[1]),
        grid=grid,
        in_specs=[SMEM, query, query, stat, stat, key, key, own, own] + plan.in_specs,
        out_specs=[query, key, key, own, own] + plan.out_specs,
        out_shape=[shape(queries), shape(keys), shape(values), shape(own_keys), shape(own_values)] + plan.out_shape,
        scratch_shapes=plan.scratch,
        compiler_params=pltpu.CompilerParams(
            collective_id=collective_id, has_side_effects=True, vmem_limit_bytes=60 * 2**20
        ),
        name="attend_back",
    )(present, queries, grads, logs, deltas, keys, values, own_keys, own_values, *plan.operands)
    return outs[:5], outs[5:]


def weight_kernel(steps, xt_top, xt_low, own_t, grad_keys, grad_values, own_gk, own_gv, vec, outs, vec_out, mats, *rest):
    n = pl.program_id(0)
    here = Here()
    cut = grad_keys.shape[1]
    sums = Scatter(
        here,
        2 * steps,
        lambda p: mats.at[p, :, :, :, here.c],
        lambda p: mats.at[p, :, :, :, here.oc],
        None,
        lambda p: outs.at[p % 2, :, pl.ds(pl.multiple_of(p // 2 * cut, cut), cut)],
        rest[:14],
    )
    tot, loc = rest[14:16]
    small = Scatter(
        here,
        1,
        lambda p: tot,
        lambda p: vec.at[:, :, :, here.oc],
        lambda p: pltpu.make_async_copy(vec.at[:, :, :, here.c], tot, loc.at[p]),
        lambda p: vec_out,
        rest[16:],
    )
    stages = sums.stages()

    @pl.when(n == 0)
    def _():
        here.greet()

    for w, (grad, own_grad) in enumerate(((grad_keys, own_gk), (grad_values, own_gv))):
        pair = halves(grad[...])
        top, low = halves(own_grad[...])
        stacked = jnp.concatenate([top, low, top], axis=0)

        @pl.loop(0, 2)
        def _(i):
            rows = pl.ds(pl.multiple_of(i * 768, 768), 768)
            made = dot3((xt_top[rows], xt_low[rows]), pair)
            made += jnp.dot(own_t[rows], stacked, preferred_element_type=F32)
            mats[2 * n + w, pl.ds(i * 2, 2)] = made.reshape((2, 2, 2, 2, 48, cut))

        sums.start(2 * n + w)
        for s in (4, 3, 2, 1):
            p = 2 * n + w - LAG * s

            @pl.when(p >= 0)
            def _():
                stages[s](p)

        if w == 1:
            for s in range(5):

                @pl.when(n == s)
                def _():
                    small.stages()[s](0)

    @pl.when(n == steps - 1)
    def _():
        for t in range(2 * steps, 2 * steps + 4 * LAG):
            for s in (4, 3, 2, 1):
                if 0 <= t - LAG * s < 2 * steps:
                    stages[s](t - LAG * s)

        @pl.loop(0, 2 * steps)
        def _(p):
            sums.done(p)

        small.done(0)


def weight_grads(xt_top, xt_low, own_t, grad_keys, grad_values, own_gk, own_gv, vec, collective_id):
    width, rows = xt_top.shape
    own_rows = own_gk.shape[0]
    steps = width // BLOCK
    cols = lambda n: pl.BlockSpec((n, BLOCK), lambda i: (0, i))
    r = width // 32
    vr, vw = vec.shape[0] // 32, vec.shape[1]
    outs, vec_sum = pl.pallas_call(
        functools.partial(weight_kernel, steps),
        grid=(steps,),
        in_specs=[
            whole((width, rows)),
            whole((width, rows)),
            whole(own_t.shape),
            cols(rows),
            cols(rows),
            cols(own_rows),
            cols(own_rows),
            ANY,
        ],
        out_specs=[whole((2, r, width)), whole((vr, vw))],
        out_shape=[jax.ShapeDtypeStruct((2, r, width), F32), jax.ShapeDtypeStruct((vr, vw), F32)],
        scratch_shapes=[pltpu.VMEM((2 * steps,) + GRID + (r, BLOCK), F32)]
        + Scatter.scratch(2 * steps, r, BLOCK)
        + [pltpu.VMEM((4, 2, 2, vr, vw), F32), pltpu.SemaphoreType.DMA((1,))]
        + Scatter.scratch(1, vr, vw),
        compiler_params=pltpu.CompilerParams(
            collective_id=collective_id, has_side_effects=True, vmem_limit_bytes=62 * 2**20
        ),
        name="weight_grads",
    )(xt_top, xt_low, own_t, grad_keys, grad_values, own_gk, own_gv, vec.reshape(GRID + (vr, vw)))
    return outs[0], outs[1], vec_sum


def media_back_kernel(plan, steps, *refs):
    feats, embed, gain, grad_keys, grad_values, own_gk, own_gv, key_w, value_w = refs[:9]
    n = plan.arrays
    out, own_out, sums = refs[9 + n : 12 + n]
    kt, kl, vt, vl, stage, sems = refs[12 + 2 * n : 18 + 2 * n]
    step = pl.program_id(0)
    here = Here()
    moved = plan.bind(here, refs[9 : 9 + n], refs[12 + n : 12 + 2 * n], refs[18 + 2 * n :])
    waves = waves_of(moved, moved.count)
    waves[0].insert(0, here.greet)
    pace = Pace(step, steps, 4, 3, waves)

    @pl.when(step == 0)
    def _():
        split_weights((key_w, value_w), ((kt, kl), (vt, vl)), stage, sems, pace)
        own_out[...] = dot3(halves(own_gk[...]), (kt[...], kl[...]), (1, 1)) + dot3(
            halves(own_gv[...]), (vt[...], vl[...]), (1, 1)
        )
        sums[...] = jnp.zeros_like(sums)

    key_pair, value_pair = halves(grad_keys[...]), halves(grad_values[...])
    for i in range(3):
        pace.at(i)
        rows = slice(i * 512, i * 512 + 512)
        out[:, rows] = dot3(key_pair, (kt[rows], kl[rows]), (1, 1)) + dot3(value_pair, (vt[rows], vl[rows]), (1, 1))
    strip = 64

    @pl.loop(0, out.shape[0] // strip)
    def _(i):
        rows = pl.ds(pl.multiple_of(i * strip, strip), strip)
        incoming = out[rows]
        unit, inv_std = unit_of(feats[rows] + embed[...])
        sums[pl.ds(0, 1)] += jnp.sum(incoming * unit, axis=0, keepdims=True)
        sums[pl.ds(1, 1)] += jnp.sum(incoming, axis=0, keepdims=True)
        scaled = incoming * gain[...]
        result = inv_std * (
            scaled
            - jnp.mean(scaled, axis=-1, keepdims=True)
            - unit * jnp.mean(scaled * unit, axis=-1, keepdims=True)
        )
        out[rows] = result
        sums[pl.ds(2 + step, 1)] += jnp.sum(result, axis=0, keepdims=True)

    run_last(step, steps, moved)


def media_backward(feats, embed, gain, grad_keys, grad_values, own_gk, own_gv, key_w, value_w, plan, collective_id):
    rows, width = feats.shape
    own_rows = own_gk.shape[0]
    row_block = pl.BlockSpec((BLOCK, width), lambda i: (i, 0))
    one_block = pl.BlockSpec((BLOCK, width), lambda i: (i, 0), pipeline_mode=pl.Buffered(1))
    steps = rows // BLOCK
    outs = pl.pallas_call(
        functools.partial(media_back_kernel, plan, steps),
        grid=(steps,),
        in_specs=[
            one_block,
            pl.BlockSpec((None, 1, width), lambda i: (i, 0, 0)),
            whole((1, width)),
            row_block,
            row_block,
            whole((own_rows, width)),
            whole((own_rows, width)),
            ANY,
            ANY,
        ]
        + plan.in_specs,
        out_specs=[one_block, whole((own_rows, width)), whole((8, width))] + plan.out_specs,
        out_shape=[
            jax.ShapeDtypeStruct((rows, width), F32),
            jax.ShapeDtypeStruct((own_rows, width), F32),
            jax.ShapeDtypeStruct((8, width), F32),
        ]
        + plan.out_shape,
        scratch_shapes=staging(width) + plan.scratch,
        compiler_params=pltpu.CompilerParams(
            collective_id=collective_id, has_side_effects=True, vmem_limit_bytes=64 * 2**20 - 2**16
        ),
        name="media_backward",
    )(feats, embed, gain, grad_keys, grad_values, own_gk, own_gv, key_w, value_w, *plan.operands)
    return outs[:3], outs[3:]


GELU_A = math.sqrt(2.0 / math.pi)
GELU_B = 0.044715


def feed_kernel(feed, cot, up, down, feed_part, new_part, grad_up_t, grad_down):
    @pl.when(pl.program_id(0) == 0)
    def _():
        grad_up_t[...] = jnp.zeros_like(grad_up_t)
        grad_down[...] = jnp.zeros_like(grad_down)

    hidden = dot(feed[...], up[...])
    grad_act = dot(cot[...], down[...], (1, 1))
    square = hidden * hidden
    bent = jnp.tanh(GELU_A * (hidden + GELU_B * hidden * square))
    activated = 0.5 * hidden * (1.0 + bent)
    slope = 0.5 * (1.0 + bent) + 0.5 * hidden * (1.0 - bent * bent) * (GELU_A * (1.0 + 3.0 * GELU_B * square))
    grad_hidden = grad_act * slope
    feed_part[...] = dot(grad_hidden, up[...], (1, 1))
    new_part[...] = dot(activated, down[...])
    grad_up_t[...] += dot(grad_hidden, feed[...], (0, 0))
    grad_down[...] += dot(activated, cot[...], (0, 0))


def feed_forward(feed, cot, up, down):
    rows, width = feed.shape
    units = up.shape[1]
    row_block = pl.BlockSpec((BLOCK, width), lambda i: (i, 0))
    one_block = pl.BlockSpec((BLOCK, width), lambda i: (i, 0), pipeline_mode=pl.Buffered(1))
    big = jax.ShapeDtypeStruct((rows, width), F32)
    slim = jax.ShapeDtypeStruct((units, width), F32)
    return pl.pallas_call(
        feed_kernel,
        grid=(rows // BLOCK,),
        in_specs=[row_block, row_block, whole((width, units)), whole((units, width))],
        out_specs=[row_block, row_block, whole((units, width)), whole((units, width))],
        out_shape=[big, big, slim, slim],
        compiler_params=pltpu.CompilerParams(vmem_limit_bytes=60 * 2**20),
        name="feed_forward",
    )(feed, cot, up, down)


def mm(left, right):
    return jnp.dot(left, right, precision=HIGH, preferred_element_type=F32)


def mm_tn(left, right):
    return lax.dot_general(left, right, (((0,), (0,)), ((), ())), precision=HIGH, preferred_element_type=F32)


def mm_nt(left, right):
    return lax.dot_general(left, right, (((1,), (1,)), ((), ())), precision=HIGH, preferred_element_type=F32)


def body_fast(
    latents,
    patch_feats,
    image_counts,
    time_index,
    query_proj,
    key_proj,
    value_proj,
    out_proj,
    up_proj,
    down_proj,
    media_gain,
    media_bias,
    latent_gain,
    latent_bias,
    feed_gain,
    feed_bias,
    time_table,
    out_cotangent,
):
    frame = lax.axis_index("frame")
    frames = lax.axis_size("frame")
    seqs, rows, width = latents.shape
    rounds, patches = patch_feats.shape[1], patch_feats.shape[3]
    lat = rows * frames
    head = width // HEADS
    strip = media_gain.shape[0]

    vectors = jnp.concatenate(
        [jnp.stack([media_gain, media_bias, latent_gain, latent_bias, feed_gain, feed_bias]), time_table], axis=0
    )
    packed = jnp.pad(vectors, ((0, 2), (0, 128 - strip)))
    slot_ids = jnp.arange(rounds, dtype=jnp.int32) * frames + frame
    present = slot_ids[None, :] < image_counts[:, None]
    picks = jnp.arange(time_index.shape[1], dtype=jnp.int32)[None, :] == slot_ids[:, None]
    slot_times = jnp.sum(jnp.where(picks[None, :, :], time_index[:, None, :], 0), axis=-1)
    feats = patch_feats.reshape(-1, width)

    (vec_all, keys, values, own_keys, own_values, queries, xt_top, xt_low), gathered, lat_blocks = opening(
        slot_times.reshape(-1), feats, latents, packed, key_proj, value_proj, query_proj, flatten(out_cotangent), out_proj, 0
    )
    key_w, value_w, query_w, cot_all, out_w = gathered
    up_held, keys = lax.optimization_barrier((up_proj, keys))
    up_cols = lax.all_to_all(
        up_held.reshape(strip, 32, -1), ("seq", "frame"), split_axis=1, concat_axis=0, tiled=True
    ).reshape(width, -1)
    mgain, mbias, lgain, lbias, fgain, fbias = (vec_all[i] for i in range(6))
    table = vec_all[6:14]
    queries = queries.reshape(seqs, lat, width)
    latent_norm, latent_unit, latent_std = norm_forward(lat_blocks.reshape(seqs, lat, width), lgain, lbias)
    own_rows = lambda v: lax.dynamic_slice_in_dim(v, frame * rows, rows, 1)
    own_norm, own_unit, own_std = own_rows(latent_norm), own_rows(latent_unit), own_rows(latent_std)
    one_hot = slot_times[:, :, None] == jnp.arange(time_table.shape[0], dtype=jnp.int32)
    slot_embed = jnp.sum(jnp.where(one_hot[..., None], table, 0.0), axis=2)
    embed = slot_embed.reshape(-1, 1, width)
    own_flat = flatten(own_norm)
    present = present.astype(jnp.int32)

    partial, row_top, row_sum = attend(present, queries, keys, values, own_keys, own_values)
    stats = jnp.concatenate([row_top.reshape(seqs, HEADS, lat), row_sum.reshape(seqs, HEADS, lat)], axis=1)
    stats = jnp.pad(stats.transpose(0, 2, 1), ((0, 0), (0, 0), (0, 128 - 2 * HEADS)))
    part_all, stat_all = group_swap(
        [partial.reshape(seqs, frames, rows, width), stats.reshape(seqs, frames, rows, 128)], 2
    )
    tops, sums = stat_all[..., :HEADS], stat_all[..., HEADS : 2 * HEADS]
    top = jnp.max(tops, axis=1)
    ratio = jnp.exp(tops - top[:, None])
    row_total = jnp.sum(sums * ratio, axis=1)
    weight = ratio / row_total[:, None]
    attended = jnp.sum(part_all.reshape(seqs, frames, rows, HEADS, head) * weight[..., None], axis=1)
    log_total = top + jnp.log(row_total)
    attended_flat = attended.reshape(seqs, rows, width)
    middle = latents + mm(flatten(attended_flat), out_w).reshape(seqs, rows, width)

    feed_norm, feed_unit, feed_std = norm_forward(middle, fgain, fbias)
    (feed_all,) = gather_all([flatten(feed_norm)], 3)
    feed_part, new_part, grad_up_t, grad_down = feed_forward(feed_all, cot_all, up_cols, down_proj)
    (grad_feed_norm,) = scatter_all([feed_part], 4)
    grad_mid_norm, grad_fgain, grad_fbias = norm_backward(
        grad_feed_norm.reshape(seqs, rows, width), feed_unit, feed_std, fgain
    )
    grad_middle = out_cotangent + grad_mid_norm
    grad_out_w = mm_tn(flatten(attended_flat), flatten(grad_middle))
    grad_own = mm_nt(flatten(grad_middle), out_w).reshape(seqs, rows, HEADS, head)
    delta = jnp.sum(grad_own * attended, axis=-1)
    back_stats = jnp.pad(jnp.concatenate([log_total, delta], axis=-1), ((0, 0), (0, 0), (0, 128 - 2 * HEADS)))
    grad_blocks, back_blocks = group_gather([grad_own.reshape(seqs, rows, width), back_stats], 5)
    back_all = back_blocks.reshape(seqs, lat, 128).transpose(0, 2, 1)
    logs_all, delta_all = (back_all[:, i * HEADS : (i + 1) * HEADS].reshape(seqs, 8, 128) for i in range(2))

    (query_part, grad_keys, grad_values, own_gk, own_gv), (new_rows,) = attend_back(
        present,
        queries,
        grad_blocks.reshape(seqs, lat, width),
        logs_all,
        delta_all,
        keys,
        values,
        own_keys,
        own_values,
        Summed([new_part]),
        10,
    )
    new_latents = middle + new_rows.reshape(seqs, rows, width)
    grad_up_t, query_part = lax.optimization_barrier((grad_up_t, query_part))
    grad_up = lax.all_to_all(
        grad_up_t.reshape(-1, 32, strip).transpose(1, 2, 0), ("seq", "frame"), split_axis=0, concat_axis=2, tiled=True
    ).reshape(strip, -1)
    (query_blocks,) = group_swap([query_part.reshape(seqs, frames, rows, width)], 6)
    grad_queries = flatten(jnp.sum(query_blocks, axis=1))

    grad_query_w = mm_tn(own_flat, grad_queries)
    grad_up, grad_query_w = lax.optimization_barrier((grad_up, grad_query_w))
    (patch_grads, own_back, media_sums), (sum_query, sum_out) = media_backward(
        feats,
        embed,
        mgain[None],
        grad_keys,
        grad_values,
        own_gk,
        own_gv,
        key_w,
        value_w,
        Summed([grad_query_w, grad_out_w]),
        7,
    )
    grad_own_norm = (mm_nt(grad_queries, query_w) + own_back).reshape(seqs, rows, width)
    grad_lat_in, grad_lgain, grad_lbias = norm_backward(grad_own_norm, own_unit, own_std, lgain)
    latent_grads = grad_middle + grad_lat_in
    grad_mgain, grad_mbias = media_sums[0], media_sums[1]
    slot_sums = media_sums[2:].reshape(seqs, rounds, width)
    grad_table = jnp.sum(jnp.where(one_hot[..., None], slot_sums[:, :, None, :], 0.0), axis=(0, 1))
    vec_grads = jnp.concatenate(
        [jnp.stack([grad_mgain, grad_mbias, grad_lgain, grad_lbias, grad_fgain, grad_fbias]), grad_table], axis=0
    )
    vec_blocks = jnp.pad(vec_grads.reshape(14, 32, strip).transpose(1, 0, 2), ((0, 0), (0, 2), (0, 128 - strip)))
    top, low = halves(own_flat)
    own_t = jnp.concatenate([top, top, low], axis=0).T
    sum_key, sum_value, sum_vec = weight_grads(
        xt_top, xt_low, own_t, grad_keys, grad_values, own_gk, own_gv, vec_blocks.reshape(-1, 128), 8
    )
    vec = sum_vec[:14, :strip]
    return (
        new_latents,
        latent_grads,
        patch_grads.reshape(patch_feats.shape),
        sum_query,
        sum_key,
        sum_value,
        sum_out,
        grad_up,
        grad_down,
        vec[0],
        vec[1],
        vec[2],
        vec[3],
        vec[4],
        vec[5],
        vec[6:],
    )


def solution(mesh):
    fast = dict(mesh.shape) == {"seq": 8, "frame": 4}
    return jax.shard_map(
        body_fast if fast else body_general,
        mesh=mesh,
        in_specs=(
            P("seq", "frame", None),
            P("seq", None, "frame", None, None),
            P("seq"),
            P("seq", None),
            P(("seq", "frame"), None),
            P(("seq", "frame"), None),
            P(("seq", "frame"), None),
            P(("seq", "frame"), None),
            P(("seq", "frame"), None),
            P(("seq", "frame"), None),
            P(("seq", "frame")),
            P(("seq", "frame")),
            P(("seq", "frame")),
            P(("seq", "frame")),
            P(("seq", "frame")),
            P(("seq", "frame")),
            P(None, ("seq", "frame")),
            P("seq", "frame", None),
        ),
        out_specs=(
            P("seq", "frame", None),
            P("seq", "frame", None),
            P("seq", None, "frame", None, None),
            P(("seq", "frame"), None),
            P(("seq", "frame"), None),
            P(("seq", "frame"), None),
            P(("seq", "frame"), None),
            P(("seq", "frame"), None),
            P(("seq", "frame"), None),
            P(("seq", "frame")),
            P(("seq", "frame")),
            P(("seq", "frame")),
            P(("seq", "frame")),
            P(("seq", "frame")),
            P(("seq", "frame")),
            P(None, ("seq", "frame")),
        ),
        check_vma=False,
    )
```

```python
import functools
import math

import jax
import jax.numpy as jnp
from jax import lax
from jax.experimental import pallas as pl
from jax.experimental.pallas import tpu as pltpu
from jax.sharding import PartitionSpec as P

HEADS = 16


HIGHEST = lax.Precision.HIGHEST
EPSILON = 1e-05
MASKED = -1e30


def product(left, right):
    return jnp.dot(left, right, precision=HIGHEST, preferred_element_type=jnp.float32)


def product_tn(left, right):
    return lax.dot_general(
        left, right, (((0,), (0,)), ((), ())), precision=HIGHEST, preferred_element_type=jnp.float32
    )


def product_nt(left, right):
    return lax.dot_general(
        left, right, (((1,), (1,)), ((), ())), precision=HIGHEST, preferred_element_type=jnp.float32
    )


def flatten(values):
    return values.reshape(-1, values.shape[-1])


def norm_forward(values, gain_vec, bias_vec):
    centred = values - jnp.mean(values, axis=-1, keepdims=True)
    inv_std = lax.rsqrt(jnp.mean(centred * centred, axis=-1, keepdims=True) + EPSILON)
    unit_vals = centred * inv_std
    return (unit_vals * gain_vec + bias_vec, unit_vals, inv_std)


def norm_backward(incoming, unit_vals, inv_std, gain_vec):
    scaled = incoming * gain_vec
    result = inv_std * (
        scaled
        - jnp.mean(scaled, axis=-1, keepdims=True)
        - unit_vals * jnp.mean(scaled * unit_vals, axis=-1, keepdims=True)
    )
    flat_in = flatten(incoming)
    return (result, jnp.sum(flat_in * flatten(unit_vals), axis=0), jnp.sum(flat_in, axis=0))


def heads_last(stats):
    return jnp.transpose(stats, (0, 2, 1))[..., None]


def per_slot(action, operands):
    return lax.map(action, operands)


def body_general(
    latents,
    patch_feats,
    image_counts,
    time_index,
    query_proj,
    key_proj,
    value_proj,
    out_proj,
    up_proj,
    down_proj,
    media_gain,
    media_bias,
    latent_gain,
    latent_bias,
    feed_gain,
    feed_bias,
    time_table,
    out_cotangent,
):
    gathered = (
        lax.all_gather(query_proj, ("seq", "frame"), axis=0, tiled=True),
        lax.all_gather(key_proj, ("seq", "frame"), axis=0, tiled=True),
        lax.all_gather(value_proj, ("seq", "frame"), axis=0, tiled=True),
        lax.all_gather(out_proj, ("seq", "frame"), axis=0, tiled=True),
        lax.all_gather(up_proj, ("seq", "frame"), axis=0, tiled=True),
        lax.all_gather(down_proj, ("seq", "frame"), axis=0, tiled=True),
        lax.all_gather(media_gain, ("seq", "frame"), axis=0, tiled=True),
        lax.all_gather(media_bias, ("seq", "frame"), axis=0, tiled=True),
        lax.all_gather(latent_gain, ("seq", "frame"), axis=0, tiled=True),
        lax.all_gather(latent_bias, ("seq", "frame"), axis=0, tiled=True),
        lax.all_gather(feed_gain, ("seq", "frame"), axis=0, tiled=True),
        lax.all_gather(feed_bias, ("seq", "frame"), axis=0, tiled=True),
        lax.all_gather(time_table, ("seq", "frame"), axis=1, tiled=True),
    )
    gathered = lax.optimization_barrier(gathered)
    (
        query_full,
        key_full,
        value_full,
        out_full,
        up_full,
        down_full,
        mgain_full,
        mbias_full,
        lgain_full,
        lbias_full,
        fgain_full,
        fbias_full,
        table_full,
    ) = gathered
    frame_index = lax.axis_index("frame")
    frame_count = lax.axis_size("frame")
    seq_local, lat_rows, model_width = latents.shape
    round_count = patch_feats.shape[1]
    patch_count = patch_feats.shape[3]
    slot_total = time_index.shape[1]
    table_rows = time_table.shape[0]
    latent_total = lat_rows * frame_count
    head_size = model_width // HEADS
    inv_root = 1.0 / math.sqrt(head_size)
    latent_all = lax.all_gather(latents, "frame", axis=1, tiled=True)
    latent_norm, latent_unit, latent_std = norm_forward(latent_all, lgain_full, lbias_full)
    row_start = frame_index * lat_rows
    own_norm = lax.dynamic_slice_in_dim(latent_norm, row_start, lat_rows, 1)
    own_unit = lax.dynamic_slice_in_dim(latent_unit, row_start, lat_rows, 1)
    own_std = lax.dynamic_slice_in_dim(latent_std, row_start, lat_rows, 1)
    queries = product(flatten(latent_norm), query_full).reshape(
        seq_local, latent_total, model_width
    )
    own_keys = product(flatten(own_norm), key_full).reshape(seq_local, lat_rows, model_width)
    own_values = product(flatten(own_norm), value_full).reshape(seq_local, lat_rows, model_width)
    slot_ids = jnp.arange(round_count, dtype=jnp.int32) * frame_count + frame_index
    present = slot_ids[None, :] < image_counts[:, None]
    picks = jnp.arange(slot_total, dtype=jnp.int32)[None, :] == slot_ids[:, None]
    slot_times = jnp.sum(jnp.where(picks[None, :, :], time_index[:, None, :], 0), axis=-1)
    one_hot = (
        slot_times.reshape(-1)[:, None] == jnp.arange(table_rows, dtype=jnp.int32)[None, :]
    ).astype(jnp.float32)
    slot_embed = product(one_hot, table_full)
    slot_feats = patch_feats.reshape(seq_local * round_count, patch_count, model_width)

    def media_forward(element):
        normed, unit_part, std_part = norm_forward(
            element[0] + element[1][None, :], mgain_full, mbias_full
        )
        return (normed, unit_part, std_part, product(normed, key_full), product(normed, value_full))

    media_norm, media_unit, media_std, media_keys, media_values = per_slot(
        media_forward, (slot_feats, slot_embed)
    )
    key_total = lat_rows + round_count * patch_count
    all_keys = jnp.concatenate(
        [own_keys, media_keys.reshape(seq_local, round_count * patch_count, model_width)], axis=1
    )
    all_values = jnp.concatenate(
        [own_values, media_values.reshape(seq_local, round_count * patch_count, model_width)],
        axis=1,
    )
    keep = jnp.concatenate(
        [jnp.ones((seq_local, lat_rows), dtype=bool), jnp.repeat(present, patch_count, axis=1)],
        axis=1,
    )
    query_four = queries.reshape(seq_local, latent_total, HEADS, head_size)
    key_four = all_keys.reshape(seq_local, key_total, HEADS, head_size)
    value_four = all_values.reshape(seq_local, key_total, HEADS, head_size)

    def masked_scores():
        raw_scores = (
            jnp.einsum(
                "bqhe,bkhe->bhqk",
                query_four,
                key_four,
                precision=HIGHEST,
                preferred_element_type=jnp.float32,
            )
            * inv_root
        )
        return jnp.where(keep[:, None, None, :], raw_scores, MASKED)

    scores = masked_scores()
    row_top = jnp.max(scores, axis=-1)
    expo = jnp.exp(scores - row_top[..., None])
    row_total = jnp.sum(expo, axis=-1)
    partial_out = jnp.einsum(
        "bhqk,bkhe->bqhe", expo, value_four, precision=HIGHEST, preferred_element_type=jnp.float32
    )
    glob_top = lax.pmax(row_top, "frame")
    ratio = jnp.exp(row_top - glob_top)
    glob_total, glob_out = lax.psum((row_total * ratio, partial_out * heads_last(ratio)), "frame")
    attended = glob_out / heads_last(glob_total)
    log_total = glob_top + jnp.log(glob_total)
    attended_flat = attended.reshape(seq_local, latent_total, model_width)
    own_attended = lax.dynamic_slice_in_dim(attended_flat, row_start, lat_rows, 1)
    middle = latents + product(flatten(own_attended), out_full).reshape(
        seq_local, lat_rows, model_width
    )
    feed_norm, feed_unit, feed_std = norm_forward(middle, fgain_full, fbias_full)
    hidden_pre = product(flatten(feed_norm), up_full)
    activated, gelu_pull = jax.vjp(jax.nn.gelu, hidden_pre)
    new_latents = middle + product(activated, down_full).reshape(seq_local, lat_rows, model_width)
    regathered = (
        lax.all_gather(query_proj, ("seq", "frame"), axis=0, tiled=True),
        lax.all_gather(key_proj, ("seq", "frame"), axis=0, tiled=True),
        lax.all_gather(value_proj, ("seq", "frame"), axis=0, tiled=True),
        lax.all_gather(out_proj, ("seq", "frame"), axis=0, tiled=True),
        lax.all_gather(up_proj, ("seq", "frame"), axis=0, tiled=True),
        lax.all_gather(down_proj, ("seq", "frame"), axis=0, tiled=True),
        lax.all_gather(media_gain, ("seq", "frame"), axis=0, tiled=True),
        lax.all_gather(media_bias, ("seq", "frame"), axis=0, tiled=True),
        lax.all_gather(latent_gain, ("seq", "frame"), axis=0, tiled=True),
        lax.all_gather(latent_bias, ("seq", "frame"), axis=0, tiled=True),
        lax.all_gather(feed_gain, ("seq", "frame"), axis=0, tiled=True),
        lax.all_gather(feed_bias, ("seq", "frame"), axis=0, tiled=True),
        lax.all_gather(time_table, ("seq", "frame"), axis=1, tiled=True),
    )
    regathered = lax.optimization_barrier(regathered)
    query_back = regathered[0]
    key_back = regathered[1]
    value_back = regathered[2]
    out_back = regathered[3]
    up_back = regathered[4]
    down_back = regathered[5]
    mgain_back = regathered[6]
    lgain_back = regathered[8]
    fgain_back = regathered[10]
    cotangent = flatten(out_cotangent)
    grad_down = product_tn(activated, cotangent)
    grad_hidden = gelu_pull(product_nt(cotangent, down_back))[0]
    grad_up = product_tn(flatten(feed_norm), grad_hidden)
    grad_feed_norm = product_nt(grad_hidden, up_back).reshape(seq_local, lat_rows, model_width)
    grad_mid_norm, grad_fgain, grad_fbias = norm_backward(
        grad_feed_norm, feed_unit, feed_std, fgain_back
    )
    grad_middle = out_cotangent + grad_mid_norm
    grad_out_w = product_tn(flatten(own_attended), flatten(grad_middle))
    grad_own_att = product_nt(flatten(grad_middle), out_back).reshape(
        seq_local, lat_rows, model_width
    )
    grad_attended = lax.all_gather(grad_own_att, "frame", axis=1, tiled=True)
    grad_four = grad_attended.reshape(seq_local, latent_total, HEADS, head_size)
    delta_rows = jnp.einsum(
        "bqhe,bqhe->bhq", grad_four, attended, precision=HIGHEST, preferred_element_type=jnp.float32
    )
    probs = jnp.exp(masked_scores() - log_total[..., None])
    grad_probs = jnp.einsum(
        "bqhe,bkhe->bhqk",
        grad_four,
        value_four,
        precision=HIGHEST,
        preferred_element_type=jnp.float32,
    )
    grad_scores = probs * (grad_probs - delta_rows[..., None]) * inv_root
    grad_query_part = jnp.einsum(
        "bhqk,bkhe->bqhe",
        grad_scores,
        key_four,
        precision=HIGHEST,
        preferred_element_type=jnp.float32,
    ).reshape(seq_local, latent_total, model_width)
    grad_keys = jnp.einsum(
        "bhqk,bqhe->bkhe",
        grad_scores,
        query_four,
        precision=HIGHEST,
        preferred_element_type=jnp.float32,
    ).reshape(seq_local, key_total, model_width)
    grad_values = jnp.einsum(
        "bhqk,bqhe->bkhe", probs, grad_four, precision=HIGHEST, preferred_element_type=jnp.float32
    ).reshape(seq_local, key_total, model_width)
    grad_query_own = lax.psum_scatter(grad_query_part, "frame", scatter_dimension=1, tiled=True)
    grad_key_lat = flatten(grad_keys[:, :lat_rows])
    grad_value_lat = flatten(grad_values[:, :lat_rows])
    grad_key_media = grad_keys[:, lat_rows:].reshape(
        seq_local * round_count, patch_count, model_width
    )
    grad_value_media = grad_values[:, lat_rows:].reshape(
        seq_local * round_count, patch_count, model_width
    )
    grad_query_w = product_tn(flatten(own_norm), flatten(grad_query_own))
    grad_key_w = product_tn(flatten(own_norm), grad_key_lat) + product_tn(
        flatten(media_norm), flatten(grad_key_media)
    )
    grad_value_w = product_tn(flatten(own_norm), grad_value_lat) + product_tn(
        flatten(media_norm), flatten(grad_value_media)
    )
    grad_own_norm = (
        product_nt(flatten(grad_query_own), query_back)
        + product_nt(grad_key_lat, key_back)
        + product_nt(grad_value_lat, value_back)
    ).reshape(seq_local, lat_rows, model_width)
    grad_lat_in, grad_lgain, grad_lbias = norm_backward(
        grad_own_norm, own_unit, own_std, lgain_back
    )
    latent_grads = grad_middle + grad_lat_in

    def media_backward(element):
        normed_grad = product_nt(element[0], key_back) + product_nt(element[1], value_back)
        feats_grad, gain_part, bias_part = norm_backward(
            normed_grad, element[2], element[3], mgain_back
        )
        return (feats_grad, gain_part, bias_part, jnp.sum(feats_grad, axis=0))

    feats_grads, gain_parts, bias_parts, slot_sums = per_slot(
        media_backward, (grad_key_media, grad_value_media, media_unit, media_std)
    )
    grad_mgain = jnp.sum(gain_parts, axis=0)
    grad_mbias = jnp.sum(bias_parts, axis=0)
    grad_table = product_tn(one_hot, slot_sums)
    patch_grads = feats_grads.reshape(patch_feats.shape)
    (
        grad_query_w,
        grad_key_w,
        grad_value_w,
        grad_out_w,
        grad_up,
        grad_down,
    ) = lax.optimization_barrier(
        (grad_query_w, grad_key_w, grad_value_w, grad_out_w, grad_up, grad_down)
    )
    summed = (
        lax.psum_scatter(grad_query_w, ("seq", "frame"), scatter_dimension=0, tiled=True),
        lax.psum_scatter(grad_key_w, ("seq", "frame"), scatter_dimension=0, tiled=True),
        lax.psum_scatter(grad_value_w, ("seq", "frame"), scatter_dimension=0, tiled=True),
        lax.psum_scatter(grad_out_w, ("seq", "frame"), scatter_dimension=0, tiled=True),
        lax.psum_scatter(grad_up, ("seq", "frame"), scatter_dimension=0, tiled=True),
        lax.psum_scatter(grad_down, ("seq", "frame"), scatter_dimension=0, tiled=True),
        lax.psum_scatter(grad_mgain, ("seq", "frame"), scatter_dimension=0, tiled=True),
        lax.psum_scatter(grad_mbias, ("seq", "frame"), scatter_dimension=0, tiled=True),
        lax.psum_scatter(grad_lgain, ("seq", "frame"), scatter_dimension=0, tiled=True),
        lax.psum_scatter(grad_lbias, ("seq", "frame"), scatter_dimension=0, tiled=True),
        lax.psum_scatter(grad_fgain, ("seq", "frame"), scatter_dimension=0, tiled=True),
        lax.psum_scatter(grad_fbias, ("seq", "frame"), scatter_dimension=0, tiled=True),
        lax.psum_scatter(grad_table, ("seq", "frame"), scatter_dimension=1, tiled=True),
    )
    return (
        new_latents,
        latent_grads,
        patch_grads,
        summed[0],
        summed[1],
        summed[2],
        summed[3],
        summed[4],
        summed[5],
        summed[6],
        summed[7],
        summed[8],
        summed[9],
        summed[10],
        summed[11],
        summed[12],
    )


MESH = pl.DeviceIdType.MESH
F32 = jnp.float32
ANY = pl.BlockSpec(memory_space=pl.ANY)
GRID = (4, 2, 2, 2)


def place(z, y, x, c):
    return (z * 2 + y, x * 2 + c)


class Here:
    def __init__(self):
        seq, frame = lax.axis_index("seq"), lax.axis_index("frame")
        self.z, self.y, self.x, self.c = z, y, x, c = seq // 2, seq % 2, frame // 2, frame % 2
        self.ox, self.oy, self.oc = ox, oy, oc = 1 - x, 1 - y, 1 - c
        self.at_x, self.at_y, self.at_c = place(z, y, ox, c), place(z, oy, x, c), place(z, y, x, oc)
        self.ahead = [lax.rem(z + k, 4) for k in range(4)]
        self.behind = [lax.rem(z + 4 - k, 4) for k in range(4)]
        self.at_z = [place(o, y, x, c) for o in self.ahead]

    def greet(self):
        barrier = pltpu.get_barrier_semaphore()
        for peer in self.at_z[1:] + [self.at_x, self.at_y, self.at_c]:
            pl.semaphore_signal(barrier, inc=1, device_id=peer, device_id_type=MESH)
        pl.semaphore_wait(barrier, 6)


def remote(src, dst, send_sem, recv_sem, peer):
    return pltpu.make_async_remote_copy(
        src_ref=src, dst_ref=dst, send_sem=send_sem, recv_sem=recv_sem, device_id=peer, device_id_type=MESH
    )


class Gather:
    lag = 1

    def __init__(self, here, shards, fulls, cuts, sems):
        self.here, self.count = here, len(cuts)
        self.loc, self.zs, self.zr, self.xs, self.xr, self.ys, self.yr, self.ds, self.dr, self.cs, self.cr = sems
        self.shard = [shards[a].at[:, lo:hi] for a, lo, hi in cuts]
        self.full = [(lambda *at, a=a, lo=lo, hi=hi: fulls[a].at[at + (slice(lo, hi),)]) for a, lo, hi in cuts]
        self.half = [shards[a].shape[0] // 2 for a, lo, hi in cuts]

    @staticmethod
    def semaphores(count):
        dma = pltpu.SemaphoreType.DMA
        shapes = [(), (3,), (3,), (4,), (4,), (4,), (4,), (2, 4), (2, 4), (4,), (4,)]
        return [dma((count,) + s) for s in shapes]

    def local(self, p):
        h = self.here
        return pltpu.make_async_copy(self.shard[p], self.full[p](h.z, h.y, h.x, h.c, slice(None)), self.loc.at[p])

    def over_z(self, p, k):
        h = self.here
        dst = self.full[p](h.z, h.y, h.x, h.c, slice(None))
        return remote(self.shard[p], dst, self.zs.at[p, k - 1], self.zr.at[p, k - 1], h.at_z[k])

    def over_x(self, p, k):
        h = self.here
        block = self.full[p](h.behind[k], h.y, h.x, h.c, slice(None))
        return remote(self.shard[p] if k == 0 else block, block, self.xs.at[p, k], self.xr.at[p, k], h.at_x)

    def over_y(self, p, k):
        h = self.here
        block = self.full[p](h.behind[k], h.y, h.x, h.c, slice(None))
        return remote(self.shard[p] if k == 0 else block, block, self.ys.at[p, k], self.yr.at[p, k], h.at_y)

    def on_y(self, p, k):
        h = self.here
        part = self.full[p](h.behind[k], h.y, h.ox, h.c, slice(self.half[p], 2 * self.half[p]))
        return remote(part, part, self.ds.at[p, 0, k], self.dr.at[p, 0, k], h.at_y)

    def on_x(self, p, k):
        h = self.here
        part = self.full[p](h.behind[k], h.oy, h.x, h.c, slice(0, self.half[p]))
        return remote(part, part, self.ds.at[p, 1, k], self.dr.at[p, 1, k], h.at_x)

    def to_core(self, p, i):
        h = self.here
        yy, xx = ((h.y, h.x), (h.y, h.ox), (h.oy, h.x), (h.oy, h.ox))[i]
        blocks = self.full[p](slice(None), yy, xx, h.c, slice(None))
        return remote(blocks, blocks, self.cs.at[p, i], self.cr.at[p, i], h.at_c)

    def own(self, p):
        self.local(p).start()
        for k in (1, 2, 3):
            self.over_z(p, k).start()
        self.over_x(p, 0).start()
        self.over_y(p, 0).start()

    def along_z(self, p):
        for k in (1, 2, 3):
            self.over_z(p, k).wait_recv()
            self.over_x(p, k).start()
            self.over_y(p, k).start()

    def across(self, p):
        for k in range(4):
            self.over_x(p, k).wait_recv()
            self.on_y(p, k).start()
            self.over_y(p, k).wait_recv()
            self.on_x(p, k).start()
        self.local(p).wait()
        for i in range(3):
            self.to_core(p, i).start()

    def corner(self, p):
        for k in range(4):
            self.on_y(p, k).wait_recv()
            self.on_x(p, k).wait_recv()
        self.to_core(p, 3).start()

    def arrived(self, p):
        for i in range(4):
            self.to_core(p, i).wait_recv()

    def done(self, p, here=False):
        if not here:
            self.arrived(p)
        for i in range(4):
            self.to_core(p, i).wait_send()
        for k in (1, 2, 3):
            self.over_z(p, k).wait_send()
        for k in range(4):
            for copy in (self.over_x, self.over_y, self.on_x, self.on_y):
                copy(p, k).wait_send()

    def stages(self):
        return (self.own, self.along_z, self.across, self.corner)


LAG = 2


def waves_of(plan, ahead):
    first, *stages = plan.stages()
    count, last, lag = plan.count, len(stages) - 1, plan.lag
    ahead = min(ahead, count)
    waves = [[functools.partial(first, p) for p in range(ahead)]]
    for t in range(count + last * lag):
        wave = [functools.partial(first, t + ahead)] if t + ahead < count else []
        order = range(last, -1, -1)
        waves.append(wave + [functools.partial(stages[s], t - s * lag) for s in order if 0 <= t - s * lag < count])
    return waves


def finish_all(plan):
    for p in range(plan.count):
        plan.done(p)


class Scatter:
    lag = LAG

    def __init__(self, here, count, mine, theirs, load, out, scratch):
        self.here, self.count, self.mine, self.theirs, self.load, self.out = here, count, mine, theirs, load, out
        self.got, self.gx, self.gy, self.hx, self.hy, self.gz = scratch[:6]
        self.cs, self.cr, self.fs, self.fr, self.ss, self.sr, self.zs, self.zr = scratch[6:]
        self.half = self.got.shape[-2] // 2

    @staticmethod
    def scratch(count, r, w):
        dma = pltpu.SemaphoreType.DMA
        leads = [(4, 2, 2, r), (4, 2, r // 2), (4, 2, r // 2), (4, r // 2), (4, r // 2), (3, r)]
        return [pltpu.VMEM((count,) + s + (w,), F32) for s in leads] + [
            dma((count,) + s) for s in ((), (), (2,), (2,), (2,), (2,), (3,), (3,))
        ]

    def to_core(self, p):
        return remote(self.theirs(p), self.got.at[p], self.cs.at[p], self.cr.at[p], self.here.at_c)

    def first(self, p, way):
        h, half, tot = self.here, self.half, self.mine(p)
        if way == 0:
            return remote(tot.at[:, :, h.ox, :half], self.gx.at[p], self.fs.at[p, 0], self.fr.at[p, 0], h.at_x)
        return remote(tot.at[:, h.oy, :, half:], self.gy.at[p], self.fs.at[p, 1], self.fr.at[p, 1], h.at_y)

    def second(self, p, way):
        h, half, tot = self.here, self.half, self.mine(p)
        if way == 0:
            return remote(tot.at[:, h.oy, h.x, :half], self.hy.at[p], self.ss.at[p, 0], self.sr.at[p, 0], h.at_y)
        return remote(tot.at[:, h.y, h.ox, half:], self.hx.at[p], self.ss.at[p, 1], self.sr.at[p, 1], h.at_x)

    def over_z(self, p, k):
        h = self.here
        src = self.mine(p).at[h.ahead[k], h.y, h.x]
        return remote(src, self.gz.at[p, k - 1], self.zs.at[p, k - 1], self.zr.at[p, k - 1], h.at_z[k])

    def start(self, p):
        if self.load is not None:
            self.load(p).start()
        self.to_core(p).start()

    def cores(self, p):
        tot, got = self.mine(p), self.got.at[p]
        if self.load is not None:
            self.load(p).wait()
        self.to_core(p).wait_recv()

        @pl.loop(0, 16)
        def _(i):
            at = (i // 4, (i // 2) % 2, i % 2)
            tot[at] = tot[at] + got[at]

        self.first(p, 0).start()
        self.first(p, 1).start()

    def sides(self, p):
        h, half, tot = self.here, self.half, self.mine(p)
        gx, gy = self.gx.at[p], self.gy.at[p]
        self.first(p, 0).wait_recv()

        @pl.loop(0, 8)
        def _(i):
            zi, yi = i // 2, i % 2
            tot[zi, yi, h.x, :half] = tot[zi, yi, h.x, :half] + gx[zi, yi]

        self.second(p, 0).start()
        self.first(p, 1).wait_recv()

        @pl.loop(0, 8)
        def _(i):
            zi, xi = i // 2, i % 2
            tot[zi, h.y, xi, half:] = tot[zi, h.y, xi, half:] + gy[zi, xi]

        self.second(p, 1).start()

    def column(self, p):
        h, half, tot = self.here, self.half, self.mine(p)
        hx, hy = self.hx.at[p], self.hy.at[p]
        self.second(p, 0).wait_recv()
        self.second(p, 1).wait_recv()

        @pl.loop(0, 4)
        def _(zi):
            tot[zi, h.y, h.x, :half] = tot[zi, h.y, h.x, :half] + hy[zi]
            tot[zi, h.y, h.x, half:] = tot[zi, h.y, h.x, half:] + hx[zi]

        for k in (1, 2, 3):
            self.over_z(p, k).start()

    def finish(self, p):
        h, gz = self.here, self.gz.at[p]
        for k in (1, 2, 3):
            self.over_z(p, k).wait_recv()
        self.out(p)[...] = (self.mine(p)[h.z, h.y, h.x] + gz[0]) + (gz[1] + gz[2])

    def done(self, p):
        self.to_core(p).wait_send()
        for way in (0, 1):
            self.first(p, way).wait_send()
            self.second(p, way).wait_send()
        for k in (1, 2, 3):
            self.over_z(p, k).wait_send()

    def stages(self):
        return (self.start, self.cores, self.sides, self.column, self.finish)


def run(wave):
    for action in wave:
        action()


class Pace:
    def __init__(self, step, steps, lead, parts, waves):
        self.step, self.steps, self.lead, self.parts = step, steps, lead, parts
        ticks, total, before = lead + steps * parts, 1 + sum(len(w) for w in waves[1:]), 0
        self.waves = [[] for _ in range(ticks)]
        for wave in waves:
            self.waves[ticks * before // total] += wave
            before += len(wave) if before else 1

    def at_lead(self, i):
        run(self.waves[i])

    def at(self, part):
        for s in range(self.steps):
            now = self.waves[self.lead + s * self.parts + part]
            if now:
                pl.when(self.step == s)(functools.partial(run, now))


def run_last(step, steps, plan):
    @pl.when(step == steps - 1)
    def _():
        finish_all(plan)


WIDE = 768


def column_cuts(shards):
    return [(a, lo, min(lo + WIDE, s.shape[1])) for a, s in enumerate(shards) for lo in range(0, s.shape[1], WIDE)]


class GroupGather:
    def __init__(self, here, shards, fulls, sems):
        self.here, self.shards, self.fulls, self.count = here, shards, fulls, len(shards)
        self.loc, self.ss, self.rs = sems

    @staticmethod
    def semaphores(count):
        dma = pltpu.SemaphoreType.DMA
        return [dma((count,)), dma((count, 3)), dma((count, 3))]

    def local(self, a):
        h = self.here
        return pltpu.make_async_copy(self.shards[a], self.fulls[a].at[:, h.x * 2 + h.c], self.loc.at[a])

    def copy(self, a, i):
        h = self.here
        mine = self.fulls[a].at[:, h.x * 2 + h.c]
        if i < 2:
            return remote(self.shards[a], mine, self.ss.at[a, i], self.rs.at[a, i], (h.at_x, h.at_c)[i])
        block = self.fulls[a].at[:, h.ox * 2 + h.c]
        return remote(block, block, self.ss.at[a, 2], self.rs.at[a, 2], h.at_c)

    def start(self):
        for a in range(self.count):
            self.local(a).start()
            self.copy(a, 0).start()
            self.copy(a, 1).start()

    def forward(self):
        for a in range(self.count):
            self.copy(a, 0).wait_recv()
            self.copy(a, 2).start()

    def done(self):
        for a in range(self.count):
            self.local(a).wait()
            self.copy(a, 0).wait_send()
            self.copy(a, 1).wait()
            self.copy(a, 2).wait()


def flat_full(full):
    return full.reshape((-1, full.shape[-1]))


def full_shapes(shards):
    return [jax.ShapeDtypeStruct(GRID + s.shape, s.dtype) for s in shards]


def gather_kernel(count, cuts, *refs):
    here = Here()
    here.greet()
    plan = Gather(here, refs[:count], refs[count : 2 * count], cuts, refs[2 * count :])
    for wave in waves_of(plan, 2):
        run(wave)
    finish_all(plan)


def gather_all(shards, collective_id):
    count = len(shards)
    cuts = column_cuts(shards)
    outs = pl.pallas_call(
        functools.partial(gather_kernel, count, cuts),
        out_shape=full_shapes(shards),
        in_specs=[ANY] * count,
        out_specs=[ANY] * count,
        scratch_shapes=Gather.semaphores(len(cuts)),
        compiler_params=pltpu.CompilerParams(collective_id=collective_id, has_side_effects=True),
        name="gather_all",
    )(*shards)
    return [flat_full(o) for o in outs]


class Summed:
    def __init__(self, parts):
        self.arrays = len(parts)
        self.rows, self.width = parts[0].shape[0] // 32, parts[0].shape[1]
        self.cut = min(256, self.width)
        self.pieces = self.width // self.cut
        self.operands = [p.reshape(GRID + (self.rows, self.width)) for p in parts]
        self.in_specs = [ANY] * len(parts)
        self.out_shape = [jax.ShapeDtypeStruct((self.rows, self.width), F32)] * len(parts)
        self.out_specs = [whole((self.rows, self.width))] * len(parts)
        n = self.count = len(parts) * self.pieces
        self.scratch = [pltpu.VMEM((n, 4, 2, 2, self.rows, self.cut), F32), pltpu.SemaphoreType.DMA((n,))]
        self.scratch += Scatter.scratch(n, self.rows, self.cut)

    def bind(self, here, ins, outs, scratch):
        tots, loc = scratch[:2]

        def cut(p):
            lo = p % self.pieces * self.cut
            return p // self.pieces, slice(lo, lo + self.cut)

        def part(p, core):
            a, cols = cut(p)
            return ins[a].at[:, :, :, core, :, cols]

        def out(p):
            a, cols = cut(p)
            return outs[a].at[:, cols]

        return Scatter(
            here,
            self.count,
            lambda p: tots.at[p],
            lambda p: part(p, here.oc),
            lambda p: pltpu.make_async_copy(part(p, here.c), tots.at[p], loc.at[p]),
            out,
            scratch[2:],
        )


def scatter_kernel(plan, *refs):
    n = plan.arrays
    here = Here()
    here.greet()
    sums = plan.bind(here, refs[:n], refs[n : 2 * n], refs[2 * n :])
    for wave in waves_of(sums, sums.count):
        run(wave)
    finish_all(sums)


def scatter_all(parts, collective_id):
    plan = Summed(parts)
    return pl.pallas_call(
        functools.partial(scatter_kernel, plan),
        out_shape=plan.out_shape,
        in_specs=plan.in_specs,
        out_specs=[pl.BlockSpec(memory_space=pltpu.VMEM)] * len(parts),
        scratch_shapes=plan.scratch,
        compiler_params=pltpu.CompilerParams(
            collective_id=collective_id, has_side_effects=True, vmem_limit_bytes=60 * 2**20
        ),
        name="scatter_all",
    )(*plan.operands)


def greet(peers):
    barrier = pltpu.get_barrier_semaphore()
    for peer in peers:
        pl.semaphore_signal(barrier, inc=1, device_id=peer, device_id_type=MESH)
    pl.semaphore_wait(barrier, len(peers))


def group_gather_kernel(count, *refs):
    shards, fulls = refs[:count], refs[count : 2 * count]
    loc, ss, rs = refs[2 * count :]
    here = Here()
    x, c, ox, at_x, at_c = here.x, here.c, here.ox, here.at_x, here.at_c
    greet([at_x, at_c])
    waits = []
    for a in range(count):
        mine = fulls[a].at[:, x * 2 + c]
        copy = pltpu.make_async_copy(shards[a], mine, loc.at[a])
        copy.start()
        over = remote(shards[a], mine, ss.at[a, 0], rs.at[a, 0], at_x)
        over.start()
        side = remote(shards[a], mine, ss.at[a, 1], rs.at[a, 1], at_c)
        side.start()
        waits.append((copy, over, side))
    last = []
    for a in range(count):
        waits[a][1].wait_recv()
        block = fulls[a].at[:, ox * 2 + c]
        on = remote(block, block, ss.at[a, 2], rs.at[a, 2], at_c)
        on.start()
        last.append(on)
    for a in range(count):
        copy, over, side = waits[a]
        copy.wait()
        over.wait_send()
        side.wait()
        last[a].wait()


def group_gather(shards, collective_id):
    count = len(shards)
    dma = pltpu.SemaphoreType.DMA
    return pl.pallas_call(
        functools.partial(group_gather_kernel, count),
        out_shape=[jax.ShapeDtypeStruct((s.shape[0], 4) + s.shape[1:], F32) for s in shards],
        in_specs=[ANY] * count,
        out_specs=[ANY] * count,
        scratch_shapes=[dma((count,)), dma((count, 3)), dma((count, 3))],
        compiler_params=pltpu.CompilerParams(collective_id=collective_id, has_side_effects=True),
        name="group_gather",
    )(*shards)


def group_swap_kernel(count, *refs):
    shards, fulls = refs[:count], refs[count : 2 * count]
    loc, ss, rs = refs[2 * count :]
    here = Here()
    z, y, x, c = here.z, here.y, here.x, here.c
    me = x * 2 + c
    peers = [(x, 1 - c), (1 - x, c), (1 - x, 1 - c)]
    greet([place(z, y, *p) for p in peers])
    waits = []
    for a in range(count):
        copy = pltpu.make_async_copy(shards[a].at[:, me], fulls[a].at[:, me], loc.at[a])
        copy.start()
        waits.append(copy)
        for k in (1, 2, 0):
            px, pc = peers[k]
            on = remote(
                shards[a].at[:, px * 2 + pc], fulls[a].at[:, me], ss.at[a, k], rs.at[a, k], place(z, y, px, pc)
            )
            on.start()
            waits.append(on)
    for copy in waits:
        copy.wait()


def group_swap(shards, collective_id):
    count = len(shards)
    dma = pltpu.SemaphoreType.DMA
    return pl.pallas_call(
        functools.partial(group_swap_kernel, count),
        out_shape=[jax.ShapeDtypeStruct(s.shape, F32) for s in shards],
        in_specs=[ANY] * count,
        out_specs=[ANY] * count,
        scratch_shapes=[dma((count,)), dma((count, 3)), dma((count, 3))],
        compiler_params=pltpu.CompilerParams(collective_id=collective_id, has_side_effects=True),
        name="group_swap",
    )(*shards)


def group_sum_kernel(parts, out, tot, got, last, loc, ss, rs):
    here = Here()
    greet([here.at_x, here.at_c])
    load = pltpu.make_async_copy(parts.at[:, :, here.c], tot, loc.at[0])
    load.start()
    side = remote(parts.at[:, :, here.oc], got, ss.at[0], rs.at[0], here.at_c)
    side.start()
    load.wait()
    side.wait_recv()
    tot[...] += got[...]
    over = remote(tot.at[:, here.ox], last, ss.at[1], rs.at[1], here.at_x)
    over.start()
    over.wait_recv()
    out[...] = tot[:, here.x] + last[...]
    side.wait_send()
    over.wait_send()


def group_sum(parts, collective_id):
    s, lat, w = parts.shape
    r = lat // 4
    dma = pltpu.SemaphoreType.DMA
    return pl.pallas_call(
        group_sum_kernel,
        out_shape=jax.ShapeDtypeStruct((s, r, w), F32),
        in_specs=[ANY],
        out_specs=pl.BlockSpec(memory_space=pltpu.VMEM),
        scratch_shapes=[
            pltpu.VMEM((s, 2, r, w), F32),
            pltpu.VMEM((s, 2, r, w), F32),
            pltpu.VMEM((s, r, w), F32),
            dma((1,)),
            dma((2,)),
            dma((2,)),
        ],
        compiler_params=pltpu.CompilerParams(collective_id=collective_id, has_side_effects=True),
        name="group_sum",
    )(parts.reshape(s, 2, 2, r, w))


def stacked(values, axis, order):
    top = lax.reduce_precision(values, 8, 7)
    terms = (top.astype(jnp.bfloat16), (values - top).astype(jnp.bfloat16))
    return jnp.concatenate([terms[i] for i in order], axis=axis)


def thin_product(left, right):
    return lax.dot_general(
        stacked(left, 0, (0, 0, 1)), stacked(right, 0, (0, 1, 0)), (((0,), (0,)), ((), ())), preferred_element_type=F32
    )


BF16 = jnp.bfloat16
HIGH = lax.Precision.HIGH
BLOCK = 256


def dot(left, right, dims=(1, 0)):
    return lax.dot_general(
        left, right, (((dims[0],), (dims[1],)), ((), ())), precision=HIGH, preferred_element_type=F32
    )


def dot3(left, right, dims=(1, 0)):
    numbers = (((dims[0],), (dims[1],)), ((), ()))
    one = functools.partial(lax.dot_general, dimension_numbers=numbers, preferred_element_type=F32)
    return one(left[0], right[0]) + (one(left[0], right[1]) + one(left[1], right[0]))


def halves(values):
    top = values.astype(BF16)
    return top, (values - top.astype(F32)).astype(BF16)


def split_weights(sources, pairs, stage, sems, pace):
    step = stage.shape[1]
    chunks = [(i, r) for i, s in enumerate(sources) for r in range(0, s.shape[0], step)]

    def copy(n):
        i, r = chunks[n]
        return pltpu.make_async_copy(sources[i].at[r : r + step], stage.at[n % 2], sems.at[n % 2])

    copy(0).start()
    for n, (i, r) in enumerate(chunks):
        if n * pace.lead % len(chunks) == 0:
            pace.at_lead(n * pace.lead // len(chunks))
        if n + 1 < len(chunks):
            copy(n + 1).start()
        copy(n).wait()
        pairs[i][0][r : r + step], pairs[i][1][r : r + step] = halves(stage[n % 2])


def unit_of(values):
    centred = values - jnp.mean(values, axis=-1, keepdims=True)
    inv_std = lax.rsqrt(jnp.mean(centred * centred, axis=-1, keepdims=True) + EPSILON)
    return centred * inv_std, inv_std


def staging(width):
    return [pltpu.VMEM((width, width), BF16)] * 4 + [pltpu.VMEM((2, 128, width), F32), pltpu.SemaphoreType.DMA((2,))]


def whole(shape, buffers=1):
    return pl.BlockSpec(shape, lambda *i: (0,) * len(shape), pipeline_mode=pl.Buffered(buffers))


def opening_kernel(cuts, *refs):
    times, feats, latents = refs[:3]
    shards, group_shard = refs[3:9], refs[9:10]
    vec, keys, values, own_keys, own_values, queries, xt_top, xt_low = refs[10:18]
    fulls, group_full = refs[18:24], refs[24:25]
    pk, top, low, own_top, own_low, lat, lat_top, lat_low, stage, load = refs[25:35]
    step = pl.program_id(0)
    here = Here()
    vectors = Gather(here, shards[:1], fulls[:1], [(0, 0, 128)], refs[35:46])
    moved = Gather(here, shards[1:], fulls[1:], cuts, refs[46:57])
    group = GroupGather(here, group_shard, group_full, refs[57:])
    waves = waves_of(moved, 2)
    cut = keys.shape[1]
    slots, chunks = top.shape[0] // BLOCK, shards[1].shape[1] // cut

    def start():
        here.greet()
        vectors.own(0)
        run(waves[0])
        group.start()
        vectors.along_z(0)
        vectors.across(0)
        vectors.corner(0)
        vectors.arrived(0)
        copy = pltpu.make_async_copy(fulls[0], pk, load.at[0])
        copy.start()
        copy.wait()
        strip = shards[1].shape[0]
        vec[...] = jnp.concatenate([pk[i // 8, i // 4 % 2, i // 2 % 2, i % 2][:, :strip] for i in range(32)], axis=1)
        own_top[...], own_low[...] = halves(unit_of(latents[...])[0] * vec[2:3] + vec[3:4])
        run(waves[1])
        group.forward()

    pl.when(step == 0)(start)
    at_step = {2: 2, 4: 3, 5: 4, slots + 1: 5, slots + 2: 6, slots + 4: 7, slots + 5: 8}
    at_step.update({slots + chunks + i: 8 + i for i in range(1, 5)})
    for s, w in at_step.items():
        pl.when(step == s)(functools.partial(run, waves[w]))

    @pl.when(step < slots)
    def _():
        embed = vec[pl.ds(6 + times[step], 1)]
        normed = unit_of(feats[...] + embed)[0] * vec[0:1] + vec[1:2]
        rows = pl.ds(pl.multiple_of(step * BLOCK, BLOCK), BLOCK)
        top[rows], low[rows] = halves(normed)
        xt_top[...], xt_low[...] = halves(jnp.swapaxes(normed, 0, 1))

    def chunk(array, n, left, right, out, own_out):
        cols = pl.ds(pl.multiple_of(n * cut, cut), cut)
        copy = pltpu.make_async_copy(fulls[array].at[:, :, :, :, :, cols], stage.at[array % 2], load.at[0])
        copy.start()
        copy.wait()
        pair = halves(stage[array % 2].reshape((-1, cut)))
        step_rows = min(512, left.shape[0])

        @pl.loop(0, left.shape[0] // step_rows)
        def _(m):
            rows = pl.ds(pl.multiple_of(m * step_rows, step_rows), step_rows)
            out[rows] = dot3((left[rows], right[rows]), pair)

        if own_out is not None:
            own_out[...] = dot3((own_top[...], own_low[...]), pair)

    half = chunks // 2
    for first in (0, 1):

        @pl.when(step == slots + first * half)
        def _():
            moved.arrived(2 * first)
            moved.arrived(2 * first + 1)

    @pl.when((step >= slots) & (step < slots + chunks))
    def _():
        chunk(1, step - slots, top, low, keys, own_keys)
        chunk(2, step - slots, top, low, values, own_values)

    @pl.when(step == slots + chunks)
    def _():
        moved.arrived(4)
        moved.arrived(5)
        group.done()
        copy = pltpu.make_async_copy(group_full[0], lat, load.at[0])
        copy.start()
        copy.wait()
        lat_top[...], lat_low[...] = halves(unit_of(lat[...].reshape(lat_top.shape))[0] * vec[2:3] + vec[3:4])

    @pl.when(step >= slots + chunks)
    def _():
        chunk(3, step - slots - chunks, lat_top, lat_low, queries, None)

    @pl.when(step == slots + 2 * chunks - 1)
    def _():
        vectors.done(0, True)
        for p in range(moved.count):
            moved.done(p, p < 6)


def opening(times, feats, latents, packed, key_w, value_w, query_w, cot, out_w, collective_id):
    rows, width = feats.shape
    seqs, own_each, _ = latents.shape
    own_rows, lat_rows = seqs * own_each, seqs * own_each * 4
    slots, cut = rows // BLOCK, 256
    chunks = width // cut
    shards = [packed, key_w, value_w, query_w, cot, out_w]
    cuts = [(a, lo, lo + WIDE) for lo in range(0, width, WIDE) for a in (0, 1)]
    cuts += [(a, lo, lo + WIDE) for a in (2, 3, 4) for lo in range(0, width, WIDE)]
    clip = lambda i, lo: jnp.clip(i - lo, 0, chunks - 1)
    chunk_of = lambda n, lo: pl.BlockSpec((n, cut), lambda i: (0, clip(i, lo)))
    turned = pl.BlockSpec((width, BLOCK), lambda i: (0, jnp.minimum(i, slots - 1)))
    full = lambda n, kind=F32: jax.ShapeDtypeStruct((n, width), kind)
    outs = pl.pallas_call(
        functools.partial(opening_kernel, cuts),
        grid=(slots + 2 * chunks,),
        in_specs=[
            SMEM,
            pl.BlockSpec((BLOCK, width), lambda i: (jnp.minimum(i, slots - 1), 0)),
            whole((own_rows, width)),
        ]
        + [ANY] * 7,
        out_specs=[
            whole((16, width)),
            chunk_of(rows, slots),
            chunk_of(rows, slots),
            chunk_of(own_rows, slots),
            chunk_of(own_rows, slots),
            chunk_of(lat_rows, slots + chunks),
            turned,
            turned,
        ]
        + [ANY] * 7,
        out_shape=[full(16), full(rows), full(rows), full(own_rows), full(own_rows), full(lat_rows)]
        + [jax.ShapeDtypeStruct((width, rows), BF16)] * 2
        + full_shapes(shards)
        + [jax.ShapeDtypeStruct((seqs, 4, own_each, width), F32)],
        scratch_shapes=[
            pltpu.VMEM(GRID + packed.shape, F32),
            pltpu.VMEM((rows, width), BF16),
            pltpu.VMEM((rows, width), BF16),
            pltpu.VMEM((own_rows, width), BF16),
            pltpu.VMEM((own_rows, width), BF16),
            pltpu.VMEM((seqs, 4, own_each, width), F32),
            pltpu.VMEM((lat_rows, width), BF16),
            pltpu.VMEM((lat_rows, width), BF16),
            pltpu.VMEM((2,) + GRID + (width // 32, cut), F32),
            pltpu.SemaphoreType.DMA((1,)),
        ]
        + Gather.semaphores(1)
        + Gather.semaphores(len(cuts))
        + GroupGather.semaphores(1),
        compiler_params=pltpu.CompilerParams(
            collective_id=collective_id, has_side_effects=True, vmem_limit_bytes=60 * 2**20
        ),
        name="opening",
    )(times, feats, latents.reshape(own_rows, width), *shards, latents)
    return outs[:8], [flat_full(o) for o in outs[9:14]], outs[14]


def pair_rows(values, first, head):
    lane = lax.broadcasted_iota(jnp.int32, values.shape, 1)
    return jnp.concatenate(
        [
            jnp.where((lane >= first) & (lane < first + head), values, 0.0),
            jnp.where((lane >= first + head) & (lane < first + 2 * head), values, 0.0),
        ],
        axis=0,
    )


def pair_merge(stacked, first, head):
    half = stacked.shape[0] // 2
    lane = lax.broadcasted_iota(jnp.int32, (half, stacked.shape[1]), 1)
    one = jnp.where((lane >= first) & (lane < first + head), stacked[:half], 0.0)
    return one + jnp.where((lane >= first + head) & (lane < first + 2 * head), stacked[half:], 0.0)


def join(left, right):
    return jnp.concatenate([left[:, :128], left[:, 128:] + right[:, :128], right[:, 128:]], axis=1)


def windows(head):
    return ((slice(0, 256), 0), (slice(128, 384), 2 * head - 128))


def score_block(present, seq, keys, own_keys, q_pair, window, inv_root):
    at = keys.shape[0]
    scores = jnp.concatenate([dot(keys[:, window], q_pair, (1, 1)), dot(own_keys[:, window], q_pair, (1, 1))], axis=0)
    row = lax.broadcasted_iota(jnp.int32, scores.shape, 0)
    keep = (row >= at) | ((row < at // 2) & (present[seq, 0] > 0)) | ((row >= at // 2) & (present[seq, 1] > 0))
    return jnp.where(keep, scores * inv_root, MASKED)


def attend_kernel(inv_root, head, present, queries, keys, values, own_keys, own_values, out, tops, sums):
    seq, group = pl.program_id(0), pl.program_id(1)
    merged = []
    for p, (window, first) in enumerate(windows(head)):
        q_pair = pair_rows(queries[:, window], first, head)
        scores = score_block(present, seq, keys, own_keys, q_pair, window, inv_root)
        top = jnp.max(scores, axis=0, keepdims=True)
        expo = jnp.exp(scores - top)
        tops[pl.ds(group * 2 + p, 1)] = top
        sums[pl.ds(group * 2 + p, 1)] = jnp.sum(expo, axis=0, keepdims=True)
        at = keys.shape[0]
        stacked = dot(expo[:at], values[:, window], (0, 0)) + dot(expo[at:], own_values[:, window], (0, 0))
        merged.append(pair_merge(stacked, first, head))
    out[...] = join(*merged)


def attend_specs(lat, media, rows):
    group = 384
    query = pl.BlockSpec((None, lat, group), lambda b, g: (b, 0, g))
    key = pl.BlockSpec((media, group), lambda b, g: (b, g))
    own = pl.BlockSpec((rows, group), lambda b, g: (b, g))
    stat = pl.BlockSpec((None, 8, 128), lambda b, g: (b, 0, 0))
    return query, key, own, stat


SMEM = pl.BlockSpec(memory_space=pltpu.SMEM)


def attend(present, queries, keys, values, own_keys, own_values):
    seqs, lat, width = queries.shape
    head = width // HEADS
    query, key, own, stat = attend_specs(lat, keys.shape[0] // seqs, own_keys.shape[0] // seqs)
    stat_shape = jax.ShapeDtypeStruct((seqs, 8, 128), F32)
    return pl.pallas_call(
        functools.partial(attend_kernel, 1.0 / math.sqrt(head), head),
        grid=(seqs, width // 384),
        in_specs=[SMEM, query, key, key, own, own],
        out_specs=[query, stat, stat],
        out_shape=[jax.ShapeDtypeStruct(queries.shape, F32), stat_shape, stat_shape],
        compiler_params=pltpu.CompilerParams(vmem_limit_bytes=60 * 2**20),
        name="attend",
    )(present, queries, keys, values, own_keys, own_values)


def attend_back_kernel(inv_root, head, plan, steps, *refs):
    present, queries, grads, logs, deltas, keys, values, own_keys, own_values = refs[:9]
    n = plan.arrays
    query_out, key_out, value_out, own_key_out, own_value_out = refs[9 + n : 14 + n]
    seq, group = pl.program_id(0), pl.program_id(1)
    step = seq * pl.num_programs(1) + group
    here = Here()
    moved = plan.bind(here, refs[9 : 9 + n], refs[14 + n : 14 + 2 * n], refs[14 + 2 * n :])
    waves = waves_of(moved, moved.count)
    waves[0].insert(0, here.greet)
    pace = Pace(step, steps, 0, 2, waves)
    merged, key_grads, value_grads = [], [], []
    at = keys.shape[0]
    for p, (window, first) in enumerate(windows(head)):
        pace.at(p)
        q_pair = pair_rows(queries[:, window], first, head)
        g_pair = pair_rows(grads[:, window], first, head)
        scores = score_block(present, seq, keys, own_keys, q_pair, window, inv_root)
        probs = jnp.exp(scores - logs[pl.ds(group * 2 + p, 1)])
        grad_probs = jnp.concatenate(
            [dot(values[:, window], g_pair, (1, 1)), dot(own_values[:, window], g_pair, (1, 1))], axis=0
        )
        grad_scores = probs * (grad_probs - deltas[pl.ds(group * 2 + p, 1)]) * inv_root
        stacked = dot(grad_scores[:at], keys[:, window], (0, 0)) + dot(grad_scores[at:], own_keys[:, window], (0, 0))
        merged.append(pair_merge(stacked, first, head))
        key_grads.append(dot(grad_scores, q_pair))
        value_grads.append(dot(probs, g_pair))
    query_out[...] = join(*merged)
    key_grad, value_grad = join(*key_grads), join(*value_grads)
    key_out[...], own_key_out[...] = key_grad[:at], key_grad[at:]
    value_out[...], own_value_out[...] = value_grad[:at], value_grad[at:]
    run_last(step, steps, moved)


def attend_back(present, queries, grads, logs, deltas, keys, values, own_keys, own_values, plan, collective_id):
    seqs, lat, width = queries.shape
    head = width // HEADS
    query, key, own, stat = attend_specs(lat, keys.shape[0] // seqs, own_keys.shape[0] // seqs)
    shape = lambda v: jax.ShapeDtypeStruct(v.shape, F32)
    grid = (seqs, width // 384)
    outs = pl.pallas_call(
        functools.partial(attend_back_kernel, 1.0 / math.sqrt(head), head, plan, grid[0] * grid[1]),
        grid=grid,
        in_specs=[SMEM, query, query, stat, stat, key, key, own, own] + plan.in_specs,
        out_specs=[query, key, key, own, own] + plan.out_specs,
        out_shape=[shape(queries), shape(keys), shape(values), shape(own_keys), shape(own_values)] + plan.out_shape,
        scratch_shapes=plan.scratch,
        compiler_params=pltpu.CompilerParams(
            collective_id=collective_id, has_side_effects=True, vmem_limit_bytes=60 * 2**20
        ),
        name="attend_back",
    )(present, queries, grads, logs, deltas, keys, values, own_keys, own_values, *plan.operands)
    return outs[:5], outs[5:]


def weight_kernel(steps, xt_top, xt_low, own_t, grad_keys, grad_values, own_gk, own_gv, vec, outs, vec_out, mats, *rest):
    n = pl.program_id(0)
    here = Here()
    cut = grad_keys.shape[1]
    sums = Scatter(
        here,
        2 * steps,
        lambda p: mats.at[p, :, :, :, here.c],
        lambda p: mats.at[p, :, :, :, here.oc],
        None,
        lambda p: outs.at[p % 2, :, pl.ds(pl.multiple_of(p // 2 * cut, cut), cut)],
        rest[:14],
    )
    tot, loc = rest[14:16]
    small = Scatter(
        here,
        1,
        lambda p: tot,
        lambda p: vec.at[:, :, :, here.oc],
        lambda p: pltpu.make_async_copy(vec.at[:, :, :, here.c], tot, loc.at[p]),
        lambda p: vec_out,
        rest[16:],
    )
    stages = sums.stages()

    @pl.when(n == 0)
    def _():
        here.greet()

    for w, (grad, own_grad) in enumerate(((grad_keys, own_gk), (grad_values, own_gv))):
        pair = halves(grad[...])
        top, low = halves(own_grad[...])
        stacked = jnp.concatenate([top, low, top], axis=0)

        @pl.loop(0, 2)
        def _(i):
            rows = pl.ds(pl.multiple_of(i * 768, 768), 768)
            made = dot3((xt_top[rows], xt_low[rows]), pair)
            made += jnp.dot(own_t[rows], stacked, preferred_element_type=F32)
            mats[2 * n + w, pl.ds(i * 2, 2)] = made.reshape((2, 2, 2, 2, 48, cut))

        sums.start(2 * n + w)
        for s in (4, 3, 2, 1):
            p = 2 * n + w - LAG * s

            @pl.when(p >= 0)
            def _():
                stages[s](p)

        if w == 1:
            for s in range(5):

                @pl.when(n == s)
                def _():
                    small.stages()[s](0)

    @pl.when(n == steps - 1)
    def _():
        for t in range(2 * steps, 2 * steps + 4 * LAG):
            for s in (4, 3, 2, 1):
                if 0 <= t - LAG * s < 2 * steps:
                    stages[s](t - LAG * s)

        @pl.loop(0, 2 * steps)
        def _(p):
            sums.done(p)

        small.done(0)


def weight_grads(xt_top, xt_low, own_t, grad_keys, grad_values, own_gk, own_gv, vec, collective_id):
    width, rows = xt_top.shape
    own_rows = own_gk.shape[0]
    steps = width // BLOCK
    cols = lambda n: pl.BlockSpec((n, BLOCK), lambda i: (0, i))
    r = width // 32
    vr, vw = vec.shape[0] // 32, vec.shape[1]
    outs, vec_sum = pl.pallas_call(
        functools.partial(weight_kernel, steps),
        grid=(steps,),
        in_specs=[
            whole((width, rows)),
            whole((width, rows)),
            whole(own_t.shape),
            cols(rows),
            cols(rows),
            cols(own_rows),
            cols(own_rows),
            ANY,
        ],
        out_specs=[whole((2, r, width)), whole((vr, vw))],
        out_shape=[jax.ShapeDtypeStruct((2, r, width), F32), jax.ShapeDtypeStruct((vr, vw), F32)],
        scratch_shapes=[pltpu.VMEM((2 * steps,) + GRID + (r, BLOCK), F32)]
        + Scatter.scratch(2 * steps, r, BLOCK)
        + [pltpu.VMEM((4, 2, 2, vr, vw), F32), pltpu.SemaphoreType.DMA((1,))]
        + Scatter.scratch(1, vr, vw),
        compiler_params=pltpu.CompilerParams(
            collective_id=collective_id, has_side_effects=True, vmem_limit_bytes=62 * 2**20
        ),
        name="weight_grads",
    )(xt_top, xt_low, own_t, grad_keys, grad_values, own_gk, own_gv, vec.reshape(GRID + (vr, vw)))
    return outs[0], outs[1], vec_sum


def media_back_kernel(plan, steps, *refs):
    feats, embed, gain, grad_keys, grad_values, own_gk, own_gv, key_w, value_w = refs[:9]
    n = plan.arrays
    out, own_out, sums = refs[9 + n : 12 + n]
    kt, kl, vt, vl, stage, sems = refs[12 + 2 * n : 18 + 2 * n]
    step = pl.program_id(0)
    here = Here()
    moved = plan.bind(here, refs[9 : 9 + n], refs[12 + n : 12 + 2 * n], refs[18 + 2 * n :])
    waves = waves_of(moved, moved.count)
    waves[0].insert(0, here.greet)
    pace = Pace(step, steps, 4, 3, waves)

    @pl.when(step == 0)
    def _():
        split_weights((key_w, value_w), ((kt, kl), (vt, vl)), stage, sems, pace)
        own_out[...] = dot3(halves(own_gk[...]), (kt[...], kl[...]), (1, 1)) + dot3(
            halves(own_gv[...]), (vt[...], vl[...]), (1, 1)
        )
        sums[...] = jnp.zeros_like(sums)

    key_pair, value_pair = halves(grad_keys[...]), halves(grad_values[...])
    for i in range(3):
        pace.at(i)
        rows = slice(i * 512, i * 512 + 512)
        out[:, rows] = dot3(key_pair, (kt[rows], kl[rows]), (1, 1)) + dot3(value_pair, (vt[rows], vl[rows]), (1, 1))
    strip = 64

    @pl.loop(0, out.shape[0] // strip)
    def _(i):
        rows = pl.ds(pl.multiple_of(i * strip, strip), strip)
        incoming = out[rows]
        unit, inv_std = unit_of(feats[rows] + embed[...])
        sums[pl.ds(0, 1)] += jnp.sum(incoming * unit, axis=0, keepdims=True)
        sums[pl.ds(1, 1)] += jnp.sum(incoming, axis=0, keepdims=True)
        scaled = incoming * gain[...]
        result = inv_std * (
            scaled
            - jnp.mean(scaled, axis=-1, keepdims=True)
            - unit * jnp.mean(scaled * unit, axis=-1, keepdims=True)
        )
        out[rows] = result
        sums[pl.ds(2 + step, 1)] += jnp.sum(result, axis=0, keepdims=True)

    run_last(step, steps, moved)


def media_backward(feats, embed, gain, grad_keys, grad_values, own_gk, own_gv, key_w, value_w, plan, collective_id):
    rows, width = feats.shape
    own_rows = own_gk.shape[0]
    row_block = pl.BlockSpec((BLOCK, width), lambda i: (i, 0))
    one_block = pl.BlockSpec((BLOCK, width), lambda i: (i, 0), pipeline_mode=pl.Buffered(1))
    steps = rows // BLOCK
    outs = pl.pallas_call(
        functools.partial(media_back_kernel, plan, steps),
        grid=(steps,),
        in_specs=[
            one_block,
            pl.BlockSpec((None, 1, width), lambda i: (i, 0, 0)),
            whole((1, width)),
            row_block,
            row_block,
            whole((own_rows, width)),
            whole((own_rows, width)),
            ANY,
            ANY,
        ]
        + plan.in_specs,
        out_specs=[one_block, whole((own_rows, width)), whole((8, width))] + plan.out_specs,
        out_shape=[
            jax.ShapeDtypeStruct((rows, width), F32),
            jax.ShapeDtypeStruct((own_rows, width), F32),
            jax.ShapeDtypeStruct((8, width), F32),
        ]
        + plan.out_shape,
        scratch_shapes=staging(width) + plan.scratch,
        compiler_params=pltpu.CompilerParams(
            collective_id=collective_id, has_side_effects=True, vmem_limit_bytes=64 * 2**20 - 2**16
        ),
        name="media_backward",
    )(feats, embed, gain, grad_keys, grad_values, own_gk, own_gv, key_w, value_w, *plan.operands)
    return outs[:3], outs[3:]


GELU_A = math.sqrt(2.0 / math.pi)
GELU_B = 0.044715


def feed_kernel(blocks, *refs):
    feed, cot, up, down, new_part, grad_up_t, grad_down, out, act, back, mats = refs[:11]
    step = pl.program_id(0)
    here = Here()
    pieces, cut = mats.shape[0], mats.shape[-1]
    sums = Scatter(
        here,
        pieces,
        lambda p: mats.at[p, :, :, :, here.c],
        lambda p: mats.at[p, :, :, :, here.oc],
        None,
        lambda p: out.at[:, p * cut : (p + 1) * cut],
        refs[11:],
    )
    waves = waves_of(sums, pieces)
    block = step - blocks * (step >= blocks).astype(jnp.int32)
    rows = pl.ds(pl.multiple_of(block * BLOCK, BLOCK), BLOCK)
    pl.when(step == 0)(here.greet)

    @pl.when(step < blocks)
    def _():
        hidden = dot(feed[...], up[...])
        grad_act = dot(cot[...], down[...], (1, 1))
        square = hidden * hidden
        bent = jnp.tanh(GELU_A * (hidden + GELU_B * hidden * square))
        slope = 0.5 * (1.0 + bent) + 0.5 * hidden * (1.0 - bent * bent) * (GELU_A * (1.0 + 3.0 * GELU_B * square))
        act[rows] = 0.5 * hidden * (1.0 + bent)
        back[rows] = grad_act * slope

    @pl.when(step == blocks)
    def _():
        for p in range(pieces):

            @pl.loop(0, 4)
            def _(zi):
                plane = pl.ds(pl.multiple_of(zi * 384, 384), 384)
                made = dot(back[plane], up[p * cut : (p + 1) * cut], (1, 1))
                mats[p, zi] = made.reshape((2, 2, 2, 48, cut))

            sums.start(p)
        grad_up_t[...] = jnp.zeros_like(grad_up_t)
        grad_down[...] = jnp.zeros_like(grad_down)

    for i in range(blocks):

        @pl.when(step == blocks + i)
        def _():
            for wave in waves[1 + 2 * i : 3 + 2 * i]:
                run(wave)

    @pl.when(step >= blocks)
    def _():
        new_part[...] = dot(act[rows], down[...])
        grad_up_t[...] += dot(back[rows], feed[...], (0, 0))
        grad_down[...] += dot(act[rows], cot[...], (0, 0))

    @pl.when(step == 2 * blocks - 1)
    def _():
        for wave in waves[1 + 2 * blocks :]:
            run(wave)
        finish_all(sums)


def feed_forward(feed, cot, up, down, collective_id):
    rows, width = feed.shape
    units, r, cut = up.shape[1], width // 32, 256
    blocks = rows // BLOCK
    big = jax.ShapeDtypeStruct((rows, width), F32)
    slim = jax.ShapeDtypeStruct((units, width), F32)
    row_block = pl.BlockSpec((BLOCK, width), lambda i: (i % blocks, 0))
    late_block = pl.BlockSpec((BLOCK, width), lambda i: (jnp.maximum(i - blocks, 0), 0))
    return pl.pallas_call(
        functools.partial(feed_kernel, blocks),
        grid=(2 * blocks,),
        in_specs=[row_block, row_block, whole((width, units)), whole((units, width))],
        out_specs=[late_block, whole((units, width)), whole((units, width)), whole((r, width))],
        out_shape=[big, slim, slim, jax.ShapeDtypeStruct((r, width), F32)],
        scratch_shapes=[pltpu.VMEM((rows, units), F32)] * 2
        + [pltpu.VMEM((width // cut,) + GRID + (r, cut), F32)]
        + Scatter.scratch(width // cut, r, cut),
        compiler_params=pltpu.CompilerParams(
            collective_id=collective_id, has_side_effects=True, vmem_limit_bytes=60 * 2**20
        ),
        name="feed_forward",
    )(feed, cot, up, down)


def mm(left, right):
    return jnp.dot(left, right, precision=HIGH, preferred_element_type=F32)


def mm_tn(left, right):
    return lax.dot_general(left, right, (((0,), (0,)), ((), ())), precision=HIGH, preferred_element_type=F32)


def mm_nt(left, right):
    return lax.dot_general(left, right, (((1,), (1,)), ((), ())), precision=HIGH, preferred_element_type=F32)


def body_fast(
    latents,
    patch_feats,
    image_counts,
    time_index,
    query_proj,
    key_proj,
    value_proj,
    out_proj,
    up_proj,
    down_proj,
    media_gain,
    media_bias,
    latent_gain,
    latent_bias,
    feed_gain,
    feed_bias,
    time_table,
    out_cotangent,
):
    frame = lax.axis_index("frame")
    frames = lax.axis_size("frame")
    seqs, rows, width = latents.shape
    rounds, patches = patch_feats.shape[1], patch_feats.shape[3]
    lat = rows * frames
    head = width // HEADS
    strip = media_gain.shape[0]

    vectors = jnp.concatenate(
        [jnp.stack([media_gain, media_bias, latent_gain, latent_bias, feed_gain, feed_bias]), time_table], axis=0
    )
    packed = jnp.pad(vectors, ((0, 2), (0, 128 - strip)))
    slot_ids = jnp.arange(rounds, dtype=jnp.int32) * frames + frame
    present = slot_ids[None, :] < image_counts[:, None]
    picks = jnp.arange(time_index.shape[1], dtype=jnp.int32)[None, :] == slot_ids[:, None]
    slot_times = jnp.sum(jnp.where(picks[None, :, :], time_index[:, None, :], 0), axis=-1)
    feats = patch_feats.reshape(-1, width)

    (vec_all, keys, values, own_keys, own_values, queries, xt_top, xt_low), gathered, lat_blocks = opening(
        slot_times.reshape(-1), feats, latents, packed, key_proj, value_proj, query_proj, flatten(out_cotangent), out_proj, 0
    )
    key_w, value_w, query_w, cot_all, out_w = gathered
    up_held, keys = lax.optimization_barrier((up_proj, keys))
    up_cols = lax.all_to_all(
        up_held.reshape(strip, 32, -1), ("seq", "frame"), split_axis=1, concat_axis=0, tiled=True
    ).reshape(width, -1)
    mgain, mbias, lgain, lbias, fgain, fbias = (vec_all[i] for i in range(6))
    table = vec_all[6:14]
    queries = queries.reshape(seqs, lat, width)
    latent_norm, latent_unit, latent_std = norm_forward(lat_blocks.reshape(seqs, lat, width), lgain, lbias)
    own_rows = lambda v: lax.dynamic_slice_in_dim(v, frame * rows, rows, 1)
    own_norm, own_unit, own_std = own_rows(latent_norm), own_rows(latent_unit), own_rows(latent_std)
    one_hot = slot_times[:, :, None] == jnp.arange(time_table.shape[0], dtype=jnp.int32)
    slot_embed = jnp.sum(jnp.where(one_hot[..., None], table, 0.0), axis=2)
    embed = slot_embed.reshape(-1, 1, width)
    own_flat = flatten(own_norm)
    present = present.astype(jnp.int32)

    partial, row_top, row_sum = attend(present, queries, keys, values, own_keys, own_values)
    stats = jnp.concatenate([row_top.reshape(seqs, HEADS, lat), row_sum.reshape(seqs, HEADS, lat)], axis=1)
    stats = jnp.pad(stats.transpose(0, 2, 1), ((0, 0), (0, 0), (0, 128 - 2 * HEADS)))
    part_all, stat_all = group_swap(
        [partial.reshape(seqs, frames, rows, width), stats.reshape(seqs, frames, rows, 128)], 2
    )
    tops, sums = stat_all[..., :HEADS], stat_all[..., HEADS : 2 * HEADS]
    top = jnp.max(tops, axis=1)
    ratio = jnp.exp(tops - top[:, None])
    row_total = jnp.sum(sums * ratio, axis=1)
    weight = ratio / row_total[:, None]
    attended = jnp.sum(part_all.reshape(seqs, frames, rows, HEADS, head) * weight[..., None], axis=1)
    log_total = top + jnp.log(row_total)
    attended_flat = attended.reshape(seqs, rows, width)
    middle = latents + mm(flatten(attended_flat), out_w).reshape(seqs, rows, width)

    feed_norm, feed_unit, feed_std = norm_forward(middle, fgain, fbias)
    (feed_all,) = gather_all([flatten(feed_norm)], 3)
    new_part, grad_up_t, grad_down, grad_feed_norm = feed_forward(feed_all, cot_all, up_cols, down_proj, 4)
    grad_up = lax.all_to_all(
        grad_up_t.reshape(-1, 32, strip).transpose(1, 2, 0), ("seq", "frame"), split_axis=0, concat_axis=2, tiled=True
    ).reshape(strip, -1)
    grad_mid_norm, grad_fgain, grad_fbias = norm_backward(
        grad_feed_norm.reshape(seqs, rows, width), feed_unit, feed_std, fgain
    )
    grad_middle = out_cotangent + grad_mid_norm
    grad_out_w = thin_product(flatten(attended_flat), flatten(grad_middle))
    grad_own = mm_nt(flatten(grad_middle), out_w).reshape(seqs, rows, HEADS, head)
    delta = jnp.sum(grad_own * attended, axis=-1)
    back_stats = jnp.pad(jnp.concatenate([log_total, delta], axis=-1), ((0, 0), (0, 0), (0, 128 - 2 * HEADS)))
    grad_blocks, back_blocks = group_gather([grad_own.reshape(seqs, rows, width), back_stats], 5)
    back_all = back_blocks.reshape(seqs, lat, 128).transpose(0, 2, 1)
    logs_all, delta_all = (back_all[:, i * HEADS : (i + 1) * HEADS].reshape(seqs, 8, 128) for i in range(2))

    (query_part, grad_keys, grad_values, own_gk, own_gv), (new_rows,) = attend_back(
        present,
        queries,
        grad_blocks.reshape(seqs, lat, width),
        logs_all,
        delta_all,
        keys,
        values,
        own_keys,
        own_values,
        Summed([new_part]),
        10,
    )
    new_latents = middle + new_rows.reshape(seqs, rows, width)
    grad_queries = flatten(group_sum(query_part, 6))

    grad_query_w = thin_product(own_flat, grad_queries)
    (patch_grads, own_back, media_sums), (sum_query, sum_out) = media_backward(
        feats,
        embed,
        mgain[None],
        grad_keys,
        grad_values,
        own_gk,
        own_gv,
        key_w,
        value_w,
        Summed([grad_query_w, grad_out_w]),
        7,
    )
    grad_own_norm = (mm_nt(grad_queries, query_w) + own_back).reshape(seqs, rows, width)
    grad_lat_in, grad_lgain, grad_lbias = norm_backward(grad_own_norm, own_unit, own_std, lgain)
    latent_grads = grad_middle + grad_lat_in
    grad_mgain, grad_mbias = media_sums[0], media_sums[1]
    slot_sums = media_sums[2:].reshape(seqs, rounds, width)
    grad_table = jnp.sum(jnp.where(one_hot[..., None], slot_sums[:, :, None, :], 0.0), axis=(0, 1))
    vec_grads = jnp.concatenate(
        [jnp.stack([grad_mgain, grad_mbias, grad_lgain, grad_lbias, grad_fgain, grad_fbias]), grad_table], axis=0
    )
    vec_blocks = jnp.pad(vec_grads.reshape(14, 32, strip).transpose(1, 0, 2), ((0, 0), (0, 2), (0, 128 - strip)))
    own_t = stacked(own_flat, 0, (0, 0, 1)).T
    sum_key, sum_value, sum_vec = weight_grads(
        xt_top, xt_low, own_t, grad_keys, grad_values, own_gk, own_gv, vec_blocks.reshape(-1, 128), 8
    )
    vec = sum_vec[:14, :strip]
    return (
        new_latents,
        latent_grads,
        patch_grads.reshape(patch_feats.shape),
        sum_query,
        sum_key,
        sum_value,
        sum_out,
        grad_up,
        grad_down,
        vec[0],
        vec[1],
        vec[2],
        vec[3],
        vec[4],
        vec[5],
        vec[6:],
    )


def solution(mesh):
    fast = dict(mesh.shape) == {"seq": 8, "frame": 4}
    return jax.shard_map(
        body_fast if fast else body_general,
        mesh=mesh,
        in_specs=(
            P("seq", "frame", None),
            P("seq", None, "frame", None, None),
            P("seq"),
            P("seq", None),
            P(("seq", "frame"), None),
            P(("seq", "frame"), None),
            P(("seq", "frame"), None),
            P(("seq", "frame"), None),
            P(("seq", "frame"), None),
            P(("seq", "frame"), None),
            P(("seq", "frame")),
            P(("seq", "frame")),
            P(("seq", "frame")),
            P(("seq", "frame")),
            P(("seq", "frame")),
            P(("seq", "frame")),
            P(None, ("seq", "frame")),
            P("seq", "frame", None),
        ),
        out_specs=(
            P("seq", "frame", None),
            P("seq", "frame", None),
            P("seq", None, "frame", None, None),
            P(("seq", "frame"), None),
            P(("seq", "frame"), None),
            P(("seq", "frame"), None),
            P(("seq", "frame"), None),
            P(("seq", "frame"), None),
            P(("seq", "frame"), None),
            P(("seq", "frame")),
            P(("seq", "frame")),
            P(("seq", "frame")),
            P(("seq", "frame")),
            P(("seq", "frame")),
            P(("seq", "frame")),
            P(None, ("seq", "frame")),
        ),
        check_vma=False,
    )
```

```python
import functools
import math

import jax
import jax.numpy as jnp
from jax import lax
from jax.experimental import pallas as pl
from jax.experimental.pallas import tpu as pltpu
from jax.sharding import PartitionSpec as P

HEADS = 16


HIGHEST = lax.Precision.HIGHEST
EPSILON = 1e-05
MASKED = -1e30


def product(left, right):
    return jnp.dot(left, right, precision=HIGHEST, preferred_element_type=jnp.float32)


def product_tn(left, right):
    return lax.dot_general(
        left, right, (((0,), (0,)), ((), ())), precision=HIGHEST, preferred_element_type=jnp.float32
    )


def product_nt(left, right):
    return lax.dot_general(
        left, right, (((1,), (1,)), ((), ())), precision=HIGHEST, preferred_element_type=jnp.float32
    )


def flatten(values):
    return values.reshape(-1, values.shape[-1])


def norm_forward(values, gain_vec, bias_vec):
    centred = values - jnp.mean(values, axis=-1, keepdims=True)
    inv_std = lax.rsqrt(jnp.mean(centred * centred, axis=-1, keepdims=True) + EPSILON)
    unit_vals = centred * inv_std
    return (unit_vals * gain_vec + bias_vec, unit_vals, inv_std)


def norm_backward(incoming, unit_vals, inv_std, gain_vec):
    scaled = incoming * gain_vec
    result = inv_std * (
        scaled
        - jnp.mean(scaled, axis=-1, keepdims=True)
        - unit_vals * jnp.mean(scaled * unit_vals, axis=-1, keepdims=True)
    )
    flat_in = flatten(incoming)
    return (result, jnp.sum(flat_in * flatten(unit_vals), axis=0), jnp.sum(flat_in, axis=0))


def heads_last(stats):
    return jnp.transpose(stats, (0, 2, 1))[..., None]


def per_slot(action, operands):
    return lax.map(action, operands)


def body_general(
    latents,
    patch_feats,
    image_counts,
    time_index,
    query_proj,
    key_proj,
    value_proj,
    out_proj,
    up_proj,
    down_proj,
    media_gain,
    media_bias,
    latent_gain,
    latent_bias,
    feed_gain,
    feed_bias,
    time_table,
    out_cotangent,
):
    gathered = (
        lax.all_gather(query_proj, ("seq", "frame"), axis=0, tiled=True),
        lax.all_gather(key_proj, ("seq", "frame"), axis=0, tiled=True),
        lax.all_gather(value_proj, ("seq", "frame"), axis=0, tiled=True),
        lax.all_gather(out_proj, ("seq", "frame"), axis=0, tiled=True),
        lax.all_gather(up_proj, ("seq", "frame"), axis=0, tiled=True),
        lax.all_gather(down_proj, ("seq", "frame"), axis=0, tiled=True),
        lax.all_gather(media_gain, ("seq", "frame"), axis=0, tiled=True),
        lax.all_gather(media_bias, ("seq", "frame"), axis=0, tiled=True),
        lax.all_gather(latent_gain, ("seq", "frame"), axis=0, tiled=True),
        lax.all_gather(latent_bias, ("seq", "frame"), axis=0, tiled=True),
        lax.all_gather(feed_gain, ("seq", "frame"), axis=0, tiled=True),
        lax.all_gather(feed_bias, ("seq", "frame"), axis=0, tiled=True),
        lax.all_gather(time_table, ("seq", "frame"), axis=1, tiled=True),
    )
    gathered = lax.optimization_barrier(gathered)
    (
        query_full,
        key_full,
        value_full,
        out_full,
        up_full,
        down_full,
        mgain_full,
        mbias_full,
        lgain_full,
        lbias_full,
        fgain_full,
        fbias_full,
        table_full,
    ) = gathered
    frame_index = lax.axis_index("frame")
    frame_count = lax.axis_size("frame")
    seq_local, lat_rows, model_width = latents.shape
    round_count = patch_feats.shape[1]
    patch_count = patch_feats.shape[3]
    slot_total = time_index.shape[1]
    table_rows = time_table.shape[0]
    latent_total = lat_rows * frame_count
    head_size = model_width // HEADS
    inv_root = 1.0 / math.sqrt(head_size)
    latent_all = lax.all_gather(latents, "frame", axis=1, tiled=True)
    latent_norm, latent_unit, latent_std = norm_forward(latent_all, lgain_full, lbias_full)
    row_start = frame_index * lat_rows
    own_norm = lax.dynamic_slice_in_dim(latent_norm, row_start, lat_rows, 1)
    own_unit = lax.dynamic_slice_in_dim(latent_unit, row_start, lat_rows, 1)
    own_std = lax.dynamic_slice_in_dim(latent_std, row_start, lat_rows, 1)
    queries = product(flatten(latent_norm), query_full).reshape(
        seq_local, latent_total, model_width
    )
    own_keys = product(flatten(own_norm), key_full).reshape(seq_local, lat_rows, model_width)
    own_values = product(flatten(own_norm), value_full).reshape(seq_local, lat_rows, model_width)
    slot_ids = jnp.arange(round_count, dtype=jnp.int32) * frame_count + frame_index
    present = slot_ids[None, :] < image_counts[:, None]
    picks = jnp.arange(slot_total, dtype=jnp.int32)[None, :] == slot_ids[:, None]
    slot_times = jnp.sum(jnp.where(picks[None, :, :], time_index[:, None, :], 0), axis=-1)
    one_hot = (
        slot_times.reshape(-1)[:, None] == jnp.arange(table_rows, dtype=jnp.int32)[None, :]
    ).astype(jnp.float32)
    slot_embed = product(one_hot, table_full)
    slot_feats = patch_feats.reshape(seq_local * round_count, patch_count, model_width)

    def media_forward(element):
        normed, unit_part, std_part = norm_forward(
            element[0] + element[1][None, :], mgain_full, mbias_full
        )
        return (normed, unit_part, std_part, product(normed, key_full), product(normed, value_full))

    media_norm, media_unit, media_std, media_keys, media_values = per_slot(
        media_forward, (slot_feats, slot_embed)
    )
    key_total = lat_rows + round_count * patch_count
    all_keys = jnp.concatenate(
        [own_keys, media_keys.reshape(seq_local, round_count * patch_count, model_width)], axis=1
    )
    all_values = jnp.concatenate(
        [own_values, media_values.reshape(seq_local, round_count * patch_count, model_width)],
        axis=1,
    )
    keep = jnp.concatenate(
        [jnp.ones((seq_local, lat_rows), dtype=bool), jnp.repeat(present, patch_count, axis=1)],
        axis=1,
    )
    query_four = queries.reshape(seq_local, latent_total, HEADS, head_size)
    key_four = all_keys.reshape(seq_local, key_total, HEADS, head_size)
    value_four = all_values.reshape(seq_local, key_total, HEADS, head_size)

    def masked_scores():
        raw_scores = (
            jnp.einsum(
                "bqhe,bkhe->bhqk",
                query_four,
                key_four,
                precision=HIGHEST,
                preferred_element_type=jnp.float32,
            )
            * inv_root
        )
        return jnp.where(keep[:, None, None, :], raw_scores, MASKED)

    scores = masked_scores()
    row_top = jnp.max(scores, axis=-1)
    expo = jnp.exp(scores - row_top[..., None])
    row_total = jnp.sum(expo, axis=-1)
    partial_out = jnp.einsum(
        "bhqk,bkhe->bqhe", expo, value_four, precision=HIGHEST, preferred_element_type=jnp.float32
    )
    glob_top = lax.pmax(row_top, "frame")
    ratio = jnp.exp(row_top - glob_top)
    glob_total, glob_out = lax.psum((row_total * ratio, partial_out * heads_last(ratio)), "frame")
    attended = glob_out / heads_last(glob_total)
    log_total = glob_top + jnp.log(glob_total)
    attended_flat = attended.reshape(seq_local, latent_total, model_width)
    own_attended = lax.dynamic_slice_in_dim(attended_flat, row_start, lat_rows, 1)
    middle = latents + product(flatten(own_attended), out_full).reshape(
        seq_local, lat_rows, model_width
    )
    feed_norm, feed_unit, feed_std = norm_forward(middle, fgain_full, fbias_full)
    hidden_pre = product(flatten(feed_norm), up_full)
    activated, gelu_pull = jax.vjp(jax.nn.gelu, hidden_pre)
    new_latents = middle + product(activated, down_full).reshape(seq_local, lat_rows, model_width)
    regathered = (
        lax.all_gather(query_proj, ("seq", "frame"), axis=0, tiled=True),
        lax.all_gather(key_proj, ("seq", "frame"), axis=0, tiled=True),
        lax.all_gather(value_proj, ("seq", "frame"), axis=0, tiled=True),
        lax.all_gather(out_proj, ("seq", "frame"), axis=0, tiled=True),
        lax.all_gather(up_proj, ("seq", "frame"), axis=0, tiled=True),
        lax.all_gather(down_proj, ("seq", "frame"), axis=0, tiled=True),
        lax.all_gather(media_gain, ("seq", "frame"), axis=0, tiled=True),
        lax.all_gather(media_bias, ("seq", "frame"), axis=0, tiled=True),
        lax.all_gather(latent_gain, ("seq", "frame"), axis=0, tiled=True),
        lax.all_gather(latent_bias, ("seq", "frame"), axis=0, tiled=True),
        lax.all_gather(feed_gain, ("seq", "frame"), axis=0, tiled=True),
        lax.all_gather(feed_bias, ("seq", "frame"), axis=0, tiled=True),
        lax.all_gather(time_table, ("seq", "frame"), axis=1, tiled=True),
    )
    regathered = lax.optimization_barrier(regathered)
    query_back = regathered[0]
    key_back = regathered[1]
    value_back = regathered[2]
    out_back = regathered[3]
    up_back = regathered[4]
    down_back = regathered[5]
    mgain_back = regathered[6]
    lgain_back = regathered[8]
    fgain_back = regathered[10]
    cotangent = flatten(out_cotangent)
    grad_down = product_tn(activated, cotangent)
    grad_hidden = gelu_pull(product_nt(cotangent, down_back))[0]
    grad_up = product_tn(flatten(feed_norm), grad_hidden)
    grad_feed_norm = product_nt(grad_hidden, up_back).reshape(seq_local, lat_rows, model_width)
    grad_mid_norm, grad_fgain, grad_fbias = norm_backward(
        grad_feed_norm, feed_unit, feed_std, fgain_back
    )
    grad_middle = out_cotangent + grad_mid_norm
    grad_out_w = product_tn(flatten(own_attended), flatten(grad_middle))
    grad_own_att = product_nt(flatten(grad_middle), out_back).reshape(
        seq_local, lat_rows, model_width
    )
    grad_attended = lax.all_gather(grad_own_att, "frame", axis=1, tiled=True)
    grad_four = grad_attended.reshape(seq_local, latent_total, HEADS, head_size)
    delta_rows = jnp.einsum(
        "bqhe,bqhe->bhq", grad_four, attended, precision=HIGHEST, preferred_element_type=jnp.float32
    )
    probs = jnp.exp(masked_scores() - log_total[..., None])
    grad_probs = jnp.einsum(
        "bqhe,bkhe->bhqk",
        grad_four,
        value_four,
        precision=HIGHEST,
        preferred_element_type=jnp.float32,
    )
    grad_scores = probs * (grad_probs - delta_rows[..., None]) * inv_root
    grad_query_part = jnp.einsum(
        "bhqk,bkhe->bqhe",
        grad_scores,
        key_four,
        precision=HIGHEST,
        preferred_element_type=jnp.float32,
    ).reshape(seq_local, latent_total, model_width)
    grad_keys = jnp.einsum(
        "bhqk,bqhe->bkhe",
        grad_scores,
        query_four,
        precision=HIGHEST,
        preferred_element_type=jnp.float32,
    ).reshape(seq_local, key_total, model_width)
    grad_values = jnp.einsum(
        "bhqk,bqhe->bkhe", probs, grad_four, precision=HIGHEST, preferred_element_type=jnp.float32
    ).reshape(seq_local, key_total, model_width)
    grad_query_own = lax.psum_scatter(grad_query_part, "frame", scatter_dimension=1, tiled=True)
    grad_key_lat = flatten(grad_keys[:, :lat_rows])
    grad_value_lat = flatten(grad_values[:, :lat_rows])
    grad_key_media = grad_keys[:, lat_rows:].reshape(
        seq_local * round_count, patch_count, model_width
    )
    grad_value_media = grad_values[:, lat_rows:].reshape(
        seq_local * round_count, patch_count, model_width
    )
    grad_query_w = product_tn(flatten(own_norm), flatten(grad_query_own))
    grad_key_w = product_tn(flatten(own_norm), grad_key_lat) + product_tn(
        flatten(media_norm), flatten(grad_key_media)
    )
    grad_value_w = product_tn(flatten(own_norm), grad_value_lat) + product_tn(
        flatten(media_norm), flatten(grad_value_media)
    )
    grad_own_norm = (
        product_nt(flatten(grad_query_own), query_back)
        + product_nt(grad_key_lat, key_back)
        + product_nt(grad_value_lat, value_back)
    ).reshape(seq_local, lat_rows, model_width)
    grad_lat_in, grad_lgain, grad_lbias = norm_backward(
        grad_own_norm, own_unit, own_std, lgain_back
    )
    latent_grads = grad_middle + grad_lat_in

    def media_backward(element):
        normed_grad = product_nt(element[0], key_back) + product_nt(element[1], value_back)
        feats_grad, gain_part, bias_part = norm_backward(
            normed_grad, element[2], element[3], mgain_back
        )
        return (feats_grad, gain_part, bias_part, jnp.sum(feats_grad, axis=0))

    feats_grads, gain_parts, bias_parts, slot_sums = per_slot(
        media_backward, (grad_key_media, grad_value_media, media_unit, media_std)
    )
    grad_mgain = jnp.sum(gain_parts, axis=0)
    grad_mbias = jnp.sum(bias_parts, axis=0)
    grad_table = product_tn(one_hot, slot_sums)
    patch_grads = feats_grads.reshape(patch_feats.shape)
    (
        grad_query_w,
        grad_key_w,
        grad_value_w,
        grad_out_w,
        grad_up,
        grad_down,
    ) = lax.optimization_barrier(
        (grad_query_w, grad_key_w, grad_value_w, grad_out_w, grad_up, grad_down)
    )
    summed = (
        lax.psum_scatter(grad_query_w, ("seq", "frame"), scatter_dimension=0, tiled=True),
        lax.psum_scatter(grad_key_w, ("seq", "frame"), scatter_dimension=0, tiled=True),
        lax.psum_scatter(grad_value_w, ("seq", "frame"), scatter_dimension=0, tiled=True),
        lax.psum_scatter(grad_out_w, ("seq", "frame"), scatter_dimension=0, tiled=True),
        lax.psum_scatter(grad_up, ("seq", "frame"), scatter_dimension=0, tiled=True),
        lax.psum_scatter(grad_down, ("seq", "frame"), scatter_dimension=0, tiled=True),
        lax.psum_scatter(grad_mgain, ("seq", "frame"), scatter_dimension=0, tiled=True),
        lax.psum_scatter(grad_mbias, ("seq", "frame"), scatter_dimension=0, tiled=True),
        lax.psum_scatter(grad_lgain, ("seq", "frame"), scatter_dimension=0, tiled=True),
        lax.psum_scatter(grad_lbias, ("seq", "frame"), scatter_dimension=0, tiled=True),
        lax.psum_scatter(grad_fgain, ("seq", "frame"), scatter_dimension=0, tiled=True),
        lax.psum_scatter(grad_fbias, ("seq", "frame"), scatter_dimension=0, tiled=True),
        lax.psum_scatter(grad_table, ("seq", "frame"), scatter_dimension=1, tiled=True),
    )
    return (
        new_latents,
        latent_grads,
        patch_grads,
        summed[0],
        summed[1],
        summed[2],
        summed[3],
        summed[4],
        summed[5],
        summed[6],
        summed[7],
        summed[8],
        summed[9],
        summed[10],
        summed[11],
        summed[12],
    )


MESH = pl.DeviceIdType.MESH
F32 = jnp.float32
ANY = pl.BlockSpec(memory_space=pl.ANY)
GRID = (4, 2, 2, 2)


def place(z, y, x, c):
    return (z * 2 + y, x * 2 + c)


class Here:
    def __init__(self):
        seq, frame = lax.axis_index("seq"), lax.axis_index("frame")
        self.z, self.y, self.x, self.c = z, y, x, c = seq // 2, seq % 2, frame // 2, frame % 2
        self.ox, self.oy, self.oc = ox, oy, oc = 1 - x, 1 - y, 1 - c
        self.at_x, self.at_y, self.at_c = place(z, y, ox, c), place(z, oy, x, c), place(z, y, x, oc)
        self.ahead = [lax.rem(z + k, 4) for k in range(4)]
        self.behind = [lax.rem(z + 4 - k, 4) for k in range(4)]
        self.at_z = [place(o, y, x, c) for o in self.ahead]

    def greet(self):
        barrier = pltpu.get_barrier_semaphore()
        for peer in self.at_z[1:] + [self.at_x, self.at_y, self.at_c]:
            pl.semaphore_signal(barrier, inc=1, device_id=peer, device_id_type=MESH)
        pl.semaphore_wait(barrier, 6)


def remote(src, dst, send_sem, recv_sem, peer):
    return pltpu.make_async_remote_copy(
        src_ref=src, dst_ref=dst, send_sem=send_sem, recv_sem=recv_sem, device_id=peer, device_id_type=MESH
    )


class Gather:
    lag = 1

    def __init__(self, here, shards, fulls, cuts, sems):
        self.here, self.count = here, len(cuts)
        self.loc, self.zs, self.zr, self.xs, self.xr, self.ys, self.yr, self.ds, self.dr, self.cs, self.cr = sems
        self.shard = [shards[a].at[:, lo:hi] for a, lo, hi in cuts]
        self.full = [(lambda *at, a=a, lo=lo, hi=hi: fulls[a].at[at + (slice(lo, hi),)]) for a, lo, hi in cuts]
        self.half = [shards[a].shape[0] // 2 for a, lo, hi in cuts]

    @staticmethod
    def semaphores(count):
        dma = pltpu.SemaphoreType.DMA
        shapes = [(), (3,), (3,), (4,), (4,), (4,), (4,), (2, 4), (2, 4), (4,), (4,)]
        return [dma((count,) + s) for s in shapes]

    def local(self, p):
        h = self.here
        return pltpu.make_async_copy(self.shard[p], self.full[p](h.z, h.y, h.x, h.c, slice(None)), self.loc.at[p])

    def over_z(self, p, k):
        h = self.here
        dst = self.full[p](h.z, h.y, h.x, h.c, slice(None))
        return remote(self.shard[p], dst, self.zs.at[p, k - 1], self.zr.at[p, k - 1], h.at_z[k])

    def over_x(self, p, k):
        h = self.here
        block = self.full[p](h.behind[k], h.y, h.x, h.c, slice(None))
        return remote(self.shard[p] if k == 0 else block, block, self.xs.at[p, k], self.xr.at[p, k], h.at_x)

    def over_y(self, p, k):
        h = self.here
        block = self.full[p](h.behind[k], h.y, h.x, h.c, slice(None))
        return remote(self.shard[p] if k == 0 else block, block, self.ys.at[p, k], self.yr.at[p, k], h.at_y)

    def on_y(self, p, k):
        h = self.here
        part = self.full[p](h.behind[k], h.y, h.ox, h.c, slice(self.half[p], 2 * self.half[p]))
        return remote(part, part, self.ds.at[p, 0, k], self.dr.at[p, 0, k], h.at_y)

    def on_x(self, p, k):
        h = self.here
        part = self.full[p](h.behind[k], h.oy, h.x, h.c, slice(0, self.half[p]))
        return remote(part, part, self.ds.at[p, 1, k], self.dr.at[p, 1, k], h.at_x)

    def to_core(self, p, i):
        h = self.here
        yy, xx = ((h.y, h.x), (h.y, h.ox), (h.oy, h.x), (h.oy, h.ox))[i]
        blocks = self.full[p](slice(None), yy, xx, h.c, slice(None))
        return remote(blocks, blocks, self.cs.at[p, i], self.cr.at[p, i], h.at_c)

    def own(self, p):
        self.local(p).start()
        for k in (1, 2, 3):
            self.over_z(p, k).start()
        self.over_x(p, 0).start()
        self.over_y(p, 0).start()

    def along_z(self, p):
        for k in (1, 2, 3):
            self.over_z(p, k).wait_recv()
            self.over_x(p, k).start()
            self.over_y(p, k).start()

    def across(self, p):
        for k in range(4):
            self.over_x(p, k).wait_recv()
            self.on_y(p, k).start()
            self.over_y(p, k).wait_recv()
            self.on_x(p, k).start()
        self.local(p).wait()
        for i in range(3):
            self.to_core(p, i).start()

    def corner(self, p):
        for k in range(4):
            self.on_y(p, k).wait_recv()
            self.on_x(p, k).wait_recv()
        self.to_core(p, 3).start()

    def arrived(self, p):
        for i in range(4):
            self.to_core(p, i).wait_recv()

    def done(self, p, here=False):
        if not here:
            self.arrived(p)
        for i in range(4):
            self.to_core(p, i).wait_send()
        for k in (1, 2, 3):
            self.over_z(p, k).wait_send()
        for k in range(4):
            for copy in (self.over_x, self.over_y, self.on_x, self.on_y):
                copy(p, k).wait_send()

    def stages(self):
        return (self.own, self.along_z, self.across, self.corner)


def waves_of(plan, ahead):
    first, *stages = plan.stages()
    count, last, lag = plan.count, len(stages) - 1, plan.lag
    ahead = min(ahead, count)
    waves = [[functools.partial(first, p) for p in range(ahead)]]
    for t in range(count + last * lag):
        wave = [functools.partial(first, t + ahead)] if t + ahead < count else []
        order = range(last + 1)
        waves.append(wave + [functools.partial(stages[s], t - s * lag) for s in order if 0 <= t - s * lag < count])
    return waves


def finish_all(plan):
    for p in range(plan.count):
        plan.done(p)


class Scatter:
    lag = 1

    def __init__(self, here, count, mine, theirs, load, out, scratch):
        self.here, self.count, self.mine, self.theirs, self.load, self.out = here, count, mine, theirs, load, out
        self.got, self.gx, self.gy, self.hx, self.hy, self.gz = scratch[:6]
        self.cs, self.cr, self.fs, self.fr, self.ss, self.sr, self.zs, self.zr = scratch[6:]
        self.half = self.got.shape[-2] // 2

    @staticmethod
    def scratch(count, r, w):
        dma = pltpu.SemaphoreType.DMA
        leads = [(4, 2, 2, r), (4, 2, r // 2), (4, 2, r // 2), (4, r // 2), (4, r // 2), (3, r)]
        return [pltpu.VMEM((count,) + s + (w,), F32) for s in leads] + [
            dma((count,) + s) for s in ((), (), (2,), (2,), (2,), (2,), (3,), (3,))
        ]

    def to_core(self, p):
        return remote(self.theirs(p), self.got.at[p], self.cs.at[p], self.cr.at[p], self.here.at_c)

    def first(self, p, way):
        h, half, tot = self.here, self.half, self.mine(p)
        if way == 0:
            return remote(tot.at[:, :, h.ox, :half], self.gx.at[p], self.fs.at[p, 0], self.fr.at[p, 0], h.at_x)
        return remote(tot.at[:, h.oy, :, half:], self.gy.at[p], self.fs.at[p, 1], self.fr.at[p, 1], h.at_y)

    def second(self, p, way):
        h, half, tot = self.here, self.half, self.mine(p)
        if way == 0:
            return remote(tot.at[:, h.oy, h.x, :half], self.hy.at[p], self.ss.at[p, 0], self.sr.at[p, 0], h.at_y)
        return remote(tot.at[:, h.y, h.ox, half:], self.hx.at[p], self.ss.at[p, 1], self.sr.at[p, 1], h.at_x)

    def over_z(self, p, k):
        h = self.here
        src = self.mine(p).at[h.ahead[k], h.y, h.x]
        return remote(src, self.gz.at[p, k - 1], self.zs.at[p, k - 1], self.zr.at[p, k - 1], h.at_z[k])

    def start(self, p):
        if self.load is not None:
            self.load(p).start()
        self.to_core(p).start()

    def cores(self, p):
        tot, got = self.mine(p), self.got.at[p]
        if self.load is not None:
            self.load(p).wait()
        self.to_core(p).wait_recv()

        @pl.loop(0, 16)
        def _(i):
            at = (i // 4, (i // 2) % 2, i % 2)
            tot[at] = tot[at] + got[at]

        self.first(p, 0).start()
        self.first(p, 1).start()

    def sides(self, p):
        h, half, tot = self.here, self.half, self.mine(p)
        gx, gy = self.gx.at[p], self.gy.at[p]
        self.first(p, 0).wait_recv()

        @pl.loop(0, 8)
        def _(i):
            zi, yi = i // 2, i % 2
            tot[zi, yi, h.x, :half] = tot[zi, yi, h.x, :half] + gx[zi, yi]

        self.second(p, 0).start()
        self.first(p, 1).wait_recv()

        @pl.loop(0, 8)
        def _(i):
            zi, xi = i // 2, i % 2
            tot[zi, h.y, xi, half:] = tot[zi, h.y, xi, half:] + gy[zi, xi]

        self.second(p, 1).start()

    def column(self, p):
        h, half, tot = self.here, self.half, self.mine(p)
        hx, hy = self.hx.at[p], self.hy.at[p]
        self.second(p, 0).wait_recv()
        self.second(p, 1).wait_recv()

        @pl.loop(0, 4)
        def _(zi):
            tot[zi, h.y, h.x, :half] = tot[zi, h.y, h.x, :half] + hy[zi]
            tot[zi, h.y, h.x, half:] = tot[zi, h.y, h.x, half:] + hx[zi]

        for k in (1, 2, 3):
            self.over_z(p, k).start()

    def finish(self, p):
        h, gz = self.here, self.gz.at[p]
        for k in (1, 2, 3):
            self.over_z(p, k).wait_recv()
        self.out(p)[...] = (self.mine(p)[h.z, h.y, h.x] + gz[0]) + (gz[1] + gz[2])

    def done(self, p):
        self.to_core(p).wait_send()
        for way in (0, 1):
            self.first(p, way).wait_send()
            self.second(p, way).wait_send()
        for k in (1, 2, 3):
            self.over_z(p, k).wait_send()

    def stages(self):
        return (self.start, self.cores, self.sides, self.column, self.finish)


def run(wave):
    for action in wave:
        action()


class Pace:
    def __init__(self, step, steps, lead, parts, waves):
        self.step, self.steps, self.lead, self.parts = step, steps, lead, parts
        ticks, total, before = lead + steps * parts, 1 + sum(len(w) for w in waves[1:]), 0
        self.waves = [[] for _ in range(ticks)]
        for wave in waves:
            self.waves[ticks * before // total] += wave
            before += len(wave) if before else 1

    def at_lead(self, i):
        run(self.waves[i])

    def at(self, part):
        for s in range(self.steps):
            now = self.waves[self.lead + s * self.parts + part]
            if now:
                pl.when(self.step == s)(functools.partial(run, now))


def run_last(step, steps, plan):
    @pl.when(step == steps - 1)
    def _():
        finish_all(plan)


WIDE = 768


def column_cuts(shards):
    return [(a, lo, min(lo + WIDE, s.shape[1])) for a, s in enumerate(shards) for lo in range(0, s.shape[1], WIDE)]


class GroupGather:
    def __init__(self, here, shards, fulls, sems):
        self.here, self.shards, self.fulls, self.count = here, shards, fulls, len(shards)
        self.loc, self.ss, self.rs = sems

    @staticmethod
    def semaphores(count):
        dma = pltpu.SemaphoreType.DMA
        return [dma((count,)), dma((count, 3)), dma((count, 3))]

    def local(self, a):
        h = self.here
        return pltpu.make_async_copy(self.shards[a], self.fulls[a].at[:, h.x * 2 + h.c], self.loc.at[a])

    def copy(self, a, i):
        h = self.here
        mine = self.fulls[a].at[:, h.x * 2 + h.c]
        if i < 2:
            return remote(self.shards[a], mine, self.ss.at[a, i], self.rs.at[a, i], (h.at_x, h.at_c)[i])
        block = self.fulls[a].at[:, h.ox * 2 + h.c]
        return remote(block, block, self.ss.at[a, 2], self.rs.at[a, 2], h.at_c)

    def start(self):
        for a in range(self.count):
            self.local(a).start()
            self.copy(a, 0).start()
            self.copy(a, 1).start()

    def forward(self):
        for a in range(self.count):
            self.copy(a, 0).wait_recv()
            self.copy(a, 2).start()

    def done(self):
        for a in range(self.count):
            self.local(a).wait()
            self.copy(a, 0).wait_send()
            self.copy(a, 1).wait()
            self.copy(a, 2).wait()


def flat_full(full):
    return full.reshape((-1, full.shape[-1]))


def full_shapes(shards):
    return [jax.ShapeDtypeStruct(GRID + s.shape, s.dtype) for s in shards]


def gather_kernel(count, cuts, *refs):
    here = Here()
    here.greet()
    plan = Gather(here, refs[:count], refs[count : 2 * count], cuts, refs[2 * count :])
    for wave in waves_of(plan, 2):
        run(wave)
    finish_all(plan)


def gather_all(shards, collective_id):
    count = len(shards)
    cuts = column_cuts(shards)
    outs = pl.pallas_call(
        functools.partial(gather_kernel, count, cuts),
        out_shape=full_shapes(shards),
        in_specs=[ANY] * count,
        out_specs=[ANY] * count,
        scratch_shapes=Gather.semaphores(len(cuts)),
        compiler_params=pltpu.CompilerParams(collective_id=collective_id, has_side_effects=True),
        name="gather_all",
    )(*shards)
    return [flat_full(o) for o in outs]


class Summed:
    def __init__(self, parts):
        self.arrays = len(parts)
        self.rows, self.width = parts[0].shape[0] // 32, parts[0].shape[1]
        self.cut = min(256, self.width)
        self.pieces = self.width // self.cut
        self.operands = [p.reshape(GRID + (self.rows, self.width)) for p in parts]
        self.in_specs = [ANY] * len(parts)
        self.out_shape = [jax.ShapeDtypeStruct((self.rows, self.width), F32)] * len(parts)
        self.out_specs = [whole((self.rows, self.width))] * len(parts)
        n = self.count = len(parts) * self.pieces
        self.scratch = [pltpu.VMEM((n, 4, 2, 2, self.rows, self.cut), F32), pltpu.SemaphoreType.DMA((n,))]
        self.scratch += Scatter.scratch(n, self.rows, self.cut)

    def bind(self, here, ins, outs, scratch):
        tots, loc = scratch[:2]

        def cut(p):
            lo = p % self.pieces * self.cut
            return p // self.pieces, slice(lo, lo + self.cut)

        def part(p, core):
            a, cols = cut(p)
            return ins[a].at[:, :, :, core, :, cols]

        def out(p):
            a, cols = cut(p)
            return outs[a].at[:, cols]

        return Scatter(
            here,
            self.count,
            lambda p: tots.at[p],
            lambda p: part(p, here.oc),
            lambda p: pltpu.make_async_copy(part(p, here.c), tots.at[p], loc.at[p]),
            out,
            scratch[2:],
        )


def scatter_kernel(plan, *refs):
    n = plan.arrays
    here = Here()
    here.greet()
    sums = plan.bind(here, refs[:n], refs[n : 2 * n], refs[2 * n :])
    for wave in waves_of(sums, sums.count):
        run(wave)
    finish_all(sums)


def scatter_all(parts, collective_id):
    plan = Summed(parts)
    return pl.pallas_call(
        functools.partial(scatter_kernel, plan),
        out_shape=plan.out_shape,
        in_specs=plan.in_specs,
        out_specs=[pl.BlockSpec(memory_space=pltpu.VMEM)] * len(parts),
        scratch_shapes=plan.scratch,
        compiler_params=pltpu.CompilerParams(
            collective_id=collective_id, has_side_effects=True, vmem_limit_bytes=60 * 2**20
        ),
        name="scatter_all",
    )(*plan.operands)


def greet(peers):
    barrier = pltpu.get_barrier_semaphore()
    for peer in peers:
        pl.semaphore_signal(barrier, inc=1, device_id=peer, device_id_type=MESH)
    pl.semaphore_wait(barrier, len(peers))


def group_gather_kernel(count, *refs):
    shards, fulls = refs[:count], refs[count : 2 * count]
    loc, ss, rs = refs[2 * count :]
    here = Here()
    x, c, ox, at_x, at_c = here.x, here.c, here.ox, here.at_x, here.at_c
    greet([at_x, at_c])
    waits = []
    for a in range(count):
        mine = fulls[a].at[:, x * 2 + c]
        copy = pltpu.make_async_copy(shards[a], mine, loc.at[a])
        copy.start()
        over = remote(shards[a], mine, ss.at[a, 0], rs.at[a, 0], at_x)
        over.start()
        side = remote(shards[a], mine, ss.at[a, 1], rs.at[a, 1], at_c)
        side.start()
        waits.append((copy, over, side))
    last = []
    for a in range(count):
        waits[a][1].wait_recv()
        block = fulls[a].at[:, ox * 2 + c]
        on = remote(block, block, ss.at[a, 2], rs.at[a, 2], at_c)
        on.start()
        last.append(on)
    for a in range(count):
        copy, over, side = waits[a]
        copy.wait()
        over.wait_send()
        side.wait()
        last[a].wait()


def group_gather(shards, collective_id):
    count = len(shards)
    dma = pltpu.SemaphoreType.DMA
    return pl.pallas_call(
        functools.partial(group_gather_kernel, count),
        out_shape=[jax.ShapeDtypeStruct((s.shape[0], 4) + s.shape[1:], F32) for s in shards],
        in_specs=[ANY] * count,
        out_specs=[ANY] * count,
        scratch_shapes=[dma((count,)), dma((count, 3)), dma((count, 3))],
        compiler_params=pltpu.CompilerParams(collective_id=collective_id, has_side_effects=True),
        name="group_gather",
    )(*shards)


def group_swap_kernel(count, *refs):
    shards, fulls = refs[:count], refs[count : 2 * count]
    loc, ss, rs = refs[2 * count :]
    here = Here()
    z, y, x, c = here.z, here.y, here.x, here.c
    me = x * 2 + c
    peers = [(x, 1 - c), (1 - x, c), (1 - x, 1 - c)]
    greet([place(z, y, *p) for p in peers])
    waits = []
    for a in range(count):
        copy = pltpu.make_async_copy(shards[a].at[:, me], fulls[a].at[:, me], loc.at[a])
        copy.start()
        waits.append(copy)
        for k in (1, 2, 0):
            px, pc = peers[k]
            on = remote(
                shards[a].at[:, px * 2 + pc], fulls[a].at[:, me], ss.at[a, k], rs.at[a, k], place(z, y, px, pc)
            )
            on.start()
            waits.append(on)
    for copy in waits:
        copy.wait()


def group_swap(shards, collective_id):
    count = len(shards)
    dma = pltpu.SemaphoreType.DMA
    return pl.pallas_call(
        functools.partial(group_swap_kernel, count),
        out_shape=[jax.ShapeDtypeStruct(s.shape, F32) for s in shards],
        in_specs=[ANY] * count,
        out_specs=[ANY] * count,
        scratch_shapes=[dma((count,)), dma((count, 3)), dma((count, 3))],
        compiler_params=pltpu.CompilerParams(collective_id=collective_id, has_side_effects=True),
        name="group_swap",
    )(*shards)


def group_sum_kernel(parts, out, tot, got, last, loc, ss, rs):
    here = Here()
    greet([here.at_x, here.at_c])
    load = pltpu.make_async_copy(parts.at[:, :, here.c], tot, loc.at[0])
    load.start()
    side = remote(parts.at[:, :, here.oc], got, ss.at[0], rs.at[0], here.at_c)
    side.start()
    load.wait()
    side.wait_recv()
    tot[...] += got[...]
    over = remote(tot.at[:, here.ox], last, ss.at[1], rs.at[1], here.at_x)
    over.start()
    over.wait_recv()
    out[...] = tot[:, here.x] + last[...]
    side.wait_send()
    over.wait_send()


def group_sum(parts, collective_id):
    s, lat, w = parts.shape
    r = lat // 4
    dma = pltpu.SemaphoreType.DMA
    return pl.pallas_call(
        group_sum_kernel,
        out_shape=jax.ShapeDtypeStruct((s, r, w), F32),
        in_specs=[ANY],
        out_specs=pl.BlockSpec(memory_space=pltpu.VMEM),
        scratch_shapes=[
            pltpu.VMEM((s, 2, r, w), F32),
            pltpu.VMEM((s, 2, r, w), F32),
            pltpu.VMEM((s, r, w), F32),
            dma((1,)),
            dma((2,)),
            dma((2,)),
        ],
        compiler_params=pltpu.CompilerParams(collective_id=collective_id, has_side_effects=True),
        name="group_sum",
    )(parts.reshape(s, 2, 2, r, w))


def stacked(values, axis, order):
    top = lax.reduce_precision(values, 8, 7)
    terms = (top.astype(jnp.bfloat16), (values - top).astype(jnp.bfloat16))
    return jnp.concatenate([terms[i] for i in order], axis=axis)


def thin_product(left, right):
    return lax.dot_general(
        stacked(left, 0, (0, 0, 1)), stacked(right, 0, (0, 1, 0)), (((0,), (0,)), ((), ())), preferred_element_type=F32
    )


BF16 = jnp.bfloat16
HIGH = lax.Precision.HIGH
BLOCK = 256


def dot(left, right, dims=(1, 0)):
    return lax.dot_general(
        left, right, (((dims[0],), (dims[1],)), ((), ())), precision=HIGH, preferred_element_type=F32
    )


def dot3(left, right, dims=(1, 0)):
    numbers = (((dims[0],), (dims[1],)), ((), ()))
    one = functools.partial(lax.dot_general, dimension_numbers=numbers, preferred_element_type=F32)
    return one(left[0], right[0]) + (one(left[0], right[1]) + one(left[1], right[0]))


def halves(values):
    top = values.astype(BF16)
    return top, (values - top.astype(F32)).astype(BF16)


def split_weights(sources, pairs, stage, sems, pace):
    step = stage.shape[1]
    chunks = [(i, r) for i, s in enumerate(sources) for r in range(0, s.shape[0], step)]

    def copy(n):
        i, r = chunks[n]
        return pltpu.make_async_copy(sources[i].at[r : r + step], stage.at[n % 2], sems.at[n % 2])

    copy(0).start()
    for n, (i, r) in enumerate(chunks):
        if n * pace.lead % len(chunks) == 0:
            pace.at_lead(n * pace.lead // len(chunks))
        if n + 1 < len(chunks):
            copy(n + 1).start()
        copy(n).wait()
        pairs[i][0][r : r + step], pairs[i][1][r : r + step] = halves(stage[n % 2])


def unit_of(values):
    centred = values - jnp.mean(values, axis=-1, keepdims=True)
    inv_std = lax.rsqrt(jnp.mean(centred * centred, axis=-1, keepdims=True) + EPSILON)
    return centred * inv_std, inv_std


def staging(width):
    return [pltpu.VMEM((width, width), BF16)] * 4 + [pltpu.VMEM((2, 128, width), F32), pltpu.SemaphoreType.DMA((2,))]


def whole(shape, buffers=1):
    return pl.BlockSpec(shape, lambda *i: (0,) * len(shape), pipeline_mode=pl.Buffered(buffers))


def opening_kernel(cuts, *refs):
    times, feats, latents = refs[:3]
    shards, group_shard = refs[3:9], refs[9:10]
    vec, keys, values, own_keys, own_values, queries, xt_top, xt_low = refs[10:18]
    fulls, group_full = refs[18:24], refs[24:25]
    pk, top, low, own_top, own_low, lat, lat_top, lat_low, stage, load = refs[25:35]
    step = pl.program_id(0)
    here = Here()
    vectors = Gather(here, shards[:1], fulls[:1], [(0, 0, 128)], refs[35:46])
    moved = Gather(here, shards[1:], fulls[1:], cuts, refs[46:57])
    group = GroupGather(here, group_shard, group_full, refs[57:])
    waves = waves_of(moved, 2)
    cut = keys.shape[1]
    slots, chunks = top.shape[0] // BLOCK, shards[1].shape[1] // cut

    def start():
        here.greet()
        vectors.own(0)
        run(waves[0])
        group.start()
        vectors.along_z(0)
        vectors.across(0)
        vectors.corner(0)
        vectors.arrived(0)
        copy = pltpu.make_async_copy(fulls[0], pk, load.at[0])
        copy.start()
        copy.wait()
        strip = shards[1].shape[0]
        vec[...] = jnp.concatenate([pk[i // 8, i // 4 % 2, i // 2 % 2, i % 2][:, :strip] for i in range(32)], axis=1)
        own_top[...], own_low[...] = halves(unit_of(latents[...])[0] * vec[2:3] + vec[3:4])
        run(waves[1])
        group.forward()

    pl.when(step == 0)(start)
    at_step = {2: 2, 4: 3, 5: 4, slots + 1: 5, slots + 2: 6, slots + 4: 7, slots + 5: 8}
    at_step.update({slots + chunks + i: 8 + i for i in range(1, 5)})
    for s, w in at_step.items():
        pl.when(step == s)(functools.partial(run, waves[w]))

    @pl.when(step < slots)
    def _():
        embed = vec[pl.ds(6 + times[step], 1)]
        normed = unit_of(feats[...] + embed)[0] * vec[0:1] + vec[1:2]
        rows = pl.ds(pl.multiple_of(step * BLOCK, BLOCK), BLOCK)
        top[rows], low[rows] = halves(normed)
        xt_top[...], xt_low[...] = halves(jnp.swapaxes(normed, 0, 1))

    def chunk(array, n, left, right, out, own_out):
        cols = pl.ds(pl.multiple_of(n * cut, cut), cut)
        copy = pltpu.make_async_copy(fulls[array].at[:, :, :, :, :, cols], stage.at[array % 2], load.at[0])
        copy.start()
        copy.wait()
        pair = halves(stage[array % 2].reshape((-1, cut)))
        step_rows = min(512, left.shape[0])

        @pl.loop(0, left.shape[0] // step_rows)
        def _(m):
            rows = pl.ds(pl.multiple_of(m * step_rows, step_rows), step_rows)
            out[rows] = dot3((left[rows], right[rows]), pair)

        if own_out is not None:
            own_out[...] = dot3((own_top[...], own_low[...]), pair)

    half = chunks // 2
    for first in (0, 1):

        @pl.when(step == slots + first * half)
        def _():
            moved.arrived(2 * first)
            moved.arrived(2 * first + 1)

    @pl.when((step >= slots) & (step < slots + chunks))
    def _():
        chunk(1, step - slots, top, low, keys, own_keys)
        chunk(2, step - slots, top, low, values, own_values)

    @pl.when(step == slots + chunks)
    def _():
        moved.arrived(4)
        moved.arrived(5)
        group.done()
        copy = pltpu.make_async_copy(group_full[0], lat, load.at[0])
        copy.start()
        copy.wait()
        lat_top[...], lat_low[...] = halves(unit_of(lat[...].reshape(lat_top.shape))[0] * vec[2:3] + vec[3:4])

    @pl.when(step >= slots + chunks)
    def _():
        chunk(3, step - slots - chunks, lat_top, lat_low, queries, None)

    @pl.when(step == slots + 2 * chunks - 1)
    def _():
        vectors.done(0, True)
        for p in range(moved.count):
            moved.done(p, p < 6)


def opening(times, feats, latents, packed, key_w, value_w, query_w, cot, out_w, collective_id):
    rows, width = feats.shape
    seqs, own_each, _ = latents.shape
    own_rows, lat_rows = seqs * own_each, seqs * own_each * 4
    slots, cut = rows // BLOCK, 256
    chunks = width // cut
    shards = [packed, key_w, value_w, query_w, cot, out_w]
    cuts = [(a, lo, lo + WIDE) for lo in range(0, width, WIDE) for a in (0, 1)]
    cuts += [(a, lo, lo + WIDE) for a in (2, 3, 4) for lo in range(0, width, WIDE)]
    clip = lambda i, lo: jnp.clip(i - lo, 0, chunks - 1)
    chunk_of = lambda n, lo: pl.BlockSpec((n, cut), lambda i: (0, clip(i, lo)))
    turned = pl.BlockSpec((width, BLOCK), lambda i: (0, jnp.minimum(i, slots - 1)))
    full = lambda n, kind=F32: jax.ShapeDtypeStruct((n, width), kind)
    outs = pl.pallas_call(
        functools.partial(opening_kernel, cuts),
        grid=(slots + 2 * chunks,),
        in_specs=[
            SMEM,
            pl.BlockSpec((BLOCK, width), lambda i: (jnp.minimum(i, slots - 1), 0)),
            whole((own_rows, width)),
        ]
        + [ANY] * 7,
        out_specs=[
            whole((16, width)),
            chunk_of(rows, slots),
            chunk_of(rows, slots),
            chunk_of(own_rows, slots),
            chunk_of(own_rows, slots),
            chunk_of(lat_rows, slots + chunks),
            turned,
            turned,
        ]
        + [ANY] * 7,
        out_shape=[full(16), full(rows), full(rows), full(own_rows), full(own_rows), full(lat_rows)]
        + [jax.ShapeDtypeStruct((width, rows), BF16)] * 2
        + full_shapes(shards)
        + [jax.ShapeDtypeStruct((seqs, 4, own_each, width), F32)],
        scratch_shapes=[
            pltpu.VMEM(GRID + packed.shape, F32),
            pltpu.VMEM((rows, width), BF16),
            pltpu.VMEM((rows, width), BF16),
            pltpu.VMEM((own_rows, width), BF16),
            pltpu.VMEM((own_rows, width), BF16),
            pltpu.VMEM((seqs, 4, own_each, width), F32),
            pltpu.VMEM((lat_rows, width), BF16),
            pltpu.VMEM((lat_rows, width), BF16),
            pltpu.VMEM((2,) + GRID + (width // 32, cut), F32),
            pltpu.SemaphoreType.DMA((1,)),
        ]
        + Gather.semaphores(1)
        + Gather.semaphores(len(cuts))
        + GroupGather.semaphores(1),
        compiler_params=pltpu.CompilerParams(
            collective_id=collective_id, has_side_effects=True, vmem_limit_bytes=60 * 2**20
        ),
        name="opening",
    )(times, feats, latents.reshape(own_rows, width), *shards, latents)
    return outs[:8], [flat_full(o) for o in outs[9:14]], outs[14]


def pair_rows(values, first, head):
    lane = lax.broadcasted_iota(jnp.int32, values.shape, 1)
    return jnp.concatenate(
        [
            jnp.where((lane >= first) & (lane < first + head), values, 0.0),
            jnp.where((lane >= first + head) & (lane < first + 2 * head), values, 0.0),
        ],
        axis=0,
    )


def pair_merge(stacked, first, head):
    half = stacked.shape[0] // 2
    lane = lax.broadcasted_iota(jnp.int32, (half, stacked.shape[1]), 1)
    one = jnp.where((lane >= first) & (lane < first + head), stacked[:half], 0.0)
    return one + jnp.where((lane >= first + head) & (lane < first + 2 * head), stacked[half:], 0.0)


def join(left, right):
    return jnp.concatenate([left[:, :128], left[:, 128:] + right[:, :128], right[:, 128:]], axis=1)


def windows(head):
    return ((slice(0, 256), 0), (slice(128, 384), 2 * head - 128))


def score_block(present, seq, keys, own_keys, q_pair, window, inv_root):
    at = keys.shape[0]
    scores = jnp.concatenate([dot(keys[:, window], q_pair, (1, 1)), dot(own_keys[:, window], q_pair, (1, 1))], axis=0)
    row = lax.broadcasted_iota(jnp.int32, scores.shape, 0)
    keep = (row >= at) | ((row < at // 2) & (present[seq, 0] > 0)) | ((row >= at // 2) & (present[seq, 1] > 0))
    return jnp.where(keep, scores * inv_root, MASKED)


def attend_kernel(inv_root, head, present, queries, keys, values, own_keys, own_values, out, tops, sums):
    seq, group = pl.program_id(0), pl.program_id(1)
    merged = []
    for p, (window, first) in enumerate(windows(head)):
        q_pair = pair_rows(queries[:, window], first, head)
        scores = score_block(present, seq, keys, own_keys, q_pair, window, inv_root)
        top = jnp.max(scores, axis=0, keepdims=True)
        expo = jnp.exp(scores - top)
        tops[pl.ds(group * 2 + p, 1)] = top
        sums[pl.ds(group * 2 + p, 1)] = jnp.sum(expo, axis=0, keepdims=True)
        at = keys.shape[0]
        stacked = dot(expo[:at], values[:, window], (0, 0)) + dot(expo[at:], own_values[:, window], (0, 0))
        merged.append(pair_merge(stacked, first, head))
    out[...] = join(*merged)


def attend_specs(lat, media, rows):
    group = 384
    query = pl.BlockSpec((None, lat, group), lambda b, g: (b, 0, g))
    key = pl.BlockSpec((media, group), lambda b, g: (b, g))
    own = pl.BlockSpec((rows, group), lambda b, g: (b, g))
    stat = pl.BlockSpec((None, 8, 128), lambda b, g: (b, 0, 0))
    return query, key, own, stat


SMEM = pl.BlockSpec(memory_space=pltpu.SMEM)


def attend(present, queries, keys, values, own_keys, own_values):
    seqs, lat, width = queries.shape
    head = width // HEADS
    query, key, own, stat = attend_specs(lat, keys.shape[0] // seqs, own_keys.shape[0] // seqs)
    stat_shape = jax.ShapeDtypeStruct((seqs, 8, 128), F32)
    return pl.pallas_call(
        functools.partial(attend_kernel, 1.0 / math.sqrt(head), head),
        grid=(seqs, width // 384),
        in_specs=[SMEM, query, key, key, own, own],
        out_specs=[query, stat, stat],
        out_shape=[jax.ShapeDtypeStruct(queries.shape, F32), stat_shape, stat_shape],
        compiler_params=pltpu.CompilerParams(vmem_limit_bytes=60 * 2**20),
        name="attend",
    )(present, queries, keys, values, own_keys, own_values)


def attend_back_kernel(inv_root, head, plan, steps, *refs):
    present, queries, grads, logs, deltas, keys, values, own_keys, own_values = refs[:9]
    n = plan.arrays
    query_out, key_out, value_out, own_key_out, own_value_out = refs[9 + n : 14 + n]
    seq, group = pl.program_id(0), pl.program_id(1)
    step = seq * pl.num_programs(1) + group
    here = Here()
    moved = plan.bind(here, refs[9 : 9 + n], refs[14 + n : 14 + 2 * n], refs[14 + 2 * n :])
    waves = waves_of(moved, moved.count)
    waves[0].insert(0, here.greet)
    pace = Pace(step, steps, 0, 2, waves)
    merged, key_grads, value_grads = [], [], []
    at = keys.shape[0]
    for p, (window, first) in enumerate(windows(head)):
        pace.at(p)
        q_pair = pair_rows(queries[:, window], first, head)
        g_pair = pair_rows(grads[:, window], first, head)
        scores = score_block(present, seq, keys, own_keys, q_pair, window, inv_root)
        probs = jnp.exp(scores - logs[pl.ds(group * 2 + p, 1)])
        grad_probs = jnp.concatenate(
            [dot(values[:, window], g_pair, (1, 1)), dot(own_values[:, window], g_pair, (1, 1))], axis=0
        )
        grad_scores = probs * (grad_probs - deltas[pl.ds(group * 2 + p, 1)]) * inv_root
        stacked = dot(grad_scores[:at], keys[:, window], (0, 0)) + dot(grad_scores[at:], own_keys[:, window], (0, 0))
        merged.append(pair_merge(stacked, first, head))
        key_grads.append(dot(grad_scores, q_pair))
        value_grads.append(dot(probs, g_pair))
    query_out[...] = join(*merged)
    key_grad, value_grad = join(*key_grads), join(*value_grads)
    key_out[...], own_key_out[...] = key_grad[:at], key_grad[at:]
    value_out[...], own_value_out[...] = value_grad[:at], value_grad[at:]
    run_last(step, steps, moved)


def attend_back(present, queries, grads, logs, deltas, keys, values, own_keys, own_values, plan, collective_id):
    seqs, lat, width = queries.shape
    head = width // HEADS
    query, key, own, stat = attend_specs(lat, keys.shape[0] // seqs, own_keys.shape[0] // seqs)
    shape = lambda v: jax.ShapeDtypeStruct(v.shape, F32)
    grid = (seqs, width // 384)
    outs = pl.pallas_call(
        functools.partial(attend_back_kernel, 1.0 / math.sqrt(head), head, plan, grid[0] * grid[1]),
        grid=grid,
        in_specs=[SMEM, query, query, stat, stat, key, key, own, own] + plan.in_specs,
        out_specs=[query, key, key, own, own] + plan.out_specs,
        out_shape=[shape(queries), shape(keys), shape(values), shape(own_keys), shape(own_values)] + plan.out_shape,
        scratch_shapes=plan.scratch,
        compiler_params=pltpu.CompilerParams(
            collective_id=collective_id, has_side_effects=True, vmem_limit_bytes=60 * 2**20
        ),
        name="attend_back",
    )(present, queries, grads, logs, deltas, keys, values, own_keys, own_values, *plan.operands)
    return outs[:5], outs[5:]


def weight_kernel(steps, xt_top, xt_low, own_t, grad_keys, grad_values, own_gk, own_gv, vec, outs, vec_out, mats, *rest):
    n = pl.program_id(0)
    here = Here()
    cut = grad_keys.shape[1]
    sums = Scatter(
        here,
        2 * steps,
        lambda p: mats.at[p, :, :, :, here.c],
        lambda p: mats.at[p, :, :, :, here.oc],
        None,
        lambda p: outs.at[p % 2, :, pl.ds(pl.multiple_of(p // 2 * cut, cut), cut)],
        rest[:14],
    )
    tot, loc = rest[14:16]
    small = Scatter(
        here,
        1,
        lambda p: tot,
        lambda p: vec.at[:, :, :, here.oc],
        lambda p: pltpu.make_async_copy(vec.at[:, :, :, here.c], tot, loc.at[p]),
        lambda p: vec_out,
        rest[16:],
    )
    stages = sums.stages()

    @pl.when(n == 0)
    def _():
        here.greet()

    for w, (grad, own_grad) in enumerate(((grad_keys, own_gk), (grad_values, own_gv))):
        pair = halves(grad[...])
        top, low = halves(own_grad[...])
        stacked = jnp.concatenate([top, low, top], axis=0)

        @pl.loop(0, 2)
        def _(i):
            rows = pl.ds(pl.multiple_of(i * 768, 768), 768)
            made = dot3((xt_top[rows], xt_low[rows]), pair)
            made += jnp.dot(own_t[rows], stacked, preferred_element_type=F32)
            mats[2 * n + w, pl.ds(i * 2, 2)] = made.reshape((2, 2, 2, 2, 48, cut))

        sums.start(2 * n + w)
        for s in (1, 2, 3, 4):
            p = 2 * n + w - s

            @pl.when(p >= 0)
            def _():
                stages[s](p)

        if w == 1:
            for s in range(5):

                @pl.when(n == s)
                def _():
                    small.stages()[s](0)

    @pl.when(n == steps - 1)
    def _():
        for t in range(2 * steps, 2 * steps + 4):
            for s in (1, 2, 3, 4):
                if t - s < 2 * steps:
                    stages[s](t - s)

        @pl.loop(0, 2 * steps)
        def _(p):
            sums.done(p)

        small.done(0)


def weight_grads(xt_top, xt_low, own_t, grad_keys, grad_values, own_gk, own_gv, vec, collective_id):
    width, rows = xt_top.shape
    own_rows = own_gk.shape[0]
    steps = width // BLOCK
    cols = lambda n: pl.BlockSpec((n, BLOCK), lambda i: (0, i))
    r = width // 32
    vr, vw = vec.shape[0] // 32, vec.shape[1]
    outs, vec_sum = pl.pallas_call(
        functools.partial(weight_kernel, steps),
        grid=(steps,),
        in_specs=[
            whole((width, rows)),
            whole((width, rows)),
            whole(own_t.shape),
            cols(rows),
            cols(rows),
            cols(own_rows),
            cols(own_rows),
            ANY,
        ],
        out_specs=[whole((2, r, width)), whole((vr, vw))],
        out_shape=[jax.ShapeDtypeStruct((2, r, width), F32), jax.ShapeDtypeStruct((vr, vw), F32)],
        scratch_shapes=[pltpu.VMEM((2 * steps,) + GRID + (r, BLOCK), F32)]
        + Scatter.scratch(2 * steps, r, BLOCK)
        + [pltpu.VMEM((4, 2, 2, vr, vw), F32), pltpu.SemaphoreType.DMA((1,))]
        + Scatter.scratch(1, vr, vw),
        compiler_params=pltpu.CompilerParams(
            collective_id=collective_id, has_side_effects=True, vmem_limit_bytes=62 * 2**20
        ),
        name="weight_grads",
    )(xt_top, xt_low, own_t, grad_keys, grad_values, own_gk, own_gv, vec.reshape(GRID + (vr, vw)))
    return outs[0], outs[1], vec_sum


def media_back_kernel(plan, steps, *refs):
    feats, embed, gain, grad_keys, grad_values, own_gk, own_gv, key_w, value_w = refs[:9]
    n = plan.arrays
    out, own_out, sums = refs[9 + n : 12 + n]
    kt, kl, vt, vl, stage, sems = refs[12 + 2 * n : 18 + 2 * n]
    step = pl.program_id(0)
    here = Here()
    moved = plan.bind(here, refs[9 : 9 + n], refs[12 + n : 12 + 2 * n], refs[18 + 2 * n :])
    waves = waves_of(moved, moved.count)
    waves[0].insert(0, here.greet)
    pace = Pace(step, steps, 4, 3, waves)

    @pl.when(step == 0)
    def _():
        split_weights((key_w, value_w), ((kt, kl), (vt, vl)), stage, sems, pace)
        own_out[...] = dot3(halves(own_gk[...]), (kt[...], kl[...]), (1, 1)) + dot3(
            halves(own_gv[...]), (vt[...], vl[...]), (1, 1)
        )
        sums[...] = jnp.zeros_like(sums)

    key_pair, value_pair = halves(grad_keys[...]), halves(grad_values[...])
    for i in range(3):
        pace.at(i)
        rows = slice(i * 512, i * 512 + 512)
        out[:, rows] = dot3(key_pair, (kt[rows], kl[rows]), (1, 1)) + dot3(value_pair, (vt[rows], vl[rows]), (1, 1))
    strip = 64

    @pl.loop(0, out.shape[0] // strip)
    def _(i):
        rows = pl.ds(pl.multiple_of(i * strip, strip), strip)
        incoming = out[rows]
        unit, inv_std = unit_of(feats[rows] + embed[...])
        sums[pl.ds(0, 1)] += jnp.sum(incoming * unit, axis=0, keepdims=True)
        sums[pl.ds(1, 1)] += jnp.sum(incoming, axis=0, keepdims=True)
        scaled = incoming * gain[...]
        result = inv_std * (
            scaled
            - jnp.mean(scaled, axis=-1, keepdims=True)
            - unit * jnp.mean(scaled * unit, axis=-1, keepdims=True)
        )
        out[rows] = result
        sums[pl.ds(2 + step, 1)] += jnp.sum(result, axis=0, keepdims=True)

    run_last(step, steps, moved)


def media_backward(feats, embed, gain, grad_keys, grad_values, own_gk, own_gv, key_w, value_w, plan, collective_id):
    rows, width = feats.shape
    own_rows = own_gk.shape[0]
    row_block = pl.BlockSpec((BLOCK, width), lambda i: (i, 0))
    one_block = pl.BlockSpec((BLOCK, width), lambda i: (i, 0), pipeline_mode=pl.Buffered(1))
    steps = rows // BLOCK
    outs = pl.pallas_call(
        functools.partial(media_back_kernel, plan, steps),
        grid=(steps,),
        in_specs=[
            one_block,
            pl.BlockSpec((None, 1, width), lambda i: (i, 0, 0)),
            whole((1, width)),
            row_block,
            row_block,
            whole((own_rows, width)),
            whole((own_rows, width)),
            ANY,
            ANY,
        ]
        + plan.in_specs,
        out_specs=[one_block, whole((own_rows, width)), whole((8, width))] + plan.out_specs,
        out_shape=[
            jax.ShapeDtypeStruct((rows, width), F32),
            jax.ShapeDtypeStruct((own_rows, width), F32),
            jax.ShapeDtypeStruct((8, width), F32),
        ]
        + plan.out_shape,
        scratch_shapes=staging(width) + plan.scratch,
        compiler_params=pltpu.CompilerParams(
            collective_id=collective_id, has_side_effects=True, vmem_limit_bytes=64 * 2**20 - 2**16
        ),
        name="media_backward",
    )(feats, embed, gain, grad_keys, grad_values, own_gk, own_gv, key_w, value_w, *plan.operands)
    return outs[:3], outs[3:]


GELU_A = math.sqrt(2.0 / math.pi)
GELU_B = 0.044715


def feed_kernel(blocks, *refs):
    feed, cot, up, down, new_part, grad_up_t, grad_down, out, act, back, mats = refs[:11]
    step = pl.program_id(0)
    here = Here()
    pieces, cut = mats.shape[0], mats.shape[-1]
    sums = Scatter(
        here,
        pieces,
        lambda p: mats.at[p, :, :, :, here.c],
        lambda p: mats.at[p, :, :, :, here.oc],
        None,
        lambda p: out.at[:, p * cut : (p + 1) * cut],
        refs[11:],
    )
    waves = waves_of(sums, pieces)
    block = step - blocks * (step >= blocks).astype(jnp.int32)
    rows = pl.ds(pl.multiple_of(block * BLOCK, BLOCK), BLOCK)
    pl.when(step == 0)(here.greet)

    @pl.when(step < blocks)
    def _():
        hidden = dot(feed[...], up[...])
        grad_act = dot(cot[...], down[...], (1, 1))
        square = hidden * hidden
        bent = jnp.tanh(GELU_A * (hidden + GELU_B * hidden * square))
        slope = 0.5 * (1.0 + bent) + 0.5 * hidden * (1.0 - bent * bent) * (GELU_A * (1.0 + 3.0 * GELU_B * square))
        act[rows] = 0.5 * hidden * (1.0 + bent)
        back[rows] = grad_act * slope

    @pl.when(step == blocks)
    def _():
        for p in range(pieces):

            @pl.loop(0, 4)
            def _(zi):
                plane = pl.ds(pl.multiple_of(zi * 384, 384), 384)
                made = dot(back[plane], up[p * cut : (p + 1) * cut], (1, 1))
                mats[p, zi] = made.reshape((2, 2, 2, 48, cut))

            sums.start(p)
        grad_up_t[...] = jnp.zeros_like(grad_up_t)
        grad_down[...] = jnp.zeros_like(grad_down)

    for i in range(blocks):

        @pl.when(step == blocks + i)
        def _():
            for wave in waves[1 + 2 * i : 3 + 2 * i]:
                run(wave)

    @pl.when(step >= blocks)
    def _():
        new_part[...] = dot(act[rows], down[...])
        grad_up_t[...] += dot(back[rows], feed[...], (0, 0))
        grad_down[...] += dot(act[rows], cot[...], (0, 0))

    @pl.when(step == 2 * blocks - 1)
    def _():
        for wave in waves[1 + 2 * blocks :]:
            run(wave)
        finish_all(sums)


def feed_forward(feed, cot, up, down, collective_id):
    rows, width = feed.shape
    units, r, cut = up.shape[1], width // 32, 256
    blocks = rows // BLOCK
    big = jax.ShapeDtypeStruct((rows, width), F32)
    slim = jax.ShapeDtypeStruct((units, width), F32)
    row_block = pl.BlockSpec((BLOCK, width), lambda i: (i % blocks, 0))
    late_block = pl.BlockSpec((BLOCK, width), lambda i: (jnp.maximum(i - blocks, 0), 0))
    return pl.pallas_call(
        functools.partial(feed_kernel, blocks),
        grid=(2 * blocks,),
        in_specs=[row_block, row_block, whole((width, units)), whole((units, width))],
        out_specs=[late_block, whole((units, width)), whole((units, width)), whole((r, width))],
        out_shape=[big, slim, slim, jax.ShapeDtypeStruct((r, width), F32)],
        scratch_shapes=[pltpu.VMEM((rows, units), F32)] * 2
        + [pltpu.VMEM((width // cut,) + GRID + (r, cut), F32)]
        + Scatter.scratch(width // cut, r, cut),
        compiler_params=pltpu.CompilerParams(
            collective_id=collective_id, has_side_effects=True, vmem_limit_bytes=60 * 2**20
        ),
        name="feed_forward",
    )(feed, cot, up, down)


def mm(left, right):
    return jnp.dot(left, right, precision=HIGH, preferred_element_type=F32)


def mm_tn(left, right):
    return lax.dot_general(left, right, (((0,), (0,)), ((), ())), precision=HIGH, preferred_element_type=F32)


def mm_nt(left, right):
    return lax.dot_general(left, right, (((1,), (1,)), ((), ())), precision=HIGH, preferred_element_type=F32)


def body_fast(
    latents,
    patch_feats,
    image_counts,
    time_index,
    query_proj,
    key_proj,
    value_proj,
    out_proj,
    up_proj,
    down_proj,
    media_gain,
    media_bias,
    latent_gain,
    latent_bias,
    feed_gain,
    feed_bias,
    time_table,
    out_cotangent,
):
    frame = lax.axis_index("frame")
    frames = lax.axis_size("frame")
    seqs, rows, width = latents.shape
    rounds, patches = patch_feats.shape[1], patch_feats.shape[3]
    lat = rows * frames
    head = width // HEADS
    strip = media_gain.shape[0]

    vectors = jnp.concatenate(
        [jnp.stack([media_gain, media_bias, latent_gain, latent_bias, feed_gain, feed_bias]), time_table], axis=0
    )
    packed = jnp.pad(vectors, ((0, 2), (0, 128 - strip)))
    slot_ids = jnp.arange(rounds, dtype=jnp.int32) * frames + frame
    present = slot_ids[None, :] < image_counts[:, None]
    picks = jnp.arange(time_index.shape[1], dtype=jnp.int32)[None, :] == slot_ids[:, None]
    slot_times = jnp.sum(jnp.where(picks[None, :, :], time_index[:, None, :], 0), axis=-1)
    feats = patch_feats.reshape(-1, width)

    (vec_all, keys, values, own_keys, own_values, queries, xt_top, xt_low), gathered, lat_blocks = opening(
        slot_times.reshape(-1), feats, latents, packed, key_proj, value_proj, query_proj, flatten(out_cotangent), out_proj, 0
    )
    key_w, value_w, query_w, cot_all, out_w = gathered
    up_held, keys = lax.optimization_barrier((up_proj, keys))
    up_cols = lax.all_to_all(
        up_held.reshape(strip, 32, -1), ("seq", "frame"), split_axis=1, concat_axis=0, tiled=True
    ).reshape(width, -1)
    mgain, mbias, lgain, lbias, fgain, fbias = (vec_all[i] for i in range(6))
    table = vec_all[6:14]
    queries = queries.reshape(seqs, lat, width)
    latent_norm, latent_unit, latent_std = norm_forward(lat_blocks.reshape(seqs, lat, width), lgain, lbias)
    own_rows = lambda v: lax.dynamic_slice_in_dim(v, frame * rows, rows, 1)
    own_norm, own_unit, own_std = own_rows(latent_norm), own_rows(latent_unit), own_rows(latent_std)
    one_hot = slot_times[:, :, None] == jnp.arange(time_table.shape[0], dtype=jnp.int32)
    slot_embed = jnp.sum(jnp.where(one_hot[..., None], table, 0.0), axis=2)
    embed = slot_embed.reshape(-1, 1, width)
    own_flat = flatten(own_norm)
    present = present.astype(jnp.int32)

    partial, row_top, row_sum = attend(present, queries, keys, values, own_keys, own_values)
    stats = jnp.concatenate([row_top.reshape(seqs, HEADS, lat), row_sum.reshape(seqs, HEADS, lat)], axis=1)
    stats = jnp.pad(stats.transpose(0, 2, 1), ((0, 0), (0, 0), (0, 128 - 2 * HEADS)))
    part_all, stat_all = group_swap(
        [partial.reshape(seqs, frames, rows, width), stats.reshape(seqs, frames, rows, 128)], 2
    )
    tops, sums = stat_all[..., :HEADS], stat_all[..., HEADS : 2 * HEADS]
    top = jnp.max(tops, axis=1)
    ratio = jnp.exp(tops - top[:, None])
    row_total = jnp.sum(sums * ratio, axis=1)
    weight = ratio / row_total[:, None]
    attended = jnp.sum(part_all.reshape(seqs, frames, rows, HEADS, head) * weight[..., None], axis=1)
    log_total = top + jnp.log(row_total)
    attended_flat = attended.reshape(seqs, rows, width)
    middle = latents + mm(flatten(attended_flat), out_w).reshape(seqs, rows, width)

    feed_norm, feed_unit, feed_std = norm_forward(middle, fgain, fbias)
    (feed_all,) = gather_all([flatten(feed_norm)], 3)
    new_part, grad_up_t, grad_down, grad_feed_norm = feed_forward(feed_all, cot_all, up_cols, down_proj, 4)
    grad_up = lax.all_to_all(
        grad_up_t.reshape(-1, 32, strip).transpose(1, 2, 0), ("seq", "frame"), split_axis=0, concat_axis=2, tiled=True
    ).reshape(strip, -1)
    grad_mid_norm, grad_fgain, grad_fbias = norm_backward(
        grad_feed_norm.reshape(seqs, rows, width), feed_unit, feed_std, fgain
    )
    grad_middle = out_cotangent + grad_mid_norm
    grad_out_w = thin_product(flatten(attended_flat), flatten(grad_middle))
    grad_own = mm_nt(flatten(grad_middle), out_w).reshape(seqs, rows, HEADS, head)
    delta = jnp.sum(grad_own * attended, axis=-1)
    back_stats = jnp.pad(jnp.concatenate([log_total, delta], axis=-1), ((0, 0), (0, 0), (0, 128 - 2 * HEADS)))
    grad_blocks, back_blocks = group_gather([grad_own.reshape(seqs, rows, width), back_stats], 5)
    back_all = back_blocks.reshape(seqs, lat, 128).transpose(0, 2, 1)
    logs_all, delta_all = (back_all[:, i * HEADS : (i + 1) * HEADS].reshape(seqs, 8, 128) for i in range(2))

    (query_part, grad_keys, grad_values, own_gk, own_gv), (new_rows,) = attend_back(
        present,
        queries,
        grad_blocks.reshape(seqs, lat, width),
        logs_all,
        delta_all,
        keys,
        values,
        own_keys,
        own_values,
        Summed([new_part]),
        10,
    )
    new_latents = middle + new_rows.reshape(seqs, rows, width)
    grad_queries = flatten(group_sum(query_part, 6))

    grad_query_w = thin_product(own_flat, grad_queries)
    (patch_grads, own_back, media_sums), (sum_query, sum_out) = media_backward(
        feats,
        embed,
        mgain[None],
        grad_keys,
        grad_values,
        own_gk,
        own_gv,
        key_w,
        value_w,
        Summed([grad_query_w, grad_out_w]),
        7,
    )
    grad_own_norm = (mm_nt(grad_queries, query_w) + own_back).reshape(seqs, rows, width)
    grad_lat_in, grad_lgain, grad_lbias = norm_backward(grad_own_norm, own_unit, own_std, lgain)
    latent_grads = grad_middle + grad_lat_in
    grad_mgain, grad_mbias = media_sums[0], media_sums[1]
    slot_sums = media_sums[2:].reshape(seqs, rounds, width)
    grad_table = jnp.sum(jnp.where(one_hot[..., None], slot_sums[:, :, None, :], 0.0), axis=(0, 1))
    vec_grads = jnp.concatenate(
        [jnp.stack([grad_mgain, grad_mbias, grad_lgain, grad_lbias, grad_fgain, grad_fbias]), grad_table], axis=0
    )
    vec_blocks = jnp.pad(vec_grads.reshape(14, 32, strip).transpose(1, 0, 2), ((0, 0), (0, 2), (0, 128 - strip)))
    own_t = stacked(own_flat, 0, (0, 0, 1)).T
    sum_key, sum_value, sum_vec = weight_grads(
        xt_top, xt_low, own_t, grad_keys, grad_values, own_gk, own_gv, vec_blocks.reshape(-1, 128), 8
    )
    vec = sum_vec[:14, :strip]
    return (
        new_latents,
        latent_grads,
        patch_grads.reshape(patch_feats.shape),
        sum_query,
        sum_key,
        sum_value,
        sum_out,
        grad_up,
        grad_down,
        vec[0],
        vec[1],
        vec[2],
        vec[3],
        vec[4],
        vec[5],
        vec[6:],
    )


def solution(mesh):
    fast = dict(mesh.shape) == {"seq": 8, "frame": 4}
    return jax.shard_map(
        body_fast if fast else body_general,
        mesh=mesh,
        in_specs=(
            P("seq", "frame", None),
            P("seq", None, "frame", None, None),
            P("seq"),
            P("seq", None),
            P(("seq", "frame"), None),
            P(("seq", "frame"), None),
            P(("seq", "frame"), None),
            P(("seq", "frame"), None),
            P(("seq", "frame"), None),
            P(("seq", "frame"), None),
            P(("seq", "frame")),
            P(("seq", "frame")),
            P(("seq", "frame")),
            P(("seq", "frame")),
            P(("seq", "frame")),
            P(("seq", "frame")),
            P(None, ("seq", "frame")),
            P("seq", "frame", None),
        ),
        out_specs=(
            P("seq", "frame", None),
            P("seq", "frame", None),
            P("seq", None, "frame", None, None),
            P(("seq", "frame"), None),
            P(("seq", "frame"), None),
            P(("seq", "frame"), None),
            P(("seq", "frame"), None),
            P(("seq", "frame"), None),
            P(("seq", "frame"), None),
            P(("seq", "frame")),
            P(("seq", "frame")),
            P(("seq", "frame")),
            P(("seq", "frame")),
            P(("seq", "frame")),
            P(("seq", "frame")),
            P(None, ("seq", "frame")),
        ),
        check_vma=False,
    )
```

```python
import functools
import math

import jax
import jax.numpy as jnp
from jax import lax
from jax.experimental import pallas as pl
from jax.experimental.pallas import tpu as pltpu
from jax.sharding import PartitionSpec as P

HEADS = 16


HIGHEST = lax.Precision.HIGHEST
EPSILON = 1e-05
MASKED = -1e30


def product(left, right):
    return jnp.dot(left, right, precision=HIGHEST, preferred_element_type=jnp.float32)


def product_tn(left, right):
    return lax.dot_general(
        left, right, (((0,), (0,)), ((), ())), precision=HIGHEST, preferred_element_type=jnp.float32
    )


def product_nt(left, right):
    return lax.dot_general(
        left, right, (((1,), (1,)), ((), ())), precision=HIGHEST, preferred_element_type=jnp.float32
    )


def flatten(values):
    return values.reshape(-1, values.shape[-1])


def norm_forward(values, gain_vec, bias_vec):
    centred = values - jnp.mean(values, axis=-1, keepdims=True)
    inv_std = lax.rsqrt(jnp.mean(centred * centred, axis=-1, keepdims=True) + EPSILON)
    unit_vals = centred * inv_std
    return (unit_vals * gain_vec + bias_vec, unit_vals, inv_std)


def norm_backward(incoming, unit_vals, inv_std, gain_vec):
    scaled = incoming * gain_vec
    result = inv_std * (
        scaled
        - jnp.mean(scaled, axis=-1, keepdims=True)
        - unit_vals * jnp.mean(scaled * unit_vals, axis=-1, keepdims=True)
    )
    flat_in = flatten(incoming)
    return (result, jnp.sum(flat_in * flatten(unit_vals), axis=0), jnp.sum(flat_in, axis=0))


def heads_last(stats):
    return jnp.transpose(stats, (0, 2, 1))[..., None]


def per_slot(action, operands):
    return lax.map(action, operands)


def body_general(
    latents,
    patch_feats,
    image_counts,
    time_index,
    query_proj,
    key_proj,
    value_proj,
    out_proj,
    up_proj,
    down_proj,
    media_gain,
    media_bias,
    latent_gain,
    latent_bias,
    feed_gain,
    feed_bias,
    time_table,
    out_cotangent,
):
    gathered = (
        lax.all_gather(query_proj, ("seq", "frame"), axis=0, tiled=True),
        lax.all_gather(key_proj, ("seq", "frame"), axis=0, tiled=True),
        lax.all_gather(value_proj, ("seq", "frame"), axis=0, tiled=True),
        lax.all_gather(out_proj, ("seq", "frame"), axis=0, tiled=True),
        lax.all_gather(up_proj, ("seq", "frame"), axis=0, tiled=True),
        lax.all_gather(down_proj, ("seq", "frame"), axis=0, tiled=True),
        lax.all_gather(media_gain, ("seq", "frame"), axis=0, tiled=True),
        lax.all_gather(media_bias, ("seq", "frame"), axis=0, tiled=True),
        lax.all_gather(latent_gain, ("seq", "frame"), axis=0, tiled=True),
        lax.all_gather(latent_bias, ("seq", "frame"), axis=0, tiled=True),
        lax.all_gather(feed_gain, ("seq", "frame"), axis=0, tiled=True),
        lax.all_gather(feed_bias, ("seq", "frame"), axis=0, tiled=True),
        lax.all_gather(time_table, ("seq", "frame"), axis=1, tiled=True),
    )
    gathered = lax.optimization_barrier(gathered)
    (
        query_full,
        key_full,
        value_full,
        out_full,
        up_full,
        down_full,
        mgain_full,
        mbias_full,
        lgain_full,
        lbias_full,
        fgain_full,
        fbias_full,
        table_full,
    ) = gathered
    frame_index = lax.axis_index("frame")
    frame_count = lax.axis_size("frame")
    seq_local, lat_rows, model_width = latents.shape
    round_count = patch_feats.shape[1]
    patch_count = patch_feats.shape[3]
    slot_total = time_index.shape[1]
    table_rows = time_table.shape[0]
    latent_total = lat_rows * frame_count
    head_size = model_width // HEADS
    inv_root = 1.0 / math.sqrt(head_size)
    latent_all = lax.all_gather(latents, "frame", axis=1, tiled=True)
    latent_norm, latent_unit, latent_std = norm_forward(latent_all, lgain_full, lbias_full)
    row_start = frame_index * lat_rows
    own_norm = lax.dynamic_slice_in_dim(latent_norm, row_start, lat_rows, 1)
    own_unit = lax.dynamic_slice_in_dim(latent_unit, row_start, lat_rows, 1)
    own_std = lax.dynamic_slice_in_dim(latent_std, row_start, lat_rows, 1)
    queries = product(flatten(latent_norm), query_full).reshape(
        seq_local, latent_total, model_width
    )
    own_keys = product(flatten(own_norm), key_full).reshape(seq_local, lat_rows, model_width)
    own_values = product(flatten(own_norm), value_full).reshape(seq_local, lat_rows, model_width)
    slot_ids = jnp.arange(round_count, dtype=jnp.int32) * frame_count + frame_index
    present = slot_ids[None, :] < image_counts[:, None]
    picks = jnp.arange(slot_total, dtype=jnp.int32)[None, :] == slot_ids[:, None]
    slot_times = jnp.sum(jnp.where(picks[None, :, :], time_index[:, None, :], 0), axis=-1)
    one_hot = (
        slot_times.reshape(-1)[:, None] == jnp.arange(table_rows, dtype=jnp.int32)[None, :]
    ).astype(jnp.float32)
    slot_embed = product(one_hot, table_full)
    slot_feats = patch_feats.reshape(seq_local * round_count, patch_count, model_width)

    def media_forward(element):
        normed, unit_part, std_part = norm_forward(
            element[0] + element[1][None, :], mgain_full, mbias_full
        )
        return (normed, unit_part, std_part, product(normed, key_full), product(normed, value_full))

    media_norm, media_unit, media_std, media_keys, media_values = per_slot(
        media_forward, (slot_feats, slot_embed)
    )
    key_total = lat_rows + round_count * patch_count
    all_keys = jnp.concatenate(
        [own_keys, media_keys.reshape(seq_local, round_count * patch_count, model_width)], axis=1
    )
    all_values = jnp.concatenate(
        [own_values, media_values.reshape(seq_local, round_count * patch_count, model_width)],
        axis=1,
    )
    keep = jnp.concatenate(
        [jnp.ones((seq_local, lat_rows), dtype=bool), jnp.repeat(present, patch_count, axis=1)],
        axis=1,
    )
    query_four = queries.reshape(seq_local, latent_total, HEADS, head_size)
    key_four = all_keys.reshape(seq_local, key_total, HEADS, head_size)
    value_four = all_values.reshape(seq_local, key_total, HEADS, head_size)

    def masked_scores():
        raw_scores = (
            jnp.einsum(
                "bqhe,bkhe->bhqk",
                query_four,
                key_four,
                precision=HIGHEST,
                preferred_element_type=jnp.float32,
            )
            * inv_root
        )
        return jnp.where(keep[:, None, None, :], raw_scores, MASKED)

    scores = masked_scores()
    row_top = jnp.max(scores, axis=-1)
    expo = jnp.exp(scores - row_top[..., None])
    row_total = jnp.sum(expo, axis=-1)
    partial_out = jnp.einsum(
        "bhqk,bkhe->bqhe", expo, value_four, precision=HIGHEST, preferred_element_type=jnp.float32
    )
    glob_top = lax.pmax(row_top, "frame")
    ratio = jnp.exp(row_top - glob_top)
    glob_total, glob_out = lax.psum((row_total * ratio, partial_out * heads_last(ratio)), "frame")
    attended = glob_out / heads_last(glob_total)
    log_total = glob_top + jnp.log(glob_total)
    attended_flat = attended.reshape(seq_local, latent_total, model_width)
    own_attended = lax.dynamic_slice_in_dim(attended_flat, row_start, lat_rows, 1)
    middle = latents + product(flatten(own_attended), out_full).reshape(
        seq_local, lat_rows, model_width
    )
    feed_norm, feed_unit, feed_std = norm_forward(middle, fgain_full, fbias_full)
    hidden_pre = product(flatten(feed_norm), up_full)
    activated, gelu_pull = jax.vjp(jax.nn.gelu, hidden_pre)
    new_latents = middle + product(activated, down_full).reshape(seq_local, lat_rows, model_width)
    regathered = (
        lax.all_gather(query_proj, ("seq", "frame"), axis=0, tiled=True),
        lax.all_gather(key_proj, ("seq", "frame"), axis=0, tiled=True),
        lax.all_gather(value_proj, ("seq", "frame"), axis=0, tiled=True),
        lax.all_gather(out_proj, ("seq", "frame"), axis=0, tiled=True),
        lax.all_gather(up_proj, ("seq", "frame"), axis=0, tiled=True),
        lax.all_gather(down_proj, ("seq", "frame"), axis=0, tiled=True),
        lax.all_gather(media_gain, ("seq", "frame"), axis=0, tiled=True),
        lax.all_gather(media_bias, ("seq", "frame"), axis=0, tiled=True),
        lax.all_gather(latent_gain, ("seq", "frame"), axis=0, tiled=True),
        lax.all_gather(latent_bias, ("seq", "frame"), axis=0, tiled=True),
        lax.all_gather(feed_gain, ("seq", "frame"), axis=0, tiled=True),
        lax.all_gather(feed_bias, ("seq", "frame"), axis=0, tiled=True),
        lax.all_gather(time_table, ("seq", "frame"), axis=1, tiled=True),
    )
    regathered = lax.optimization_barrier(regathered)
    query_back = regathered[0]
    key_back = regathered[1]
    value_back = regathered[2]
    out_back = regathered[3]
    up_back = regathered[4]
    down_back = regathered[5]
    mgain_back = regathered[6]
    lgain_back = regathered[8]
    fgain_back = regathered[10]
    cotangent = flatten(out_cotangent)
    grad_down = product_tn(activated, cotangent)
    grad_hidden = gelu_pull(product_nt(cotangent, down_back))[0]
    grad_up = product_tn(flatten(feed_norm), grad_hidden)
    grad_feed_norm = product_nt(grad_hidden, up_back).reshape(seq_local, lat_rows, model_width)
    grad_mid_norm, grad_fgain, grad_fbias = norm_backward(
        grad_feed_norm, feed_unit, feed_std, fgain_back
    )
    grad_middle = out_cotangent + grad_mid_norm
    grad_out_w = product_tn(flatten(own_attended), flatten(grad_middle))
    grad_own_att = product_nt(flatten(grad_middle), out_back).reshape(
        seq_local, lat_rows, model_width
    )
    grad_attended = lax.all_gather(grad_own_att, "frame", axis=1, tiled=True)
    grad_four = grad_attended.reshape(seq_local, latent_total, HEADS, head_size)
    delta_rows = jnp.einsum(
        "bqhe,bqhe->bhq", grad_four, attended, precision=HIGHEST, preferred_element_type=jnp.float32
    )
    probs = jnp.exp(masked_scores() - log_total[..., None])
    grad_probs = jnp.einsum(
        "bqhe,bkhe->bhqk",
        grad_four,
        value_four,
        precision=HIGHEST,
        preferred_element_type=jnp.float32,
    )
    grad_scores = probs * (grad_probs - delta_rows[..., None]) * inv_root
    grad_query_part = jnp.einsum(
        "bhqk,bkhe->bqhe",
        grad_scores,
        key_four,
        precision=HIGHEST,
        preferred_element_type=jnp.float32,
    ).reshape(seq_local, latent_total, model_width)
    grad_keys = jnp.einsum(
        "bhqk,bqhe->bkhe",
        grad_scores,
        query_four,
        precision=HIGHEST,
        preferred_element_type=jnp.float32,
    ).reshape(seq_local, key_total, model_width)
    grad_values = jnp.einsum(
        "bhqk,bqhe->bkhe", probs, grad_four, precision=HIGHEST, preferred_element_type=jnp.float32
    ).reshape(seq_local, key_total, model_width)
    grad_query_own = lax.psum_scatter(grad_query_part, "frame", scatter_dimension=1, tiled=True)
    grad_key_lat = flatten(grad_keys[:, :lat_rows])
    grad_value_lat = flatten(grad_values[:, :lat_rows])
    grad_key_media = grad_keys[:, lat_rows:].reshape(
        seq_local * round_count, patch_count, model_width
    )
    grad_value_media = grad_values[:, lat_rows:].reshape(
        seq_local * round_count, patch_count, model_width
    )
    grad_query_w = product_tn(flatten(own_norm), flatten(grad_query_own))
    grad_key_w = product_tn(flatten(own_norm), grad_key_lat) + product_tn(
        flatten(media_norm), flatten(grad_key_media)
    )
    grad_value_w = product_tn(flatten(own_norm), grad_value_lat) + product_tn(
        flatten(media_norm), flatten(grad_value_media)
    )
    grad_own_norm = (
        product_nt(flatten(grad_query_own), query_back)
        + product_nt(grad_key_lat, key_back)
        + product_nt(grad_value_lat, value_back)
    ).reshape(seq_local, lat_rows, model_width)
    grad_lat_in, grad_lgain, grad_lbias = norm_backward(
        grad_own_norm, own_unit, own_std, lgain_back
    )
    latent_grads = grad_middle + grad_lat_in

    def media_backward(element):
        normed_grad = product_nt(element[0], key_back) + product_nt(element[1], value_back)
        feats_grad, gain_part, bias_part = norm_backward(
            normed_grad, element[2], element[3], mgain_back
        )
        return (feats_grad, gain_part, bias_part, jnp.sum(feats_grad, axis=0))

    feats_grads, gain_parts, bias_parts, slot_sums = per_slot(
        media_backward, (grad_key_media, grad_value_media, media_unit, media_std)
    )
    grad_mgain = jnp.sum(gain_parts, axis=0)
    grad_mbias = jnp.sum(bias_parts, axis=0)
    grad_table = product_tn(one_hot, slot_sums)
    patch_grads = feats_grads.reshape(patch_feats.shape)
    (
        grad_query_w,
        grad_key_w,
        grad_value_w,
        grad_out_w,
        grad_up,
        grad_down,
    ) = lax.optimization_barrier(
        (grad_query_w, grad_key_w, grad_value_w, grad_out_w, grad_up, grad_down)
    )
    summed = (
        lax.psum_scatter(grad_query_w, ("seq", "frame"), scatter_dimension=0, tiled=True),
        lax.psum_scatter(grad_key_w, ("seq", "frame"), scatter_dimension=0, tiled=True),
        lax.psum_scatter(grad_value_w, ("seq", "frame"), scatter_dimension=0, tiled=True),
        lax.psum_scatter(grad_out_w, ("seq", "frame"), scatter_dimension=0, tiled=True),
        lax.psum_scatter(grad_up, ("seq", "frame"), scatter_dimension=0, tiled=True),
        lax.psum_scatter(grad_down, ("seq", "frame"), scatter_dimension=0, tiled=True),
        lax.psum_scatter(grad_mgain, ("seq", "frame"), scatter_dimension=0, tiled=True),
        lax.psum_scatter(grad_mbias, ("seq", "frame"), scatter_dimension=0, tiled=True),
        lax.psum_scatter(grad_lgain, ("seq", "frame"), scatter_dimension=0, tiled=True),
        lax.psum_scatter(grad_lbias, ("seq", "frame"), scatter_dimension=0, tiled=True),
        lax.psum_scatter(grad_fgain, ("seq", "frame"), scatter_dimension=0, tiled=True),
        lax.psum_scatter(grad_fbias, ("seq", "frame"), scatter_dimension=0, tiled=True),
        lax.psum_scatter(grad_table, ("seq", "frame"), scatter_dimension=1, tiled=True),
    )
    return (
        new_latents,
        latent_grads,
        patch_grads,
        summed[0],
        summed[1],
        summed[2],
        summed[3],
        summed[4],
        summed[5],
        summed[6],
        summed[7],
        summed[8],
        summed[9],
        summed[10],
        summed[11],
        summed[12],
    )


MESH = pl.DeviceIdType.MESH
F32 = jnp.float32
ANY = pl.BlockSpec(memory_space=pl.ANY)
GRID = (4, 2, 2, 2)


def place(z, y, x, c):
    return (z * 2 + y, x * 2 + c)


class Here:
    def __init__(self):
        seq, frame = lax.axis_index("seq"), lax.axis_index("frame")
        self.z, self.y, self.x, self.c = z, y, x, c = seq // 2, seq % 2, frame // 2, frame % 2
        self.ox, self.oy, self.oc = ox, oy, oc = 1 - x, 1 - y, 1 - c
        self.at_x, self.at_y, self.at_c = place(z, y, ox, c), place(z, oy, x, c), place(z, y, x, oc)
        self.ahead = [lax.rem(z + k, 4) for k in range(4)]
        self.behind = [lax.rem(z + 4 - k, 4) for k in range(4)]
        self.at_z = [place(o, y, x, c) for o in self.ahead]

    def greet(self):
        barrier = pltpu.get_barrier_semaphore()
        for peer in self.at_z[1:] + [self.at_x, self.at_y, self.at_c]:
            pl.semaphore_signal(barrier, inc=1, device_id=peer, device_id_type=MESH)
        pl.semaphore_wait(barrier, 6)


def remote(src, dst, send_sem, recv_sem, peer):
    return pltpu.make_async_remote_copy(
        src_ref=src, dst_ref=dst, send_sem=send_sem, recv_sem=recv_sem, device_id=peer, device_id_type=MESH
    )


class Gather:
    lag = 1

    def __init__(self, here, shards, fulls, cuts, sems):
        self.here, self.count = here, len(cuts)
        self.loc, self.zs, self.zr, self.xs, self.xr, self.ys, self.yr, self.ds, self.dr, self.cs, self.cr = sems
        self.shard = [shards[a].at[:, lo:hi] for a, lo, hi in cuts]
        self.full = [(lambda *at, a=a, lo=lo, hi=hi: fulls[a].at[at + (slice(lo, hi),)]) for a, lo, hi in cuts]
        self.half = [shards[a].shape[0] // 2 for a, lo, hi in cuts]

    @staticmethod
    def semaphores(count):
        dma = pltpu.SemaphoreType.DMA
        shapes = [(), (3,), (3,), (4,), (4,), (4,), (4,), (2, 4), (2, 4), (4,), (4,)]
        return [dma((count,) + s) for s in shapes]

    def local(self, p):
        h = self.here
        return pltpu.make_async_copy(self.shard[p], self.full[p](h.z, h.y, h.x, h.c, slice(None)), self.loc.at[p])

    def over_z(self, p, k):
        h = self.here
        dst = self.full[p](h.z, h.y, h.x, h.c, slice(None))
        return remote(self.shard[p], dst, self.zs.at[p, k - 1], self.zr.at[p, k - 1], h.at_z[k])

    def over_x(self, p, k):
        h = self.here
        block = self.full[p](h.behind[k], h.y, h.x, h.c, slice(None))
        return remote(self.shard[p] if k == 0 else block, block, self.xs.at[p, k], self.xr.at[p, k], h.at_x)

    def over_y(self, p, k):
        h = self.here
        block = self.full[p](h.behind[k], h.y, h.x, h.c, slice(None))
        return remote(self.shard[p] if k == 0 else block, block, self.ys.at[p, k], self.yr.at[p, k], h.at_y)

    def on_y(self, p, k):
        h = self.here
        part = self.full[p](h.behind[k], h.y, h.ox, h.c, slice(self.half[p], 2 * self.half[p]))
        return remote(part, part, self.ds.at[p, 0, k], self.dr.at[p, 0, k], h.at_y)

    def on_x(self, p, k):
        h = self.here
        part = self.full[p](h.behind[k], h.oy, h.x, h.c, slice(0, self.half[p]))
        return remote(part, part, self.ds.at[p, 1, k], self.dr.at[p, 1, k], h.at_x)

    def to_core(self, p, i):
        h = self.here
        yy, xx = ((h.y, h.x), (h.y, h.ox), (h.oy, h.x), (h.oy, h.ox))[i]
        blocks = self.full[p](slice(None), yy, xx, h.c, slice(None))
        return remote(blocks, blocks, self.cs.at[p, i], self.cr.at[p, i], h.at_c)

    def own(self, p):
        self.local(p).start()
        for k in (1, 2, 3):
            self.over_z(p, k).start()
        self.over_x(p, 0).start()
        self.over_y(p, 0).start()

    def along_z(self, p):
        for k in (1, 2, 3):
            self.over_z(p, k).wait_recv()
            self.over_x(p, k).start()
            self.over_y(p, k).start()

    def across(self, p):
        for k in range(4):
            self.over_x(p, k).wait_recv()
            self.on_y(p, k).start()
            self.over_y(p, k).wait_recv()
            self.on_x(p, k).start()
        self.local(p).wait()
        for i in range(3):
            self.to_core(p, i).start()

    def corner(self, p):
        for k in range(4):
            self.on_y(p, k).wait_recv()
            self.on_x(p, k).wait_recv()
        self.to_core(p, 3).start()

    def arrived(self, p):
        for i in range(4):
            self.to_core(p, i).wait_recv()

    def done(self, p, here=False):
        if not here:
            self.arrived(p)
        for i in range(4):
            self.to_core(p, i).wait_send()
        for k in (1, 2, 3):
            self.over_z(p, k).wait_send()
        for k in range(4):
            for copy in (self.over_x, self.over_y, self.on_x, self.on_y):
                copy(p, k).wait_send()

    def stages(self):
        return (self.own, self.along_z, self.across, self.corner)


LAG = 2


def waves_of(plan, ahead):
    first, *stages = plan.stages()
    count, last, lag = plan.count, len(stages) - 1, plan.lag
    ahead = min(ahead, count)
    waves = [[functools.partial(first, p) for p in range(ahead)]]
    for t in range(count + last * lag):
        wave = [functools.partial(first, t + ahead)] if t + ahead < count else []
        order = range(last, -1, -1)
        waves.append(wave + [functools.partial(stages[s], t - s * lag) for s in order if 0 <= t - s * lag < count])
    return waves


def finish_all(plan):
    for p in range(plan.count):
        plan.done(p)


class Scatter:
    lag = LAG

    def __init__(self, here, count, mine, theirs, load, out, scratch):
        self.here, self.count, self.mine, self.theirs, self.load, self.out = here, count, mine, theirs, load, out
        self.got, self.gx, self.gy, self.hx, self.hy, self.gz = scratch[:6]
        self.cs, self.cr, self.fs, self.fr, self.ss, self.sr, self.zs, self.zr = scratch[6:]
        self.half = self.got.shape[-2] // 2

    @staticmethod
    def scratch(count, r, w):
        dma = pltpu.SemaphoreType.DMA
        leads = [(4, 2, 2, r), (4, 2, r // 2), (4, 2, r // 2), (4, r // 2), (4, r // 2), (3, r)]
        return [pltpu.VMEM((count,) + s + (w,), F32) for s in leads] + [
            dma((count,) + s) for s in ((), (), (2,), (2,), (2,), (2,), (3,), (3,))
        ]

    def to_core(self, p):
        return remote(self.theirs(p), self.got.at[p], self.cs.at[p], self.cr.at[p], self.here.at_c)

    def first(self, p, way):
        h, half, tot = self.here, self.half, self.mine(p)
        if way == 0:
            return remote(tot.at[:, :, h.ox, :half], self.gx.at[p], self.fs.at[p, 0], self.fr.at[p, 0], h.at_x)
        return remote(tot.at[:, h.oy, :, half:], self.gy.at[p], self.fs.at[p, 1], self.fr.at[p, 1], h.at_y)

    def second(self, p, way):
        h, half, tot = self.here, self.half, self.mine(p)
        if way == 0:
            return remote(tot.at[:, h.oy, h.x, :half], self.hy.at[p], self.ss.at[p, 0], self.sr.at[p, 0], h.at_y)
        return remote(tot.at[:, h.y, h.ox, half:], self.hx.at[p], self.ss.at[p, 1], self.sr.at[p, 1], h.at_x)

    def over_z(self, p, k):
        h = self.here
        src = self.mine(p).at[h.ahead[k], h.y, h.x]
        return remote(src, self.gz.at[p, k - 1], self.zs.at[p, k - 1], self.zr.at[p, k - 1], h.at_z[k])

    def start(self, p):
        if self.load is not None:
            self.load(p).start()
        self.to_core(p).start()

    def cores(self, p):
        tot, got = self.mine(p), self.got.at[p]
        if self.load is not None:
            self.load(p).wait()
        self.to_core(p).wait_recv()

        @pl.loop(0, 16)
        def _(i):
            at = (i // 4, (i // 2) % 2, i % 2)
            tot[at] = tot[at] + got[at]

        self.first(p, 0).start()
        self.first(p, 1).start()

    def sides(self, p):
        h, half, tot = self.here, self.half, self.mine(p)
        gx, gy = self.gx.at[p], self.gy.at[p]
        self.first(p, 0).wait_recv()

        @pl.loop(0, 8)
        def _(i):
            zi, yi = i // 2, i % 2
            tot[zi, yi, h.x, :half] = tot[zi, yi, h.x, :half] + gx[zi, yi]

        self.second(p, 0).start()
        self.first(p, 1).wait_recv()

        @pl.loop(0, 8)
        def _(i):
            zi, xi = i // 2, i % 2
            tot[zi, h.y, xi, half:] = tot[zi, h.y, xi, half:] + gy[zi, xi]

        self.second(p, 1).start()

    def column(self, p):
        h, half, tot = self.here, self.half, self.mine(p)
        hx, hy = self.hx.at[p], self.hy.at[p]
        self.second(p, 0).wait_recv()
        self.second(p, 1).wait_recv()

        @pl.loop(0, 4)
        def _(zi):
            tot[zi, h.y, h.x, :half] = tot[zi, h.y, h.x, :half] + hy[zi]
            tot[zi, h.y, h.x, half:] = tot[zi, h.y, h.x, half:] + hx[zi]

        for k in (1, 2, 3):
            self.over_z(p, k).start()

    def finish(self, p):
        h, gz = self.here, self.gz.at[p]
        for k in (1, 2, 3):
            self.over_z(p, k).wait_recv()
        self.out(p)[...] = (self.mine(p)[h.z, h.y, h.x] + gz[0]) + (gz[1] + gz[2])

    def done(self, p):
        self.to_core(p).wait_send()
        for way in (0, 1):
            self.first(p, way).wait_send()
            self.second(p, way).wait_send()
        for k in (1, 2, 3):
            self.over_z(p, k).wait_send()

    def stages(self):
        return (self.start, self.cores, self.sides, self.column, self.finish)


def run(wave):
    for action in wave:
        action()


class Pace:
    def __init__(self, step, steps, lead, parts, waves):
        self.step, self.steps, self.lead, self.parts = step, steps, lead, parts
        ticks, total, before = lead + steps * parts, 1 + sum(len(w) for w in waves[1:]), 0
        self.waves = [[] for _ in range(ticks)]
        for wave in waves:
            self.waves[ticks * before // total] += wave
            before += len(wave) if before else 1

    def at_lead(self, i):
        run(self.waves[i])

    def at(self, part):
        for s in range(self.steps):
            now = self.waves[self.lead + s * self.parts + part]
            if now:
                pl.when(self.step == s)(functools.partial(run, now))


def run_last(step, steps, plan):
    @pl.when(step == steps - 1)
    def _():
        finish_all(plan)


WIDE = 768


def column_cuts(shards):
    return [(a, lo, min(lo + WIDE, s.shape[1])) for a, s in enumerate(shards) for lo in range(0, s.shape[1], WIDE)]


class GroupGather:
    def __init__(self, here, shards, fulls, sems):
        self.here, self.shards, self.fulls, self.count = here, shards, fulls, len(shards)
        self.loc, self.ss, self.rs = sems

    @staticmethod
    def semaphores(count):
        dma = pltpu.SemaphoreType.DMA
        return [dma((count,)), dma((count, 3)), dma((count, 3))]

    def local(self, a):
        h = self.here
        return pltpu.make_async_copy(self.shards[a], self.fulls[a].at[:, h.x * 2 + h.c], self.loc.at[a])

    def copy(self, a, i):
        h = self.here
        mine = self.fulls[a].at[:, h.x * 2 + h.c]
        if i < 2:
            return remote(self.shards[a], mine, self.ss.at[a, i], self.rs.at[a, i], (h.at_x, h.at_c)[i])
        block = self.fulls[a].at[:, h.ox * 2 + h.c]
        return remote(block, block, self.ss.at[a, 2], self.rs.at[a, 2], h.at_c)

    def start(self):
        for a in range(self.count):
            self.local(a).start()
            self.copy(a, 0).start()
            self.copy(a, 1).start()

    def forward(self):
        for a in range(self.count):
            self.copy(a, 0).wait_recv()
            self.copy(a, 2).start()

    def done(self):
        for a in range(self.count):
            self.local(a).wait()
            self.copy(a, 0).wait_send()
            self.copy(a, 1).wait()
            self.copy(a, 2).wait()


def flat_full(full):
    return full.reshape((-1, full.shape[-1]))


def full_shapes(shards):
    return [jax.ShapeDtypeStruct(GRID + s.shape, s.dtype) for s in shards]


def gather_kernel(count, cuts, *refs):
    here = Here()
    here.greet()
    plan = Gather(here, refs[:count], refs[count : 2 * count], cuts, refs[2 * count :])
    for wave in waves_of(plan, 2):
        run(wave)
    finish_all(plan)


def gather_all(shards, collective_id):
    count = len(shards)
    cuts = column_cuts(shards)
    outs = pl.pallas_call(
        functools.partial(gather_kernel, count, cuts),
        out_shape=full_shapes(shards),
        in_specs=[ANY] * count,
        out_specs=[ANY] * count,
        scratch_shapes=Gather.semaphores(len(cuts)),
        compiler_params=pltpu.CompilerParams(collective_id=collective_id, has_side_effects=True),
        name="gather_all",
    )(*shards)
    return [flat_full(o) for o in outs]


class Summed:
    def __init__(self, parts):
        self.arrays = len(parts)
        self.rows, self.width = parts[0].shape[0] // 32, parts[0].shape[1]
        self.cut = min(256, self.width)
        self.pieces = self.width // self.cut
        self.operands = [p.reshape(GRID + (self.rows, self.width)) for p in parts]
        self.in_specs = [ANY] * len(parts)
        self.out_shape = [jax.ShapeDtypeStruct((self.rows, self.width), F32)] * len(parts)
        self.out_specs = [whole((self.rows, self.width))] * len(parts)
        n = self.count = len(parts) * self.pieces
        self.scratch = [pltpu.VMEM((n, 4, 2, 2, self.rows, self.cut), F32), pltpu.SemaphoreType.DMA((n,))]
        self.scratch += Scatter.scratch(n, self.rows, self.cut)

    def bind(self, here, ins, outs, scratch):
        tots, loc = scratch[:2]

        def cut(p):
            lo = p % self.pieces * self.cut
            return p // self.pieces, slice(lo, lo + self.cut)

        def part(p, core):
            a, cols = cut(p)
            return ins[a].at[:, :, :, core, :, cols]

        def out(p):
            a, cols = cut(p)
            return outs[a].at[:, cols]

        return Scatter(
            here,
            self.count,
            lambda p: tots.at[p],
            lambda p: part(p, here.oc),
            lambda p: pltpu.make_async_copy(part(p, here.c), tots.at[p], loc.at[p]),
            out,
            scratch[2:],
        )


def scatter_kernel(plan, *refs):
    n = plan.arrays
    here = Here()
    here.greet()
    sums = plan.bind(here, refs[:n], refs[n : 2 * n], refs[2 * n :])
    for wave in waves_of(sums, sums.count):
        run(wave)
    finish_all(sums)


def scatter_all(parts, collective_id):
    plan = Summed(parts)
    return pl.pallas_call(
        functools.partial(scatter_kernel, plan),
        out_shape=plan.out_shape,
        in_specs=plan.in_specs,
        out_specs=[pl.BlockSpec(memory_space=pltpu.VMEM)] * len(parts),
        scratch_shapes=plan.scratch,
        compiler_params=pltpu.CompilerParams(
            collective_id=collective_id, has_side_effects=True, vmem_limit_bytes=60 * 2**20
        ),
        name="scatter_all",
    )(*plan.operands)


def greet(peers):
    barrier = pltpu.get_barrier_semaphore()
    for peer in peers:
        pl.semaphore_signal(barrier, inc=1, device_id=peer, device_id_type=MESH)
    pl.semaphore_wait(barrier, len(peers))


def group_gather_kernel(count, *refs):
    shards, fulls = refs[:count], refs[count : 2 * count]
    loc, ss, rs = refs[2 * count :]
    here = Here()
    x, c, ox, at_x, at_c = here.x, here.c, here.ox, here.at_x, here.at_c
    greet([at_x, at_c])
    waits = []
    for a in range(count):
        mine = fulls[a].at[:, x * 2 + c]
        copy = pltpu.make_async_copy(shards[a], mine, loc.at[a])
        copy.start()
        over = remote(shards[a], mine, ss.at[a, 0], rs.at[a, 0], at_x)
        over.start()
        side = remote(shards[a], mine, ss.at[a, 1], rs.at[a, 1], at_c)
        side.start()
        waits.append((copy, over, side))
    last = []
    for a in range(count):
        waits[a][1].wait_recv()
        block = fulls[a].at[:, ox * 2 + c]
        on = remote(block, block, ss.at[a, 2], rs.at[a, 2], at_c)
        on.start()
        last.append(on)
    for a in range(count):
        copy, over, side = waits[a]
        copy.wait()
        over.wait_send()
        side.wait()
        last[a].wait()


def group_gather(shards, collective_id):
    count = len(shards)
    dma = pltpu.SemaphoreType.DMA
    return pl.pallas_call(
        functools.partial(group_gather_kernel, count),
        out_shape=[jax.ShapeDtypeStruct((s.shape[0], 4) + s.shape[1:], F32) for s in shards],
        in_specs=[ANY] * count,
        out_specs=[ANY] * count,
        scratch_shapes=[dma((count,)), dma((count, 3)), dma((count, 3))],
        compiler_params=pltpu.CompilerParams(collective_id=collective_id, has_side_effects=True),
        name="group_gather",
    )(*shards)


def group_swap_kernel(count, *refs):
    shards, fulls = refs[:count], refs[count : 2 * count]
    loc, ss, rs = refs[2 * count :]
    here = Here()
    z, y, x, c = here.z, here.y, here.x, here.c
    me = x * 2 + c
    peers = [(x, 1 - c), (1 - x, c), (1 - x, 1 - c)]
    greet([place(z, y, *p) for p in peers])
    waits = []
    for a in range(count):
        copy = pltpu.make_async_copy(shards[a].at[:, me], fulls[a].at[:, me], loc.at[a])
        copy.start()
        waits.append(copy)
        for k in (1, 2, 0):
            px, pc = peers[k]
            on = remote(
                shards[a].at[:, px * 2 + pc], fulls[a].at[:, me], ss.at[a, k], rs.at[a, k], place(z, y, px, pc)
            )
            on.start()
            waits.append(on)
    for copy in waits:
        copy.wait()


def group_swap(shards, collective_id):
    count = len(shards)
    dma = pltpu.SemaphoreType.DMA
    return pl.pallas_call(
        functools.partial(group_swap_kernel, count),
        out_shape=[jax.ShapeDtypeStruct(s.shape, F32) for s in shards],
        in_specs=[ANY] * count,
        out_specs=[ANY] * count,
        scratch_shapes=[dma((count,)), dma((count, 3)), dma((count, 3))],
        compiler_params=pltpu.CompilerParams(collective_id=collective_id, has_side_effects=True),
        name="group_swap",
    )(*shards)


def group_sum_kernel(parts, out, tot, got, last, loc, ss, rs):
    here = Here()
    greet([here.at_x, here.at_c])
    load = pltpu.make_async_copy(parts.at[:, :, here.c], tot, loc.at[0])
    load.start()
    side = remote(parts.at[:, :, here.oc], got, ss.at[0], rs.at[0], here.at_c)
    side.start()
    load.wait()
    side.wait_recv()
    tot[...] += got[...]
    over = remote(tot.at[:, here.ox], last, ss.at[1], rs.at[1], here.at_x)
    over.start()
    over.wait_recv()
    out[...] = tot[:, here.x] + last[...]
    side.wait_send()
    over.wait_send()


def group_sum(parts, collective_id):
    s, lat, w = parts.shape
    r = lat // 4
    dma = pltpu.SemaphoreType.DMA
    return pl.pallas_call(
        group_sum_kernel,
        out_shape=jax.ShapeDtypeStruct((s, r, w), F32),
        in_specs=[ANY],
        out_specs=pl.BlockSpec(memory_space=pltpu.VMEM),
        scratch_shapes=[
            pltpu.VMEM((s, 2, r, w), F32),
            pltpu.VMEM((s, 2, r, w), F32),
            pltpu.VMEM((s, r, w), F32),
            dma((1,)),
            dma((2,)),
            dma((2,)),
        ],
        compiler_params=pltpu.CompilerParams(collective_id=collective_id, has_side_effects=True),
        name="group_sum",
    )(parts.reshape(s, 2, 2, r, w))


def stacked(values, axis, order):
    top = lax.reduce_precision(values, 8, 7)
    terms = (top.astype(jnp.bfloat16), (values - top).astype(jnp.bfloat16))
    return jnp.concatenate([terms[i] for i in order], axis=axis)


def thin_product(left, right):
    return lax.dot_general(
        stacked(left, 0, (0, 0, 1)), stacked(right, 0, (0, 1, 0)), (((0,), (0,)), ((), ())), preferred_element_type=F32
    )


BF16 = jnp.bfloat16
HIGH = lax.Precision.HIGH
BLOCK = 256


def dot(left, right, dims=(1, 0)):
    return lax.dot_general(
        left, right, (((dims[0],), (dims[1],)), ((), ())), precision=HIGH, preferred_element_type=F32
    )


def dot3(left, right, dims=(1, 0)):
    numbers = (((dims[0],), (dims[1],)), ((), ()))
    one = functools.partial(lax.dot_general, dimension_numbers=numbers, preferred_element_type=F32)
    return one(left[0], right[0]) + (one(left[0], right[1]) + one(left[1], right[0]))


def halves(values):
    top = values.astype(BF16)
    return top, (values - top.astype(F32)).astype(BF16)


def split_weights(sources, pairs, stage, sems, pace):
    step = stage.shape[1]
    chunks = [(i, r) for i, s in enumerate(sources) for r in range(0, s.shape[0], step)]

    def copy(n):
        i, r = chunks[n]
        return pltpu.make_async_copy(sources[i].at[r : r + step], stage.at[n % 2], sems.at[n % 2])

    copy(0).start()
    for n, (i, r) in enumerate(chunks):
        if n * pace.lead % len(chunks) == 0:
            pace.at_lead(n * pace.lead // len(chunks))
        if n + 1 < len(chunks):
            copy(n + 1).start()
        copy(n).wait()
        pairs[i][0][r : r + step], pairs[i][1][r : r + step] = halves(stage[n % 2])


def unit_of(values):
    centred = values - jnp.mean(values, axis=-1, keepdims=True)
    inv_std = lax.rsqrt(jnp.mean(centred * centred, axis=-1, keepdims=True) + EPSILON)
    return centred * inv_std, inv_std


def staging(width):
    return [pltpu.VMEM((width, width), BF16)] * 4 + [pltpu.VMEM((2, 128, width), F32), pltpu.SemaphoreType.DMA((2,))]


def whole(shape, buffers=1):
    return pl.BlockSpec(shape, lambda *i: (0,) * len(shape), pipeline_mode=pl.Buffered(buffers))


def opening_kernel(cuts, *refs):
    times, feats, latents = refs[:3]
    shards, group_shard = refs[3:9], refs[9:10]
    vec, keys, values, own_keys, own_values, queries, xt_top, xt_low = refs[10:18]
    fulls, group_full = refs[18:24], refs[24:25]
    pk, top, low, own_top, own_low, lat, lat_top, lat_low, stage, load = refs[25:35]
    step = pl.program_id(0)
    here = Here()
    vectors = Gather(here, shards[:1], fulls[:1], [(0, 0, 128)], refs[35:46])
    moved = Gather(here, shards[1:], fulls[1:], cuts, refs[46:57])
    group = GroupGather(here, group_shard, group_full, refs[57:])
    waves = waves_of(moved, 2)
    cut = keys.shape[1]
    slots, chunks = top.shape[0] // BLOCK, shards[1].shape[1] // cut

    def start():
        here.greet()
        vectors.own(0)
        run(waves[0])
        group.start()
        vectors.along_z(0)
        vectors.across(0)
        vectors.corner(0)
        vectors.arrived(0)
        copy = pltpu.make_async_copy(fulls[0], pk, load.at[0])
        copy.start()
        copy.wait()
        strip = shards[1].shape[0]
        vec[...] = jnp.concatenate([pk[i // 8, i // 4 % 2, i // 2 % 2, i % 2][:, :strip] for i in range(32)], axis=1)
        own_top[...], own_low[...] = halves(unit_of(latents[...])[0] * vec[2:3] + vec[3:4])
        run(waves[1])
        group.forward()

    pl.when(step == 0)(start)
    at_step = {2: 2, 4: 3, 5: 4, slots + 1: 5, slots + 2: 6, slots + 4: 7, slots + 5: 8}
    ending, late = len(waves) - 9, slots + chunks + 1
    at_step = {s: waves[w] for s, w in at_step.items()}
    for i in range(5):
        at_step[late + i] = sum(waves[9 + ending * i // 5 : 9 + ending * (i + 1) // 5], [])
    for s, wave in at_step.items():
        pl.when(step == s)(functools.partial(run, wave))

    @pl.when(step < slots)
    def _():
        embed = vec[pl.ds(6 + times[step], 1)]
        normed = unit_of(feats[...] + embed)[0] * vec[0:1] + vec[1:2]
        rows = pl.ds(pl.multiple_of(step * BLOCK, BLOCK), BLOCK)
        top[rows], low[rows] = halves(normed)
        xt_top[...], xt_low[...] = halves(jnp.swapaxes(normed, 0, 1))

    def chunk(array, n, left, right, out, own_out):
        cols = pl.ds(pl.multiple_of(n * cut, cut), cut)
        copy = pltpu.make_async_copy(fulls[array].at[:, :, :, :, :, cols], stage.at[array % 2], load.at[0])
        copy.start()
        copy.wait()
        pair = halves(stage[array % 2].reshape((-1, cut)))
        step_rows = min(512, left.shape[0])

        @pl.loop(0, left.shape[0] // step_rows)
        def _(m):
            rows = pl.ds(pl.multiple_of(m * step_rows, step_rows), step_rows)
            out[rows] = dot3((left[rows], right[rows]), pair)

        if own_out is not None:
            own_out[...] = dot3((own_top[...], own_low[...]), pair)

    half = chunks // 2
    for first in (0, 1):

        @pl.when(step == slots + first * half)
        def _():
            moved.arrived(2 * first)
            moved.arrived(2 * first + 1)

    @pl.when((step >= slots) & (step < slots + chunks))
    def _():
        chunk(1, step - slots, top, low, keys, own_keys)
        chunk(2, step - slots, top, low, values, own_values)

    @pl.when(step == slots + chunks)
    def _():
        moved.arrived(4)
        moved.arrived(5)
        group.done()
        copy = pltpu.make_async_copy(group_full[0], lat, load.at[0])
        copy.start()
        copy.wait()
        lat_top[...], lat_low[...] = halves(unit_of(lat[...].reshape(lat_top.shape))[0] * vec[2:3] + vec[3:4])

    @pl.when(step >= slots + chunks)
    def _():
        chunk(3, step - slots - chunks, lat_top, lat_low, queries, None)

    @pl.when(step == slots + 2 * chunks - 1)
    def _():
        vectors.done(0, True)
        for p in range(moved.count):
            moved.done(p, p < 6)


def opening(times, feats, latents, packed, key_w, value_w, query_w, cot, out_w, collective_id):
    rows, width = feats.shape
    seqs, own_each, _ = latents.shape
    own_rows, lat_rows = seqs * own_each, seqs * own_each * 4
    slots, cut = rows // BLOCK, 256
    chunks = width // cut
    shards = [packed, key_w, value_w, query_w, cot, out_w]
    cuts = [(a, lo, lo + WIDE) for lo in range(0, width, WIDE) for a in (0, 1)]
    cuts += [(a, lo, lo + WIDE) for a in (2, 3) for lo in range(0, width, WIDE)]
    cuts += [(4, lo, lo + cut) for lo in range(0, width, cut)]
    clip = lambda i, lo: jnp.clip(i - lo, 0, chunks - 1)
    chunk_of = lambda n, lo: pl.BlockSpec((n, cut), lambda i: (0, clip(i, lo)))
    turned = pl.BlockSpec((width, BLOCK), lambda i: (0, jnp.minimum(i, slots - 1)))
    full = lambda n, kind=F32: jax.ShapeDtypeStruct((n, width), kind)
    outs = pl.pallas_call(
        functools.partial(opening_kernel, cuts),
        grid=(slots + 2 * chunks,),
        in_specs=[
            SMEM,
            pl.BlockSpec((BLOCK, width), lambda i: (jnp.minimum(i, slots - 1), 0)),
            whole((own_rows, width)),
        ]
        + [ANY] * 7,
        out_specs=[
            whole((16, width)),
            chunk_of(rows, slots),
            chunk_of(rows, slots),
            chunk_of(own_rows, slots),
            chunk_of(own_rows, slots),
            chunk_of(lat_rows, slots + chunks),
            turned,
            turned,
        ]
        + [ANY] * 7,
        out_shape=[full(16), full(rows), full(rows), full(own_rows), full(own_rows), full(lat_rows)]
        + [jax.ShapeDtypeStruct((width, rows), BF16)] * 2
        + full_shapes(shards)
        + [jax.ShapeDtypeStruct((seqs, 4, own_each, width), F32)],
        scratch_shapes=[
            pltpu.VMEM(GRID + packed.shape, F32),
            pltpu.VMEM((rows, width), BF16),
            pltpu.VMEM((rows, width), BF16),
            pltpu.VMEM((own_rows, width), BF16),
            pltpu.VMEM((own_rows, width), BF16),
            pltpu.VMEM((seqs, 4, own_each, width), F32),
            pltpu.VMEM((lat_rows, width), BF16),
            pltpu.VMEM((lat_rows, width), BF16),
            pltpu.VMEM((2,) + GRID + (width // 32, cut), F32),
            pltpu.SemaphoreType.DMA((1,)),
        ]
        + Gather.semaphores(1)
        + Gather.semaphores(len(cuts))
        + GroupGather.semaphores(1),
        compiler_params=pltpu.CompilerParams(
            collective_id=collective_id, has_side_effects=True, vmem_limit_bytes=60 * 2**20
        ),
        name="opening",
    )(times, feats, latents.reshape(own_rows, width), *shards, latents)
    return outs[:8], [flat_full(o) for o in outs[9:14]], outs[14]


def pair_rows(values, first, head):
    lane = lax.broadcasted_iota(jnp.int32, values.shape, 1)
    return jnp.concatenate(
        [
            jnp.where((lane >= first) & (lane < first + head), values, 0.0),
            jnp.where((lane >= first + head) & (lane < first + 2 * head), values, 0.0),
        ],
        axis=0,
    )


def pair_merge(stacked, first, head):
    half = stacked.shape[0] // 2
    lane = lax.broadcasted_iota(jnp.int32, (half, stacked.shape[1]), 1)
    one = jnp.where((lane >= first) & (lane < first + head), stacked[:half], 0.0)
    return one + jnp.where((lane >= first + head) & (lane < first + 2 * head), stacked[half:], 0.0)


def join(left, right):
    return jnp.concatenate([left[:, :128], left[:, 128:] + right[:, :128], right[:, 128:]], axis=1)


def windows(head):
    return ((slice(0, 256), 0), (slice(128, 384), 2 * head - 128))


def score_block(present, seq, keys, own_keys, q_pair, window, inv_root):
    at = keys.shape[0]
    scores = jnp.concatenate([dot(keys[:, window], q_pair, (1, 1)), dot(own_keys[:, window], q_pair, (1, 1))], axis=0)
    row = lax.broadcasted_iota(jnp.int32, scores.shape, 0)
    keep = (row >= at) | ((row < at // 2) & (present[seq, 0] > 0)) | ((row >= at // 2) & (present[seq, 1] > 0))
    return jnp.where(keep, scores * inv_root, MASKED)


def attend_kernel(inv_root, head, present, queries, keys, values, own_keys, own_values, out, tops, sums):
    seq, group = pl.program_id(0), pl.program_id(1)
    merged = []
    for p, (window, first) in enumerate(windows(head)):
        q_pair = pair_rows(queries[:, window], first, head)
        scores = score_block(present, seq, keys, own_keys, q_pair, window, inv_root)
        top = jnp.max(scores, axis=0, keepdims=True)
        expo = jnp.exp(scores - top)
        tops[pl.ds(group * 2 + p, 1)] = top
        sums[pl.ds(group * 2 + p, 1)] = jnp.sum(expo, axis=0, keepdims=True)
        at = keys.shape[0]
        stacked = dot(expo[:at], values[:, window], (0, 0)) + dot(expo[at:], own_values[:, window], (0, 0))
        merged.append(pair_merge(stacked, first, head))
    out[...] = join(*merged)


def attend_specs(lat, media, rows):
    group = 384
    query = pl.BlockSpec((None, lat, group), lambda b, g: (b, 0, g))
    key = pl.BlockSpec((media, group), lambda b, g: (b, g))
    own = pl.BlockSpec((rows, group), lambda b, g: (b, g))
    stat = pl.BlockSpec((None, 8, 128), lambda b, g: (b, 0, 0))
    return query, key, own, stat


SMEM = pl.BlockSpec(memory_space=pltpu.SMEM)


def attend(present, queries, keys, values, own_keys, own_values):
    seqs, lat, width = queries.shape
    head = width // HEADS
    query, key, own, stat = attend_specs(lat, keys.shape[0] // seqs, own_keys.shape[0] // seqs)
    stat_shape = jax.ShapeDtypeStruct((seqs, 8, 128), F32)
    return pl.pallas_call(
        functools.partial(attend_kernel, 1.0 / math.sqrt(head), head),
        grid=(seqs, width // 384),
        in_specs=[SMEM, query, key, key, own, own],
        out_specs=[query, stat, stat],
        out_shape=[jax.ShapeDtypeStruct(queries.shape, F32), stat_shape, stat_shape],
        compiler_params=pltpu.CompilerParams(vmem_limit_bytes=60 * 2**20),
        name="attend",
    )(present, queries, keys, values, own_keys, own_values)


def attend_back_kernel(inv_root, head, plan, steps, *refs):
    present, queries, grads, logs, deltas, keys, values, own_keys, own_values = refs[:9]
    n = plan.arrays
    query_out, key_out, value_out, own_key_out, own_value_out = refs[9 + n : 14 + n]
    seq, group = pl.program_id(0), pl.program_id(1)
    step = seq * pl.num_programs(1) + group
    here = Here()
    moved = plan.bind(here, refs[9 : 9 + n], refs[14 + n : 14 + 2 * n], refs[14 + 2 * n :])
    waves = waves_of(moved, moved.count)
    waves[0].insert(0, here.greet)
    pace = Pace(step, steps, 0, 2, waves)
    merged, key_grads, value_grads = [], [], []
    at = keys.shape[0]
    for p, (window, first) in enumerate(windows(head)):
        pace.at(p)
        q_pair = pair_rows(queries[:, window], first, head)
        g_pair = pair_rows(grads[:, window], first, head)
        scores = score_block(present, seq, keys, own_keys, q_pair, window, inv_root)
        probs = jnp.exp(scores - logs[pl.ds(group * 2 + p, 1)])
        grad_probs = jnp.concatenate(
            [dot(values[:, window], g_pair, (1, 1)), dot(own_values[:, window], g_pair, (1, 1))], axis=0
        )
        grad_scores = probs * (grad_probs - deltas[pl.ds(group * 2 + p, 1)]) * inv_root
        stacked = dot(grad_scores[:at], keys[:, window], (0, 0)) + dot(grad_scores[at:], own_keys[:, window], (0, 0))
        merged.append(pair_merge(stacked, first, head))
        key_grads.append(dot(grad_scores, q_pair))
        value_grads.append(dot(probs, g_pair))
    query_out[...] = join(*merged)
    key_grad, value_grad = join(*key_grads), join(*value_grads)
    key_out[...], own_key_out[...] = key_grad[:at], key_grad[at:]
    value_out[...], own_value_out[...] = value_grad[:at], value_grad[at:]
    run_last(step, steps, moved)


def attend_back(present, queries, grads, logs, deltas, keys, values, own_keys, own_values, plan, collective_id):
    seqs, lat, width = queries.shape
    head = width // HEADS
    query, key, own, stat = attend_specs(lat, keys.shape[0] // seqs, own_keys.shape[0] // seqs)
    shape = lambda v: jax.ShapeDtypeStruct(v.shape, F32)
    grid = (seqs, width // 384)
    outs = pl.pallas_call(
        functools.partial(attend_back_kernel, 1.0 / math.sqrt(head), head, plan, grid[0] * grid[1]),
        grid=grid,
        in_specs=[SMEM, query, query, stat, stat, key, key, own, own] + plan.in_specs,
        out_specs=[query, key, key, own, own] + plan.out_specs,
        out_shape=[shape(queries), shape(keys), shape(values), shape(own_keys), shape(own_values)] + plan.out_shape,
        scratch_shapes=plan.scratch,
        compiler_params=pltpu.CompilerParams(
            collective_id=collective_id, has_side_effects=True, vmem_limit_bytes=60 * 2**20
        ),
        name="attend_back",
    )(present, queries, grads, logs, deltas, keys, values, own_keys, own_values, *plan.operands)
    return outs[:5], outs[5:]


def weight_kernel(steps, xt_top, xt_low, own_t, grad_keys, grad_values, own_gk, own_gv, vec, outs, vec_out, mats, *rest):
    n = pl.program_id(0)
    here = Here()
    cut = grad_keys.shape[1]
    sums = Scatter(
        here,
        2 * steps,
        lambda p: mats.at[p, :, :, :, here.c],
        lambda p: mats.at[p, :, :, :, here.oc],
        None,
        lambda p: outs.at[p % 2, :, pl.ds(pl.multiple_of(p // 2 * cut, cut), cut)],
        rest[:14],
    )
    tot, loc = rest[14:16]
    small = Scatter(
        here,
        1,
        lambda p: tot,
        lambda p: vec.at[:, :, :, here.oc],
        lambda p: pltpu.make_async_copy(vec.at[:, :, :, here.c], tot, loc.at[p]),
        lambda p: vec_out,
        rest[16:],
    )
    stages = sums.stages()

    @pl.when(n == 0)
    def _():
        here.greet()

    for w, (grad, own_grad) in enumerate(((grad_keys, own_gk), (grad_values, own_gv))):
        pair = halves(grad[...])
        top, low = halves(own_grad[...])
        stacked = jnp.concatenate([top, low, top], axis=0)

        @pl.loop(0, 2)
        def _(i):
            rows = pl.ds(pl.multiple_of(i * 768, 768), 768)
            made = dot3((xt_top[rows], xt_low[rows]), pair)
            made += jnp.dot(own_t[rows], stacked, preferred_element_type=F32)
            mats[2 * n + w, pl.ds(i * 2, 2)] = made.reshape((2, 2, 2, 2, 48, cut))

        sums.start(2 * n + w)
        for s in (1, 2, 3, 4):
            p = 2 * n + w - s

            @pl.when(p >= 0)
            def _():
                stages[s](p)

        if w == 1:
            for s in range(5):

                @pl.when(n == s)
                def _():
                    small.stages()[s](0)

    @pl.when(n == steps - 1)
    def _():
        for t in range(2 * steps, 2 * steps + 4):
            for s in (1, 2, 3, 4):
                if t - s < 2 * steps:
                    stages[s](t - s)

        @pl.loop(0, 2 * steps)
        def _(p):
            sums.done(p)

        small.done(0)


def weight_grads(xt_top, xt_low, own_t, grad_keys, grad_values, own_gk, own_gv, vec, collective_id):
    width, rows = xt_top.shape
    own_rows = own_gk.shape[0]
    steps = width // BLOCK
    cols = lambda n: pl.BlockSpec((n, BLOCK), lambda i: (0, i))
    r = width // 32
    vr, vw = vec.shape[0] // 32, vec.shape[1]
    outs, vec_sum = pl.pallas_call(
        functools.partial(weight_kernel, steps),
        grid=(steps,),
        in_specs=[
            whole((width, rows)),
            whole((width, rows)),
            whole(own_t.shape),
            cols(rows),
            cols(rows),
            cols(own_rows),
            cols(own_rows),
            ANY,
        ],
        out_specs=[whole((2, r, width)), whole((vr, vw))],
        out_shape=[jax.ShapeDtypeStruct((2, r, width), F32), jax.ShapeDtypeStruct((vr, vw), F32)],
        scratch_shapes=[pltpu.VMEM((2 * steps,) + GRID + (r, BLOCK), F32)]
        + Scatter.scratch(2 * steps, r, BLOCK)
        + [pltpu.VMEM((4, 2, 2, vr, vw), F32), pltpu.SemaphoreType.DMA((1,))]
        + Scatter.scratch(1, vr, vw),
        compiler_params=pltpu.CompilerParams(
            collective_id=collective_id, has_side_effects=True, vmem_limit_bytes=62 * 2**20
        ),
        name="weight_grads",
    )(xt_top, xt_low, own_t, grad_keys, grad_values, own_gk, own_gv, vec.reshape(GRID + (vr, vw)))
    return outs[0], outs[1], vec_sum


def media_back_kernel(plan, steps, *refs):
    feats, embed, gain, grad_keys, grad_values, own_gk, own_gv, key_w, value_w = refs[:9]
    n = plan.arrays
    out, own_out, sums = refs[9 + n : 12 + n]
    kt, kl, vt, vl, stage, sems = refs[12 + 2 * n : 18 + 2 * n]
    step = pl.program_id(0)
    here = Here()
    moved = plan.bind(here, refs[9 : 9 + n], refs[12 + n : 12 + 2 * n], refs[18 + 2 * n :])
    waves = waves_of(moved, moved.count)
    waves[0].insert(0, here.greet)
    pace = Pace(step, steps, 4, 3, waves)

    @pl.when(step == 0)
    def _():
        split_weights((key_w, value_w), ((kt, kl), (vt, vl)), stage, sems, pace)
        own_out[...] = dot3(halves(own_gk[...]), (kt[...], kl[...]), (1, 1)) + dot3(
            halves(own_gv[...]), (vt[...], vl[...]), (1, 1)
        )
        sums[...] = jnp.zeros_like(sums)

    key_pair, value_pair = halves(grad_keys[...]), halves(grad_values[...])
    for i in range(3):
        pace.at(i)
        rows = slice(i * 512, i * 512 + 512)
        out[:, rows] = dot3(key_pair, (kt[rows], kl[rows]), (1, 1)) + dot3(value_pair, (vt[rows], vl[rows]), (1, 1))
    strip = 64

    @pl.loop(0, out.shape[0] // strip)
    def _(i):
        rows = pl.ds(pl.multiple_of(i * strip, strip), strip)
        incoming = out[rows]
        unit, inv_std = unit_of(feats[rows] + embed[...])
        sums[pl.ds(0, 1)] += jnp.sum(incoming * unit, axis=0, keepdims=True)
        sums[pl.ds(1, 1)] += jnp.sum(incoming, axis=0, keepdims=True)
        scaled = incoming * gain[...]
        result = inv_std * (
            scaled
            - jnp.mean(scaled, axis=-1, keepdims=True)
            - unit * jnp.mean(scaled * unit, axis=-1, keepdims=True)
        )
        out[rows] = result
        sums[pl.ds(2 + step, 1)] += jnp.sum(result, axis=0, keepdims=True)

    run_last(step, steps, moved)


def media_backward(feats, embed, gain, grad_keys, grad_values, own_gk, own_gv, key_w, value_w, plan, collective_id):
    rows, width = feats.shape
    own_rows = own_gk.shape[0]
    row_block = pl.BlockSpec((BLOCK, width), lambda i: (i, 0))
    one_block = pl.BlockSpec((BLOCK, width), lambda i: (i, 0), pipeline_mode=pl.Buffered(1))
    steps = rows // BLOCK
    outs = pl.pallas_call(
        functools.partial(media_back_kernel, plan, steps),
        grid=(steps,),
        in_specs=[
            one_block,
            pl.BlockSpec((None, 1, width), lambda i: (i, 0, 0)),
            whole((1, width)),
            row_block,
            row_block,
            whole((own_rows, width)),
            whole((own_rows, width)),
            ANY,
            ANY,
        ]
        + plan.in_specs,
        out_specs=[one_block, whole((own_rows, width)), whole((8, width))] + plan.out_specs,
        out_shape=[
            jax.ShapeDtypeStruct((rows, width), F32),
            jax.ShapeDtypeStruct((own_rows, width), F32),
            jax.ShapeDtypeStruct((8, width), F32),
        ]
        + plan.out_shape,
        scratch_shapes=staging(width) + plan.scratch,
        compiler_params=pltpu.CompilerParams(
            collective_id=collective_id, has_side_effects=True, vmem_limit_bytes=64 * 2**20 - 2**16
        ),
        name="media_backward",
    )(feats, embed, gain, grad_keys, grad_values, own_gk, own_gv, key_w, value_w, *plan.operands)
    return outs[:3], outs[3:]


GELU_A = math.sqrt(2.0 / math.pi)
GELU_B = 0.044715


def feed_kernel(blocks, *refs):
    feed, cot, up, down, new_part, grad_up_t, grad_down, out, act, back, mats = refs[:11]
    step = pl.program_id(0)
    here = Here()
    pieces, cut = mats.shape[0], mats.shape[-1]
    sums = Scatter(
        here,
        pieces,
        lambda p: mats.at[p, :, :, :, here.c],
        lambda p: mats.at[p, :, :, :, here.oc],
        None,
        lambda p: out.at[:, p * cut : (p + 1) * cut],
        refs[11:],
    )
    waves = waves_of(sums, pieces)
    block = step - blocks * (step >= blocks).astype(jnp.int32)
    rows = pl.ds(pl.multiple_of(block * BLOCK, BLOCK), BLOCK)
    pl.when(step == 0)(here.greet)

    @pl.when(step < blocks)
    def _():
        hidden = dot(feed[...], up[...])
        grad_act = dot(cot[...], down[...], (1, 1))
        square = hidden * hidden
        bent = jnp.tanh(GELU_A * (hidden + GELU_B * hidden * square))
        slope = 0.5 * (1.0 + bent) + 0.5 * hidden * (1.0 - bent * bent) * (GELU_A * (1.0 + 3.0 * GELU_B * square))
        act[rows] = 0.5 * hidden * (1.0 + bent)
        back[rows] = grad_act * slope

    @pl.when(step == blocks)
    def _():
        for p in range(pieces):

            @pl.loop(0, 4)
            def _(zi):
                plane = pl.ds(pl.multiple_of(zi * 384, 384), 384)
                made = dot(back[plane], up[p * cut : (p + 1) * cut], (1, 1))
                mats[p, zi] = made.reshape((2, 2, 2, 48, cut))

            sums.start(p)
        grad_up_t[...] = jnp.zeros_like(grad_up_t)
        grad_down[...] = jnp.zeros_like(grad_down)

    for i in range(blocks):

        @pl.when(step == blocks + i)
        def _():
            for wave in waves[1 + 2 * i : 3 + 2 * i]:
                run(wave)

    @pl.when(step >= blocks)
    def _():
        new_part[...] = dot(act[rows], down[...])
        grad_up_t[...] += dot(back[rows], feed[...], (0, 0))
        grad_down[...] += dot(act[rows], cot[...], (0, 0))

    @pl.when(step == 2 * blocks - 1)
    def _():
        for wave in waves[1 + 2 * blocks :]:
            run(wave)
        finish_all(sums)


def feed_forward(feed, cot, up, down, collective_id):
    rows, width = feed.shape
    units, r, cut = up.shape[1], width // 32, 256
    blocks = rows // BLOCK
    big = jax.ShapeDtypeStruct((rows, width), F32)
    slim = jax.ShapeDtypeStruct((units, width), F32)
    row_block = pl.BlockSpec((BLOCK, width), lambda i: (i % blocks, 0))
    late_block = pl.BlockSpec((BLOCK, width), lambda i: (jnp.maximum(i - blocks, 0), 0))
    return pl.pallas_call(
        functools.partial(feed_kernel, blocks),
        grid=(2 * blocks,),
        in_specs=[row_block, row_block, whole((width, units)), whole((units, width))],
        out_specs=[late_block, whole((units, width)), whole((units, width)), whole((r, width))],
        out_shape=[big, slim, slim, jax.ShapeDtypeStruct((r, width), F32)],
        scratch_shapes=[pltpu.VMEM((rows, units), F32)] * 2
        + [pltpu.VMEM((width // cut,) + GRID + (r, cut), F32)]
        + Scatter.scratch(width // cut, r, cut),
        compiler_params=pltpu.CompilerParams(
            collective_id=collective_id, has_side_effects=True, vmem_limit_bytes=60 * 2**20
        ),
        name="feed_forward",
    )(feed, cot, up, down)


def mm(left, right):
    return jnp.dot(left, right, precision=HIGH, preferred_element_type=F32)


def mm_tn(left, right):
    return lax.dot_general(left, right, (((0,), (0,)), ((), ())), precision=HIGH, preferred_element_type=F32)


def mm_nt(left, right):
    return lax.dot_general(left, right, (((1,), (1,)), ((), ())), precision=HIGH, preferred_element_type=F32)


def body_fast(
    latents,
    patch_feats,
    image_counts,
    time_index,
    query_proj,
    key_proj,
    value_proj,
    out_proj,
    up_proj,
    down_proj,
    media_gain,
    media_bias,
    latent_gain,
    latent_bias,
    feed_gain,
    feed_bias,
    time_table,
    out_cotangent,
):
    frame = lax.axis_index("frame")
    frames = lax.axis_size("frame")
    seqs, rows, width = latents.shape
    rounds, patches = patch_feats.shape[1], patch_feats.shape[3]
    lat = rows * frames
    head = width // HEADS
    strip = media_gain.shape[0]

    vectors = jnp.concatenate(
        [jnp.stack([media_gain, media_bias, latent_gain, latent_bias, feed_gain, feed_bias]), time_table], axis=0
    )
    packed = jnp.pad(vectors, ((0, 2), (0, 128 - strip)))
    slot_ids = jnp.arange(rounds, dtype=jnp.int32) * frames + frame
    present = slot_ids[None, :] < image_counts[:, None]
    picks = jnp.arange(time_index.shape[1], dtype=jnp.int32)[None, :] == slot_ids[:, None]
    slot_times = jnp.sum(jnp.where(picks[None, :, :], time_index[:, None, :], 0), axis=-1)
    feats = patch_feats.reshape(-1, width)

    (vec_all, keys, values, own_keys, own_values, queries, xt_top, xt_low), gathered, lat_blocks = opening(
        slot_times.reshape(-1), feats, latents, packed, key_proj, value_proj, query_proj, flatten(out_cotangent), out_proj, 0
    )
    key_w, value_w, query_w, cot_all, out_w = gathered
    up_held, keys = lax.optimization_barrier((up_proj, keys))
    up_cols = lax.all_to_all(
        up_held.reshape(strip, 32, -1), ("seq", "frame"), split_axis=1, concat_axis=0, tiled=True
    ).reshape(width, -1)
    mgain, mbias, lgain, lbias, fgain, fbias = (vec_all[i] for i in range(6))
    table = vec_all[6:14]
    queries = queries.reshape(seqs, lat, width)
    latent_norm, latent_unit, latent_std = norm_forward(lat_blocks.reshape(seqs, lat, width), lgain, lbias)
    own_rows = lambda v: lax.dynamic_slice_in_dim(v, frame * rows, rows, 1)
    own_norm, own_unit, own_std = own_rows(latent_norm), own_rows(latent_unit), own_rows(latent_std)
    one_hot = slot_times[:, :, None] == jnp.arange(time_table.shape[0], dtype=jnp.int32)
    slot_embed = jnp.sum(jnp.where(one_hot[..., None], table, 0.0), axis=2)
    embed = slot_embed.reshape(-1, 1, width)
    own_flat = flatten(own_norm)
    present = present.astype(jnp.int32)

    partial, row_top, row_sum = attend(present, queries, keys, values, own_keys, own_values)
    stats = jnp.concatenate([row_top.reshape(seqs, HEADS, lat), row_sum.reshape(seqs, HEADS, lat)], axis=1)
    stats = jnp.pad(stats.transpose(0, 2, 1), ((0, 0), (0, 0), (0, 128 - 2 * HEADS)))
    part_all, stat_all = group_swap(
        [partial.reshape(seqs, frames, rows, width), stats.reshape(seqs, frames, rows, 128)], 2
    )
    tops, sums = stat_all[..., :HEADS], stat_all[..., HEADS : 2 * HEADS]
    top = jnp.max(tops, axis=1)
    ratio = jnp.exp(tops - top[:, None])
    row_total = jnp.sum(sums * ratio, axis=1)
    weight = ratio / row_total[:, None]
    attended = jnp.sum(part_all.reshape(seqs, frames, rows, HEADS, head) * weight[..., None], axis=1)
    log_total = top + jnp.log(row_total)
    attended_flat = attended.reshape(seqs, rows, width)
    middle = latents + mm(flatten(attended_flat), out_w).reshape(seqs, rows, width)

    feed_norm, feed_unit, feed_std = norm_forward(middle, fgain, fbias)
    (feed_all,) = gather_all([flatten(feed_norm)], 3)
    new_part, grad_up_t, grad_down, grad_feed_norm = feed_forward(feed_all, cot_all, up_cols, down_proj, 4)
    grad_up = lax.all_to_all(
        grad_up_t.reshape(-1, 32, strip).transpose(1, 2, 0), ("seq", "frame"), split_axis=0, concat_axis=2, tiled=True
    ).reshape(strip, -1)
    grad_mid_norm, grad_fgain, grad_fbias = norm_backward(
        grad_feed_norm.reshape(seqs, rows, width), feed_unit, feed_std, fgain
    )
    grad_middle = out_cotangent + grad_mid_norm
    grad_out_w = thin_product(flatten(attended_flat), flatten(grad_middle))
    grad_own = mm_nt(flatten(grad_middle), out_w).reshape(seqs, rows, HEADS, head)
    delta = jnp.sum(grad_own * attended, axis=-1)
    back_stats = jnp.pad(jnp.concatenate([log_total, delta], axis=-1), ((0, 0), (0, 0), (0, 128 - 2 * HEADS)))
    grad_blocks, back_blocks = group_gather([grad_own.reshape(seqs, rows, width), back_stats], 5)
    back_all = back_blocks.reshape(seqs, lat, 128).transpose(0, 2, 1)
    logs_all, delta_all = (back_all[:, i * HEADS : (i + 1) * HEADS].reshape(seqs, 8, 128) for i in range(2))

    (query_part, grad_keys, grad_values, own_gk, own_gv), (new_rows,) = attend_back(
        present,
        queries,
        grad_blocks.reshape(seqs, lat, width),
        logs_all,
        delta_all,
        keys,
        values,
        own_keys,
        own_values,
        Summed([new_part]),
        10,
    )
    new_latents = middle + new_rows.reshape(seqs, rows, width)
    grad_queries = flatten(group_sum(query_part, 6))

    grad_query_w = thin_product(own_flat, grad_queries)
    (patch_grads, own_back, media_sums), (sum_query, sum_out) = media_backward(
        feats,
        embed,
        mgain[None],
        grad_keys,
        grad_values,
        own_gk,
        own_gv,
        key_w,
        value_w,
        Summed([grad_query_w, grad_out_w]),
        7,
    )
    grad_own_norm = (mm_nt(grad_queries, query_w) + own_back).reshape(seqs, rows, width)
    grad_lat_in, grad_lgain, grad_lbias = norm_backward(grad_own_norm, own_unit, own_std, lgain)
    latent_grads = grad_middle + grad_lat_in
    grad_mgain, grad_mbias = media_sums[0], media_sums[1]
    slot_sums = media_sums[2:].reshape(seqs, rounds, width)
    grad_table = jnp.sum(jnp.where(one_hot[..., None], slot_sums[:, :, None, :], 0.0), axis=(0, 1))
    vec_grads = jnp.concatenate(
        [jnp.stack([grad_mgain, grad_mbias, grad_lgain, grad_lbias, grad_fgain, grad_fbias]), grad_table], axis=0
    )
    vec_blocks = jnp.pad(vec_grads.reshape(14, 32, strip).transpose(1, 0, 2), ((0, 0), (0, 2), (0, 128 - strip)))
    own_t = stacked(own_flat, 0, (0, 0, 1)).T
    sum_key, sum_value, sum_vec = weight_grads(
        xt_top, xt_low, own_t, grad_keys, grad_values, own_gk, own_gv, vec_blocks.reshape(-1, 128), 8
    )
    vec = sum_vec[:14, :strip]
    return (
        new_latents,
        latent_grads,
        patch_grads.reshape(patch_feats.shape),
        sum_query,
        sum_key,
        sum_value,
        sum_out,
        grad_up,
        grad_down,
        vec[0],
        vec[1],
        vec[2],
        vec[3],
        vec[4],
        vec[5],
        vec[6:],
    )


def solution(mesh):
    fast = dict(mesh.shape) == {"seq": 8, "frame": 4}
    return jax.shard_map(
        body_fast if fast else body_general,
        mesh=mesh,
        in_specs=(
            P("seq", "frame", None),
            P("seq", None, "frame", None, None),
            P("seq"),
            P("seq", None),
            P(("seq", "frame"), None),
            P(("seq", "frame"), None),
            P(("seq", "frame"), None),
            P(("seq", "frame"), None),
            P(("seq", "frame"), None),
            P(("seq", "frame"), None),
            P(("seq", "frame")),
            P(("seq", "frame")),
            P(("seq", "frame")),
            P(("seq", "frame")),
            P(("seq", "frame")),
            P(("seq", "frame")),
            P(None, ("seq", "frame")),
            P("seq", "frame", None),
        ),
        out_specs=(
            P("seq", "frame", None),
            P("seq", "frame", None),
            P("seq", None, "frame", None, None),
            P(("seq", "frame"), None),
            P(("seq", "frame"), None),
            P(("seq", "frame"), None),
            P(("seq", "frame"), None),
            P(("seq", "frame"), None),
            P(("seq", "frame"), None),
            P(("seq", "frame")),
            P(("seq", "frame")),
            P(("seq", "frame")),
            P(("seq", "frame")),
            P(("seq", "frame")),
            P(("seq", "frame")),
            P(None, ("seq", "frame")),
        ),
        check_vma=False,
    )
```
